32 devices in a mesh: dp: 8 (over z, y), tensor: 4 (over x, core).
Axes of the slice: x: 2, y: 2, z: 4, core: 2. Of those that a mesh axis runs over, the one named last changes fastest.
Arguments:
- tokens: bfloat16 [32, 1024, 768], P('dp', 'tensor'), may hold values from -6 to 6
- lengths: int32 [32, 2], P('dp'), may hold values from 1 to 1023, as said below
- cotangent: bfloat16 [32, 1024, 768], P('dp', 'tensor'), may hold values from -6 to 6
- norm_gain: float32 [768], replicated, may hold values from 0.5 to 1.5
- w_z: bfloat16 [768, 1536], P('dp', 'tensor'), may hold values from -0.21875 to 0.21875
- w_x: bfloat16 [768, 1536], P('dp', 'tensor'), may hold values from -0.21875 to 0.21875
- w_bc: bfloat16 [768, 256], P('dp'), may hold values from -0.21875 to 0.21875
- w_dt: bfloat16 [768, 24], P('dp', 'tensor'), may hold values from -0.21875 to 0.21875
- conv_x: float32 [4, 1536], P(None, 'tensor'), may hold values from -3 to 3
- bias_x: float32 [1536], P('tensor'), may hold values from -1.5 to 1.5
- conv_bc: float32 [4, 256], replicated, may hold values from -3 to 3
- bias_bc: float32 [256], replicated, may hold values from -1.5 to 1.5
- dt_bias: float32 [24], P('tensor'), may hold values from -7 to -2
- a_log: float32 [24], P('tensor'), may hold values from 0 to 2.8
- skip_d: float32 [24], P('tensor'), may hold values from 0.5 to 1.5
- out_gain: float32 [1536], P('tensor'), may hold values from 0.5 to 1.5
- w_out: bfloat16 [768, 1536], P('dp', 'tensor'), may hold values from -0.15625 to 0.15625
Outputs:
- output: bfloat16 [32, 1024, 768], P('dp', 'tensor')
- input_grad: bfloat16 [32, 1024, 768], P('dp', 'tensor')
- grad_norm_gain: float32 [768], replicated
- grad_w_z: float32 [768, 1536], P('dp', 'tensor')
- grad_w_x: float32 [768, 1536], P('dp', 'tensor')
- grad_w_bc: float32 [768, 256], P(('dp', 'tensor'))
- grad_w_dt: float32 [768, 24], P('dp', 'tensor')
- grad_conv_x: float32 [4, 1536], P(None, 'tensor')
- grad_bias_x: float32 [1536], P('tensor')
- grad_conv_bc: float32 [4, 256], replicated
- grad_bias_bc: float32 [256], replicated
- grad_dt_bias: float32 [24], P('tensor')
- grad_a_log: float32 [24], P('tensor')
- grad_skip_d: float32 [24], P('tensor')
- grad_out_gain: float32 [1536], P('tensor')
- grad_w_out: float32 [768, 1536], P('dp', 'tensor')
The draws below stay inside these ranges and needn't reach their ends.
Inputs may be any that keep to these rules, and one draw needn't show every extreme that they name: Each row holds the lengths of the two sequences packed from a slot's first position, together at most 1024; the rest of the slot is padding. One of the two is longer than 768.
All inputs are finite; a program needn't handle non-finite values.
Results may differ from the reference program's by a relative error of at most 0.015.
Values may be sent and summed in bfloat16 or wider, within the bound.
No kernel may reach another device: no remote copies, remote signals or barrier semaphores. Data moves between devices by JAX's collectives and lax.ppermute only.
A program may use at most 256 MiB of HBM per device.

```python
import jax
import jax.numpy as jnp
from jax import lax

D = 768
INNER = 1536
HEADS = 24
HEAD_DIM = 64
STATE = 128
CONV = 4
GROUP = 256
SLOT_TOK = 1024
BATCH = 32
SEG_DEV = 256


def draw_lengths(key, part):
    key = jax.random.fold_in(key, 17)
    first_key, second_key, third_key = jax.random.split(key, 3)
    spare = jax.random.randint(first_key, (BATCH,), 0, SEG_DEV - 1)
    spare = jnp.where(jnp.arange(BATCH) == 0, 0, spare)
    longer = SLOT_TOK - 1 - spare
    shorter = jax.random.randint(second_key, (BATCH,), 1, SLOT_TOK - longer + 1)
    order = jax.random.randint(third_key, (BATCH,), 0, 2)
    front = jnp.where(order == 1, longer, shorter)
    behind = jnp.where(order == 1, shorter, longer)
    return jnp.stack([front, behind], axis=1).astype(jnp.int32)


def shard_levels(own_key, dims, shards, low, top_value):
    level, own = 1.0, jax.random.fold_in(own_key, 6)
    for axis_at, shards_of in shards:
        steps = jnp.exp(jax.random.uniform(jax.random.fold_in(own, axis_at), (shards_of,), jnp.float32, low / len(shards), top_value / len(shards)))
        level = level * jnp.repeat(steps, dims[axis_at] // shards_of).reshape([-1 if axis == axis_at else 1 for axis in range(len(dims))])
    return level


def gaussian(key, dims, spread, bound, cuts=(), dtype=jnp.bfloat16):
    entries = spread * jax.random.normal(key, dims, jnp.float32)
    if cuts:
        entries = entries * shard_levels(key, dims, cuts, -0.22, 0.18)
    return jnp.clip(entries, -bound, bound).astype(dtype)


def setup_inputs(seed: int = 0) -> dict:
    streams_of = jax.random.split(jax.random.key(seed), 18)
    return {
        "tokens": gaussian(streams_of[0], (BATCH, SLOT_TOK, D), 1.0, 6.0, ((0, 8), (1, 4))),
        "lengths": draw_lengths(jax.random.fold_in(streams_of[17], 71), 0),
        "cotangent": gaussian(streams_of[2], (BATCH, SLOT_TOK, D), 1.0, 6.0, ((0, 8), (1, 4))),
        "norm_gain": jnp.clip(1.0 + 0.1 * jax.random.normal(streams_of[3], (D,), jnp.float32), 0.5, 1.5),
        "w_z": gaussian(streams_of[4], (D, INNER), D ** -0.5, 0.21875, ((0, 8), (1, 4))),
        "w_x": gaussian(streams_of[5], (D, INNER), D ** -0.5, 0.21875, ((0, 8), (1, 4))),
        "w_bc": gaussian(streams_of[6], (D, 2 * STATE), D ** -0.5, 0.21875, ((0, 8),)),
        "w_dt": gaussian(streams_of[7], (D, HEADS), D ** -0.5, 0.21875, ((0, 8), (1, 4))),
        "conv_x": gaussian(streams_of[8], (CONV, INNER), CONV ** -0.5, 3.0, ((1, 4),), jnp.float32),
        "bias_x": gaussian(streams_of[9], (INNER,), 0.3, 1.5, ((0, 4),), jnp.float32),
        "conv_bc": gaussian(streams_of[10], (CONV, 2 * STATE), CONV ** -0.5, 3.0, (), jnp.float32),
        "bias_bc": gaussian(streams_of[11], (2 * STATE,), 0.3, 1.5, (), jnp.float32),
        "dt_bias": jnp.clip(-7.0 + 5.0 * jax.random.uniform(streams_of[12], (HEADS,), jnp.float32) ** shard_levels(streams_of[12], (HEADS,), ((0, 4),), -0.2, 0.2), -7.0, -2.0),
        "a_log": jnp.clip(2.8 * jax.random.uniform(streams_of[13], (HEADS,), jnp.float32) ** shard_levels(streams_of[13], (HEADS,), ((0, 4),), -0.2, 0.2), 0.0, 2.8),
        "skip_d": jnp.clip(0.5 + 1.0 * jax.random.uniform(streams_of[14], (HEADS,), jnp.float32) ** shard_levels(streams_of[14], (HEADS,), ((0, 4),), -0.2, 0.2), 0.5, 1.5),
        "out_gain": jnp.clip(1.0 + 0.1 * jax.random.normal(streams_of[15], (INNER,), jnp.float32), 0.5, 1.5),
        "w_out": gaussian(streams_of[16], (D, INNER), INNER ** -0.5, 0.15625, ((0, 8), (1, 4))),
    }


EPS = 1e-05
precise = lax.Precision.HIGHEST

@jax.custom_vjp
def low(v):
    return lax.optimization_barrier(v.astype(jnp.bfloat16)).astype(jnp.float32)

@jax.custom_vjp
def low_back(v):
    return v

def low_keep(v):
    return (low(v), None)

def low_pass(kept, grad):
    return (grad,)

def back_keep(v):
    return (v, None)

def back_low(kept, grad):
    return (low(grad),)
low.defvjp(low_keep, low_pass)
low_back.defvjp(back_keep, back_low)

def mat_high(left, right):
    return jnp.dot(left, right, precision=precise)

def causal_conv(values, weight, bias, seg_ids):
    conv_sum = bias + weight[0] * values
    for offset in range(1, CONV):
        shifted = jnp.pad(values, ((offset, 0), (0, 0)))[:-offset]
        shifted_ids = jnp.pad(seg_ids, (offset, 0), constant_values=-1)[:-offset]
        keep_mask = (shifted_ids == seg_ids).astype(jnp.float32)[:, None]
        conv_sum = conv_sum + weight[offset] * shifted * keep_mask
    return conv_sum

def mixer_scan(x_conv, b_in, c_out, step_size, log_decay, skip_d, seg_ids):
    slot_len = x_conv.shape[0]
    group_count = slot_len // GROUP
    x_heads = x_conv.reshape(group_count, GROUP, HEADS, HEAD_DIM)
    b_group = b_in.reshape(group_count, GROUP, STATE)
    c_group = c_out.reshape(group_count, GROUP, STATE)
    step_group = step_size.reshape(group_count, GROUP, HEADS)
    cum_decay = jnp.cumsum(log_decay.reshape(group_count, GROUP, HEADS), axis=1)
    seg_group = seg_ids.reshape(group_count, GROUP)
    places = jnp.arange(GROUP)
    same_seq = (seg_group[:, :, None] == seg_group[:, None, :]) & (places[:, None] >= places[None, :])
    cum_heads = jnp.transpose(cum_decay, (0, 2, 1))
    log_gaps = cum_heads[:, :, :, None] - cum_heads[:, :, None, :]
    inside = same_seq[:, None]
    kernel = jnp.where(inside, jnp.exp(jnp.where(inside, log_gaps, 0.0)), 0.0)
    scores = low_back(jnp.einsum('cqn,ckn->cqk', c_group, b_group, precision=precise))
    step_heads = jnp.transpose(step_group, (0, 2, 1))
    weights = low(scores[:, None] * kernel * step_heads[:, :, None, :])
    within = jnp.einsum('chqk,ckhp->cqhp', weights, x_heads, precision=precise)
    last_seg = seg_group[:, -1]
    tail_mask = (seg_group == last_seg[:, None]).astype(jnp.float32)[:, :, None]
    to_end = jnp.exp(cum_decay[:, -1:, :] - cum_decay) * step_group * tail_mask
    b_weighted = low(to_end[:, :, :, None] * b_group[:, :, None, :])
    states = low_back(jnp.einsum('cqhn,cqhp->chnp', b_weighted, x_heads, precision=precise))
    group_decay = jnp.exp(cum_decay[:, -1, :])
    follows = jnp.concatenate([jnp.zeros((1,), jnp.float32), (last_seg[1:] == last_seg[:-1]).astype(jnp.float32)])
    factors = group_decay * follows[:, None]

    def carry_step(carried, inputs):
        state_now, factor = inputs
        return (factor[:, None, None] * carried + state_now, carried)
    start_state = jnp.zeros((HEADS, STATE, HEAD_DIM), jnp.float32)
    _, previous = lax.scan(carry_step, start_state, (states, factors))
    prev_low = low(previous)
    from_prev = low_back(jnp.einsum('cqn,chnp->cqhp', c_group, prev_low, precision=precise))
    prev_seg = jnp.concatenate([jnp.full((1,), -1, jnp.int32), last_seg[:-1]])
    enters = (seg_group == prev_seg[:, None]).astype(jnp.float32)
    reach_in = jnp.exp(cum_decay) * enters[:, :, None]
    combined = within + reach_in[..., None] * from_prev + skip_d[:, None] * x_heads
    return combined.reshape(slot_len, INNER)

def block_forward(stream, param_set, seg_ids):
    norm_gain, w_z, w_x, w_bc, w_dt, conv_x, bias_x, conv_bc, bias_bc, dt_bias, a_log, skip_d, out_gain, w_out = param_set
    row_scale = lax.rsqrt(lax.optimization_barrier(jnp.mean(stream * stream, axis=-1, keepdims=True)) + EPS)
    normed = low(stream * row_scale * norm_gain)
    gate_in = low_back(mat_high(normed, w_z))
    inner_x = low_back(mat_high(normed, w_x))
    state_in = low_back(mat_high(normed, w_bc))
    dt_raw = low_back(mat_high(normed, w_dt))
    x_conv = low(jax.nn.silu(causal_conv(inner_x, conv_x, bias_x, seg_ids)))
    bc_conv = jax.nn.silu(causal_conv(state_in, conv_bc, bias_bc, seg_ids))
    b_in = low(bc_conv[:, :STATE])
    c_out = low(bc_conv[:, STATE:])
    step_size = jax.nn.softplus(dt_raw + dt_bias)
    decay_rate = -jnp.exp(a_log)
    log_decay = step_size * decay_rate
    mixer_out = low_back(mixer_scan(x_conv, b_in, c_out, step_size, log_decay, skip_d, seg_ids))
    gated_out = mixer_out * jax.nn.silu(gate_in)
    gscale = lax.rsqrt(lax.optimization_barrier(jnp.mean(gated_out * gated_out, axis=-1, keepdims=True)) + EPS)
    gnormed = low(gated_out * gscale * out_gain)
    branch = low_back(mat_high(gnormed, w_out.T))
    return stream + branch

def reference(tokens, lengths, cotangent, norm_gain, w_z, w_x, w_bc, w_dt, conv_x, bias_x, conv_bc, bias_bc, dt_bias, a_log, skip_d, out_gain, w_out):
    params = tuple((v.astype(jnp.float32) for v in (norm_gain, w_z, w_x, w_bc, w_dt, conv_x, bias_x, conv_bc, bias_bc, dt_bias, a_log, skip_d, out_gain, w_out)))
    positions = jnp.arange(SLOT_TOK)

    def one_slot(grad_sums, inputs):
        slot_tokens, slot_lengths, slot_cot = inputs
        first_end = slot_lengths[0]
        second_end = first_end + slot_lengths[1]
        seg_ids = (positions >= first_end).astype(jnp.int32) + (positions >= second_end).astype(jnp.int32)
        valid_rows = (positions < second_end).astype(jnp.float32)[:, None]
        stream = slot_tokens.astype(jnp.float32)

        def apply_block(stream_in, param_set):
            return block_forward(stream_in, param_set, seg_ids)
        layer_out, pull_back = jax.vjp(apply_block, stream, params)
        stream_grad, dparams = pull_back(slot_cot.astype(jnp.float32) * valid_rows)
        grad_sums = jax.tree.map(jnp.add, grad_sums, dparams)
        return (grad_sums, (layer_out.astype(jnp.bfloat16), stream_grad.astype(jnp.bfloat16)))
    zero_grads = tuple((jnp.zeros_like(v) for v in params))
    grad_sums, (outputs, input_grads) = lax.scan(one_slot, zero_grads, (tokens, lengths, cotangent))
    return (outputs, input_grads, grad_sums[0], grad_sums[1], grad_sums[2], grad_sums[3], grad_sums[4], grad_sums[5], grad_sums[6], grad_sums[7], grad_sums[8], grad_sums[9], grad_sums[10], grad_sums[11], grad_sums[12], grad_sums[13])
```

```python
import functools

import jax
import jax.numpy as jnp
from jax import lax
from jax.experimental import pallas as pl
from jax.experimental.pallas import tpu as pltpu
from jax.sharding import PartitionSpec as P

INNER = 1536
L = 256
HD = 64
SPAN = 32
EPS = 1e-05
LOG2E = 1.4426950408889634
F32 = jnp.float32
BF = jnp.bfloat16
VMEM_LIMIT = 56 * 1024 * 1024


def dot(a, b):
    return jnp.dot(a, b, preferred_element_type=F32)


def dot_nt(a, b):
    return lax.dot_general(a, b, (((1,), (1,)), ((), ())), preferred_element_type=F32)


def dot_high(a, b):
    return jnp.dot(a, b, preferred_element_type=F32, precision=lax.Precision.HIGHEST)


def sigmoid(v):
    return 0.5 * jnp.tanh(0.5 * v) + 0.5


def lane_iota(rows):
    return lax.broadcasted_iota(jnp.int32, (rows, 128), 1)


def row_iota(rows, lanes):
    return lax.broadcasted_iota(jnp.int32, (rows, lanes), 0)


def seg_of(idx, fe, se):
    return (idx >= fe).astype(jnp.int32) + (idx >= se).astype(jnp.int32)


def ends(sc, s):
    return sc[2 * s], sc[2 * s + 1]


def cross_mask(rows, k, fe, se):
    idx = row_iota(rows, 1)
    cut = ((idx >= fe) & (idx - k < fe)) | ((idx >= se) & (idx - k < se))
    return jnp.where(cut, 0.0, 1.0).astype(F32)


def pair_cols(cols, first):
    lane = lane_iota(cols.shape[0])
    left = jnp.broadcast_to(cols[:, first : first + 1], cols.shape)
    right = jnp.broadcast_to(cols[:, first + 1 : first + 2], cols.shape)
    return jnp.where(lane < HD, left, right)


def group_cols(cols):
    return jnp.concatenate([pair_cols(cols, 2 * p) for p in range(3)], axis=1)


def head_sum_matrix(offset, rows=384):
    r = lax.broadcasted_iota(jnp.int32, (rows, 128), 0)
    c = lax.broadcasted_iota(jnp.int32, (rows, 128), 1)
    return jnp.where(c == offset + r // HD, 1.0, 0.0)


def to_lane0(packed, s, i):
    return pltpu.roll(packed, (256 - s * SPAN - i * 6) % 128, 1)


def rows_of(s, length=L):
    return pl.ds(pl.multiple_of(s * length, length), length)


def conv_forward(v, h, taps, bias, fe, se):
    ext = jnp.concatenate([h, v], axis=0)
    acc = bias + taps[0] * v
    for k in range(1, 4):
        acc = acc + (taps[k] * pltpu.roll(ext, k, 0)[8:]) * cross_mask(L, k, fe, se)
    return acc


def conv_backward(dconv, v_ext, taps, fe, se):
    zeros = jnp.zeros((8, dconv.shape[1]), F32)
    out, tap_grads = None, []
    for k in range(4):
        part = dconv if k == 0 else dconv * cross_mask(L, k, fe, se)
        ext = jnp.concatenate([zeros, part], axis=0)
        if k:
            ext = pltpu.roll(ext, ext.shape[0] - k, 0)
        tap_grads.append(jnp.sum(ext * v_ext, axis=0, keepdims=True))
        out = taps[k] * ext if out is None else out + taps[k] * ext
    return out, tap_grads


def assemble(dst, blocks, me, at):
    count, rows, width = blocks.shape[1:]
    for n in range(count):
        start = pl.multiple_of((n ^ me) * rows, rows) if count > 1 else 0
        dst[pl.ds(start, rows), at : at + width] = blocks[0, n]


def assemble_either(dst, i, me, mine, other):
    @pl.when(i % 2 == 0)
    def _():
        for blocks, at in mine:
            assemble(dst, blocks, me, at)

    @pl.when(i % 2 == 1)
    def _():
        for blocks, at in other:
            assemble(dst, blocks, me, at)


def k1_body(
    sc, tok, halo, gain, wam, war, wbm, wbr, par, cbc, bbc,
    nrm, xo, dslo, inno, sto, blow, clow, sin, dbc, pk, ct,
    wbuf, innx, dtacc, bt,
):
    ph = pl.program_id(0)
    i = pl.program_id(1)
    me_t, me_dp = sc[8], sc[9]
    t = i ^ me_t

    @pl.when((ph == 0) & (i == 0))
    def _():
        def norm(v):
            v = v.astype(F32)
            r = lax.rsqrt(jnp.mean(v * v, axis=-1, keepdims=True) + EPS)
            return (v * r * gain[...]).astype(BF)

        @pl.loop(0, 4)
        def _(s):
            nrm[rows_of(s)] = norm(tok[rows_of(s)])

        nrm[4 * L :] = norm(halo[...])
        dtacc[...] = jnp.zeros_like(dtacc)
        sin[...] = jnp.zeros_like(sin)

    @pl.when(ph == 0)
    def _():
        assemble_either(wbuf, i, me_dp, [(wam, 0), (wbm, 256)], [(war, 0), (wbr, 256)])
        turn = 64 * (t % 2)

        @pl.loop(0, 4)
        def _(s):
            p = dot(nrm[rows_of(s)], wbuf[...])
            innx[i, rows_of(s)] = p[:, :384]
            last = p[:, 384:]
            lane = lane_iota(L)
            sin[t // 2, rows_of(s)] += pltpu.roll(jnp.where(lane < 64, last, 0.0), turn, 1)
            dtacc[...] += pltpu.roll(
                jnp.where(lane >= 64, last, 0.0), (s * SPAN + i * 6 + 64) % 128, 1
            )

        p = dot(nrm[4 * L :], wbuf[...])
        innx[i, 4 * L :] = p[:, :384]
        sin[t // 2, 4 * L :] += pltpu.roll(jnp.where(lane_iota(64) < 64, p[:, 384:], 0.0), turn, 1)

    @pl.when((ph == 0) & (i == 3))
    def _():
        for q, low_out in ((0, blow), (1, clow)):
            cols = slice(128 * q, 128 * q + 128)
            taps = [cbc[k : k + 1, cols] for k in range(4)]

            @pl.loop(0, 4)
            def _(s):
                fe, se = sc[2 * s], sc[2 * s + 1]
                h = sin[q, pl.ds(pl.multiple_of(4 * L + 16 * s + 8, 8), 8)]
                acc = conv_forward(sin[q, rows_of(s)], h, taps, bbc[:, cols], fe, se)
                sg = sigmoid(acc)
                low = (acc * sg).astype(BF)
                low_out[rows_of(s)] = low
                dbc[q, rows_of(s)] = sg * (1.0 + acc * (1.0 - sg))
                if q == 0:
                    bt[s] = (acc * sg).T.astype(BF)

        dtb = jnp.zeros((1, 128), F32)
        alog = jnp.zeros((1, 128), F32)
        for g in range(4):
            for s in range(4):
                dtb += pltpu.roll(par[g, 6:7, :128], s * SPAN + g * 6, 1)
                alog += pltpu.roll(par[g, 7:8, :128], s * SPAN + g * 6, 1)
        raw = dtacc[...] + dtb
        step = jnp.maximum(raw, 0.0) + jnp.log1p(jnp.exp(-jnp.abs(raw)))
        sig = 1.0 / (1.0 + jnp.exp(-raw))
        decay = step * -jnp.exp(alog)
        lower = jnp.where(
            lax.broadcasted_iota(jnp.int32, (L, L), 0) >= lax.broadcasted_iota(jnp.int32, (L, L), 1),
            1.0,
            0.0,
        )
        cum = dot_high(lower, decay)
        row = row_iota(L, 128)
        slot = lane_iota(L) // SPAN
        tail = jnp.zeros((L, 128), F32)
        enters = jnp.zeros((L, 128), F32)
        follows = jnp.zeros((8, 128), F32)
        slot8 = lane_iota(8) // SPAN
        inner_block = jnp.where(me_t > 0, 1.0, 0.0)
        for s in range(4):
            fe, se = ends(sc, s)
            seg = seg_of(row, fe, se)
            last = seg_of(L - 1, fe, se)
            before = seg_of(-1, fe, se)
            here = slot == s
            tail = jnp.where(here & (seg == last), 1.0, tail)
            enters = jnp.where(here & (seg == before), inner_block, enters)
            follows = jnp.where(
                (slot8 == s), jnp.where(last == before, inner_block, 0.0), follows
            )
        cum_last = cum[L - 1 : L]
        cum2 = cum * LOG2E
        pk[0] = cum2
        pk[1] = step
        pk[2] = sig
        pk[3] = jnp.exp(cum_last - cum) * step * tail
        pk[4] = jnp.exp(cum) * enters
        pk[5] = decay
        pk[6] = jnp.broadcast_to(jnp.exp(cum_last) * follows[0:1], (L, 128))
        ct[...] = cum2.T

    @pl.when(ph == 1)
    def _():
        taps = [par[i, k : k + 1] for k in range(4)]
        bias = par[i, 4:5]

        @pl.loop(0, 4)
        def _(s):
            fe, se = sc[2 * s], sc[2 * s + 1]
            v = innx[i, rows_of(s)]
            h = innx[i, pl.ds(pl.multiple_of(4 * L + 16 * s + 8, 8), 8)]
            acc = conv_forward(v, h, taps, bias, fe, se)
            sg = sigmoid(acc)
            low = (acc * sg).astype(BF)
            xo[0, rows_of(s)] = low
            dslo[0, rows_of(s)] = (sg * (1.0 + acc * (1.0 - sg))).astype(BF)
            inno[0, rows_of(s)] = v.astype(BF)
            te = group_cols(to_lane0(pk[3], s, i))
            xs = (low.astype(F32) * te).astype(BF)
            sto[rows_of(s, 128)] = dot(bt[s], xs).astype(BF)

        inno[0, 4 * L :] = innx[i, 4 * L :].astype(BF)
        high, rest = [], []
        for s in range(4):
            f = group_cols(to_lane0(pk[6, 0:8], s, i))[0:1]
            high.append(f)
        f = jnp.concatenate(high, axis=0)
        fh = f.astype(BF).astype(F32)
        sto[512:528] = jnp.concatenate([fh, f - fh, jnp.zeros((8, 384), F32)], axis=0).astype(BF)


def k2_body(sc, nrm, wm, wr, x, blow, clow, pk, ct, gate, within, wbuf, scores):
    i = pl.program_id(0)
    me_dp = sc[9]
    assemble_either(wbuf, i, me_dp, [(wm, 0)], [(wr, 0)])

    @pl.when(i == 0)
    def _():
        @pl.loop(0, 4)
        def _(s):
            fe, se = sc[2 * s], sc[2 * s + 1]
            q = lax.broadcasted_iota(jnp.int32, (L, L), 0)
            k = lax.broadcasted_iota(jnp.int32, (L, L), 1)
            same = (q >= k) & (seg_of(q, fe, se) == seg_of(k, fe, se))
            scores[s] = jnp.where(same, dot_nt(clow[rows_of(s)], blow[rows_of(s)]), 0.0)

    @pl.loop(0, 4)
    def _(s):
        gate[0, rows_of(s)] = dot(nrm[rows_of(s)], wbuf[...])
        cum = to_lane0(pk[0], s, i)
        step = to_lane0(pk[1], s, i)
        lane = lane_iota(L)
        for p in range(3):
            xs = x[0, rows_of(s), 128 * p : 128 * p + 128].astype(F32) * pair_cols(step, 2 * p)
            top = jnp.zeros((128, 128), F32)
            low = jnp.zeros((128, 128), F32)
            for b in range(2):
                h = 2 * p + b
                half = jnp.where((lane < HD) == (b == 0), xs, 0.0).astype(BF)
                cq = cum[:, h : h + 1]
                ck = ct[pl.ds(s * SPAN + i * 6 + h, 1), :]
                g0 = jnp.minimum(cq[:128] - ck[:, :128], 0.0)
                w0 = (jnp.exp2(g0) * scores[s, :128, :128]).astype(BF)
                g1 = jnp.minimum(cq[128:] - ck, 0.0)
                w1 = (jnp.exp2(g1) * scores[s, 128:, :]).astype(BF)
                top = top + dot(w0, half[:128])
                low = low + dot(w1, half)
            within[0, pl.ds(pl.multiple_of(s * L, L), 128), 128 * p : 128 * p + 128] = top
            within[0, pl.ds(pl.multiple_of(s * L + 128, 128), 128), 128 * p : 128 * p + 128] = low


def k3_body(
    sc, within, gate_in, x, r1, r2, r3, pk, clow, par, wm, wr, tok, cot,
    out, gno, dgo, dyo, dpo, dpk, dco, small,
    mo, gt, scaled, prev, sums, branch, dbr, wbuf, frow,
):
    ph = pl.program_id(0)
    i = pl.program_id(1)
    me_t, me_dp = sc[8], sc[9]

    @pl.when((ph == 0) & (i == 0))
    def _():
        sums[...] = jnp.zeros_like(sums)
        branch[...] = jnp.zeros_like(branch)
        dpk[...] = jnp.zeros_like(dpk)
        dco[...] = jnp.zeros_like(dco)
        small[...] = jnp.zeros_like(small)

        @pl.loop(0, 4)
        def _(s):
            se = sc[2 * s + 1]
            keep = row_iota(L, 1) < se
            dbr[rows_of(s)] = jnp.where(keep, cot[rows_of(s)].astype(F32), 0.0).astype(BF)

    def reach_of(s):
        return group_cols(to_lane0(pk[4], s, i))

    @pl.when(ph == 0)
    def _():
        frow[...] = r1[512:528].astype(F32)

        @pl.loop(0, 4)
        def _(s):
            srow = rows_of(s, 128)
            f = frow[pl.ds(s, 1)] + frow[pl.ds(s + 4, 1)]
            pv = r1[srow].astype(F32) + r2[srow].astype(F32) + f * r3[srow].astype(F32)
            pv = pv.astype(BF)
            prev[i, srow] = pv
            from_prev = dot(clow[rows_of(s)], pv)
            xf = x[0, rows_of(s)].astype(F32)
            mixed = within[0, rows_of(s)] + reach_of(s) * from_prev + par[i, 8:9] * xf
            gv = gate_in[0, rows_of(s)]
            gated = mixed * (gv * sigmoid(gv))
            mo[i, rows_of(s)] = mixed
            gt[i, rows_of(s)] = gv
            sums[0, rows_of(s)] += jnp.sum(gated * gated, axis=1, keepdims=True)

    @pl.when(ph == 1)
    def _():
        assemble_either(wbuf, i, me_dp, [(wm, 0)], [(wr, 0)])
        gain = par[i, 5:6]

        @pl.loop(0, 4)
        def _(s):
            r = rows_of(s)
            gscale = lax.rsqrt(sums[0, r, 0:1] * (1.0 / INNER) + EPS)
            gv = gt[i, r]
            gated = mo[i, r] * (gv * sigmoid(gv))
            gs = gated * gscale
            gn = (gs * gain).astype(BF)
            gno[0, r] = gn
            branch[r] += dot_nt(gn, wbuf[...])
            dgn = dot(dbr[r], wbuf[...])
            small[i, 0:1] += jnp.sum(dgn * gs, axis=0, keepdims=True)
            sv = dgn * gain
            scaled[i, r] = sv
            sums[1, r] += jnp.sum(sv * gated, axis=1, keepdims=True)

    @pl.when((ph == 1) & (i == 3))
    def _():
        @pl.loop(0, 4)
        def _(s):
            r = rows_of(s)
            out[r] = (tok[r].astype(F32) + branch[r]).astype(BF)

    @pl.when(ph == 2)
    def _():
        @pl.loop(0, 4)
        def _(s):
            r = rows_of(s)
            srow = rows_of(s, 128)
            gscale = lax.rsqrt(sums[0, r, 0:1] * (1.0 / INNER) + EPS)
            coef = gscale * gscale * gscale * (sums[1, r, 0:1] * (1.0 / INNER))
            gv = gt[i, r]
            mixed = mo[i, r]
            sg = sigmoid(gv)
            silu = gv * sg
            dgated = gscale * scaled[i, r] - (mixed * silu) * coef
            dgo[0, r] = (dgated * mixed * (sg * (1.0 + gv * (1.0 - sg)))).astype(BF)
            dy = (dgated * silu).astype(BF)
            dyo[0, r] = dy
            dyf = dy.astype(F32)
            dprev = dyf * reach_of(s)
            dlow = dprev.astype(BF)
            pv = prev[i, srow]
            cs = clow[r]
            from_prev = dot(cs, pv)
            dco[r] += dot_nt(dlow, pv)
            dpo[srow] = lax.dot_general(
                cs, dlow, (((0,), (0,)), ((), ())), preferred_element_type=F32
            ).astype(BF)
            pick = head_sum_matrix(s * SPAN + i * 6).astype(BF)
            dpk[...] += dot((dprev * from_prev).astype(BF), pick)
            small[i, 1:2] += jnp.sum(dyf * x[0, r].astype(F32), axis=0, keepdims=True)

        high = []
        for s in range(4):
            high.append(group_cols(to_lane0(pk[6, 0:8], s, i))[0:1])
        f = jnp.concatenate(high, axis=0)
        fh = f.astype(BF).astype(F32)
        dpo[512:528] = jnp.concatenate([fh, f - fh, jnp.zeros((8, 384), F32)], axis=0).astype(BF)


def put_grad(i, me_dp, keep, send, value, at):
    count, rows = keep.shape[1], keep.shape[2]
    width = value.shape[1]

    def store(ref):
        for n in range(count):
            part = value[n * rows : (n + 1) * rows].astype(BF)
            if count > 1:
                ref[i // 2, n ^ me_dp, :, at : at + width] = part
            else:
                ref[i // 2, 0, :, at : at + width] = part

    @pl.when(i % 2 == 0)
    def _():
        store(keep)

    @pl.when(i % 2 == 1)
    def _():
        store(send)


def k4_body(
    sc, nrm, cot, gn, dg, wm, wr, ok, os, zk, zs, dn, nt, dt, wbuf,
):
    i = pl.program_id(0)
    me_dp = sc[9]

    @pl.when(i == 0)
    def _():
        @pl.loop(0, 4)
        def _(s):
            r = rows_of(s)
            nt[:, r] = nrm[r].T
            keep = row_iota(L, 1) < sc[2 * s + 1]
            dt[:, r] = jnp.where(keep, cot[r].astype(F32), 0.0).T.astype(BF)

        dn[...] = jnp.zeros_like(dn)

    assemble_either(wbuf, i, me_dp, [(wm, 0)], [(wr, 0)])
    put_grad(i, me_dp, ok, os, dot(dt[...], gn[0]), 0)
    put_grad(i, me_dp, zk, zs, dot(nt[...], dg[0]), 0)

    @pl.loop(0, 4)
    def _(s):
        dn[rows_of(s)] += dot_nt(dg[0, rows_of(s)], wbuf[...])


def k5_body(sc, x, dy, blow, clow, pk, ct, par, dxo, bco, pko, scores, dsc, rowl):
    i = pl.program_id(0)

    @pl.when(i == 0)
    def _():
        pko[...] = jnp.zeros_like(pko)
        dsc[...] = jnp.zeros_like(dsc)
        rowl[...] = jnp.zeros_like(rowl)

        @pl.loop(0, 4)
        def _(s):
            fe, se = sc[2 * s], sc[2 * s + 1]
            k = lax.broadcasted_iota(jnp.int32, (L, L), 0)
            q = lax.broadcasted_iota(jnp.int32, (L, L), 1)
            same = (q >= k) & (seg_of(q, fe, se) == seg_of(k, fe, se))
            scores[s] = jnp.where(same, dot_nt(blow[rows_of(s)], clow[rows_of(s)]), 0.0)

    @pl.loop(0, 4)
    def _(s):
        cum = to_lane0(pk[0], s, i)
        step = to_lane0(pk[1], s, i)
        lane = lane_iota(L)
        lane_half = lane_iota(128)
        col_top = jnp.zeros((128, 128), F32)
        col_low = jnp.zeros((128, 128), F32)
        for p in range(3):
            cols = slice(128 * p, 128 * p + 128)
            dyp = dy[0, rows_of(s), cols]
            dyf = dyp.astype(F32)
            steps = pair_cols(step, 2 * p)
            xs = x[0, rows_of(s), cols].astype(F32) * steps
            top = jnp.zeros((128, 128), F32)
            low = jnp.zeros((128, 128), F32)
            for b in range(2):
                h = 2 * p + b
                mine = (lane < HD) == (b == 0)
                xh = jnp.where(mine, xs, 0.0).astype(BF)
                dyh = jnp.where(mine, dyf, 0.0).astype(BF)
                ck = cum[:, h : h + 1]
                row = s * SPAN + i * 6 + h
                cq = ct[pl.ds(row, 1), :]
                kern = jnp.exp2(jnp.minimum(cq - ck[:128], 0.0))
                grad = dot_nt(xh[:128], dyp) * kern
                sc0 = scores[s, :128, :]
                wt = (kern * sc0).astype(BF)
                dsc[s, :128, :] += grad
                lg = grad * sc0
                col_top = jnp.where(lane_half == h, jnp.sum(lg, axis=1, keepdims=True), col_top)
                over_k = jnp.sum(lg, axis=0, keepdims=True)
                top = top + dot(wt, dyh)
                kern = jnp.exp2(jnp.minimum(cq[:, 128:] - ck[128:], 0.0))
                grad = dot_nt(xh[128:], dyp[128:]) * kern
                sc1 = scores[s, 128:, 128:]
                wt = (kern * sc1).astype(BF)
                dsc[s, 128:, 128:] += grad
                lg = grad * sc1
                col_low = jnp.where(lane_half == h, jnp.sum(lg, axis=1, keepdims=True), col_low)
                over_low = jnp.sum(lg, axis=0, keepdims=True)
                low = low + dot(wt, dyh[128:])
                rowl[pl.ds(row, 1), :] = over_k + jnp.concatenate(
                    [jnp.zeros((1, 128), F32), over_low], axis=1
                )
            skip = par[i, 8:9, cols]
            dxo[0, rows_of(s), cols] = (
                jnp.concatenate([top, low], axis=0) * steps + skip * dyf
            )
        col = jnp.concatenate([col_top, col_low], axis=0)
        pko[0] += pltpu.roll(col, s * SPAN + i * 6, 1)

    @pl.when(i == 3)
    def _():
        pko[1] = rowl[...].T - pko[0]

        @pl.loop(0, 4)
        def _(s):
            fe, se = sc[2 * s], sc[2 * s + 1]
            k = lax.broadcasted_iota(jnp.int32, (L, L), 0)
            q = lax.broadcasted_iota(jnp.int32, (L, L), 1)
            same = (q >= k) & (seg_of(q, fe, se) == seg_of(k, fe, se))
            ds = jnp.where(same, dsc[s], 0.0)
            bco[0, rows_of(s)] = dot(ds.astype(BF), clow[rows_of(s)])
            bco[1, rows_of(s)] = dot(ds.T.astype(BF), blow[rows_of(s)])


def k6_body(
    sc, nrm, x, dsl, inn, dxl, q1, q2, q3, r1, r2, r3, blow, pk, par, cbc,
    bc5, dc3, dpk3, pk5, sin, dbc, wam, war, wbm, wbr, dnz,
    gk, gs, dn, small, sbc, sdt,
    nt, wbuf, wbc, din, dbacc, dte, dfac, gbuf, fqrow, frow,
):
    i = pl.program_id(0)
    me_t, me_dp = sc[8], sc[9]

    @pl.when(i == 0)
    def _():
        @pl.loop(0, 4)
        def _(s):
            r = rows_of(s)
            nt[:, r] = nrm[r].T

        nt[:, 4 * L :] = nrm[4 * L :].T
        dn[0 : 4 * L] = dnz[...]
        dn[4 * L :] = jnp.zeros((64, dn.shape[1]), F32)
        dbacc[...] = jnp.zeros_like(dbacc)
        dte[...] = jnp.zeros_like(dte)
        dfac[...] = jnp.zeros_like(dfac)
        small[...] = jnp.zeros_like(small)

    @pl.when(i < 4)
    def _():
        assemble_either(wbuf, i, me_dp, [(wam, 0), (wbm, 256)], [(war, 0), (wbr, 256)])
        wbc[i] = wbuf[:, 384:]
        taps = [par[i, k : k + 1] for k in range(4)]
        fqrow[...] = q1[512:528].astype(F32)
        frow[...] = r1[512:528].astype(F32)

        @pl.loop(0, 4)
        def _(s):
            fe, se = sc[2 * s], sc[2 * s + 1]
            r = rows_of(s)
            srow = rows_of(s, 128)
            fq = fqrow[pl.ds(s, 1)] + fqrow[pl.ds(s + 4, 1)]
            g = q1[srow].astype(F32) + q2[srow].astype(F32) + fq * q3[srow].astype(F32)
            fr = frow[pl.ds(s, 1)] + frow[pl.ds(s + 4, 1)]
            pv = r1[srow].astype(F32) + r2[srow].astype(F32) + fr * r3[srow].astype(F32)
            pick = head_sum_matrix(s * SPAN + i * 6)
            gp = jnp.broadcast_to(jnp.sum(g * pv, axis=0, keepdims=True), (8, 384))
            dfac[...] += dot_high(gp, pick)
            glow = g.astype(BF)
            u = dot(blow[r], glow)
            te = group_cols(to_lane0(pk[3], s, i))
            xf = x[0, r].astype(F32)
            dte[...] += dot((xf * u).astype(BF), pick.astype(BF))
            dbacc[r] += dot_nt((te * xf).astype(BF), glow)
            dconv = (dxl[0, r] + te * u) * dsl[0, r].astype(F32)
            small[i, 4:5] += jnp.sum(dconv, axis=0, keepdims=True)
            hrow = pl.ds(pl.multiple_of(4 * L + 16 * s, 16), 16)
            v_ext = jnp.concatenate(
                [inn[0, hrow].astype(F32)[8:], inn[0, r].astype(F32)], axis=0
            )
            dv, tap_grads = conv_backward(dconv, v_ext, taps, fe, se)
            for k in range(4):
                small[i, k : k + 1] += tap_grads[k]
            din[r] = dv[8:].astype(BF)
            din[hrow] = jnp.concatenate([jnp.zeros((8, 384), F32), dv[:8]], axis=0).astype(BF)
            dn[r] += dot_nt(din[r], wbuf[:, :384])

        dn[4 * L :] += dot_nt(din[4 * L :], wbuf[:, :384])
        put_grad(i, me_dp, gk, gs, dot(nt[...], din[...]), 0)

    @pl.when(i == 4)
    def _():
        for q in range(2):
            taps = [cbc[k : k + 1, 128 * q : 128 * q + 128] for k in range(4)]
            sbc[q] = jnp.zeros((8, 128), F32)

            @pl.loop(0, 4)
            def _(s):
                fe, se = sc[2 * s], sc[2 * s + 1]
                r = rows_of(s)
                grad = bc5[q, r] + (dbacc[r] if q == 0 else dc3[r])
                dconv = grad * dbc[q, r]
                hrow = pl.ds(pl.multiple_of(4 * L + 16 * s, 16), 16)
                v_ext = jnp.concatenate([sin[q, hrow][8:], sin[q, r]], axis=0)
                dv, tap_grads = conv_backward(dconv, v_ext, taps, fe, se)
                sbc[q, 4:5] += jnp.sum(dconv, axis=0, keepdims=True)
                for k in range(4):
                    sbc[q, k : k + 1] += tap_grads[k]
                gbuf[q, r] = dv[8:]
                gbuf[q, hrow] = jnp.concatenate([jnp.zeros((8, 128), F32), dv[:8]], axis=0)

        end_terms = dte[...] * pk[3]
        row = row_iota(L, 128)
        last = jnp.sum(end_terms, axis=0, keepdims=True) + dfac[0:1] * pk[6, 0:1]
        dcum = dpk3[...] + pk5[1] - end_terms + jnp.where(row == L - 1, last, 0.0)
        upper = jnp.where(
            lax.broadcasted_iota(jnp.int32, (L, L), 0) <= lax.broadcasted_iota(jnp.int32, (L, L), 1),
            1.0,
            0.0,
        )
        dlog = dot_high(upper, dcum)
        alog = jnp.zeros((1, 128), F32)
        for g in range(4):
            for s in range(4):
                alog += pltpu.roll(par[g, 7:8, :128], s * SPAN + g * 6, 1)
        step, sig = pk[1], pk[2]
        ratio = jnp.where(step > 1e-30, sig / jnp.maximum(step, 1e-30), 1.0)
        ddt = ratio * (pk5[0] + end_terms) - sig * jnp.exp(alog) * dlog
        sdt[...] = jnp.concatenate(
            [
                jnp.sum(ddt, axis=0, keepdims=True),
                jnp.sum(dlog * pk[5], axis=0, keepdims=True),
                jnp.zeros((6, 128), F32),
            ],
            axis=0,
        )
        for n in range(4):
            t = n ^ me_t
            turn = (64 * (t % 2)) % 128
            lane = lane_iota(L)

            @pl.loop(0, 4)
            def _(s):
                r = rows_of(s)
                a = pltpu.roll(gbuf[t // 2, r], turn, 1)
                d = pltpu.roll(ddt, (320 - s * SPAN - n * 6) % 128, 1)
                piece = jnp.where(lane < 64, a, jnp.where(lane < 70, d, 0.0)).astype(BF)
                din[r, 0:128] = piece
                dn[r] += dot_nt(piece, wbc[n])

            a = pltpu.roll(gbuf[t // 2, 4 * L :], turn, 1)
            piece = jnp.where(lane_iota(64) < 64, a, 0.0).astype(BF)
            din[4 * L :, 0:128] = piece
            dn[4 * L :] += dot_nt(piece, wbc[n])
            put_grad_static(n, me_dp, gk, gs, dot(nt[...], din[:, 0:128]), 384)


def put_grad_static(n, me_dp, keep, send, value, at):
    ref = keep if n % 2 == 0 else send
    count, rows = ref.shape[1], ref.shape[2]
    width = value.shape[1]
    for m in range(count):
        part = value[m * rows : (m + 1) * rows].astype(BF)
        place = m ^ me_dp if count > 1 else 0
        ref[n // 2, place, :, at : at + width] = part


def k7_body(sc, dn, hr, tok, cot, gain, ig, ng):
    s = pl.program_id(0)

    @pl.when(s == 0)
    def _():
        ng[...] = jnp.zeros_like(ng)

    d = dn[...]
    extra = hr[...].astype(F32)
    width = d.shape[1]
    d = jnp.concatenate([d[: L - 16], d[L - 16 :] + extra], axis=0)
    tv = tok[...].astype(F32)
    r = lax.rsqrt(jnp.mean(tv * tv, axis=-1, keepdims=True) + EPS)
    tr = tv * r
    ng[0:1] += jnp.sum(d * tr, axis=0, keepdims=True)
    gd = gain[...] * d
    inner = jnp.sum(gd * tr, axis=-1, keepdims=True) * (1.0 / width)
    keep = row_iota(L, 1) < sc[2 * s + 1]
    res = jnp.where(keep, cot[...].astype(F32), 0.0)
    ig[...] = (res + r * (gd - tr * inner)).astype(BF)


def full(shape):
    return pl.BlockSpec(shape, lambda *a: (0,) * len(shape))


def call(body, grid, in_specs, out_specs, out_shapes, scratch, cost, name):
    flops, moved = cost
    return pl.pallas_call(
        body,
        grid_spec=pltpu.PrefetchScalarGridSpec(
            num_scalar_prefetch=1,
            grid=grid,
            in_specs=in_specs,
            out_specs=out_specs,
            scratch_shapes=scratch,
        ),
        out_shape=out_shapes,
        compiler_params=pltpu.CompilerParams(vmem_limit_bytes=VMEM_LIMIT),
        cost_estimate=pl.CostEstimate(flops=flops, bytes_accessed=moved, transcendentals=0),
        name=name,
    )


def sds(shape, dtype):
    return jax.ShapeDtypeStruct(shape, dtype)


def flip(value, axis, bit):
    count = lax.axis_size(axis)
    return lax.ppermute(value, axis, [(a, a ^ bit) for a in range(count)])


def stack2(a, b, at):
    return jnp.stack([a, b], axis=at)


def per_device(
    tokens, lengths, cotangent, norm_gain, w_z, w_x, w_bc, w_dt, conv_x, bias_x, conv_bc, bias_bc,
    dt_bias, a_log, skip_d, out_gain, w_out,
):
    tcount = lax.axis_size("tensor")
    dpcount = lax.axis_size("dp")
    me_t = lax.axis_index("tensor")
    me_dp = lax.axis_index("dp")
    slots, own_len, dim = tokens.shape
    rows = slots * own_len
    shard = w_z.shape[0]
    cols = w_z.shape[1]
    heads = w_dt.shape[1]
    fast = shard % 16 == 0 and dpcount & (dpcount - 1) == 0 and dpcount >= 2
    count = dpcount if fast else 1
    brow = shard if fast else dim

    first = lengths[:, 0] - me_t * own_len
    second = first + lengths[:, 1]
    sc = jnp.concatenate(
        [
            jnp.stack([first, second], axis=1).reshape(-1),
            jnp.stack([me_t, me_dp]),
            jnp.zeros((6,), jnp.int32),
        ]
    ).astype(jnp.int32)
    tok = tokens.reshape(rows, dim)
    cot = cotangent.reshape(rows, dim)
    gain = norm_gain.reshape(1, dim)

    bq = w_bc.shape[1] // tcount
    state = w_bc.shape[1] // 2
    own_bc = lax.dynamic_slice_in_dim(w_bc, me_t * bq, bq, 1)
    p1 = jnp.concatenate(
        [w_x, own_bc, w_dt, jnp.zeros((shard, 128 - bq - heads), BF)], axis=1
    )
    tail = tokens[:, own_len - 16 :, :].reshape(slots * 16, dim)
    halo = lax.ppermute(tail, "tensor", [(a, a + 1) for a in range(tcount - 1)])

    def gather_z(v):
        v = v[None]
        bit = dpcount // 2
        while bit > 1:
            v = stack2(v, flip(v, "dp", bit), 1)
            v = v.reshape((-1,) + v.shape[2:])
            bit //= 2
        return v

    def add_y(v, at):
        return stack2(v, flip(v, "dp", 1), at)

    def add_x(v):
        return stack2(v, flip(v, "tensor", 2), 0)

    def order_xy(v):
        v = add_y(add_x(v), 2)
        return v.reshape(2, count, brow, v.shape[-1])

    def order_yx(v):
        v = add_x(add_y(v, 1))
        return v.reshape(2, count, brow, v.shape[-1])

    def core(v):
        return flip(v, "tensor", 1)

    if fast:
        z1 = gather_z(p1)
        wam = order_xy(z1[..., :256])
        wbm = order_yx(z1[..., 256:])
    else:
        z1 = lax.all_gather(p1, "dp", axis=0, tiled=True)[None]
        wam = add_x(z1[..., :256])
        wbm = add_x(z1[..., 256:])
    war, wbr = core(wam), core(wbm)
    if fast:
        z2 = gather_z(jnp.stack([w_z, w_out]))
        wzm = order_xy(z2[:, 0])
        wom = order_yx(z2[:, 1])
    else:
        wzm = add_x(lax.all_gather(w_z, "dp", axis=0, tiled=True)[None])
        wom = add_x(lax.all_gather(w_out, "dp", axis=0, tiled=True)[None])
    wzr, wor = core(wzm), core(wom)

    def lanes(v):
        return jnp.pad(v, (0, cols - v.shape[0]))[None]

    par = jnp.concatenate(
        [
            conv_x,
            bias_x[None],
            out_gain[None],
            lanes(dt_bias),
            lanes(a_log),
            jnp.repeat(skip_d, cols // heads)[None],
            jnp.zeros((7, cols), F32),
        ],
        axis=0,
    )
    par = add_x(par)
    par = stack2(par, core(par), 1).reshape(4, 16, cols)
    bbc = bias_bc.reshape(1, -1)

    srows = slots * state
    wblock = (1, count, brow, 256)
    wide = (1, count, brow, cols)
    group = (1, rows, cols)
    erows = rows + 64

    def by_phase(phase, rank):
        def index(p, i, sc):
            return (jnp.where(p == phase, i, jnp.where(p < phase, 0, 3)),) + (0,) * (rank - 1)

        return index

    def w_phase(phase):
        def index(p, i, sc):
            return (jnp.where(p == phase, i // 2, jnp.where(p < phase, 0, 1)), 0, 0, 0)

        return index

    def abs_phase(phase):
        def index(p, i, sc):
            return (0, jnp.where(p == phase, i, jnp.where(p < phase, 0, 3)) ^ sc[8])

        return index

    nrm, xl, dsl, inn, st, blow, clow, sin, dbc, pk, ct = call(
        k1_body,
        (2, 4),
        [full((rows, dim)), full((64, dim)), full((1, dim))]
        + [pl.BlockSpec(wblock, w_phase(0))] * 4
        + [full((4, 16, cols)), full((4, 2 * state)), full((1, 2 * state))],
        [
            full((erows, dim)),
            pl.BlockSpec(group, by_phase(1, 3)),
            pl.BlockSpec(group, by_phase(1, 3)),
            pl.BlockSpec((1, erows, cols), by_phase(1, 3)),
            pl.BlockSpec((srows + 16, cols), abs_phase(1)),
            full((rows, state)),
            full((rows, state)),
            full((2, erows, state)),
            full((2, rows, state)),
            full((7, L, 128)),
            full((128, L)),
        ],
        [
            sds((erows, dim), BF),
            sds((4, rows, cols), BF),
            sds((4, rows, cols), BF),
            sds((4, erows, cols), BF),
            sds((srows + 16, 4 * cols), BF),
            sds((rows, state), BF),
            sds((rows, state), BF),
            sds((2, erows, state), F32),
            sds((2, rows, state), F32),
            sds((7, L, 128), F32),
            sds((128, L), F32),
        ],
        [
            pltpu.VMEM((dim, 512), BF),
            pltpu.VMEM((4, erows, cols), F32),
            pltpu.VMEM((L, 128), F32),
            pltpu.VMEM((4, state, L), BF),
        ],
        (int(8e9), int(4e7)),
        "project_and_states",
    )(sc, tok, halo, gain, wam, war, wbm, wbr, par, conv_bc, bbc)

    def carry(mine, hops):
        one = lax.ppermute(mine, "tensor", hops[0])
        f = mine[srows : srows + 4].astype(F32) + mine[srows + 4 : srows + 8].astype(F32)
        width = mine.shape[1]
        end = mine[:srows].astype(F32).reshape(slots, state, width) + f[:, None] * one[
            :srows
        ].astype(F32).reshape(slots, state, width)
        end = end.astype(BF).reshape(srows, width)
        two = lax.ppermute(end, "tensor", hops[1])
        three = lax.ppermute(two, "tensor", hops[2])
        return one, two, three

    r1, r2, r3 = carry(st, ([(0, 1), (2, 3)], [(1, 2)], [(2, 3)]))

    def by_i(rank):
        return lambda i, sc: (jnp.minimum(i, 3),) + (0,) * (rank - 1)

    def w_i(i, sc):
        return (jnp.minimum(i, 3) // 2, 0, 0, 0)

    def abs_i(i, sc):
        return (0, jnp.minimum(i, 3) ^ sc[8])

    gate, within = call(
        k2_body,
        (4,),
        [
            full((erows, dim)),
            pl.BlockSpec(wide, w_i),
            pl.BlockSpec(wide, w_i),
            pl.BlockSpec(group, by_i(3)),
            full((rows, state)),
            full((rows, state)),
            full((7, L, 128)),
            full((128, L)),
        ],
        [pl.BlockSpec(group, by_i(3))] * 2,
        [sds((4, rows, cols), F32)] * 2,
        [pltpu.VMEM((dim, cols), BF), pltpu.VMEM((slots, L, L), F32)],
        (int(1.5e10), int(4e7)),
        "gate_and_within",
    )(sc, nrm, wzm, wzr, xl, blow, clow, pk, ct)

    out, gn, dg, dy, dp, dpk3, dc3, small3 = call(
        k3_body,
        (3, 4),
        [
            pl.BlockSpec(group, by_phase(0, 3)),
            pl.BlockSpec(group, by_phase(0, 3)),
            pl.BlockSpec(group, lambda p, i, sc: (jnp.where(p == 1, 3, i), 0, 0)),
            pl.BlockSpec((srows + 16, cols), abs_phase(0)),
            pl.BlockSpec((srows, cols), abs_phase(0)),
            pl.BlockSpec((srows, cols), abs_phase(0)),
            full((7, L, 128)),
            full((rows, state)),
            full((4, 16, cols)),
            pl.BlockSpec(wide, w_phase(1)),
            pl.BlockSpec(wide, w_phase(1)),
            full((rows, dim)),
            full((rows, dim)),
        ],
        [
            full((rows, dim)),
            pl.BlockSpec(group, by_phase(1, 3)),
            pl.BlockSpec(group, by_phase(2, 3)),
            pl.BlockSpec(group, by_phase(2, 3)),
            pl.BlockSpec((srows + 16, cols), abs_phase(2)),
            full((L, 128)),
            full((rows, state)),
            full((4, 8, cols)),
        ],
        [
            sds((rows, dim), BF),
            sds((4, rows, cols), BF),
            sds((4, rows, cols), BF),
            sds((4, rows, cols), BF),
            sds((srows + 16, 4 * cols), BF),
            sds((L, 128), F32),
            sds((rows, state), F32),
            sds((4, 8, cols), F32),
        ],
        [
            pltpu.VMEM((4, rows, cols), F32),
            pltpu.VMEM((4, rows, cols), F32),
            pltpu.VMEM((4, rows, cols), F32),
            pltpu.VMEM((4, srows, cols), BF),
            pltpu.VMEM((2, rows, 128), F32),
            pltpu.VMEM((rows, dim), F32),
            pltpu.VMEM((rows, dim), BF),
            pltpu.VMEM((dim, cols), BF),
            pltpu.VMEM((16, cols), F32),
        ],
        (int(1.2e10), int(4e7)),
        "gated_norm",
    )(sc, within, gate, xl, r1, r2, r3, pk, clow, par, wom, wor, tok, cot)

    q1, q2, q3 = carry(dp, ([(1, 0), (3, 2)], [(2, 1)], [(1, 0)]))

    gshape = (2, count, brow, cols)
    ok, osend, zk, zsend, dnz = call(
        k4_body,
        (4,),
        [
            full((erows, dim)),
            full((rows, dim)),
            pl.BlockSpec(group, by_i(3)),
            pl.BlockSpec(group, by_i(3)),
            pl.BlockSpec(wide, w_i),
            pl.BlockSpec(wide, w_i),
        ],
        [full(gshape)] * 4 + [full((rows, dim))],
        [sds(gshape, BF)] * 4 + [sds((rows, dim), F32)],
        [
            pltpu.VMEM((dim, rows), BF),
            pltpu.VMEM((dim, rows), BF),
            pltpu.VMEM((dim, cols), BF),
        ],
        (int(7.2e9), int(2e7)),
        "outer_weight_grads",
    )(sc, nrm, cot, gn, dg, wzm, wzr)

    def summed(a, b):
        return (a.astype(F32) + b.astype(F32)).astype(BF)

    def halve(v, axis):
        return lax.index_in_dim(v, 0, axis, False), lax.index_in_dim(v, 1, axis, False)

    def reduce_step(v, axis, mesh_axis, bit):
        keep, send = halve(v, axis)
        return summed(keep, flip(send, mesh_axis, bit))

    def reduce_xy(v):
        v = reduce_step(v, 0, "tensor", 2)
        v = v.reshape((count // 2, 2) + v.shape[1:])
        return reduce_step(v, 1, "dp", 1)

    def reduce_yx(v):
        v = v.reshape((2, count // 2, 2) + v.shape[2:])
        v = reduce_step(v, 2, "dp", 1)
        return reduce_step(v, 0, "tensor", 2)

    def reduce_z(v):
        bit = 2
        while bit < dpcount:
            v = v.reshape((v.shape[0] // 2, 2) + v.shape[1:])
            v = reduce_step(v, 1, "dp", bit)
            bit *= 2
        return v[0].astype(F32)

    def reduce_slow(v):
        v = reduce_step(v, 0, "tensor", 2)[0]
        v = v.reshape(dpcount, shard, v.shape[-1])
        got = lax.all_to_all(v, "dp", split_axis=0, concat_axis=0, tiled=True)
        return got.astype(F32).sum(axis=0)

    def reduce_core(keep, send):
        return summed(keep, flip(send, "tensor", 1))

    vo = reduce_core(ok, osend)
    vz = reduce_core(zk, zsend)
    if fast:
        grad_w_out = reduce_z(reduce_xy(vo))
        grad_w_z = reduce_z(reduce_yx(vz))
    else:
        grad_w_out = reduce_slow(vo)
        grad_w_z = reduce_slow(vz)

    dxl, bc5, pk5 = call(
        k5_body,
        (4,),
        [
            pl.BlockSpec(group, by_i(3)),
            pl.BlockSpec(group, by_i(3)),
            full((rows, state)),
            full((rows, state)),
            full((7, L, 128)),
            full((128, L)),
            full((4, 16, cols)),
        ],
        [pl.BlockSpec(group, by_i(3)), full((2, rows, state)), full((2, L, 128))],
        [
            sds((4, rows, cols), F32),
            sds((2, rows, state), F32),
            sds((2, L, 128), F32),
        ],
        [
            pltpu.VMEM((slots, L, L), F32),
            pltpu.VMEM((slots, L, L), F32),
            pltpu.VMEM((128, L), F32),
        ],
        (int(2e10), int(4e7)),
        "within_backward",
    )(sc, xl, dy, blow, clow, pk, ct, par)

    g1 = (2, count, brow, 512)
    gk, gsend, dn, small6, sbc, sdt = call(
        k6_body,
        (5,),
        [
            full((erows, dim)),
            pl.BlockSpec(group, by_i(3)),
            pl.BlockSpec(group, by_i(3)),
            pl.BlockSpec((1, erows, cols), by_i(3)),
            pl.BlockSpec(group, by_i(3)),
            pl.BlockSpec((srows + 16, cols), abs_i),
            pl.BlockSpec((srows, cols), abs_i),
            pl.BlockSpec((srows, cols), abs_i),
            pl.BlockSpec((srows + 16, cols), abs_i),
            pl.BlockSpec((srows, cols), abs_i),
            pl.BlockSpec((srows, cols), abs_i),
            full((rows, state)),
            full((7, L, 128)),
            full((4, 16, cols)),
            full((4, 2 * state)),
            full((2, rows, state)),
            full((rows, state)),
            full((L, 128)),
            full((2, L, 128)),
            full((2, erows, state)),
            full((2, rows, state)),
        ]
        + [pl.BlockSpec(wblock, w_i)] * 4
        + [full((rows, dim))],
        [
            full(g1),
            full(g1),
            full((erows, dim)),
            full((4, 8, cols)),
            full((2, 8, state)),
            full((8, 128)),
        ],
        [
            sds(g1, BF),
            sds(g1, BF),
            sds((erows, dim), F32),
            sds((4, 8, cols), F32),
            sds((2, 8, state), F32),
            sds((8, 128), F32),
        ],
        [
            pltpu.VMEM((dim, erows), BF),
            pltpu.VMEM((dim, 512), BF),
            pltpu.VMEM((4, dim, 128), BF),
            pltpu.VMEM((erows, cols), BF),
            pltpu.VMEM((rows, state), F32),
            pltpu.VMEM((L, 128), F32),
            pltpu.VMEM((8, 128), F32),
            pltpu.VMEM((2, erows, state), F32),
            pltpu.VMEM((16, cols), F32),
            pltpu.VMEM((16, cols), F32),
        ],
        (int(1e10), int(4e7)),
        "states_backward",
    )(
        sc, nrm, xl, dsl, inn, dxl, q1, q2, q3, r1, r2, r3, blow, pk, par, conv_bc,
        bc5, dc3, dpk3, pk5, sin, dbc, wam, war, wbm, wbr, dnz,
    )

    hr = lax.ppermute(dn[rows:].astype(BF), "tensor", [(a + 1, a) for a in range(tcount - 1)])
    v1 = reduce_core(gk, gsend)
    if fast:
        ga = reduce_xy(v1[..., :256])
        gb = reduce_yx(v1[..., 256:])
        grad1 = reduce_z(jnp.concatenate([ga, gb], axis=-1))
    else:
        grad1 = reduce_slow(v1)

    ig, ng = call(
        k7_body,
        (slots,),
        [
            pl.BlockSpec((L, dim), lambda s, sc: (s, 0)),
            pl.BlockSpec((16, dim), lambda s, sc: (s, 0)),
            pl.BlockSpec((L, dim), lambda s, sc: (s, 0)),
            pl.BlockSpec((L, dim), lambda s, sc: (s, 0)),
            full((1, dim)),
        ],
        [pl.BlockSpec((L, dim), lambda s, sc: (s, 0)), full((8, dim))],
        [sds((rows, dim), BF), sds((8, dim), F32)],
        [],
        (int(1e8), int(1e7)),
        "input_grad",
    )(sc, dn, hr, tok, cot, gain)

    dts = sdt[:2].reshape(2, slots, SPAN)[:, :, : 4 * heads].sum(axis=1).reshape(2, 4, heads)
    dts = jnp.pad(jnp.swapaxes(dts, 0, 1), ((0, 0), (0, 0), (0, cols - heads)))
    skip_sum = small3[:, 1:2]
    mine = jnp.concatenate(
        [small6[:, :5], small3[:, 0:1], skip_sum, dts, jnp.zeros((4, 7, cols), F32)], axis=1
    )
    flat = jnp.concatenate(
        [
            jnp.concatenate([sbc[0, :5], sbc[1, :5]], axis=1).reshape(-1),
            ng[0],
        ]
    )
    flat = jnp.pad(flat, (0, 8 * cols - flat.shape[0])).reshape(8, cols)
    mine = mine.reshape(2, 2, 16, cols)
    send = jnp.concatenate([mine[:, 1].reshape(32, cols), flat], axis=0)
    got = flip(send, "tensor", 1)
    own = mine[:, 0] + got[:32].reshape(2, 16, cols)
    flat = flat + got[32:]
    got = flip(jnp.concatenate([own[1], flat], axis=0), "tensor", 2)
    both = jnp.concatenate([own[0], flat], axis=0) + got
    bit = 1
    while bit < dpcount:
        both = both + flip(both, "dp", bit)
        bit *= 2
    own, flat = both[:16], both[16:].reshape(-1)
    bcs = flat[: 5 * 2 * state].reshape(5, 2 * state)
    ngain = flat[5 * 2 * state : 5 * 2 * state + dim]
    skip_grad = own[6].reshape(heads, cols // heads).sum(axis=1)

    mine_bc = grad1[:, cols : cols + bq]
    parts = mine_bc.reshape(tcount, shard // tcount, bq)
    got = lax.all_to_all(parts, "tensor", split_axis=0, concat_axis=0, tiled=True)
    grad_w_bc = jnp.swapaxes(got, 0, 1).reshape(shard // tcount, bq * tcount)

    return (
        out.reshape(tokens.shape),
        ig.reshape(tokens.shape),
        ngain,
        grad_w_z,
        grad1[:, :cols],
        grad_w_bc,
        grad1[:, cols + bq : cols + bq + heads],
        own[:4],
        own[4],
        bcs[:4],
        bcs[4],
        own[7, :heads],
        own[8, :heads],
        skip_grad,
        own[5],
        grad_w_out,
    )


def solution(mesh):
    return jax.shard_map(
        per_device,
        mesh=mesh,
        in_specs=(
            P("dp", "tensor", None), P("dp", None), P("dp", "tensor", None), P(),
            P("dp", "tensor"), P("dp", "tensor"), P("dp", None), P("dp", "tensor"),
            P(None, "tensor"), P("tensor"), P(), P(),
            P("tensor"), P("tensor"), P("tensor"), P("tensor"), P("dp", "tensor"),
        ),
        out_specs=(
            P("dp", "tensor", None), P("dp", "tensor", None), P(),
            P("dp", "tensor"), P("dp", "tensor"), P(("dp", "tensor"), None), P("dp", "tensor"),
            P(None, "tensor"), P("tensor"), P(), P(),
            P("tensor"), P("tensor"), P("tensor"), P("tensor"), P("dp", "tensor"),
        ),
        check_vma=False,
    )
```

```python
import functools

import jax
import jax.numpy as jnp
from jax import lax
from jax.experimental import pallas as pl
from jax.experimental.pallas import tpu as pltpu
from jax.sharding import PartitionSpec as P

INNER = 1536
L = 256
HD = 64
SPAN = 32
EPS = 1e-05
LOG2E = 1.4426950408889634
F32 = jnp.float32
BF = jnp.bfloat16
CHUNK = 64
WIDE = 768
VMEM_MIB = 40
K5_MIB = 58


def dot(a, b):
    return jnp.dot(a, b, preferred_element_type=F32)


def dot_nt(a, b):
    return lax.dot_general(a, b, (((1,), (1,)), ((), ())), preferred_element_type=F32)


def dot_high(a, b):
    return jnp.dot(a, b, preferred_element_type=F32, precision=lax.Precision.HIGHEST)


def sigmoid(v):
    return 0.5 * jnp.tanh(0.5 * v) + 0.5


def lane_iota(rows):
    return lax.broadcasted_iota(jnp.int32, (rows, 128), 1)


def row_iota(rows, lanes):
    return lax.broadcasted_iota(jnp.int32, (rows, lanes), 0)


def seg_of(idx, fe, se):
    return (idx >= fe).astype(jnp.int32) + (idx >= se).astype(jnp.int32)


def ends(sc, s):
    return sc[2 * s], sc[2 * s + 1]


def pair_cols(cols, first):
    lane = lane_iota(cols.shape[0])
    left = jnp.broadcast_to(cols[:, first : first + 1], cols.shape)
    right = jnp.broadcast_to(cols[:, first + 1 : first + 2], cols.shape)
    return jnp.where(lane < HD, left, right)


def head_pick():
    r = lax.broadcasted_iota(jnp.int32, (WIDE, 128), 0)
    c = lax.broadcasted_iota(jnp.int32, (WIDE, 128), 1)
    return jnp.where(c == r // HD, 1.0, 0.0)


def head_spread():
    r = lax.broadcasted_iota(jnp.int32, (256, WIDE), 0)
    c = lax.broadcasted_iota(jnp.int32, (256, WIDE), 1)
    return jnp.where(r % 128 == c // HD, 1.0, 0.0).astype(BF)


def expand(dst, cols, spread):
    high = cols.astype(BF)
    low = (cols - high.astype(F32)).astype(BF)
    both = jnp.concatenate([high, low], axis=1)
    for n in range(3):
        dst[:, 256 * n : 256 * n + 256] = dot(both, spread[:, 256 * n : 256 * n + 256])


def three_terms(v):
    high = v.astype(BF).astype(F32)
    mid = (v - high).astype(BF).astype(F32)
    return high, mid, v - high - mid


def tile_spread():
    r = lax.broadcasted_iota(jnp.int32, (256, 2 * WIDE), 0)
    h = lax.broadcasted_iota(jnp.int32, (256, 2 * WIDE), 1) // 128
    return jnp.where((r == h) | (r == h + 128) | (r == h + 144), 1.0, 0.0).astype(BF)


def expand_tiles(dst, cols, spread):
    high, mid, low = three_terms(cols)
    lane = lane_iota(L)
    rest = jnp.where(lane < 16, mid, pltpu.roll(low, 16, 1))
    left = jnp.concatenate([high, rest], axis=1).astype(BF)
    for n in range(6):
        dst[:, 256 * n : 256 * n + 256] = dot(left, spread[:, 256 * n : 256 * n + 256])


def to_lane0(packed, s, g):
    return pltpu.roll(packed, (256 - s * SPAN - g * 12) % 128, 1)


def from_lane0(cols, s, g):
    return pltpu.roll(cols, s * SPAN + g * 12, 1)


def rows_of(s, length=L):
    return pl.ds(pl.multiple_of(s * length, length), length)


def tile(j):
    return slice(128 * j, 128 * j + 128)


def conv_forward(ext, taps, bias, masks, first=0, length=L):
    acc = bias + taps[0] * ext[8 + first : 8 + first + length]
    for k in range(1, 4):
        acc = acc + (taps[k] * ext[8 + first - k : 8 + first - k + length]) * masks[k - 1]
    return acc


def conv_backward(ext, v_ext, taps, masks):
    out, tap_grads = None, []
    for k in range(4):
        part = ext[k : 264 + k]
        if k:
            part = part * masks[k - 1]
        tap_grads.append(jnp.sum(part * v_ext, axis=0, keepdims=True))
        out = taps[k] * part if out is None else out + taps[k] * part
    return out, tap_grads


def slot_masks(packed, s):
    cols = pltpu.roll(packed[...], (128 - 4 * s) % 128, 1)
    return [jnp.broadcast_to(cols[:, k : k + 1], cols.shape) for k in (1, 2, 3)]


def place_rows(dst, blocks, me, at, first=0, width=None, lead=0):
    count, rows = blocks.shape[1:3]
    width = blocks.shape[3] - first if width is None else width
    for n in range(count):
        start = pl.multiple_of((n ^ me) * rows, rows) if count > 1 else 0
        dst[pl.ds(start, rows), at : at + width] = blocks[lead, n, :, first : first + width]


def place_pair(dst, mine, other, me):
    place_rows(dst, mine, me, 0)
    place_rows(dst, other, me, 384)


def place_p1(dst, am, bm, ar, br, me, pieces):
    place_rows(dst, am, me, 0)
    place_rows(dst, bm, me, 256, 0, 128)
    place_rows(dst, ar, me, 384)
    place_rows(dst, br, me, 640, 0, 128)
    place_rows(pieces, bm, me, 0, 128, 128)
    place_rows(pieces, br, me, 128, 128, 128)


def half_at(c, me_t):
    return pl.ds(pl.multiple_of(384 * (c ^ (me_t % 2)), 128), 384)


def k1_body(
    sc, tok, halo, gain, am, ar, bm, br, par, cbc, bbc,
    nrm, inx, blow, clow, bto, sin, dbc,
    cumo, stepo, sigo, eto, reacho, decayo, faco, uvo, masko, backo, ct,
    wbuf, wpc, pcs, dtacc, ext,
):
    g = pl.program_id(0)
    me_t, me_dp = sc[8], sc[9]

    @pl.when(g == 0)
    def _():
        def norm(v):
            v = v.astype(F32)
            r = lax.rsqrt(jnp.mean(v * v, axis=-1, keepdims=True) + EPS)
            return (v * r * gain[...]).astype(BF)

        @pl.loop(0, 16)
        def _(s):
            nrm[rows_of(s, 64)] = norm(tok[rows_of(s, 64)])

        nrm[4 * L :] = norm(halo[...])
        dtacc[...] = jnp.zeros_like(dtacc)
        sin[...] = jnp.zeros_like(sin)

    place_p1(wbuf, am, bm, ar, br, me_dp, wpc)
    for n in range(3):
        cols = slice(256 * n, 256 * n + 256)
        inx[0, :, cols] = dot(nrm[...], wbuf[:, cols]).astype(BF)
    pcs[...] = dot(nrm[...], wpc[...])

    for c in range(2):
        i = 2 * g + c
        t = i ^ me_t
        turn = 64 * (t % 2)

        @pl.loop(0, 4)
        def _(s):
            last = pcs[rows_of(s), tile(c)]
            lane = lane_iota(L)
            sin[t // 2, rows_of(s)] += pltpu.roll(jnp.where(lane < 64, last, 0.0), turn, 1)
            dtacc[...] += pltpu.roll(
                jnp.where(lane >= 64, last, 0.0), (s * SPAN + i * 6 + 64) % 128, 1
            )

        last = pcs[4 * L :, tile(c)]
        sin[t // 2, 4 * L :] += pltpu.roll(jnp.where(lane_iota(64) < 64, last, 0.0), turn, 1)

    @pl.when(g == 1)
    def _():
        dtb = jnp.zeros((1, 128), F32)
        alog = jnp.zeros((1, 128), F32)
        for i in range(4):
            for s in range(4):
                at = slice(384 * (i % 2), 384 * (i % 2) + 128)
                dtb += pltpu.roll(par[i // 2, 6:7, at], s * SPAN + i * 6, 1)
                alog += pltpu.roll(par[i // 2, 7:8, at], s * SPAN + i * 6, 1)
        raw = dtacc[...] + dtb
        step = jnp.maximum(raw, 0.0) + jnp.log1p(jnp.exp(-jnp.abs(raw)))
        sig = 1.0 / (1.0 + jnp.exp(-raw))
        decay = step * -jnp.exp(alog)
        lower = jnp.where(
            lax.broadcasted_iota(jnp.int32, (L, L), 0) >= lax.broadcasted_iota(jnp.int32, (L, L), 1),
            1.0,
            0.0,
        )
        cum = dot_high(lower, decay)
        row = row_iota(L, 128)
        lane = lane_iota(L)
        slot = lane // SPAN
        tail = jnp.zeros((L, 128), F32)
        enters = jnp.zeros((L, 128), F32)
        follows = jnp.zeros((8, 128), F32)
        masks = jnp.ones((L, 128), F32)
        row_b = row_iota(L + 8, 128) - 8
        lane_b = lane_iota(L + 8)
        back_masks = jnp.ones((L + 8, 128), F32)
        slot8 = lane_iota(8) // SPAN
        inner_block = jnp.where(me_t > 0, 1.0, 0.0)
        back = lane % 4
        for s in range(4):
            fe, se = ends(sc, s)
            seg = seg_of(row, fe, se)
            last = seg_of(L - 1, fe, se)
            before = seg_of(-1, fe, se)
            here = slot == s
            tail = jnp.where(here & (seg == last), 1.0, tail)
            enters = jnp.where(here & (seg == before), inner_block, enters)
            follows = jnp.where(
                (slot8 == s), jnp.where(last == before, inner_block, 0.0), follows
            )
            masks = jnp.where((lane // 4 == s) & (seg != seg_of(row - back, fe, se)), 0.0, masks)
            cut = seg_of(row_b, fe, se) != seg_of(row_b + lane_b % 4, fe, se)
            back_masks = jnp.where((lane_b // 4 == s) & cut, 0.0, back_masks)
        cum_last = cum[L - 1 : L]
        cum2 = cum * LOG2E
        cumo[...] = cum2
        stepo[...] = step
        sigo[...] = sig
        eto[...] = jnp.exp(cum_last - cum) * tail
        reacho[...] = jnp.exp(cum) * enters
        decayo[...] = decay
        faco[...] = jnp.exp(cum_last) * follows
        uvo[...] = jnp.exp2(-jnp.abs(cum2 - cum2[127:128]))
        masko[...] = masks
        backo[...] = back_masks
        ct[...] = cum2.T
        for q, low_out in ((0, blow), (1, clow)):
            taps = [cbc[k : k + 1, tile(q)] for k in range(4)]

            @pl.loop(0, 4)
            def _(s):
                ext[0:8] = sin[q, pl.ds(pl.multiple_of(4 * L + 16 * s + 8, 8), 8)]
                ext[8:] = sin[q, rows_of(s)]
                acc = conv_forward(ext, taps, bbc[:, tile(q)], slot_masks(masko, s))
                sg = sigmoid(acc)
                low = acc * sg
                low_out[rows_of(s)] = low.astype(BF)
                dbc[q, rows_of(s)] = sg + low * (1.0 - sg)
                if q == 0:
                    bto[rows_of(s, 128)] = low.T.astype(BF)


def factor_rows(fac, g):
    rows = []
    for s in range(4):
        f = to_lane0(fac[...], s, g)
        rows.append(jnp.concatenate([pair_cols(f, 2 * j)[0:1] for j in range(6)], axis=1))
    f = jnp.concatenate(rows, axis=0)
    high = f.astype(BF).astype(F32)
    return jnp.concatenate([high, f - high, jnp.zeros((8, WIDE), F32)], axis=0).astype(BF)


def k2_body(g, sc, inx, halo, par, bt, stepp, etp, fac, mask, *rest):
    xo, xso, dslo, sto, xe, ext, spread, stepx, stepe = rest[-9:]
    s = pl.program_id(0)
    me_t = sc[8]

    @pl.when(s == 0)
    def _():
        spread[...] = head_spread()

    masks = slot_masks(mask, s)
    step = to_lane0(stepp[...], s, g)
    expand(stepx, step, spread)
    expand(stepe, step * to_lane0(etp[...], s, g), spread)
    for j in range(6):
        ext[j, 0:8] = halo[0, :, tile(j)].astype(F32)[8:]
        ext[j, 8:] = inx[0, :, tile(j)].astype(F32)
    for n in range(L // CHUNK):
        r = slice(CHUNK * n, CHUNK * n + CHUNK)
        mr = [m[r] for m in masks]
        for j in range(6):
            taps = [0.5 * par[0, k : k + 1, tile(j)] for k in range(4)]
            half = conv_forward(ext.at[j], taps, 0.5 * par[0, 4:5, tile(j)], mr, CHUNK * n, CHUNK)
            th = jnp.tanh(half)
            up = 1.0 + th
            act = half * up
            xo[0, r, tile(j)] = act.astype(BF)
            dslo[0, r, tile(j)] = ((0.5 * up) * (1.0 + half * (1.0 - th))).astype(BF)
            xso[0, r, tile(j)] = (act * stepx[r, tile(j)]).astype(BF)
            xe[r, tile(j)] = (act * stepe[r, tile(j)]).astype(BF)
    for c in range(2):
        sto[rows_of(s, 128), half_at(c, me_t)] = dot(
            bt[...], xe[:, 384 * c : 384 * c + 384]
        ).astype(BF)

    @pl.when(s == 3)
    def _():
        f = factor_rows(fac, g)
        for c in range(2):
            sto[512:528, half_at(c, me_t)] = f[:, 384 * c : 384 * c + 384]


def by_head(pair):
    lane = lane_iota(128)
    zero = jnp.zeros_like(pair)
    return jnp.concatenate(
        [jnp.where(lane < HD, pair, zero), jnp.where(lane < HD, zero, pair)], axis=0
    )


def diag_mask(d, fe, se, key_rows):
    r = lax.broadcasted_iota(jnp.int32, (128, 128), 0) + 128 * d
    c = lax.broadcasted_iota(jnp.int32, (128, 128), 1) + 128 * d
    order = (c >= r) if key_rows else (r >= c)
    return order & (seg_of(r, fe, se) == seg_of(c, fe, se))


def cross_half(fe, se, key_rows):
    r = lax.broadcasted_iota(jnp.int32, (128, 128), 0) + (0 if key_rows else 128)
    c = lax.broadcasted_iota(jnp.int32, (128, 128), 1) + (128 if key_rows else 0)
    return seg_of(r, fe, se) == seg_of(c, fe, se)


def k3_body(g, sc, xs, blow, clow, cump, uvp, ct, *rest):
    within, scores, cross, spread, uvx, tiles, cumx = rest[-7:]
    s = pl.program_id(0)
    fe, se = sc[2 * s], sc[2 * s + 1]

    @pl.when(s == 0)
    def _():
        spread[...] = head_spread()
        tiles[...] = tile_spread()


    for d in range(2):
        r = slice(128 * d, 128 * d + 128)
        scores[d] = jnp.where(diag_mask(d, fe, se, False), dot_nt(clow[r], blow[r]), 0.0)
    cross[...] = jnp.where(cross_half(fe, se, False), dot_nt(clow[128:], blow[:128]), 0.0).astype(BF)

    expand_tiles(cumx, to_lane0(cump[...], s, g), tiles)
    expand(uvx, to_lane0(uvp[...], s, g), spread)
    for j in range(6):
        for d in range(2):
            r = slice(128 * d, 128 * d + 128)
            pair = xs[0, r, tile(j)]
            parts = []
            for b in range(2):
                h = 2 * j + b
                gap = cumx[r, tile(h)] - ct[pl.ds(s * SPAN + g * 12 + h, 1), :][:, r]
                parts.append((jnp.exp2(jnp.minimum(gap, 0.0)) * scores[d]).astype(BF))
            total = dot(jnp.concatenate(parts, axis=1), by_head(pair))
            if d == 1:
                xv = (xs[0, :128, tile(j)].astype(F32) * uvx[:128, tile(j)]).astype(BF)
                total = total + dot(cross[...], xv) * uvx[128:, tile(j)]
            within[0, r, tile(j)] = total


def k4_body(sc, nrm, cot, wzm, wzr, wom, wor, gate, dgn, dbro, wz, wo):
    g = pl.program_id(0)
    n = pl.program_id(1)
    me_dp = sc[9]

    @pl.when((g == 0) & (n == 0))
    def _():
        @pl.loop(0, 16)
        def _(n):
            s = n // 4
            r = rows_of(n, 64)
            keep = row_iota(64, 1) + 64 * (n % 4) < sc[2 * s + 1]
            dbro[r] = jnp.where(keep, cot[r].astype(F32), 0.0).astype(BF)

    @pl.when(n == 0)
    def _():
        place_pair(wz, wzm, wzr, me_dp)
        place_pair(wo, wom, wor, me_dp)

    cols = pl.ds(pl.multiple_of(n * 256, 256), 256)
    gate[0] = dot(nrm[0 : 4 * L], wz[:, cols]).astype(BF)
    dgn[0] = dot(dbro[...], wo[:, cols]).astype(BF)


def k5_body(
    sc, within, gate, dgn, x, r1, r2, r3, reachp, fac, clow, par, wom, wor, tok,
    out, gno, dgo, dyo, dpo, prevo, rowsum, dco, small,
    mo, sums, branch, wbuf, gnb, frow, dlow, seg_h, seg_l, pick, pv, spread, reachx,
):
    ph = pl.program_id(0)
    g = pl.program_id(1)
    s = pl.program_id(2)
    me_t, me_dp = sc[8], sc[9]
    r = rows_of(s)
    first = (g == 0) & (s == 0)

    @pl.when((ph == 0) & first)
    def _():
        rowsum[...] = jnp.zeros_like(rowsum)
        dco[...] = jnp.zeros_like(dco)
        small[...] = jnp.zeros_like(small)
        pick[...] = head_pick().astype(BF)
        spread[...] = head_spread()

    expand(reachx, to_lane0(reachp[...], s, g), spread)

    @pl.when(ph == 0)
    def _():
        srow = rows_of(s, 128)
        for c in range(2):
            at = half_at(c, me_t)
            frow[...] = r1[512:528, at].astype(F32)
            f = frow[pl.ds(s, 1)] + frow[pl.ds(s + 4, 1)]
            p = r1[srow, at].astype(F32) + r2[srow, at].astype(F32) + f * r3[srow, at].astype(F32)
            pv[:, 384 * c : 384 * c + 384] = p.astype(BF)
        prevo[g, srow] = pv[...]
        sq = jnp.zeros((L, 128), F32)
        dd = jnp.zeros((L, 128), F32)
        for j in range(6):
            from_prev = dot(clow[...], pv[:, tile(j)])
            mixed = (
                within[0, :, tile(j)]
                + reachx[:, tile(j)] * from_prev
                + par[0, 8:9, tile(j)] * x[0, :, tile(j)].astype(F32)
            )
            mo[g, r, tile(j)] = mixed
            gv = gate[0, :, tile(j)].astype(F32)
            gated = mixed * (gv * sigmoid(gv))
            sq = sq + gated * gated
            dd = dd + dgn[0, :, tile(j)].astype(F32) * par[0, 5:6, tile(j)] * gated
        sq = jnp.broadcast_to(jnp.sum(sq, axis=1, keepdims=True), (L, 128))
        dd = jnp.broadcast_to(jnp.sum(dd, axis=1, keepdims=True), (L, 128))

        @pl.when(g == 0)
        def _():
            sums[0, r] = sq
            sums[1, r] = dd

        @pl.when(g == 1)
        def _():
            sq2 = sums[0, r] + sq
            dd2 = sums[1, r] + dd
            gscale = lax.rsqrt(sq2 * (1.0 / INNER) + EPS)
            sums[0, r] = gscale
            sums[1, r] = gscale * gscale * gscale * (dd2 * (1.0 / INNER))

    @pl.when(ph == 1)
    def _():
        gscale = sums[0, r]
        coef = sums[1, r]
        srow = rows_of(s, 128)
        for j in range(6):
            gv = gate[0, :, tile(j)].astype(F32)
            mixed = mo[g, r, tile(j)]
            sg = sigmoid(gv)
            silu = gv * sg
            gated = mixed * silu
            gs = gated * gscale
            gain = par[0, 5:6, tile(j)]
            gn = (gs * gain).astype(BF)
            gno[0, :, tile(j)] = gn
            gnb[r, tile(j)] = gn
            d = dgn[0, :, tile(j)].astype(F32)
            small[g, 0:1, tile(j)] += jnp.sum(d * gs, axis=0, keepdims=True)
            dgated = gscale * (d * gain) - gated * coef
            dgo[0, :, tile(j)] = (dgated * mixed * (sg + silu * (1.0 - sg))).astype(BF)
            dy = (dgated * silu).astype(BF)
            dyo[0, :, tile(j)] = dy
            dyf = dy.astype(F32)
            dlow[:, tile(j)] = (dyf * reachx[:, tile(j)]).astype(BF)
            dx_skip = dyf * x[0, :, tile(j)].astype(F32)
            small[g, 1:2, tile(j)] += jnp.sum(dx_skip, axis=0, keepdims=True)
            v = dyf * mixed - par[0, 8:9, tile(j)] * dx_skip
            high = v.astype(BF)
            seg_h[:, tile(j)] = high
            seg_l[:, tile(j)] = (v - high.astype(F32)).astype(BF)
        seg = dot(seg_h[...], pick[...]) + dot(seg_l[...], pick[...])
        rowsum[...] += from_lane0(seg, s, g)
        dco[r] += dot_nt(dlow[...], prevo[g, srow])
        for c in range(2):
            dpo[srow, half_at(c, me_t)] = lax.dot_general(
                clow[...],
                dlow[:, 384 * c : 384 * c + 384],
                (((0,), (0,)), ((), ())),
                preferred_element_type=F32,
            ).astype(BF)

        @pl.when(s == 3)
        def _():
            f = factor_rows(fac, g)
            for c in range(2):
                dpo[512:528, half_at(c, me_t)] = f[:, 384 * c : 384 * c + 384]
            place_pair(wbuf, wom, wor, me_dp)

        @pl.when((s == 3) & (g == 0))
        def _():
            branch[...] = dot_nt(gnb[...], wbuf[...])

        @pl.when((s == 3) & (g == 1))
        def _():
            branch[...] += dot_nt(gnb[...], wbuf[...])

            @pl.loop(0, 16)
            def _(n):
                q = rows_of(n, 64)
                out[q] = (tok[q].astype(F32) + branch[q]).astype(BF)


def store_grad(ref, lead, me_dp, value_ref, first, width, at=0):
    count, rows = ref.shape[-3], ref.shape[-2]
    for n in range(count):
        place = n ^ me_dp if count > 1 else 0
        part = value_ref[n * rows : (n + 1) * rows, first : first + width].astype(BF)
        ref[lead + (place, slice(None), slice(at, at + width))] = part


def add_weighted(total, val, w, lead=()):
    @pl.loop(0, total.shape[0] // 64)
    def _(n):
        r = rows_of(n, 64)
        part = total[r]
        for j in range(w.shape[1] // 128):
            v = val[j, r] if lead else val[r, tile(j)]
            part = part + v * w[r, tile(j)].astype(F32)
        total[r] = part


def k6_body(sc, nrm, dbr, gn, dg, wzm, wzr, ok, os, zk, zs, nt, ngz, dt, val, wz):
    g = pl.program_id(0)
    me_dp = sc[9]
    place_pair(wz, wzm, wzr, me_dp)

    @pl.when(g == 0)
    def _():
        ngz[...] = jnp.zeros_like(ngz)

        @pl.loop(0, 4)
        def _(s):
            nt[:, rows_of(s)] = nrm[rows_of(s)].T
            dt[:, rows_of(s)] = dbr[rows_of(s)].T

        nt[:, 4 * L :] = nrm[4 * L :].T

    for lhs, rhs, keep, send in ((dt, gn, ok, os), (nt, dg, zk, zs)):
        for n in range(3):
            cols = slice(256 * n, 256 * n + 256)
            val[:, cols] = dot(lhs[:, : 4 * L], rhs[0, :, cols])
        store_grad(keep, (0,), me_dp, val, 0, 384)
        store_grad(send, (0,), me_dp, val, 384, 384)
    add_weighted(ngz, val, wz)


def k7_body(g, sc, xs, dy, blow, clow, cump, uvp, ct, *rest):
    dxo, bco, pko, scores, cross, xvb, udb, spread, uvx, tiles, cumx, pick, corr = rest[-13:]
    s = pl.program_id(0)

    @pl.when(s == 0)
    def _():
        spread[...] = head_spread()
        tiles[...] = tile_spread()
        pick[...] = head_pick().astype(BF)
        pko[...] = jnp.zeros_like(pko)

    fe, se = sc[2 * s], sc[2 * s + 1]

    for d in range(2):
        r = slice(128 * d, 128 * d + 128)
        scores[d] = jnp.where(diag_mask(d, fe, se, True), dot_nt(blow[r], clow[r]), 0.0)
    cross[...] = jnp.where(cross_half(fe, se, True), dot_nt(blow[:128], clow[128:]), 0.0).astype(BF)

    expand_tiles(cumx, to_lane0(cump[...], s, g), tiles)
    expand(uvx, to_lane0(uvp[...], s, g), spread)
    totals = [jnp.zeros((128, 128), F32), jnp.zeros((128, 128), F32)]
    crossq = cross[...].astype(F32).T.astype(BF)
    for j in range(6):
        for d in range(2):
            r = slice(128 * d, 128 * d + 128)
            xp = xs[0, r, tile(j)]
            dyp = dy[0, r, tile(j)]
            grads = dot_nt(by_head(xp), dyp)
            parts = []
            for b in range(2):
                h = 2 * j + b
                gap = ct[pl.ds(s * SPAN + g * 12 + h, 1), :][:, r] - cumx[r, tile(h)]
                kern = jnp.exp2(jnp.minimum(gap, 0.0))
                totals[d] = totals[d] + grads[128 * b : 128 * b + 128] * kern
                parts.append((kern * scores[d]).astype(BF))
            dx = dot(jnp.concatenate(parts, axis=1), by_head(dyp))
            scaled = (xp if d == 0 else dyp).astype(F32) * uvx[r, tile(j)]
            low = scaled.astype(BF)
            diff = low.astype(F32) - scaled
            if d == 0:
                xvb[:, tile(j)] = low
                top, xdiff = dx, diff
            else:
                udb[:, tile(j)] = low
                off = dot(cross[...], low)
                dxo[0, r, tile(j)] = dx
                dxo[0, :128, tile(j)] = top + off * uvx[:128, tile(j)]
                corr[:128, tile(j)] = (xdiff * off).astype(BF)
                corr[128:, tile(j)] = (diff * dot(crossq, xvb[:, tile(j)])).astype(BF)
    dcr = dot_nt(xvb[...], udb[...])
    pko[...] += from_lane0(dot(corr[...], pick[...]), s, g)
    d0 = jnp.where(diag_mask(0, fe, se, True), totals[0], 0.0)
    d1 = jnp.where(diag_mask(1, fe, se, True), totals[1], 0.0)
    dl = jnp.where(cross_half(fe, se, True), dcr, 0.0)
    c0, c1, b0, b1 = clow[:128], clow[128:], blow[:128], blow[128:]
    bco[0, 0:128] = dot(d0.astype(BF), c0) + dot(dl.astype(BF), c1)
    bco[0, 128:] = dot(d1.astype(BF), c1)
    bco[1, 0:128] = dot(d0.T.astype(BF), b0)
    bco[1, 128:] = dot(d1.T.astype(BF), b1) + dot(dl.T.astype(BF), b0)


def k8_body(
    g, last, sc, nt, xs, dy, dsl, inx, halo, dxw, q1, q2, q3, prev, blow, stepp, etp, back, par,
    am, ar, bm, br, *rest,
):
    if last:
        (
            fac, sigp, decay, gain, ngz, nga, cbc, bc7a, bc7b, corr_a, corr_b, dc3, rowsum, sin, dbc, sega, enda, dba,
            keep, send, din, seg, end, dba_o, small, ngx, din5, sbc, sdt, ngo,
            val, hsum, gsc, gf, glow, xe, seg_h, seg_l, pick, wbuf, wpc, gbuf, pcs, pblk, ub, ext, spread, stepx, etx,
        ) = rest
    else:
        (
            keep, send, din, seg, end, dba_o, small, ngx,
            val, hsum, gsc, gf, glow, xe, seg_h, seg_l, pick, wbuf, ub, ext, spread, stepx, etx,
        ) = rest
    s = pl.program_id(0)
    me_t, me_dp = sc[8], sc[9]
    r = rows_of(s)
    hrow = pl.ds(pl.multiple_of(4 * L + 16 * s, 16), 16)

    @pl.when(s == 0)
    def _():
        seg[...] = jnp.zeros_like(seg)
        end[...] = jnp.zeros_like(end)
        small[...] = jnp.zeros_like(small)
        pick[...] = head_pick().astype(BF)
        ext[:, 0:8] = jnp.zeros((6, 8, 128), F32)
        ext[:, 264:] = jnp.zeros((6, 8, 128), F32)
        spread[...] = head_spread()

    srow = rows_of(s, 128)
    for c in range(2):
        at = half_at(c, me_t)
        gf[...] = q1[512:528, at].astype(F32)
        f = gf[pl.ds(s, 1)] + gf[pl.ds(s + 4, 1)]
        v = q1[srow, at].astype(F32) + q2[srow, at].astype(F32) + f * q3[srow, at].astype(F32)
        gsc[:, 384 * c : 384 * c + 384] = v
        glow[:, 384 * c : 384 * c + 384] = v.astype(BF)
    for n in range(3):
        cols = slice(256 * n, 256 * n + 256)
        ub[:, cols] = dot(blow[...], glow[:, cols])
    masks = slot_masks(back, s)
    expand(stepx, to_lane0(stepp[...], s, g), spread)
    expand(etx, to_lane0(etp[...], s, g), spread)
    ends_row, gp_row = [], []
    for j in range(6):
        taps = [par[0, k : k + 1, tile(j)] for k in range(4)]
        xf = xs[0, :, tile(j)].astype(F32)
        ec = etx[:, tile(j)]
        eu = ub[:, tile(j)] * ec
        xe[:, tile(j)] = (xf * ec).astype(BF)
        ends_row.append(jnp.sum(xf * eu, axis=0, keepdims=True))
        gp_row.append(
            jnp.sum(gsc[:, tile(j)] * prev[0, srow, tile(j)].astype(F32), axis=0, keepdims=True)
        )
        dxi = dxw[0, :, tile(j)] + eu
        v = xf * dxi
        high = v.astype(BF)
        seg_h[:, tile(j)] = high
        seg_l[:, tile(j)] = (v - high.astype(F32)).astype(BF)
        dx = dxi * stepx[:, tile(j)] + par[0, 8:9, tile(j)] * dy[0, :, tile(j)].astype(F32)
        dconv = dx * dsl[0, :, tile(j)].astype(F32)
        small[4:5, tile(j)] += jnp.sum(dconv, axis=0, keepdims=True)
        v_ext = jnp.concatenate(
            [halo[0, :, tile(j)].astype(F32)[8:], inx[0, :, tile(j)].astype(F32)], axis=0
        )
        ext[j, 8:264] = dconv
        dv, tap_grads = conv_backward(ext.at[j], v_ext, taps, masks)
        for k in range(4):
            small[k : k + 1, tile(j)] += tap_grads[k]
        din[r, tile(j)] = dv[8:].astype(BF)
        din[hrow, tile(j)] = jnp.concatenate([jnp.zeros((8, 128), F32), dv[:8]], axis=0).astype(BF)
    seg[...] += from_lane0(dot(seg_h[...], pick[...]) + dot(seg_l[...], pick[...]), s, g)
    dba_o[r] = dot_nt(xe[...], glow[...])
    rows = jnp.concatenate(
        [
            jnp.concatenate(ends_row, axis=1),
            jnp.concatenate(gp_row, axis=1),
            jnp.zeros((6, WIDE), F32),
        ],
        axis=0,
    )
    end[...] += from_lane0(dot_high(rows, pick[...].astype(F32)), s, g)

    @pl.when(s == 3)
    def _():
        for n in range(3):
            cols = slice(256 * n, 256 * n + 256)
            hsum[...] = dot(nt[:, 4 * L :], din[4 * L :, cols])
            val[:, cols] = dot(nt[:, : 4 * L], din[: 4 * L, cols]) + hsum[...]
        store_grad(keep, (), me_dp, val, 0, 384)
        store_grad(send, (), me_dp, val, 384, 384)
        place_rows(wbuf, am, me_dp, 0)
        place_rows(wbuf, ar, me_dp, 384)
        place_rows(wbuf, bm, me_dp, 256, 0, 128, g if last else 0)
        place_rows(wbuf, br, me_dp, 640, 0, 128, g if last else 0)
        ngx[...] = ngz[...] + nga[...] if last else jnp.zeros_like(ngx)
        add_weighted(ngx, val, wbuf)

    if not last:
        return

    @pl.when(s == 3)
    def _():
        for q in range(2):
            taps = [cbc[k : k + 1, tile(q)] for k in range(4)]
            sbc[q] = jnp.zeros((8, 128), F32)

            @pl.loop(0, 4)
            def _(n):
                rn = rows_of(n)
                if q == 0:
                    grad = bc7a[0, rn] + bc7b[0, rn] + dba_o[rn] + dba[rn]
                else:
                    grad = bc7a[1, rn] + bc7b[1, rn] + dc3[rn]
                dconv = grad * dbc[q, rn]
                hn = pl.ds(pl.multiple_of(4 * L + 16 * n, 16), 16)
                v_ext = jnp.concatenate([sin[q, hn][8:], sin[q, rn]], axis=0)
                ext[q, 8:264] = dconv
                dv, tap_grads = conv_backward(ext.at[q], v_ext, taps, slot_masks(back, n))
                sbc[q, 4:5] += jnp.sum(dconv, axis=0, keepdims=True)
                for k in range(4):
                    sbc[q, k : k + 1] += tap_grads[k]
                gbuf[q, rn] = dv[8:]
                gbuf[q, hn] = jnp.concatenate([jnp.zeros((8, 128), F32), dv[:8]], axis=0)

        row = row_iota(L, 128)
        corr = corr_a[...] + corr_b[...]
        col = seg[...] + sega[...] + jnp.where(row < 128, corr, 0.0)
        ends_all = end[...] + enda[...]
        at_last = ends_all[0:1] + ends_all[1:2] * fac[0:1]
        dcum = rowsum[...] + jnp.where(row < 128, 0.0, corr) - col + jnp.where(row == L - 1, at_last, 0.0)
        upper = jnp.where(
            lax.broadcasted_iota(jnp.int32, (L, L), 0) <= lax.broadcasted_iota(jnp.int32, (L, L), 1),
            1.0,
            0.0,
        )
        dlog = dot_high(upper, dcum)
        alog = jnp.zeros((1, 128), F32)
        for i in range(4):
            at = slice(384 * (i % 2), 384 * (i % 2) + 128)
            for n in range(4):
                alog += pltpu.roll(par[i // 2, 7:8, at], n * SPAN + i * 6, 1)
        step_all, sig = stepp[...], sigp[...]
        ratio = jnp.where(step_all > 1e-30, sig / jnp.maximum(step_all, 1e-30), 1.0)
        ddt = ratio * col - sig * jnp.exp(alog) * dlog
        sdt[...] = jnp.concatenate(
            [
                jnp.sum(ddt, axis=0, keepdims=True),
                jnp.sum(dlog * decay[...], axis=0, keepdims=True),
                jnp.zeros((6, 128), F32),
            ],
            axis=0,
        )
        for n in range(4):
            t = n ^ me_t
            turn = (64 * (t % 2)) % 128

            @pl.loop(0, 4)
            def _(m):
                rm = rows_of(m)
                lane = lane_iota(L)
                a = pltpu.roll(gbuf[t // 2, rm], turn, 1)
                d = pltpu.roll(ddt, (320 - m * SPAN - n * 6) % 128, 1)
                piece = jnp.where(lane < 64, a, jnp.where(lane < 70, d, 0.0))
                din5[rm, tile(n)] = piece.astype(BF)

            a = pltpu.roll(gbuf[t // 2, 4 * L :], turn, 1)
            din5[4 * L :, tile(n)] = jnp.where(lane_iota(64) < 64, a, 0.0).astype(BF)
        for n in range(2):
            cols = slice(256 * n, 256 * n + 256)
            hsum[...] = dot(nt[:, 4 * L :], din5[4 * L :, cols])
            v = dot(nt[:, : 4 * L], din5[: 4 * L, cols]) + hsum[...]
            pcs[2 * n] = v[:, :128]
            pcs[2 * n + 1] = v[:, 128:]
            place_rows(wpc, bm, me_dp, 256 * n, 128, 128, n)
            place_rows(wpc, br, me_dp, 256 * n + 128, 128, 128, n)
        add_weighted(ngx, pcs, wpc, (0,))
        ngo[...] = (
            lax.dot_general(
                jnp.ones((8, 128), F32),
                ngx[...],
                (((1,), (1,)), ((), ())),
                preferred_element_type=F32,
                precision=lax.Precision.HIGHEST,
            )
            / gain[...]
        )
        count, brow = keep.shape[0], keep.shape[1]
        for n in range(4):
            ref = keep if n % 2 == 0 else send
            at = slice(384 + 128 * (n // 2), 512 + 128 * (n // 2))
            if count == 1:
                ref[0, :, at] = pcs[n].astype(BF)
                continue
            t = n ^ me_t
            quarter = brow // 4
            for m in range(count):
                for c in range(4):
                    pblk[quarter * c : quarter * c + quarter] = pcs[
                        c ^ me_t, pl.ds(pl.multiple_of(brow * m + quarter * t, 8), quarter)
                    ]
                both = jnp.where(
                    lane_iota(brow) < 64, pblk[...], pcs[n, brow * m : brow * m + brow]
                )
                ref[m ^ me_dp, :, at] = both.astype(BF)


def k9z_body(sc, dg, wzm, wzr, dn, wz):
    place_pair(wz, wzm, wzr, sc[9])
    dn[...] = dot_nt(dg[0], wz[...])


def k9_body(sc, din0, din1, din5, dna, dnb, am, ar, bm, br, dn, wx, wpc):
    g = pl.program_id(0)
    place_p1(wx, am, bm, ar, br, sc[9], wpc)

    @pl.when(g == 0)
    def _():
        dn[...] = dot_nt(din0[...], wx[...])

    @pl.when(g == 1)
    def _():
        dn[...] += dot_nt(din1[...], wx[...])
        dn[: 4 * L] += dna[...] + dnb[...]

    dn[...] += dot_nt(din5[...], wpc[...])


def k10_body(sc, dn, hr, tok, cot, gain, ig):
    s = pl.program_id(0)
    d = dn[...]
    extra = hr[...].astype(F32)
    width = d.shape[1]
    d = jnp.concatenate([d[: L - 16], d[L - 16 :] + extra], axis=0)
    tv = tok[...].astype(F32)
    r = lax.rsqrt(jnp.mean(tv * tv, axis=-1, keepdims=True) + EPS)
    tr = tv * r
    gd = gain[...] * d
    inner = jnp.sum(gd * tr, axis=-1, keepdims=True) * (1.0 / width)
    keep = row_iota(L, 1) < sc[2 * s + 1]
    res = jnp.where(keep, cot[...].astype(F32), 0.0)
    ig[...] = (res + r * (gd - tr * inner)).astype(BF)


def full(shape):
    return pl.BlockSpec(shape, lambda *a: (0,) * len(shape))


def call(body, grid, in_specs, out_specs, out_shapes, scratch, cost, name, aliases=None, vmem_mib=VMEM_MIB):
    flops, moved = cost
    return pl.pallas_call(
        body,
        grid_spec=pltpu.PrefetchScalarGridSpec(
            num_scalar_prefetch=1,
            grid=grid,
            in_specs=in_specs,
            out_specs=out_specs,
            scratch_shapes=scratch,
        ),
        out_shape=out_shapes,
        compiler_params=pltpu.CompilerParams(vmem_limit_bytes=vmem_mib * 2**20),
        cost_estimate=pl.CostEstimate(flops=flops, bytes_accessed=moved, transcendentals=0),
        input_output_aliases=aliases or {},
        name=name,
    )


def sds(shape, dtype):
    return pltpu.HBM(shape, dtype)


def anywhere(count):
    return [pl.BlockSpec(memory_space=pl.ANY)] * count


def flip(value, axis, bit):
    count = lax.axis_size(axis)
    return lax.ppermute(value, axis, [(a, a ^ bit) for a in range(count)])


def meet(*values):
    return lax.optimization_barrier(values)


def per_device(
    tokens, lengths, cotangent, norm_gain, w_z, w_x, w_bc, w_dt, conv_x, bias_x, conv_bc, bias_bc,
    dt_bias, a_log, skip_d, out_gain, w_out,
):
    tcount = lax.axis_size("tensor")
    dpcount = lax.axis_size("dp")
    me_t = lax.axis_index("tensor")
    me_dp = lax.axis_index("dp")
    slots, own_len, dim = tokens.shape
    rows = slots * own_len
    shard = w_z.shape[0]
    cols = w_z.shape[1]
    heads = w_dt.shape[1]
    fast = shard % 32 == 0 and dpcount & (dpcount - 1) == 0 and dpcount >= 8
    count = dpcount if fast else 1
    brow = shard if fast else dim

    first = lengths[:, 0] - me_t * own_len
    second = first + lengths[:, 1]
    sc = jnp.concatenate(
        [
            jnp.stack([first, second], axis=1).reshape(-1),
            jnp.stack([me_t, me_dp]),
            jnp.zeros((6,), jnp.int32),
        ]
    ).astype(jnp.int32)
    tok = tokens.reshape(rows, dim)
    cot = cotangent.reshape(rows, dim)
    gain = norm_gain.reshape(1, dim)

    bq = w_bc.shape[1] // tcount
    state = w_bc.shape[1] // 2
    own_bc = lax.dynamic_slice_in_dim(w_bc, me_t * bq, bq, 1)
    p1 = jnp.concatenate(
        [w_x, own_bc, w_dt, jnp.zeros((shard, 128 - bq - heads), BF)], axis=1
    )
    tail = tokens[:, own_len - 16 :, :].reshape(slots * 16, dim)
    def add_y(v, at):
        return jnp.stack([v, flip(v, "dp", 1)], axis=at)

    def add_x(v):
        return jnp.stack([v, flip(v, "tensor", 2)], axis=0)

    def blocks(v):
        return v.reshape(2, count, brow, v.shape[-1])

    def core(v):
        return flip(v, "tensor", 1)

    par = jnp.concatenate(
        [
            conv_x,
            bias_x[None],
            out_gain[None],
            jnp.pad(dt_bias, (0, cols - heads))[None],
            jnp.pad(a_log, (0, cols - heads))[None],
            jnp.repeat(skip_d, cols // heads)[None],
            jnp.zeros((7, cols), F32),
        ],
        axis=0,
    )
    bbc = bias_bc.reshape(1, -1)

    def grown(v, got, at):
        v = jnp.stack([v, got], axis=at)
        return v.reshape(v.shape[: at - 1] + (-1,) + v.shape[at + 1 :])

    if fast:
        v = p1[None]
        w2 = jnp.stack([w_z, w_out])[None]
        bit = dpcount // 2
        got = flip(v, "dp", bit)
        got, w2, sc, par, tail, gain = meet(got, w2, sc, par, tail, gain)
        v = grown(v, got, 1)
        while bit > 4:
            bit //= 2
            v = grown(v, flip(v, "dp", bit), 1)
            w2 = grown(w2, flip(w2, "dp", 2 * bit), 1)
        halo = lax.ppermute(tail, "tensor", [(a, a + 1) for a in range(tcount - 1)])
        got, w2, parx, halo = meet(flip(v, "dp", 2), w2, flip(par, "tensor", 2), halo)
        par = jnp.stack([par, parx], axis=0)
        v = grown(v, got, 1)
        az, bz = v[..., :256], v[..., 256:]
        ax, by, parc, w2z = meet(
            flip(az, "tensor", 2), flip(bz, "dp", 1), core(par), flip(w2, "dp", 4)
        )
        w2 = grown(w2, w2z, 1)
        par = jnp.concatenate([par, parc], axis=-1)
        ax = jnp.stack([az, ax], axis=0)
        by = jnp.stack([bz, by], axis=1)
        ay, bx, w2z, par = meet(flip(ax, "dp", 1), flip(by, "tensor", 2), flip(w2, "dp", 2), par)
        w2 = grown(w2, w2z, 1)
        wam = blocks(jnp.stack([ax, ay], axis=2))
        wbm = blocks(jnp.stack([by, bx], axis=0))
        zz, oz = w2[:, 0], w2[:, 1]
        zx, oy = flip(zz, "tensor", 2), flip(oz, "dp", 1)
        war, wbr = core(wam), core(wbm)
    else:
        halo = lax.ppermute(tail, "tensor", [(a, a + 1) for a in range(tcount - 1)])
        par = add_x(par)
        par = jnp.concatenate([par, core(par)], axis=-1)
        z1 = lax.all_gather(p1, "dp", axis=0, tiled=True)[None]
        wam = add_x(z1[..., :256])
        wbm = add_x(z1[..., 256:])
        war, wbr = core(wam), core(wbm)

    srows = slots * state
    wide = 2 * cols
    erows = rows + 64
    p1block = (1, count, brow, 256)
    wblock = (1, count, brow, cols)
    vmem = pltpu.VMEM

    def w_g(g, *a):
        return (g, 0, 0, 0)

    nrm, inx, blow, clow, bt, sin, dbc, cump, stepp, sigp, etp, reachp, decay, fac, uvp, mask, back, ct = call(
        k1_body,
        (2,),
        [full((rows, dim)), full((64, dim)), full((1, dim))]
        + [pl.BlockSpec(p1block, w_g)] * 4
        + [full((2, 16, wide)), full((4, 2 * state)), full((1, 2 * state))],
        [
            full((erows, dim)),
            pl.BlockSpec((1, erows, wide), lambda g, sc: (g, 0, 0)),
            full((rows, state)),
            full((rows, state)),
            full((srows, L)),
            full((2, erows, state)),
            full((2, rows, state)),
        ]
        + [full((L, 128))] * 6
        + [full((8, 128)), full((L, 128)), full((L, 128)), full((L + 8, 128)), full((128, L))],
        [
            sds((erows, dim), BF),
            sds((2, erows, wide), BF),
            sds((rows, state), BF),
            sds((rows, state), BF),
            sds((srows, L), BF),
            sds((2, erows, state), F32),
            sds((2, rows, state), F32),
        ]
        + [sds((L, 128), F32)] * 6
        + [sds((8, 128), F32), sds((L, 128), F32), sds((L, 128), F32), sds((L + 8, 128), F32)]
        + [sds((128, L), F32)],
        [
            vmem((dim, wide), BF),
            vmem((dim, 256), BF),
            vmem((erows, 256), F32),
            vmem((L, 128), F32),
            vmem((L + 8, 128), F32),
        ],
        (int(7e9), int(2e7)),
        "projections",
    )(sc, tok, halo, gain, wam, war, wbm, wbr, par, conv_bc, bbc)

    def gs(g, s, sc):
        return (g, s, 0)

    def halo_gs(g, s, sc):
        return (g, rows // 16 + s, 0)

    def by_s(g, s, sc):
        return (s, 0)

    def mirror(g, sc):
        return (0, g ^ (sc[8] // 2))

    group = (1, L, wide)

    def gsel(g):
        return lambda s, sc: (g, s, 0)

    def conv_and_states(g, inx, kept):
        return call(
            functools.partial(k2_body, g),
            (slots,),
            [
                pl.BlockSpec(group, gsel(g)),
                pl.BlockSpec((1, 16, wide), lambda s, sc: (g, rows // 16 + s, 0)),
                pl.BlockSpec((1, 16, wide), lambda s, sc: (g, 0, 0)),
                pl.BlockSpec((state, L), lambda s, sc: (s, 0)),
                full((L, 128)),
                full((L, 128)),
                full((8, 128)),
                full((L, 128)),
            ]
            + anywhere(len(kept)),
            [pl.BlockSpec(group, gsel(g))] * 3
            + [pl.BlockSpec((srows + 16, wide), lambda s, sc: mirror(g, sc))],
            [sds((2, rows, wide), BF)] * 3 + [sds((srows + 16, 2 * wide), BF)],
            [
                vmem((L, wide), BF),
                vmem((6, L + 8, 128), F32),
                vmem((256, wide), BF),
                vmem((L, wide), F32),
                vmem((L, wide), F32),
            ],
            (int(5e9) if g else 1, int(2e7) if g else 1),
            "conv_and_states_%d" % g,
            {9 + n: n for n in range(len(kept))},
        )(sc, inx, inx, par, bt, stepp, etp, fac, mask, *kept)

    if fast:
        inx0, zx, oy = meet(inx, zx, oy)
        zx = jnp.stack([zz, zx], axis=0)
        oy = jnp.stack([oz, oy], axis=1)
        zy, ox = flip(zx, "dp", 1), flip(oy, "tensor", 2)
        xl, xs, dsl, st = conv_and_states(1, inx, conv_and_states(0, inx0, []))
        st, zy, ox = meet(st, zy, ox)
        wzm = blocks(jnp.stack([zx, zy], axis=2))
        wom = blocks(jnp.stack([oy, ox], axis=0))
        wzr, wor = core(wzm), core(wom)
    else:
        xl, xs, dsl, st = conv_and_states(1, inx, conv_and_states(0, inx, []))
        wzm = add_x(lax.all_gather(w_z, "dp", axis=0, tiled=True)[None])
        wom = add_x(lax.all_gather(w_out, "dp", axis=0, tiled=True)[None])
        wzr, wor = core(wzm), core(wom)

    def end_state(mine, one):
        f = mine[srows : srows + 4].astype(F32) + mine[srows + 4 : srows + 8].astype(F32)
        width = mine.shape[1]
        end = mine[:srows].astype(F32).reshape(slots, state, width) + f[:, None] * one[
            :srows
        ].astype(F32).reshape(slots, state, width)
        return end.astype(BF).reshape(srows, width)

    r1 = lax.ppermute(st, "tensor", [(0, 1), (2, 3)])
    end = end_state(st, r1)
    r2 = lax.ppermute(end, "tensor", [(1, 2)])
    xs3, _ = meet(xs, end)

    def within_of(g, kept):
        return call(
            functools.partial(k3_body, g),
            (slots,),
            [
                pl.BlockSpec(group, gsel(g)),
                pl.BlockSpec((L, state), lambda s, sc: (s, 0)),
                pl.BlockSpec((L, state), lambda s, sc: (s, 0)),
                full((L, 128)),
                full((L, 128)),
                full((128, L)),
            ]
            + anywhere(len(kept)),
            pl.BlockSpec(group, gsel(g)),
            sds((2, rows, wide), F32),
            [
                vmem((2, 128, 128), F32),
                vmem((128, 128), BF),
                vmem((256, wide), BF),
                vmem((L, wide), F32),
                vmem((256, 2 * wide), BF),
                vmem((L, 2 * wide), F32),
            ],
            (int(5e9), int(1e7)),
            "within_%d" % g,
            {7 + n: n for n in range(len(kept))},
        )(sc, xs3, blow, clow, cump, uvp, ct, *kept)

    within = within_of(1, [within_of(0, [])])
    nrm4, within = meet(nrm, within)

    gate, dgn, dbr = call(
        k4_body,
        (2, 3),
        [full((erows, dim)), full((rows, dim))] + [pl.BlockSpec(wblock, w_g)] * 4,
        [pl.BlockSpec((1, rows, 256), lambda g, n, sc: (g, 0, n))] * 2 + [full((rows, dim))],
        [sds((2, rows, wide), BF)] * 2 + [sds((rows, dim), BF)],
        [vmem((dim, wide), BF), vmem((dim, wide), BF)],
        (int(5e9), int(2e7)),
        "gate_and_out_backward",
    )(sc, nrm4, cot, wzm, wzr, wom, wor)

    gate, r2 = meet(gate, r2)
    r3 = lax.ppermute(r2, "tensor", [(2, 3)])

    def p_gs(phase):
        def index(p, g, s, sc):
            return (
                jnp.where(p == phase, g, 0 if phase else 1),
                jnp.where(p == phase, s, 0 if phase else slots - 1),
                0,
            )

        return index

    def p_mirror(phase):
        def index(p, g, s, sc):
            return mirror(jnp.where(p == phase, g, 0 if phase else 1), sc)

        return index

    def pgs(p, g, s, sc):
        return (g, s, 0)

    def p_w(p, g, s, sc):
        return (jnp.where(p == 1, g, 0), 0, 0, 0)

    out, gn, dg, dy, dp, prev, rowsum, dc5, small5 = call(
        k5_body,
        (2, 2, slots),
        [
            pl.BlockSpec(group, p_gs(0)),
            pl.BlockSpec(group, pgs),
            pl.BlockSpec(group, pgs),
            pl.BlockSpec(group, pgs),
            pl.BlockSpec((srows + 16, wide), p_mirror(0)),
            pl.BlockSpec((srows, wide), p_mirror(0)),
            pl.BlockSpec((srows, wide), p_mirror(0)),
            full((L, 128)),
            full((8, 128)),
            pl.BlockSpec((L, state), lambda p, g, s, sc: (s, 0)),
            pl.BlockSpec((1, 16, wide), lambda p, g, s, sc: (g, 0, 0)),
            pl.BlockSpec(wblock, p_w),
            pl.BlockSpec(wblock, p_w),
            full((rows, dim)),
        ],
        [
            full((rows, dim)),
            pl.BlockSpec(group, p_gs(1)),
            pl.BlockSpec(group, p_gs(1)),
            pl.BlockSpec(group, p_gs(1)),
            pl.BlockSpec((srows + 16, wide), p_mirror(1)),
            full((2, srows, wide)),
            full((L, 128)),
            full((rows, state)),
            full((2, 8, wide)),
        ],
        [
            sds((rows, dim), BF),
            sds((2, rows, wide), BF),
            sds((2, rows, wide), BF),
            sds((2, rows, wide), BF),
            sds((srows + 16, 2 * wide), BF),
            sds((2, srows, wide), BF),
            sds((L, 128), F32),
            sds((rows, state), F32),
            sds((2, 8, wide), F32),
        ],
        [
            vmem((2, rows, wide), F32),
            vmem((2, rows, 128), F32),
            vmem((rows, dim), F32),
            vmem((dim, wide), BF),
            vmem((rows, wide), BF),
            vmem((16, cols), F32),
            vmem((L, wide), BF),
            vmem((L, wide), BF),
            vmem((L, wide), BF),
            vmem((wide, 128), BF),
            vmem((state, wide), BF),
            vmem((256, wide), BF),
            vmem((L, wide), F32),
        ],
        (int(1.5e10), int(4e7)),
        "gated_norm",
        vmem_mib=K5_MIB,
    )(sc, within, gate, dgn, xl, r1, r2, r3, reachp, fac, clow, par, wom, wor, tok)

    q1 = lax.ppermute(dp, "tensor", [(1, 0), (3, 2)])

    gshape = (2, count, brow, cols)
    ok, osend, zk, zsend, nt, ngz = call(
        k6_body,
        (2,),
        [full((erows, dim)), full((rows, dim))]
        + [pl.BlockSpec((1, rows, wide), lambda g, sc: (g, 0, 0))] * 2
        + [pl.BlockSpec(wblock, w_g)] * 2,
        [pl.BlockSpec((1,) + gshape[1:], w_g)] * 4 + [full((dim, erows)), full((dim, 128))],
        [sds(gshape, BF)] * 4 + [sds((dim, erows), BF), sds((dim, 128), F32)],
        [vmem((dim, rows), BF), vmem((dim, wide), F32), vmem((dim, wide), BF)],
        (int(5e9), int(2e7)),
        "outer_weight_grads",
    )(sc, nrm, dbr, gn, dg, wzm, wzr)

    osend, q1 = meet(osend, q1)
    dy1, end = meet(dy, end_state(dp, q1))
    q2 = lax.ppermute(end, "tensor", [(2, 1)])

    def summed(a, b):
        return (a.astype(F32) + b.astype(F32)).astype(BF)

    def reduce_step(v, axis, mesh_axis, bit):
        keep = lax.index_in_dim(v, 0, axis, False)
        send = lax.index_in_dim(v, 1, axis, False)
        return summed(keep, flip(send, mesh_axis, bit))

    def reduce_x(v, axis):
        return reduce_step(v, axis, "tensor", 2)

    def reduce_dp(v, bit):
        v = v.reshape((v.shape[0] // 2, 2) + v.shape[1:])
        return reduce_step(v, 1, "dp", bit)

    def finish(v, bit):
        while bit < dpcount:
            v = reduce_dp(v, bit)
            bit *= 2
        return v[0].astype(F32)

    def reduce_slow(v):
        v = v.reshape(dpcount, shard, v.shape[-1])
        got = lax.all_to_all(v, "dp", split_axis=0, concat_axis=0, tiled=True)
        return got.astype(F32).sum(axis=0)

    def reduce_core(keep, send):
        return summed(keep, core(send))

    if fast:
        osr, zsr = core(osend), core(zsend)
    else:
        grad_w_out = reduce_slow(reduce_x(reduce_core(ok, osend), 0)[0])
        grad_w_z = reduce_slow(reduce_x(reduce_core(zk, zsend), 0)[0])

    def within_backward(g, dy, kept):
        return call(
            functools.partial(k7_body, g),
            (slots,),
            [
                pl.BlockSpec(group, gsel(g)),
                pl.BlockSpec(group, gsel(g)),
                pl.BlockSpec((L, state), lambda s, sc: (s, 0)),
                pl.BlockSpec((L, state), lambda s, sc: (s, 0)),
                full((L, 128)),
                full((L, 128)),
                full((128, L)),
            ]
            + anywhere(len(kept)),
            [
                pl.BlockSpec(group, gsel(g)),
                pl.BlockSpec((2, L, state), lambda s, sc: (0, s, 0)),
                full((L, 128)),
            ],
            [sds((2, rows, wide), F32), sds((2, rows, state), F32), sds((L, 128), F32)],
            [
                vmem((2, 128, 128), F32),
                vmem((128, 128), BF),
                vmem((128, wide), BF),
                vmem((128, wide), BF),
                vmem((256, wide), BF),
                vmem((L, wide), F32),
                vmem((256, 2 * wide), BF),
                vmem((L, 2 * wide), F32),
                vmem((wide, 128), BF),
                vmem((L, wide), BF),
            ],
            (int(1e10) if g else 1, int(2e7) if g else 1),
            "within_backward_%d" % g,
            {8 + n: n for n in range(len(kept))},
        )(sc, xs, dy, blow, clow, cump, uvp, ct, *kept)

    dxw, bc7a, corr_a = within_backward(1, dy1, [])
    if fast:
        dy0, osr, zsr, dxw = meet(dy, osr, zsr, dxw)
        vo = summed(ok, osr).reshape((2, count // 2, 2, brow, cols))
        vor = flip(vo[:, :, 1], "dp", 1)
    else:
        dy0 = dy
    dxw, bc7b, corr_b = within_backward(0, dy0, [dxw])

    def states_backward(g, last, nt, extra_in, extra_specs):
        width = cols + 256 if last else cols
        gshape = (count, brow, width)

        def at(s, sc):
            return (g, s, 0)

        in_specs = [
            full((dim, erows)),
            pl.BlockSpec(group, at),
            pl.BlockSpec(group, at),
            pl.BlockSpec(group, at),
            pl.BlockSpec(group, at),
            pl.BlockSpec((1, 16, wide), lambda s, sc: (g, rows // 16 + s, 0)),
            pl.BlockSpec(group, at),
            pl.BlockSpec((srows + 16, wide), lambda s, sc: mirror(g, sc)),
            pl.BlockSpec((srows, wide), lambda s, sc: mirror(g, sc)),
            pl.BlockSpec((srows, wide), lambda s, sc: mirror(g, sc)),
            pl.BlockSpec((1, srows, wide), lambda s, sc: (g, 0, 0)),
            pl.BlockSpec((L, state), lambda s, sc: (s, 0)),
            full((L, 128)),
            full((L, 128)),
            full((L + 8, 128)),
            full((2, 16, wide)) if last else pl.BlockSpec((1, 16, wide), lambda s, sc: (g, 0, 0)),
            pl.BlockSpec(p1block, lambda s, sc: (g, 0, 0, 0)),
            pl.BlockSpec(p1block, lambda s, sc: (g, 0, 0, 0)),
        ]
        if last:
            in_specs += [full((2,) + p1block[1:])] * 2
        else:
            in_specs += [pl.BlockSpec(p1block, lambda s, sc: (g, 0, 0, 0))] * 2
        in_specs += extra_specs
        outs = [
            (gshape, BF),
            (gshape, BF),
            ((erows, wide), BF),
            ((L, 128), F32),
            ((8, 128), F32),
            ((rows, state), F32),
            ((8, wide), F32),
            ((dim, 128), F32),
        ]
        scratch = [
            vmem((dim, wide), F32),
            vmem((dim, 256), F32),
            vmem((state, wide), F32),
            vmem((16, cols), F32),
            vmem((state, wide), BF),
            vmem((L, wide), BF),
            vmem((L, wide), BF),
            vmem((L, wide), BF),
            vmem((wide, 128), BF),
            vmem((dim, wide), BF),
        ]
        if last:
            outs += [((erows, 512), BF), ((2, 8, state), F32), ((8, 128), F32), ((8, dim), F32)]
            scratch += [
                vmem((dim, 512), BF),
                vmem((2, erows, state), F32),
                vmem((4, dim, 128), F32),
                vmem((brow, 128), F32),
            ]
        scratch += [vmem((L, wide), F32), vmem((6, L + 16, 128), F32), vmem((256, wide), BF)]
        scratch += [vmem((L, wide), F32), vmem((L, wide), F32)]
        return call(
            functools.partial(k8_body, g, last),
            (slots,),
            in_specs,
            [full(shape) for shape, _ in outs],
            [sds(shape, dtype) for shape, dtype in outs],
            scratch,
            (int(1e10), int(2e7)),
            "states_backward_%d" % g,
        )(sc, nt, xs, dy, dsl, inx, inx, dxw, q1, q2, q3, prev, blow, stepp, etp, back, par, wam, war, wbm, wbr, *extra_in)

    def normed_grad_z(g, dg):
        return call(
            k9z_body,
            (1,),
            [
                pl.BlockSpec((1, rows, wide), lambda i, sc: (g, 0, 0)),
                pl.BlockSpec(wblock, lambda i, sc: (g, 0, 0, 0)),
                pl.BlockSpec(wblock, lambda i, sc: (g, 0, 0, 0)),
            ],
            full((rows, dim)),
            sds((rows, dim), F32),
            [vmem((dim, wide), BF)],
            (1, 1),
            "normed_grad_z%d" % g,
        )(sc, dg, wzm, wzr)

    dga, dxw = meet(dg, dxw)
    dna = normed_grad_z(1, dga)
    if fast:
        dxw, q2, dna, vor, zk = meet(dxw, q2, dna, vor, zk)
        vo = summed(vo[:, :, 0], vor)
        vor = flip(vo[1], "tensor", 2)
        vz = summed(zk, zsr).reshape((2, count // 2, 2, brow, cols))
        vzr = flip(vz[:, :, 1], "dp", 1)
    else:
        dxw, q2, dna = meet(dxw, q2, dna)
    q3 = lax.ppermute(q2, "tensor", [(1, 0)])
    ka, sa, din1, seg1, end1, dba1, small1, nga = states_backward(1, False, nt, [], [])
    if fast:
        sa, vor, vzr = meet(sa, vor, vzr)
        vo = summed(vo[0], vor)
        vz = summed(vz[:, :, 0], vzr)
        vzr = flip(vz[1], "tensor", 2)
    sar = core(sa)
    dgb, _ = meet(dg, sa)
    dnb = normed_grad_z(0, dgb)
    nt0, sar, dnb = meet(nt, sar, dnb)
    va = summed(ka, sar)
    xa = flip(va, "tensor", 2)
    ks, ss, din0, _, _, _, small0, _, din5, sbc, sdt, ngo = states_backward(
        0,
        True,
        nt0,
        [fac, sigp, decay, gain, ngz, nga, conv_bc, bc7a, bc7b, corr_a, corr_b, dc5, rowsum, sin, dbc, seg1, end1, dba1],
        [
            full((8, 128)),
            full((L, 128)),
            full((L, 128)),
            full((1, dim)),
            full((dim, 128)),
            full((dim, 128)),
            full((4, 2 * state)),
            full((2, rows, state)),
            full((2, rows, state)),
            full((L, 128)),
            full((L, 128)),
            full((rows, state)),
            full((L, 128)),
            full((2, erows, state)),
            full((2, rows, state)),
            full((L, 128)),
            full((8, 128)),
            full((rows, state)),
        ],
    )

    if fast:
        ss, xa, vzr = meet(ss, xa, vzr)
        vw = jnp.stack([vo, summed(vz[0], vzr)]).reshape((2, count // 4, 2, brow, cols))
        vwr = flip(vw[:, :, 1], "dp", 2)
    dts = sdt[:2].reshape(2, slots, SPAN)[:, :, : 4 * heads].sum(axis=1).reshape(2, 2, 2, heads)
    dts = jnp.pad(dts, ((0, 0), (0, 0), (0, 0), (0, cols - heads)))
    dts = jnp.swapaxes(dts, 0, 1).reshape(2, 2, wide)
    mine = jnp.concatenate(
        [
            jnp.stack([small0[:5], small1[:5]]),
            small5[:, :2],
            dts,
            jnp.zeros((2, 7, wide), F32),
        ],
        axis=1,
    )
    flat = jnp.concatenate(
        [jnp.concatenate([sbc[0, :5], sbc[1, :5]], axis=1).reshape(-1), ngo[0]]
    )
    flat = jnp.pad(flat, (0, 8 * cols - flat.shape[0])).reshape(8, cols)
    send = jnp.concatenate([mine[:, :, cols:].reshape(32, cols), flat], axis=0)
    din0, ssr, got = meet(din0, core(ss), core(send))
    own = mine[:, :, :cols] + got[:32].reshape(2, 16, cols)
    flat = flat + got[32:]
    vb = summed(ks, ssr)
    px = flip(vb[..., cols + 128 :], "tensor", 2)
    vx = summed(vb[..., :cols], xa)
    if fast:
        vx = vx.reshape((count // 2, 2) + vx.shape[1:])
        vxr = flip(vx[:, 1], "dp", 1)
    both = jnp.concatenate([own[0], flat], axis=0)
    got = flip(jnp.concatenate([own[1], flat], axis=0), "tensor", 2)

    dn = call(
        k9_body,
        (2,),
        [
            full((erows, wide)),
            full((erows, wide)),
            pl.BlockSpec((erows, 256), lambda g, sc: (0, g)),
            full((rows, dim)),
            full((rows, dim)),
        ]
        + [pl.BlockSpec(p1block, w_g)] * 4,
        full((erows, dim)),
        sds((erows, dim), F32),
        [vmem((dim, wide), BF), vmem((dim, 256), BF)],
        (int(6e9), int(2e7)),
        "normed_grad",
    )(sc, din0, din1, din5, dna, dnb, wam, war, wbm, wbr)

    if fast:
        dn, px, vxr, got, vwr = meet(dn, px, vxr, got, vwr)
        vw = summed(vw[:, :, 0], vwr).reshape((2, count // 8, 2, brow, cols))
        vwr = flip(vw[:, :, 1], "dp", 4)
        vx = summed(vx[:, 0], vxr)
        vp = summed(vb[..., cols : cols + 128], px)
        vp = vp.reshape((count // 2, 2) + vp.shape[1:])
        vpr = flip(vp[:, 1], "dp", 1)
        both = both + got
        got = flip(both, "dp", 1)
    hr = lax.ppermute(dn[rows:].astype(BF), "tensor", [(a + 1, a) for a in range(tcount - 1)])
    if fast:
        hr, vpr, got, vwr = meet(hr, vpr, got, vwr)
        vw = summed(vw[:, :, 0], vwr)
        grad_w_out, grad_w_z = finish(vw[0], 8), finish(vw[1], 8)
        v1 = jnp.concatenate([vx, summed(vp[:, 0], vpr)], axis=-1)
        v1 = v1.reshape((count // 4, 2) + v1.shape[1:])
        v1r = flip(v1[:, 1], "dp", 2)
        both = both + got
        got = flip(both, "dp", 2)

    ig = call(
        k10_body,
        (slots,),
        [
            pl.BlockSpec((L, dim), lambda s, sc: (s, 0)),
            pl.BlockSpec((16, dim), lambda s, sc: (s, 0)),
            pl.BlockSpec((L, dim), lambda s, sc: (s, 0)),
            pl.BlockSpec((L, dim), lambda s, sc: (s, 0)),
            full((1, dim)),
        ],
        pl.BlockSpec((L, dim), lambda s, sc: (s, 0)),
        sds((rows, dim), BF),
        [],
        (int(1e9), int(1e7)),
        "input_grad",
    )(sc, dn, hr, tok, cot, gain)

    if fast:
        ig, v1r, got = meet(ig, v1r, got)
        v1 = summed(v1[:, 0], v1r)
        both = both + got
        bit = 4
        while bit < dpcount:
            both = both + flip(both, "dp", bit)
            v1 = reduce_dp(v1, bit)
            bit *= 2
        grad1 = v1[0].astype(F32)
    else:
        both = lax.psum(both + got, "dp")
        v1 = jnp.concatenate([vx, summed(vb[..., cols : cols + 128], px)], axis=-1)
        grad1 = reduce_slow(v1)
    own, flat = both[:16], both[16:].reshape(-1)
    bcs = flat[: 5 * 2 * state].reshape(5, 2 * state)
    ngain = flat[5 * 2 * state : 5 * 2 * state + dim]
    skip_grad = own[6].reshape(heads, cols // heads).sum(axis=1)

    mine_bc = grad1[:, cols : cols + bq]
    if fast:
        got = mine_bc.reshape(tcount, shard // tcount, bq)
    else:
        parts = mine_bc.reshape(tcount, shard // tcount, bq)
        got = lax.all_to_all(parts, "tensor", split_axis=0, concat_axis=0, tiled=True)
    grad_w_bc = jnp.swapaxes(got, 0, 1).reshape(shard // tcount, bq * tcount)

    return (
        out.reshape(tokens.shape),
        ig.reshape(tokens.shape),
        ngain,
        grad_w_z,
        grad1[:, :cols],
        grad_w_bc,
        grad1[:, cols + bq : cols + bq + heads],
        own[:4],
        own[4],
        bcs[:4],
        bcs[4],
        own[7, :heads],
        own[8, :heads],
        skip_grad,
        own[5],
        grad_w_out,
    )


def solution(mesh):
    return jax.shard_map(
        per_device,
        mesh=mesh,
        in_specs=(
            P("dp", "tensor", None), P("dp", None), P("dp", "tensor", None), P(),
            P("dp", "tensor"), P("dp", "tensor"), P("dp", None), P("dp", "tensor"),
            P(None, "tensor"), P("tensor"), P(), P(),
            P("tensor"), P("tensor"), P("tensor"), P("tensor"), P("dp", "tensor"),
        ),
        out_specs=(
            P("dp", "tensor", None), P("dp", "tensor", None), P(),
            P("dp", "tensor"), P("dp", "tensor"), P(("dp", "tensor"), None), P("dp", "tensor"),
            P(None, "tensor"), P("tensor"), P(), P(),
            P("tensor"), P("tensor"), P("tensor"), P("tensor"), P("dp", "tensor"),
        ),
        check_vma=False,
    )
```

```python
import functools

import jax
import jax.numpy as jnp
from jax import lax
from jax.experimental import pallas as pl
from jax.experimental.pallas import tpu as pltpu
from jax.sharding import PartitionSpec as P

INNER = 1536
L = 256
HD = 64
SPAN = 32
EPS = 1e-05
LOG2E = 1.4426950408889634
F32 = jnp.float32
BF = jnp.bfloat16
CHUNK = 64
WIDE = 768
VMEM_MIB = 40
K5_MIB = 58


def dot(a, b):
    return jnp.dot(a, b, preferred_element_type=F32)


def dot_nt(a, b):
    return lax.dot_general(a, b, (((1,), (1,)), ((), ())), preferred_element_type=F32)


def dot_high(a, b):
    return jnp.dot(a, b, preferred_element_type=F32, precision=lax.Precision.HIGHEST)


def sigmoid(v):
    return 0.5 * jnp.tanh(0.5 * v) + 0.5


def lane_iota(rows):
    return lax.broadcasted_iota(jnp.int32, (rows, 128), 1)


def row_iota(rows, lanes):
    return lax.broadcasted_iota(jnp.int32, (rows, lanes), 0)


def seg_of(idx, fe, se):
    return (idx >= fe).astype(jnp.int32) + (idx >= se).astype(jnp.int32)


def ends(sc, s):
    return sc[2 * s], sc[2 * s + 1]


def pair_cols(cols, first):
    lane = lane_iota(cols.shape[0])
    left = jnp.broadcast_to(cols[:, first : first + 1], cols.shape)
    right = jnp.broadcast_to(cols[:, first + 1 : first + 2], cols.shape)
    return jnp.where(lane < HD, left, right)


def head_pick():
    r = lax.broadcasted_iota(jnp.int32, (WIDE, 128), 0)
    c = lax.broadcasted_iota(jnp.int32, (WIDE, 128), 1)
    return jnp.where(c == r // HD, 1.0, 0.0)


def head_spread():
    r = lax.broadcasted_iota(jnp.int32, (256, WIDE), 0)
    c = lax.broadcasted_iota(jnp.int32, (256, WIDE), 1)
    return jnp.where(r % 128 == c // HD, 1.0, 0.0).astype(BF)


def expand(dst, cols, spread):
    high = cols.astype(BF)
    low = (cols - high.astype(F32)).astype(BF)
    both = jnp.concatenate([high, low], axis=1)
    for n in range(3):
        dst[:, 256 * n : 256 * n + 256] = dot(both, spread[:, 256 * n : 256 * n + 256])


def three_terms(v):
    high = v.astype(BF).astype(F32)
    mid = (v - high).astype(BF).astype(F32)
    return high, mid, v - high - mid


def tile_spread():
    r = lax.broadcasted_iota(jnp.int32, (256, 2 * WIDE), 0)
    h = lax.broadcasted_iota(jnp.int32, (256, 2 * WIDE), 1) // 128
    return jnp.where((r == h) | (r == h + 128) | (r == h + 144), 1.0, 0.0).astype(BF)


def expand_tiles(dst, cols, spread):
    high, mid, low = three_terms(cols)
    lane = lane_iota(L)
    rest = jnp.where(lane < 16, mid, pltpu.roll(low, 16, 1))
    left = jnp.concatenate([high, rest], axis=1).astype(BF)
    for n in range(6):
        dst[:, 256 * n : 256 * n + 256] = dot(left, spread[:, 256 * n : 256 * n + 256])


def to_lane0(packed, s, g):
    return pltpu.roll(packed, (256 - s * SPAN - g * 12) % 128, 1)


def from_lane0(cols, s, g):
    return pltpu.roll(cols, s * SPAN + g * 12, 1)


def rows_of(s, length=L):
    return pl.ds(pl.multiple_of(s * length, length), length)


def tile(j):
    return slice(128 * j, 128 * j + 128)


def conv_forward(ext, taps, bias, masks, first=0, length=L):
    acc = bias + taps[0] * ext[8 + first : 8 + first + length]
    for k in range(1, 4):
        acc = acc + (taps[k] * ext[8 + first - k : 8 + first - k + length]) * masks[k - 1]
    return acc


def conv_backward(ext, v_ext, taps, masks):
    out, tap_grads = None, []
    for k in range(4):
        part = ext[k : 264 + k]
        if k:
            part = part * masks[k - 1]
        tap_grads.append(jnp.sum(part * v_ext, axis=0, keepdims=True))
        out = taps[k] * part if out is None else out + taps[k] * part
    return out, tap_grads


def slot_masks(packed, s):
    cols = pltpu.roll(packed[...], (128 - 4 * s) % 128, 1)
    return [jnp.broadcast_to(cols[:, k : k + 1], cols.shape) for k in (1, 2, 3)]


def place_rows(dst, blocks, me, at, first=0, width=None, lead=0):
    count, rows = blocks.shape[1:3]
    width = blocks.shape[3] - first if width is None else width
    for n in range(count):
        start = pl.multiple_of((n ^ me) * rows, rows) if count > 1 else 0
        dst[pl.ds(start, rows), at : at + width] = blocks[lead, n, :, first : first + width]


def place_pair(dst, mine, other, me):
    place_rows(dst, mine, me, 0)
    place_rows(dst, other, me, 384)


def place_p1(dst, am, bm, ar, br, me, pieces):
    place_rows(dst, am, me, 0)
    place_rows(dst, bm, me, 256, 0, 128)
    place_rows(dst, ar, me, 384)
    place_rows(dst, br, me, 640, 0, 128)
    place_rows(pieces, bm, me, 0, 128, 128)
    place_rows(pieces, br, me, 128, 128, 128)


def half_at(c, me_t):
    return pl.ds(pl.multiple_of(384 * (c ^ (me_t % 2)), 128), 384)


def k0_body(sc, conv_x, bias_x, out_gain, dt_bias, a_log, skip_d, norm_gain, bias_bc, par, gain, bbc, row):
    par[...] = jnp.zeros_like(par)
    par[0:4] = conv_x[...]
    par[4] = bias_x[...]
    par[5] = out_gain[...]
    par[6, : dt_bias.shape[0]] = dt_bias[...]
    par[7, : a_log.shape[0]] = a_log[...]
    row[...] = jnp.zeros_like(row)
    row[0, : skip_d.shape[0]] = skip_d[...]
    r = lax.broadcasted_iota(jnp.int32, (128, 384), 0)
    c = lax.broadcasted_iota(jnp.int32, (128, 384), 1)
    par[8:9] = dot_high(row[...], jnp.where(r == c // HD, 1.0, 0.0))[0:1]
    gain[0] = norm_gain[...]
    bbc[0] = bias_bc[...]


def k1_body(
    sc, tok, halo, gain, am, ar, bm, br, par, cbc, bbc,
    nrm, inx, blow, clow, bto, sin, dbc,
    cumo, stepo, sigo, eto, reacho, decayo, faco, uvo, masko, backo, ct,
    wbuf, wbc, wdt, pcs, ext,
):
    g = pl.program_id(0)
    me_t, me_dp = sc[8], sc[9]

    @pl.when(g == 0)
    def _():
        def norm(v):
            v = v.astype(F32)
            r = lax.rsqrt(jnp.mean(v * v, axis=-1, keepdims=True) + EPS)
            return (v * r * gain[...]).astype(BF)

        @pl.loop(0, 16)
        def _(s):
            nrm[rows_of(s, 64)] = norm(tok[rows_of(s, 64)])

        nrm[4 * L :] = norm(halo[...])
        wbc[...] = jnp.zeros_like(wbc)
        wdt[...] = jnp.zeros_like(wdt)

    place_rows(wbuf, am, me_dp, 0)
    place_rows(wbuf, bm, me_dp, 256, 0, 128)
    place_rows(wbuf, ar, me_dp, 384)
    place_rows(wbuf, br, me_dp, 640, 0, 128)
    count, brow = bm.shape[1:3]
    for c, blocks in ((0, bm), (1, br)):
        i = 2 * g + c
        t = i ^ me_t
        at = pl.ds(pl.multiple_of(128 * (t // 2), 128), 128)
        for n in range(count):
            start = pl.multiple_of((n ^ me_dp) * brow, brow) if count > 1 else 0
            r = pl.ds(start, brow)
            piece = blocks[0, n, :, 128:].astype(F32)
            lane = lane_iota(brow)
            own = pltpu.roll(jnp.where(lane < 64, piece, 0.0), 64 * (t % 2), 1)
            wbc[r, at] += own.astype(BF)
            own = pltpu.roll(jnp.where(lane >= 64, piece, 0.0), (i * 6 + 64) % 128, 1)
            wdt[r] += own.astype(BF)
    for n in range(3):
        cols = slice(256 * n, 256 * n + 256)
        inx[0, :, cols] = dot(nrm[...], wbuf[:, cols]).astype(BF)

    @pl.when(g == 1)
    def _():
        pcs[...] = dot(nrm[...], wbc[...])
        sin[0] = pcs[:, :128]
        sin[1] = pcs[:, 128:]
        pcs[0 : 4 * L, 0:128] = dot(nrm[0 : 4 * L], wdt[...])
        dtacc = pcs[0:L, 0:128]
        for s in range(1, 4):
            dtacc = dtacc + pltpu.roll(pcs[L * s : L * s + L, 0:128], s * SPAN, 1)
        dtb = jnp.zeros((1, 128), F32)
        alog = jnp.zeros((1, 128), F32)
        for i in range(4):
            for s in range(4):
                at = slice(384 * (i % 2), 384 * (i % 2) + 128)
                dtb += pltpu.roll(par[i // 2, 6:7, at], s * SPAN + i * 6, 1)
                alog += pltpu.roll(par[i // 2, 7:8, at], s * SPAN + i * 6, 1)
        raw = dtacc + dtb
        step = jnp.maximum(raw, 0.0) + jnp.log1p(jnp.exp(-jnp.abs(raw)))
        sig = 1.0 / (1.0 + jnp.exp(-raw))
        decay = step * -jnp.exp(alog)
        lower = jnp.where(
            lax.broadcasted_iota(jnp.int32, (L, L), 0) >= lax.broadcasted_iota(jnp.int32, (L, L), 1),
            1.0,
            0.0,
        )
        cum = dot_high(lower, decay)
        row = row_iota(L, 128)
        lane = lane_iota(L)
        slot = lane // SPAN
        tail = jnp.zeros((L, 128), F32)
        enters = jnp.zeros((L, 128), F32)
        follows = jnp.zeros((8, 128), F32)
        masks = jnp.ones((L, 128), F32)
        row_b = row_iota(L + 8, 128) - 8
        lane_b = lane_iota(L + 8)
        back_masks = jnp.ones((L + 8, 128), F32)
        slot8 = lane_iota(8) // SPAN
        inner_block = jnp.where(me_t > 0, 1.0, 0.0)
        back = lane % 4
        for s in range(4):
            fe, se = ends(sc, s)
            seg = seg_of(row, fe, se)
            last = seg_of(L - 1, fe, se)
            before = seg_of(-1, fe, se)
            here = slot == s
            tail = jnp.where(here & (seg == last), 1.0, tail)
            enters = jnp.where(here & (seg == before), inner_block, enters)
            follows = jnp.where(
                (slot8 == s), jnp.where(last == before, inner_block, 0.0), follows
            )
            masks = jnp.where((lane // 4 == s) & (seg != seg_of(row - back, fe, se)), 0.0, masks)
            cut = seg_of(row_b, fe, se) != seg_of(row_b + lane_b % 4, fe, se)
            back_masks = jnp.where((lane_b // 4 == s) & cut, 0.0, back_masks)
        cum_last = cum[L - 1 : L]
        cum2 = cum * LOG2E
        cumo[...] = cum2
        stepo[...] = step
        sigo[...] = sig
        eto[...] = jnp.exp(cum_last - cum) * tail
        reacho[...] = jnp.exp(cum) * enters
        decayo[...] = decay
        faco[...] = jnp.exp(cum_last) * follows
        uvo[...] = jnp.exp2(-jnp.abs(cum2 - cum2[127:128]))
        masko[...] = masks
        backo[...] = back_masks
        ct[...] = cum2.T
        for q, low_out in ((0, blow), (1, clow)):
            taps = [cbc[k : k + 1, tile(q)] for k in range(4)]

            @pl.loop(0, 4)
            def _(s):
                ext[0:8] = sin[q, pl.ds(pl.multiple_of(4 * L + 16 * s + 8, 8), 8)]
                ext[8:] = sin[q, rows_of(s)]
                acc = conv_forward(ext, taps, bbc[:, tile(q)], slot_masks(masko, s))
                sg = sigmoid(acc)
                low = acc * sg
                low_out[rows_of(s)] = low.astype(BF)
                dbc[q, rows_of(s)] = sg + low * (1.0 - sg)
                if q == 0:
                    bto[rows_of(s, 128)] = low.T.astype(BF)


def factor_rows(fac, g):
    rows = []
    for s in range(4):
        f = to_lane0(fac[...], s, g)
        rows.append(jnp.concatenate([pair_cols(f, 2 * j)[0:1] for j in range(6)], axis=1))
    f = jnp.concatenate(rows, axis=0)
    high = f.astype(BF).astype(F32)
    return jnp.concatenate([high, f - high, jnp.zeros((8, WIDE), F32)], axis=0).astype(BF)


def k2_body(g, sc, inx, halo, par, bt, stepp, etp, fac, mask, *rest):
    xo, xso, dslo, sto, xe, ext, spread, stepx, stepe = rest[-9:]
    s = pl.program_id(0)
    me_t = sc[8]

    @pl.when(s == 0)
    def _():
        spread[...] = head_spread()

    masks = slot_masks(mask, s)
    step = to_lane0(stepp[...], s, g)
    expand(stepx, step, spread)
    expand(stepe, step * to_lane0(etp[...], s, g), spread)
    for j in range(6):
        ext[j, 0:8] = halo[0, :, tile(j)].astype(F32)[8:]
        ext[j, 8:] = inx[0, :, tile(j)].astype(F32)
    for n in range(L // CHUNK):
        r = slice(CHUNK * n, CHUNK * n + CHUNK)
        mr = [m[r] for m in masks]
        for j in range(6):
            taps = [0.5 * par[0, k : k + 1, tile(j)] for k in range(4)]
            half = conv_forward(ext.at[j], taps, 0.5 * par[0, 4:5, tile(j)], mr, CHUNK * n, CHUNK)
            th = jnp.tanh(half)
            up = 1.0 + th
            act = half * up
            xo[0, r, tile(j)] = act.astype(BF)
            dslo[0, r, tile(j)] = ((0.5 * up) * (1.0 + half * (1.0 - th))).astype(BF)
            xso[0, r, tile(j)] = (act * stepx[r, tile(j)]).astype(BF)
            xe[r, tile(j)] = (act * stepe[r, tile(j)]).astype(BF)
    for c in range(2):
        sto[rows_of(s, 128), half_at(c, me_t)] = dot(
            bt[...], xe[:, 384 * c : 384 * c + 384]
        ).astype(BF)

    @pl.when(s == 3)
    def _():
        f = factor_rows(fac, g)
        for c in range(2):
            sto[512:528, half_at(c, me_t)] = f[:, 384 * c : 384 * c + 384]


def by_head(pair):
    lane = lane_iota(128)
    zero = jnp.zeros_like(pair)
    return jnp.concatenate(
        [jnp.where(lane < HD, pair, zero), jnp.where(lane < HD, zero, pair)], axis=0
    )


def diag_mask(d, fe, se, key_rows):
    r = lax.broadcasted_iota(jnp.int32, (128, 128), 0) + 128 * d
    c = lax.broadcasted_iota(jnp.int32, (128, 128), 1) + 128 * d
    order = (c >= r) if key_rows else (r >= c)
    return order & (seg_of(r, fe, se) == seg_of(c, fe, se))


def cross_half(fe, se, key_rows):
    r = lax.broadcasted_iota(jnp.int32, (128, 128), 0) + (0 if key_rows else 128)
    c = lax.broadcasted_iota(jnp.int32, (128, 128), 1) + (128 if key_rows else 0)
    return seg_of(r, fe, se) == seg_of(c, fe, se)


def k3_body(g, sc, xs, blow, clow, cump, uvp, ct, *rest):
    within, scores, cross, spread, uvx, tiles, cumx = rest[-7:]
    s = pl.program_id(0)
    fe, se = sc[2 * s], sc[2 * s + 1]

    @pl.when(s == 0)
    def _():
        spread[...] = head_spread()
        tiles[...] = tile_spread()


    for d in range(2):
        r = slice(128 * d, 128 * d + 128)
        scores[d] = jnp.where(diag_mask(d, fe, se, False), dot_nt(clow[r], blow[r]), 0.0)
    cross[...] = jnp.where(cross_half(fe, se, False), dot_nt(clow[128:], blow[:128]), 0.0).astype(BF)

    expand_tiles(cumx, to_lane0(cump[...], s, g), tiles)
    expand(uvx, to_lane0(uvp[...], s, g), spread)
    for j in range(6):
        for d in range(2):
            r = slice(128 * d, 128 * d + 128)
            pair = xs[0, r, tile(j)]
            parts = []
            for b in range(2):
                h = 2 * j + b
                gap = cumx[r, tile(h)] - ct[pl.ds(s * SPAN + g * 12 + h, 1), :][:, r]
                parts.append((jnp.exp2(jnp.minimum(gap, 0.0)) * scores[d]).astype(BF))
            total = dot(jnp.concatenate(parts, axis=1), by_head(pair))
            if d == 1:
                xv = (xs[0, :128, tile(j)].astype(F32) * uvx[:128, tile(j)]).astype(BF)
                total = total + dot(cross[...], xv) * uvx[128:, tile(j)]
            within[0, r, tile(j)] = total


def k4_body(sc, nrm, cot, wzm, wzr, wom, wor, gate, dgn, dbro, wz, wo):
    g = pl.program_id(0)
    n = pl.program_id(1)
    me_dp = sc[9]

    @pl.when((g == 0) & (n == 0))
    def _():
        @pl.loop(0, 16)
        def _(n):
            s = n // 4
            r = rows_of(n, 64)
            keep = row_iota(64, 1) + 64 * (n % 4) < sc[2 * s + 1]
            dbro[r] = jnp.where(keep, cot[r].astype(F32), 0.0).astype(BF)

    @pl.when(n == 0)
    def _():
        place_pair(wz, wzm, wzr, me_dp)
        place_pair(wo, wom, wor, me_dp)

    cols = pl.ds(pl.multiple_of(n * 256, 256), 256)
    gate[0] = dot(nrm[0 : 4 * L], wz[:, cols]).astype(BF)
    dgn[0] = dot(dbro[...], wo[:, cols]).astype(BF)


def k5_body(
    sc, within, gate, dgn, x, r1, r2, r3, reachp, fac, clow, par, wom, wor, tok,
    out, gno, dgo, dyo, dpo, prevo, rowsum, dco, small,
    mo, sums, branch, wbuf, gnb, frow, dlow, seg_h, seg_l, pick, pv, spread, reachx,
):
    ph = pl.program_id(0)
    g = pl.program_id(1)
    s = pl.program_id(2)
    me_t, me_dp = sc[8], sc[9]
    r = rows_of(s)
    first = (g == 0) & (s == 0)

    @pl.when((ph == 0) & first)
    def _():
        rowsum[...] = jnp.zeros_like(rowsum)
        dco[...] = jnp.zeros_like(dco)
        small[...] = jnp.zeros_like(small)
        pick[...] = head_pick().astype(BF)
        spread[...] = head_spread()

    expand(reachx, to_lane0(reachp[...], s, g), spread)

    @pl.when(ph == 0)
    def _():
        srow = rows_of(s, 128)
        for c in range(2):
            at = half_at(c, me_t)
            frow[...] = r1[512:528, at].astype(F32)
            f = frow[pl.ds(s, 1)] + frow[pl.ds(s + 4, 1)]
            p = r1[srow, at].astype(F32) + r2[srow, at].astype(F32) + f * r3[srow, at].astype(F32)
            pv[:, 384 * c : 384 * c + 384] = p.astype(BF)
        prevo[g, srow] = pv[...]
        sq = jnp.zeros((L, 128), F32)
        dd = jnp.zeros((L, 128), F32)
        for j in range(6):
            from_prev = dot(clow[...], pv[:, tile(j)])
            mixed = (
                within[0, :, tile(j)]
                + reachx[:, tile(j)] * from_prev
                + par[0, 8:9, tile(j)] * x[0, :, tile(j)].astype(F32)
            )
            mo[g, r, tile(j)] = mixed
            gv = gate[0, :, tile(j)].astype(F32)
            gated = mixed * (gv * sigmoid(gv))
            sq = sq + gated * gated
            dd = dd + dgn[0, :, tile(j)].astype(F32) * par[0, 5:6, tile(j)] * gated
        sq = jnp.broadcast_to(jnp.sum(sq, axis=1, keepdims=True), (L, 128))
        dd = jnp.broadcast_to(jnp.sum(dd, axis=1, keepdims=True), (L, 128))

        @pl.when(g == 0)
        def _():
            sums[0, r] = sq
            sums[1, r] = dd

        @pl.when(g == 1)
        def _():
            sq2 = sums[0, r] + sq
            dd2 = sums[1, r] + dd
            gscale = lax.rsqrt(sq2 * (1.0 / INNER) + EPS)
            sums[0, r] = gscale
            sums[1, r] = gscale * gscale * gscale * (dd2 * (1.0 / INNER))

    @pl.when(ph == 1)
    def _():
        gscale = sums[0, r]
        coef = sums[1, r]
        srow = rows_of(s, 128)
        for j in range(6):
            gv = gate[0, :, tile(j)].astype(F32)
            mixed = mo[g, r, tile(j)]
            sg = sigmoid(gv)
            silu = gv * sg
            gated = mixed * silu
            gs = gated * gscale
            gain = par[0, 5:6, tile(j)]
            gn = (gs * gain).astype(BF)
            gno[0, :, tile(j)] = gn
            gnb[r, tile(j)] = gn
            d = dgn[0, :, tile(j)].astype(F32)
            small[g, 0:1, tile(j)] += jnp.sum(d * gs, axis=0, keepdims=True)
            dgated = gscale * (d * gain) - gated * coef
            dgo[0, :, tile(j)] = (dgated * mixed * (sg + silu * (1.0 - sg))).astype(BF)
            dy = (dgated * silu).astype(BF)
            dyo[0, :, tile(j)] = dy
            dyf = dy.astype(F32)
            dlow[:, tile(j)] = (dyf * reachx[:, tile(j)]).astype(BF)
            dx_skip = dyf * x[0, :, tile(j)].astype(F32)
            small[g, 1:2, tile(j)] += jnp.sum(dx_skip, axis=0, keepdims=True)
            v = dyf * mixed - par[0, 8:9, tile(j)] * dx_skip
            high = v.astype(BF)
            seg_h[:, tile(j)] = high
            seg_l[:, tile(j)] = (v - high.astype(F32)).astype(BF)
        seg = dot(seg_h[...], pick[...]) + dot(seg_l[...], pick[...])
        rowsum[...] += from_lane0(seg, s, g)
        dco[r] += dot_nt(dlow[...], prevo[g, srow])
        for c in range(2):
            dpo[srow, half_at(c, me_t)] = lax.dot_general(
                clow[...],
                dlow[:, 384 * c : 384 * c + 384],
                (((0,), (0,)), ((), ())),
                preferred_element_type=F32,
            ).astype(BF)

        @pl.when(s == 3)
        def _():
            f = factor_rows(fac, g)
            for c in range(2):
                dpo[512:528, half_at(c, me_t)] = f[:, 384 * c : 384 * c + 384]
            place_pair(wbuf, wom, wor, me_dp)

        @pl.when((s == 3) & (g == 0))
        def _():
            branch[...] = dot_nt(gnb[...], wbuf[...])

        @pl.when((s == 3) & (g == 1))
        def _():
            branch[...] += dot_nt(gnb[...], wbuf[...])

            @pl.loop(0, 16)
            def _(n):
                q = rows_of(n, 64)
                out[q] = (tok[q].astype(F32) + branch[q]).astype(BF)


def store_grad(ref, lead, me_dp, value_ref, first, width, at=0):
    count, rows = ref.shape[-3], ref.shape[-2]
    for n in range(count):
        place = n ^ me_dp if count > 1 else 0
        part = value_ref[n * rows : (n + 1) * rows, first : first + width].astype(BF)
        ref[lead + (place, slice(None), slice(at, at + width))] = part


def add_weighted(total, val, w, lead=()):
    @pl.loop(0, total.shape[0] // 64)
    def _(n):
        r = rows_of(n, 64)
        part = total[r]
        for j in range(w.shape[1] // 128):
            v = val[j, r] if lead else val[r, tile(j)]
            part = part + v * w[r, tile(j)].astype(F32)
        total[r] = part


def k6_body(sc, nrm, dbr, gn, dg, wzm, wzr, ok, os, zk, zs, nt, ngz, dt, val, wz):
    g = pl.program_id(0)
    me_dp = sc[9]
    place_pair(wz, wzm, wzr, me_dp)

    @pl.when(g == 0)
    def _():
        ngz[...] = jnp.zeros_like(ngz)

        @pl.loop(0, 4)
        def _(s):
            nt[:, rows_of(s)] = nrm[rows_of(s)].T
            dt[:, rows_of(s)] = dbr[rows_of(s)].T

        nt[:, 4 * L :] = nrm[4 * L :].T

    for lhs, rhs, keep, send in ((dt, gn, ok, os), (nt, dg, zk, zs)):
        for n in range(3):
            cols = slice(256 * n, 256 * n + 256)
            val[:, cols] = dot(lhs[:, : 4 * L], rhs[0, :, cols])
        store_grad(keep, (0,), me_dp, val, 0, 384)
        store_grad(send, (0,), me_dp, val, 384, 384)
    add_weighted(ngz, val, wz)


def k7_body(g, sc, xs, dy, blow, clow, cump, uvp, ct, *rest):
    dxo, bco, pko, scores, cross, xvb, udb, spread, uvx, tiles, cumx, pick, corr = rest[-13:]
    s = pl.program_id(0)

    @pl.when(s == 0)
    def _():
        spread[...] = head_spread()
        tiles[...] = tile_spread()
        pick[...] = head_pick().astype(BF)
        pko[...] = jnp.zeros_like(pko)

    fe, se = sc[2 * s], sc[2 * s + 1]

    for d in range(2):
        r = slice(128 * d, 128 * d + 128)
        scores[d] = jnp.where(diag_mask(d, fe, se, True), dot_nt(blow[r], clow[r]), 0.0)
    cross[...] = jnp.where(cross_half(fe, se, True), dot_nt(blow[:128], clow[128:]), 0.0).astype(BF)

    expand_tiles(cumx, to_lane0(cump[...], s, g), tiles)
    expand(uvx, to_lane0(uvp[...], s, g), spread)
    totals = [jnp.zeros((128, 128), F32), jnp.zeros((128, 128), F32)]
    crossq = cross[...].astype(F32).T.astype(BF)
    for j in range(6):
        for d in range(2):
            r = slice(128 * d, 128 * d + 128)
            xp = xs[0, r, tile(j)]
            dyp = dy[0, r, tile(j)]
            grads = dot_nt(by_head(xp), dyp)
            parts = []
            for b in range(2):
                h = 2 * j + b
                gap = ct[pl.ds(s * SPAN + g * 12 + h, 1), :][:, r] - cumx[r, tile(h)]
                kern = jnp.exp2(jnp.minimum(gap, 0.0))
                totals[d] = totals[d] + grads[128 * b : 128 * b + 128] * kern
                parts.append((kern * scores[d]).astype(BF))
            dx = dot(jnp.concatenate(parts, axis=1), by_head(dyp))
            scaled = (xp if d == 0 else dyp).astype(F32) * uvx[r, tile(j)]
            low = scaled.astype(BF)
            diff = low.astype(F32) - scaled
            if d == 0:
                xvb[:, tile(j)] = low
                top, xdiff = dx, diff
            else:
                udb[:, tile(j)] = low
                off = dot(cross[...], low)
                dxo[0, r, tile(j)] = dx
                dxo[0, :128, tile(j)] = top + off * uvx[:128, tile(j)]
                corr[:128, tile(j)] = (xdiff * off).astype(BF)
                corr[128:, tile(j)] = (diff * dot(crossq, xvb[:, tile(j)])).astype(BF)
    dcr = dot_nt(xvb[...], udb[...])
    pko[...] += from_lane0(dot(corr[...], pick[...]), s, g)
    d0 = jnp.where(diag_mask(0, fe, se, True), totals[0], 0.0)
    d1 = jnp.where(diag_mask(1, fe, se, True), totals[1], 0.0)
    dl = jnp.where(cross_half(fe, se, True), dcr, 0.0)
    c0, c1, b0, b1 = clow[:128], clow[128:], blow[:128], blow[128:]
    bco[0, 0:128] = dot(d0.astype(BF), c0) + dot(dl.astype(BF), c1)
    bco[0, 128:] = dot(d1.astype(BF), c1)
    bco[1, 0:128] = dot(d0.T.astype(BF), b0)
    bco[1, 128:] = dot(d1.T.astype(BF), b1) + dot(dl.T.astype(BF), b0)


def k8_body(
    g, last, sc, nt, xs, dy, dsl, inx, halo, dxw, q1, q2, q3, prev, blow, stepp, etp, back, par,
    am, ar, bm, br, *rest,
):
    if last:
        (
            fac, sigp, decay, gain, ngz, nga, cbc, small1, small5, bc7a, bc7b, corr_a, corr_b, dc3, rowsum, sin, dbc, sega, enda, dba,
            keep, send, din, seg, end, dba_o, small, ngx, din5, skeep, ssend,
            val, hsum, gsc, gf, glow, xe, seg_h, seg_l, pick, wbuf, wpc, gbuf, pcs, pblk, sbc, spack, ub, ext, spread, stepx, etx,
        ) = rest
    else:
        (
            keep, send, din, seg, end, dba_o, small, ngx,
            val, hsum, gsc, gf, glow, xe, seg_h, seg_l, pick, wbuf, ub, ext, spread, stepx, etx,
        ) = rest
    s = pl.program_id(0)
    me_t, me_dp = sc[8], sc[9]
    r = rows_of(s)
    hrow = pl.ds(pl.multiple_of(4 * L + 16 * s, 16), 16)

    @pl.when(s == 0)
    def _():
        seg[...] = jnp.zeros_like(seg)
        end[...] = jnp.zeros_like(end)
        small[...] = jnp.zeros_like(small)
        pick[...] = head_pick().astype(BF)
        ext[:, 0:8] = jnp.zeros((6, 8, 128), F32)
        ext[:, 264:] = jnp.zeros((6, 8, 128), F32)
        spread[...] = head_spread()

    srow = rows_of(s, 128)
    for c in range(2):
        at = half_at(c, me_t)
        gf[...] = q1[512:528, at].astype(F32)
        f = gf[pl.ds(s, 1)] + gf[pl.ds(s + 4, 1)]
        v = q1[srow, at].astype(F32) + q2[srow, at].astype(F32) + f * q3[srow, at].astype(F32)
        gsc[:, 384 * c : 384 * c + 384] = v
        glow[:, 384 * c : 384 * c + 384] = v.astype(BF)
    for n in range(3):
        cols = slice(256 * n, 256 * n + 256)
        ub[:, cols] = dot(blow[...], glow[:, cols])
    masks = slot_masks(back, s)
    expand(stepx, to_lane0(stepp[...], s, g), spread)
    expand(etx, to_lane0(etp[...], s, g), spread)
    ends_row, gp_row = [], []
    for j in range(6):
        taps = [par[0, k : k + 1, tile(j)] for k in range(4)]
        xf = xs[0, :, tile(j)].astype(F32)
        ec = etx[:, tile(j)]
        eu = ub[:, tile(j)] * ec
        xe[:, tile(j)] = (xf * ec).astype(BF)
        ends_row.append(jnp.sum(xf * eu, axis=0, keepdims=True))
        gp_row.append(
            jnp.sum(gsc[:, tile(j)] * prev[0, srow, tile(j)].astype(F32), axis=0, keepdims=True)
        )
        dxi = dxw[0, :, tile(j)] + eu
        v = xf * dxi
        high = v.astype(BF)
        seg_h[:, tile(j)] = high
        seg_l[:, tile(j)] = (v - high.astype(F32)).astype(BF)
        dx = dxi * stepx[:, tile(j)] + par[0, 8:9, tile(j)] * dy[0, :, tile(j)].astype(F32)
        dconv = dx * dsl[0, :, tile(j)].astype(F32)
        small[4:5, tile(j)] += jnp.sum(dconv, axis=0, keepdims=True)
        v_ext = jnp.concatenate(
            [halo[0, :, tile(j)].astype(F32)[8:], inx[0, :, tile(j)].astype(F32)], axis=0
        )
        ext[j, 8:264] = dconv
        dv, tap_grads = conv_backward(ext.at[j], v_ext, taps, masks)
        for k in range(4):
            small[k : k + 1, tile(j)] += tap_grads[k]
        din[r, tile(j)] = dv[8:].astype(BF)
        din[hrow, tile(j)] = jnp.concatenate([jnp.zeros((8, 128), F32), dv[:8]], axis=0).astype(BF)
    seg[...] += from_lane0(dot(seg_h[...], pick[...]) + dot(seg_l[...], pick[...]), s, g)
    dba_o[r] = dot_nt(xe[...], glow[...])
    rows = jnp.concatenate(
        [
            jnp.concatenate(ends_row, axis=1),
            jnp.concatenate(gp_row, axis=1),
            jnp.zeros((6, WIDE), F32),
        ],
        axis=0,
    )
    end[...] += from_lane0(dot_high(rows, pick[...].astype(F32)), s, g)

    @pl.when(s == 3)
    def _():
        for n in range(3):
            cols = slice(256 * n, 256 * n + 256)
            hsum[...] = dot(nt[:, 4 * L :], din[4 * L :, cols])
            val[:, cols] = dot(nt[:, : 4 * L], din[: 4 * L, cols]) + hsum[...]
        store_grad(keep, (), me_dp, val, 0, 384)
        store_grad(send, (), me_dp, val, 384, 384)
        place_rows(wbuf, am, me_dp, 0)
        place_rows(wbuf, ar, me_dp, 384)
        place_rows(wbuf, bm, me_dp, 256, 0, 128, g if last else 0)
        place_rows(wbuf, br, me_dp, 640, 0, 128, g if last else 0)
        ngx[...] = ngz[...] + nga[...] if last else jnp.zeros_like(ngx)
        add_weighted(ngx, val, wbuf)

    if not last:
        return

    @pl.when(s == 3)
    def _():
        for q in range(2):
            taps = [cbc[k : k + 1, tile(q)] for k in range(4)]
            sbc[q] = jnp.zeros((8, 128), F32)

            @pl.loop(0, 4)
            def _(n):
                rn = rows_of(n)
                if q == 0:
                    grad = bc7a[0, rn] + bc7b[0, rn] + dba_o[rn] + dba[rn]
                else:
                    grad = bc7a[1, rn] + bc7b[1, rn] + dc3[rn]
                dconv = grad * dbc[q, rn]
                hn = pl.ds(pl.multiple_of(4 * L + 16 * n, 16), 16)
                v_ext = jnp.concatenate([sin[q, hn][8:], sin[q, rn]], axis=0)
                ext[q, 8:264] = dconv
                dv, tap_grads = conv_backward(ext.at[q], v_ext, taps, slot_masks(back, n))
                sbc[q, 4:5] += jnp.sum(dconv, axis=0, keepdims=True)
                for k in range(4):
                    sbc[q, k : k + 1] += tap_grads[k]
                gbuf[q, rn] = dv[8:]
                gbuf[q, hn] = jnp.concatenate([jnp.zeros((8, 128), F32), dv[:8]], axis=0)

        row = row_iota(L, 128)
        corr = corr_a[...] + corr_b[...]
        col = seg[...] + sega[...] + jnp.where(row < 128, corr, 0.0)
        ends_all = end[...] + enda[...]
        at_last = ends_all[0:1] + ends_all[1:2] * fac[0:1]
        dcum = rowsum[...] + jnp.where(row < 128, 0.0, corr) - col + jnp.where(row == L - 1, at_last, 0.0)
        upper = jnp.where(
            lax.broadcasted_iota(jnp.int32, (L, L), 0) <= lax.broadcasted_iota(jnp.int32, (L, L), 1),
            1.0,
            0.0,
        )
        dlog = dot_high(upper, dcum)
        alog = jnp.zeros((1, 128), F32)
        for i in range(4):
            at = slice(384 * (i % 2), 384 * (i % 2) + 128)
            for n in range(4):
                alog += pltpu.roll(par[i // 2, 7:8, at], n * SPAN + i * 6, 1)
        step_all, sig = stepp[...], sigp[...]
        ratio = jnp.where(step_all > 1e-30, sig / jnp.maximum(step_all, 1e-30), 1.0)
        ddt = ratio * col - sig * jnp.exp(alog) * dlog
        dts = jnp.concatenate(
            [
                jnp.sum(ddt, axis=0, keepdims=True),
                jnp.sum(dlog * decay[...], axis=0, keepdims=True),
                jnp.zeros((6, 128), F32),
            ],
            axis=0,
        )
        dts = dts + pltpu.roll(dts, 64, 1)
        dts = dts + pltpu.roll(dts, 32, 1)
        spack[...] = jnp.zeros_like(spack)
        for x in range(2):
            spack[x, 0:5] = (small if x == 0 else small1)[0:5]
            spack[x, 5:7] = small5[x, 0:2]
            for c in range(2):
                own = pltpu.roll(dts, (128 - 6 * (2 * x + c)) % 128, 1)
                own = jnp.where(lane_iota(8) < 6, own, 0.0)
                spack[x, 7:9, 384 * c : 384 * c + 128] = own[0:2]
            skeep[16 * x : 16 * x + 16] = spack[x, :, :384]
            ssend[16 * x : 16 * x + 16] = spack[x, :, 384:]
        ssend[32:40] = jnp.zeros((8, 384), F32)
        for q in range(2):
            ssend[32:37, tile(q)] = sbc[q, 0:5]
        for n in range(4):
            t = n ^ me_t
            turn = (64 * (t % 2)) % 128

            @pl.loop(0, 4)
            def _(m):
                rm = rows_of(m)
                lane = lane_iota(L)
                a = pltpu.roll(gbuf[t // 2, rm], turn, 1)
                d = pltpu.roll(ddt, (320 - m * SPAN - n * 6) % 128, 1)
                piece = jnp.where(lane < 64, a, jnp.where(lane < 70, d, 0.0))
                din5[rm, tile(n)] = piece.astype(BF)

            a = pltpu.roll(gbuf[t // 2, 4 * L :], turn, 1)
            din5[4 * L :, tile(n)] = jnp.where(lane_iota(64) < 64, a, 0.0).astype(BF)
        for n in range(2):
            cols = slice(256 * n, 256 * n + 256)
            hsum[...] = dot(nt[:, 4 * L :], din5[4 * L :, cols])
            v = dot(nt[:, : 4 * L], din5[: 4 * L, cols]) + hsum[...]
            pcs[2 * n] = v[:, :128]
            pcs[2 * n + 1] = v[:, 128:]
            place_rows(wpc, bm, me_dp, 256 * n, 128, 128, n)
            place_rows(wpc, br, me_dp, 256 * n + 128, 128, 128, n)
        add_weighted(ngx, pcs, wpc, (0,))
        gain_grad = (
            lax.dot_general(
                jnp.ones((8, 128), F32),
                ngx[...],
                (((1,), (1,)), ((), ())),
                preferred_element_type=F32,
                precision=lax.Precision.HIGHEST,
            )
            / gain[...]
        )
        ssend[37:38] = gain_grad[0:1, :384]
        ssend[38:39] = gain_grad[0:1, 384:]
        count, brow = keep.shape[0], keep.shape[1]
        for n in range(4):
            ref = keep if n % 2 == 0 else send
            at = slice(384 + 128 * (n // 2), 512 + 128 * (n // 2))
            if count == 1:
                ref[0, :, at] = pcs[n].astype(BF)
                continue
            t = n ^ me_t
            quarter = brow // 4
            for m in range(count):
                for c in range(4):
                    pblk[quarter * c : quarter * c + quarter] = pcs[
                        c ^ me_t, pl.ds(pl.multiple_of(brow * m + quarter * t, 8), quarter)
                    ]
                both = jnp.where(
                    lane_iota(brow) < 64, pblk[...], pcs[n, brow * m : brow * m + brow]
                )
                ref[m ^ me_dp, :, at] = both.astype(BF)


def k9z_body(sc, dg, wzm, wzr, dn, wz):
    place_pair(wz, wzm, wzr, sc[9])
    dn[...] = dot_nt(dg[0], wz[...])


def k9_body(sc, din0, din1, din5, dna, dnb, am, ar, bm, br, dn, wx, wpc):
    g = pl.program_id(0)
    place_p1(wx, am, bm, ar, br, sc[9], wpc)

    @pl.when(g == 0)
    def _():
        dn[...] = dot_nt(din0[...], wx[...])

    @pl.when(g == 1)
    def _():
        dn[...] += dot_nt(din1[...], wx[...])
        dn[: 4 * L] += dna[...] + dnb[...]

    dn[...] += dot_nt(din5[...], wpc[...])


def k10_body(sc, dn, hr, tok, cot, gain, ig):
    s = pl.program_id(0)
    d = dn[...]
    extra = hr[...].astype(F32)
    width = d.shape[1]
    d = jnp.concatenate([d[: L - 16], d[L - 16 :] + extra], axis=0)
    tv = tok[...].astype(F32)
    r = lax.rsqrt(jnp.mean(tv * tv, axis=-1, keepdims=True) + EPS)
    tr = tv * r
    gd = gain[...] * d
    inner = jnp.sum(gd * tr, axis=-1, keepdims=True) * (1.0 / width)
    keep = row_iota(L, 1) < sc[2 * s + 1]
    res = jnp.where(keep, cot[...].astype(F32), 0.0)
    ig[...] = (res + r * (gd - tr * inner)).astype(BF)


def FINAL_SHAPES(dim, cols, heads, state, shard, tcount):
    return [
        (dim,), (shard, cols), (shard // tcount, 2 * state), (heads, shard), (4, cols), (cols,),
        (4, 2 * state), (2 * state,), (heads,), (heads,), (heads,), (cols,),
    ]


def k11_body(
    sc, va, vr, both, got,
    ngain, wx, wbc, wdt, cx, bx, cb, bb, dtb, alog, skip, og,
    g, sm,
):
    g[...] = va[...].astype(F32) + vr[...].astype(F32)
    sm[...] = both[...] + got[...]
    wx[...] = g[:, :384]
    quarter = g.shape[0] // 4
    lane = lane_iota(quarter)
    parts = [g[quarter * c : quarter * c + quarter, 384:512] for c in range(4)]
    for t in range(2):
        wbc[:, tile(t)] = jnp.where(lane < 64, parts[2 * t], pltpu.roll(parts[2 * t + 1], 64, 1))
    wdt[...] = pltpu.roll(g[:, 384:512], 64, 1).T[: wdt.shape[0]]
    cx[...] = sm[0:4]
    bx[...] = sm[4]
    og[...] = sm[5]
    r = lax.broadcasted_iota(jnp.int32, (384, 128), 0)
    c = lax.broadcasted_iota(jnp.int32, (384, 128), 1)
    sums = dot_high(sm[0:8], jnp.where(c == r // HD, 1.0, 0.0))
    skip[...] = sums[6, : skip.shape[0]]
    dtb[...] = sm[7, : dtb.shape[0]]
    alog[...] = sm[8, : alog.shape[0]]
    cb[...] = sm[16:20, : cb.shape[1]]
    bb[...] = sm[20, : bb.shape[0]]
    half = sm.shape[1]
    ngain[0:half] = sm[21]
    ngain[half : 2 * half] = sm[22]


def full(shape):
    return pl.BlockSpec(shape, lambda *a: (0,) * len(shape))


def call(body, grid, in_specs, out_specs, out_shapes, scratch, cost, name, aliases=None, vmem_mib=VMEM_MIB):
    flops, moved = cost
    return pl.pallas_call(
        body,
        grid_spec=pltpu.PrefetchScalarGridSpec(
            num_scalar_prefetch=1,
            grid=grid,
            in_specs=in_specs,
            out_specs=out_specs,
            scratch_shapes=scratch,
        ),
        out_shape=out_shapes,
        compiler_params=pltpu.CompilerParams(vmem_limit_bytes=vmem_mib * 2**20),
        cost_estimate=pl.CostEstimate(flops=flops, bytes_accessed=moved, transcendentals=0),
        input_output_aliases=aliases or {},
        name=name,
    )


def sds(shape, dtype):
    return pltpu.HBM(shape, dtype)


def anywhere(count):
    return [pl.BlockSpec(memory_space=pl.ANY)] * count


def flip(value, axis, bit):
    count = lax.axis_size(axis)
    return lax.ppermute(value, axis, [(a, a ^ bit) for a in range(count)])


def meet(*values):
    return lax.optimization_barrier(values)


def per_device(
    tokens, lengths, cotangent, norm_gain, w_z, w_x, w_bc, w_dt, conv_x, bias_x, conv_bc, bias_bc,
    dt_bias, a_log, skip_d, out_gain, w_out,
):
    tcount = lax.axis_size("tensor")
    dpcount = lax.axis_size("dp")
    me_t = lax.axis_index("tensor")
    me_dp = lax.axis_index("dp")
    slots, own_len, dim = tokens.shape
    rows = slots * own_len
    shard = w_z.shape[0]
    cols = w_z.shape[1]
    heads = w_dt.shape[1]
    fast = shard % 32 == 0 and dpcount & (dpcount - 1) == 0 and dpcount >= 8
    count = dpcount if fast else 1
    brow = shard if fast else dim

    first = lengths[:, 0] - me_t * own_len
    second = first + lengths[:, 1]
    sc = jnp.concatenate(
        [
            jnp.stack([first, second], axis=1).reshape(-1),
            jnp.stack([me_t, me_dp]),
            jnp.zeros((6,), jnp.int32),
        ]
    ).astype(jnp.int32)
    tok = tokens.reshape(rows, dim)
    cot = cotangent.reshape(rows, dim)

    bq = w_bc.shape[1] // tcount
    state = w_bc.shape[1] // 2
    own_bc = lax.dynamic_slice_in_dim(w_bc, me_t * bq, bq, 1)
    p1 = jnp.concatenate(
        [w_x, own_bc, w_dt, jnp.zeros((shard, 128 - bq - heads), BF)], axis=1
    )
    tail = tokens[:, own_len - 16 :, :].reshape(slots * 16, dim)
    def add_y(v, at):
        return jnp.stack([v, flip(v, "dp", 1)], axis=at)

    def add_x(v):
        return jnp.stack([v, flip(v, "tensor", 2)], axis=0)

    def blocks(v):
        return v.reshape(2, count, brow, v.shape[-1])

    def core(v):
        return flip(v, "tensor", 1)

    par, gain, bbc = call(
        k0_body,
        (1,),
        [
            full(v.shape)
            for v in (conv_x, bias_x, out_gain, dt_bias, a_log, skip_d, norm_gain, bias_bc)
        ],
        [full((16, cols)), full((1, dim)), full((1, 2 * state))],
        [sds((16, cols), F32), sds((1, dim), F32), sds((1, 2 * state), F32)],
        [pltpu.VMEM((8, 128), F32)],
        (1, 1),
        "parameters",
        vmem_mib=K5_MIB,
    )(sc, conv_x, bias_x, out_gain, dt_bias, a_log, skip_d, norm_gain, bias_bc)

    def grown(v, got, at):
        v = jnp.stack([v, got], axis=at)
        return v.reshape(v.shape[: at - 1] + (-1,) + v.shape[at + 1 :])

    if fast:
        v = p1[None]
        w2 = jnp.stack([w_z, w_out])[None]
        bit = dpcount // 2
        got = flip(v, "dp", bit)
        got, w2, sc, par, tail, gain = meet(got, w2, sc, par, tail, gain)
        v = grown(v, got, 1)
        while bit > 4:
            bit //= 2
            v = grown(v, flip(v, "dp", bit), 1)
            w2 = grown(w2, flip(w2, "dp", 2 * bit), 1)
        halo = lax.ppermute(tail, "tensor", [(a, a + 1) for a in range(tcount - 1)])
        got, w2, parx, halo = meet(flip(v, "dp", 2), w2, flip(par, "tensor", 2), halo)
        par = jnp.stack([par, parx], axis=0)
        v = grown(v, got, 1)
        az, bz = v[..., :256], v[..., 256:]
        ax, by, parc, w2z = meet(
            flip(az, "tensor", 2), flip(bz, "dp", 1), core(par), flip(w2, "dp", 4)
        )
        w2 = grown(w2, w2z, 1)
        par = jnp.concatenate([par, parc], axis=-1)
        ax = jnp.stack([az, ax], axis=0)
        by = jnp.stack([bz, by], axis=1)
        ay, bx, w2z, par = meet(flip(ax, "dp", 1), flip(by, "tensor", 2), flip(w2, "dp", 2), par)
        w2 = grown(w2, w2z, 1)
        wam = blocks(jnp.stack([ax, ay], axis=2))
        wbm = blocks(jnp.stack([by, bx], axis=0))
        zz, oz = w2[:, 0], w2[:, 1]
        zx, oy = flip(zz, "tensor", 2), flip(oz, "dp", 1)
        war, wbr = core(wam), core(wbm)
    else:
        halo = lax.ppermute(tail, "tensor", [(a, a + 1) for a in range(tcount - 1)])
        par = add_x(par)
        par = jnp.concatenate([par, core(par)], axis=-1)
        z1 = lax.all_gather(p1, "dp", axis=0, tiled=True)[None]
        wam = add_x(z1[..., :256])
        wbm = add_x(z1[..., 256:])
        war, wbr = core(wam), core(wbm)

    srows = slots * state
    wide = 2 * cols
    erows = rows + 64
    p1block = (1, count, brow, 256)
    wblock = (1, count, brow, cols)
    vmem = pltpu.VMEM

    def w_g(g, *a):
        return (g, 0, 0, 0)

    nrm, inx, blow, clow, bt, sin, dbc, cump, stepp, sigp, etp, reachp, decay, fac, uvp, mask, back, ct = call(
        k1_body,
        (2,),
        [full((rows, dim)), full((64, dim)), full((1, dim))]
        + [pl.BlockSpec(p1block, w_g)] * 4
        + [full((2, 16, wide)), full((4, 2 * state)), full((1, 2 * state))],
        [
            full((erows, dim)),
            pl.BlockSpec((1, erows, wide), lambda g, sc: (g, 0, 0)),
            full((rows, state)),
            full((rows, state)),
            full((srows, L)),
            full((2, erows, state)),
            full((2, rows, state)),
        ]
        + [full((L, 128))] * 6
        + [full((8, 128)), full((L, 128)), full((L, 128)), full((L + 8, 128)), full((128, L))],
        [
            sds((erows, dim), BF),
            sds((2, erows, wide), BF),
            sds((rows, state), BF),
            sds((rows, state), BF),
            sds((srows, L), BF),
            sds((2, erows, state), F32),
            sds((2, rows, state), F32),
        ]
        + [sds((L, 128), F32)] * 6
        + [sds((8, 128), F32), sds((L, 128), F32), sds((L, 128), F32), sds((L + 8, 128), F32)]
        + [sds((128, L), F32)],
        [
            vmem((dim, wide), BF),
            vmem((dim, 256), BF),
            vmem((dim, 128), BF),
            vmem((erows, 256), F32),
            vmem((L + 8, 128), F32),
        ],
        (int(7e9), int(2e7)),
        "projections",
    )(sc, tok, halo, gain, wam, war, wbm, wbr, par, conv_bc, bbc)

    def gs(g, s, sc):
        return (g, s, 0)

    def halo_gs(g, s, sc):
        return (g, rows // 16 + s, 0)

    def by_s(g, s, sc):
        return (s, 0)

    def mirror(g, sc):
        return (0, g ^ (sc[8] // 2))

    group = (1, L, wide)

    def gsel(g):
        return lambda s, sc: (g, s, 0)

    def conv_and_states(g, inx, kept):
        return call(
            functools.partial(k2_body, g),
            (slots,),
            [
                pl.BlockSpec(group, gsel(g)),
                pl.BlockSpec((1, 16, wide), lambda s, sc: (g, rows // 16 + s, 0)),
                pl.BlockSpec((1, 16, wide), lambda s, sc: (g, 0, 0)),
                pl.BlockSpec((state, L), lambda s, sc: (s, 0)),
                full((L, 128)),
                full((L, 128)),
                full((8, 128)),
                full((L, 128)),
            ]
            + anywhere(len(kept)),
            [pl.BlockSpec(group, gsel(g))] * 3
            + [pl.BlockSpec((srows + 16, wide), lambda s, sc: mirror(g, sc))],
            [sds((2, rows, wide), BF)] * 3 + [sds((srows + 16, 2 * wide), BF)],
            [
                vmem((L, wide), BF),
                vmem((6, L + 8, 128), F32),
                vmem((256, wide), BF),
                vmem((L, wide), F32),
                vmem((L, wide), F32),
            ],
            (int(5e9) if g else 1, int(2e7) if g else 1),
            "conv_and_states_%d" % g,
            {9 + n: n for n in range(len(kept))},
        )(sc, inx, inx, par, bt, stepp, etp, fac, mask, *kept)

    if fast:
        inx0, zx, oy = meet(inx, zx, oy)
        zx = jnp.stack([zz, zx], axis=0)
        oy = jnp.stack([oz, oy], axis=1)
        zy, ox = flip(zx, "dp", 1), flip(oy, "tensor", 2)
        xl, xs, dsl, st = conv_and_states(1, inx, conv_and_states(0, inx0, []))
        st, zy, ox = meet(st, zy, ox)
        wzm = blocks(jnp.stack([zx, zy], axis=2))
        wom = blocks(jnp.stack([oy, ox], axis=0))
        wzr, wor = core(wzm), core(wom)
    else:
        xl, xs, dsl, st = conv_and_states(1, inx, conv_and_states(0, inx, []))
        wzm = add_x(lax.all_gather(w_z, "dp", axis=0, tiled=True)[None])
        wom = add_x(lax.all_gather(w_out, "dp", axis=0, tiled=True)[None])
        wzr, wor = core(wzm), core(wom)

    def end_state(mine, one):
        f = mine[srows : srows + 4].astype(F32) + mine[srows + 4 : srows + 8].astype(F32)
        width = mine.shape[1]
        end = mine[:srows].astype(F32).reshape(slots, state, width) + f[:, None] * one[
            :srows
        ].astype(F32).reshape(slots, state, width)
        return end.astype(BF).reshape(srows, width)

    r1 = lax.ppermute(st, "tensor", [(0, 1), (2, 3)])
    end = end_state(st, r1)
    r2 = lax.ppermute(end, "tensor", [(1, 2)])
    xs3, _ = meet(xs, end)

    def within_of(g, kept):
        return call(
            functools.partial(k3_body, g),
            (slots,),
            [
                pl.BlockSpec(group, gsel(g)),
                pl.BlockSpec((L, state), lambda s, sc: (s, 0)),
                pl.BlockSpec((L, state), lambda s, sc: (s, 0)),
                full((L, 128)),
                full((L, 128)),
                full((128, L)),
            ]
            + anywhere(len(kept)),
            pl.BlockSpec(group, gsel(g)),
            sds((2, rows, wide), F32),
            [
                vmem((2, 128, 128), F32),
                vmem((128, 128), BF),
                vmem((256, wide), BF),
                vmem((L, wide), F32),
                vmem((256, 2 * wide), BF),
                vmem((L, 2 * wide), F32),
            ],
            (int(5e9), int(1e7)),
            "within_%d" % g,
            {7 + n: n for n in range(len(kept))},
        )(sc, xs3, blow, clow, cump, uvp, ct, *kept)

    within = within_of(1, [within_of(0, [])])
    nrm4, within = meet(nrm, within)

    gate, dgn, dbr = call(
        k4_body,
        (2, 3),
        [full((erows, dim)), full((rows, dim))] + [pl.BlockSpec(wblock, w_g)] * 4,
        [pl.BlockSpec((1, rows, 256), lambda g, n, sc: (g, 0, n))] * 2 + [full((rows, dim))],
        [sds((2, rows, wide), BF)] * 2 + [sds((rows, dim), BF)],
        [vmem((dim, wide), BF), vmem((dim, wide), BF)],
        (int(5e9), int(2e7)),
        "gate_and_out_backward",
    )(sc, nrm4, cot, wzm, wzr, wom, wor)

    gate, r2 = meet(gate, r2)
    r3 = lax.ppermute(r2, "tensor", [(2, 3)])

    def p_gs(phase):
        def index(p, g, s, sc):
            return (
                jnp.where(p == phase, g, 0 if phase else 1),
                jnp.where(p == phase, s, 0 if phase else slots - 1),
                0,
            )

        return index

    def p_mirror(phase):
        def index(p, g, s, sc):
            return mirror(jnp.where(p == phase, g, 0 if phase else 1), sc)

        return index

    def pgs(p, g, s, sc):
        return (g, s, 0)

    def p_w(p, g, s, sc):
        return (jnp.where(p == 1, g, 0), 0, 0, 0)

    out, gn, dg, dy, dp, prev, rowsum, dc5, small5 = call(
        k5_body,
        (2, 2, slots),
        [
            pl.BlockSpec(group, p_gs(0)),
            pl.BlockSpec(group, pgs),
            pl.BlockSpec(group, pgs),
            pl.BlockSpec(group, pgs),
            pl.BlockSpec((srows + 16, wide), p_mirror(0)),
            pl.BlockSpec((srows, wide), p_mirror(0)),
            pl.BlockSpec((srows, wide), p_mirror(0)),
            full((L, 128)),
            full((8, 128)),
            pl.BlockSpec((L, state), lambda p, g, s, sc: (s, 0)),
            pl.BlockSpec((1, 16, wide), lambda p, g, s, sc: (g, 0, 0)),
            pl.BlockSpec(wblock, p_w),
            pl.BlockSpec(wblock, p_w),
            full((rows, dim)),
        ],
        [
            full((rows, dim)),
            pl.BlockSpec(group, p_gs(1)),
            pl.BlockSpec(group, p_gs(1)),
            pl.BlockSpec(group, p_gs(1)),
            pl.BlockSpec((srows + 16, wide), p_mirror(1)),
            full((2, srows, wide)),
            full((L, 128)),
            full((rows, state)),
            full((2, 8, wide)),
        ],
        [
            sds((rows, dim), BF),
            sds((2, rows, wide), BF),
            sds((2, rows, wide), BF),
            sds((2, rows, wide), BF),
            sds((srows + 16, 2 * wide), BF),
            sds((2, srows, wide), BF),
            sds((L, 128), F32),
            sds((rows, state), F32),
            sds((2, 8, wide), F32),
        ],
        [
            vmem((2, rows, wide), F32),
            vmem((2, rows, 128), F32),
            vmem((rows, dim), F32),
            vmem((dim, wide), BF),
            vmem((rows, wide), BF),
            vmem((16, cols), F32),
            vmem((L, wide), BF),
            vmem((L, wide), BF),
            vmem((L, wide), BF),
            vmem((wide, 128), BF),
            vmem((state, wide), BF),
            vmem((256, wide), BF),
            vmem((L, wide), F32),
        ],
        (int(1.5e10), int(4e7)),
        "gated_norm",
        vmem_mib=K5_MIB,
    )(sc, within, gate, dgn, xl, r1, r2, r3, reachp, fac, clow, par, wom, wor, tok)

    q1 = lax.ppermute(dp, "tensor", [(1, 0), (3, 2)])

    gshape = (2, count, brow, cols)
    ok, osend, zk, zsend, nt, ngz = call(
        k6_body,
        (2,),
        [full((erows, dim)), full((rows, dim))]
        + [pl.BlockSpec((1, rows, wide), lambda g, sc: (g, 0, 0))] * 2
        + [pl.BlockSpec(wblock, w_g)] * 2,
        [pl.BlockSpec((1,) + gshape[1:], w_g)] * 4 + [full((dim, erows)), full((dim, 128))],
        [sds(gshape, BF)] * 4 + [sds((dim, erows), BF), sds((dim, 128), F32)],
        [vmem((dim, rows), BF), vmem((dim, wide), F32), vmem((dim, wide), BF)],
        (int(5e9), int(2e7)),
        "outer_weight_grads",
        vmem_mib=K5_MIB,
    )(sc, nrm, dbr, gn, dg, wzm, wzr)

    osend, q1 = meet(osend, q1)
    dy1, end = meet(dy, end_state(dp, q1))
    q2 = lax.ppermute(end, "tensor", [(2, 1)])

    def summed(a, b):
        return (a.astype(F32) + b.astype(F32)).astype(BF)

    def reduce_step(v, axis, mesh_axis, bit):
        keep = lax.index_in_dim(v, 0, axis, False)
        send = lax.index_in_dim(v, 1, axis, False)
        return summed(keep, flip(send, mesh_axis, bit))

    def reduce_x(v, axis):
        return reduce_step(v, axis, "tensor", 2)

    def reduce_dp(v, bit):
        v = v.reshape((v.shape[0] // 2, 2) + v.shape[1:])
        return reduce_step(v, 1, "dp", bit)

    def finish(v, bit):
        while bit < dpcount:
            v = reduce_dp(v, bit)
            bit *= 2
        return v[0].astype(F32)

    def reduce_slow(v):
        v = v.reshape(dpcount, shard, v.shape[-1])
        got = lax.all_to_all(v, "dp", split_axis=0, concat_axis=0, tiled=True)
        return got.astype(F32).sum(axis=0)

    def reduce_core(keep, send):
        return summed(keep, core(send))

    if fast:
        osr, zsr = core(osend), core(zsend)
    else:
        grad_w_out = reduce_slow(reduce_x(reduce_core(ok, osend), 0)[0])
        grad_w_z = reduce_slow(reduce_x(reduce_core(zk, zsend), 0)[0])

    def within_backward(g, dy, kept):
        return call(
            functools.partial(k7_body, g),
            (slots,),
            [
                pl.BlockSpec(group, gsel(g)),
                pl.BlockSpec(group, gsel(g)),
                pl.BlockSpec((L, state), lambda s, sc: (s, 0)),
                pl.BlockSpec((L, state), lambda s, sc: (s, 0)),
                full((L, 128)),
                full((L, 128)),
                full((128, L)),
            ]
            + anywhere(len(kept)),
            [
                pl.BlockSpec(group, gsel(g)),
                pl.BlockSpec((2, L, state), lambda s, sc: (0, s, 0)),
                full((L, 128)),
            ],
            [sds((2, rows, wide), F32), sds((2, rows, state), F32), sds((L, 128), F32)],
            [
                vmem((2, 128, 128), F32),
                vmem((128, 128), BF),
                vmem((128, wide), BF),
                vmem((128, wide), BF),
                vmem((256, wide), BF),
                vmem((L, wide), F32),
                vmem((256, 2 * wide), BF),
                vmem((L, 2 * wide), F32),
                vmem((wide, 128), BF),
                vmem((L, wide), BF),
            ],
            (int(1e10) if g else 1, int(2e7) if g else 1),
            "within_backward_%d" % g,
            {8 + n: n for n in range(len(kept))},
        )(sc, xs, dy, blow, clow, cump, uvp, ct, *kept)

    dxw, bc7a, corr_a = within_backward(1, dy1, [])
    if fast:
        dy0, osr, zsr, dxw = meet(dy, osr, zsr, dxw)
        vo = summed(ok, osr).reshape((2, count // 2, 2, brow, cols))
        vor = flip(vo[:, :, 1], "dp", 1)
    else:
        dy0 = dy
    dxw, bc7b, corr_b = within_backward(0, dy0, [dxw])

    def states_backward(g, last, nt, extra_in, extra_specs):
        width = cols + 256 if last else cols
        gshape = (count, brow, width)

        def at(s, sc):
            return (g, s, 0)

        in_specs = [
            full((dim, erows)),
            pl.BlockSpec(group, at),
            pl.BlockSpec(group, at),
            pl.BlockSpec(group, at),
            pl.BlockSpec(group, at),
            pl.BlockSpec((1, 16, wide), lambda s, sc: (g, rows // 16 + s, 0)),
            pl.BlockSpec(group, at),
            pl.BlockSpec((srows + 16, wide), lambda s, sc: mirror(g, sc)),
            pl.BlockSpec((srows, wide), lambda s, sc: mirror(g, sc)),
            pl.BlockSpec((srows, wide), lambda s, sc: mirror(g, sc)),
            pl.BlockSpec((1, srows, wide), lambda s, sc: (g, 0, 0)),
            pl.BlockSpec((L, state), lambda s, sc: (s, 0)),
            full((L, 128)),
            full((L, 128)),
            full((L + 8, 128)),
            full((2, 16, wide)) if last else pl.BlockSpec((1, 16, wide), lambda s, sc: (g, 0, 0)),
            pl.BlockSpec(p1block, lambda s, sc: (g, 0, 0, 0)),
            pl.BlockSpec(p1block, lambda s, sc: (g, 0, 0, 0)),
        ]
        if last:
            in_specs += [full((2,) + p1block[1:])] * 2
        else:
            in_specs += [pl.BlockSpec(p1block, lambda s, sc: (g, 0, 0, 0))] * 2
        in_specs += extra_specs
        outs = [
            (gshape, BF),
            (gshape, BF),
            ((erows, wide), BF),
            ((L, 128), F32),
            ((8, 128), F32),
            ((rows, state), F32),
            ((8, wide), F32),
            ((dim, 128), F32),
        ]
        scratch = [
            vmem((dim, wide), F32),
            vmem((dim, 256), F32),
            vmem((state, wide), F32),
            vmem((16, cols), F32),
            vmem((state, wide), BF),
            vmem((L, wide), BF),
            vmem((L, wide), BF),
            vmem((L, wide), BF),
            vmem((wide, 128), BF),
            vmem((dim, wide), BF),
        ]
        if last:
            outs += [((erows, 512), BF), ((32, cols), F32), ((40, cols), F32)]
            scratch += [
                vmem((dim, 512), BF),
                vmem((2, erows, state), F32),
                vmem((4, dim, 128), F32),
                vmem((brow, 128), F32),
                vmem((2, 8, state), F32),
                vmem((2, 16, wide), F32),
            ]
        scratch += [vmem((L, wide), F32), vmem((6, L + 16, 128), F32), vmem((256, wide), BF)]
        scratch += [vmem((L, wide), F32), vmem((L, wide), F32)]
        return call(
            functools.partial(k8_body, g, last),
            (slots,),
            in_specs,
            [full(shape) for shape, _ in outs],
            [sds(shape, dtype) for shape, dtype in outs],
            scratch,
            (int(1e10), int(2e7)),
            "states_backward_%d" % g,
        )(sc, nt, xs, dy, dsl, inx, inx, dxw, q1, q2, q3, prev, blow, stepp, etp, back, par, wam, war, wbm, wbr, *extra_in)

    def normed_grad_z(g, dg):
        return call(
            k9z_body,
            (1,),
            [
                pl.BlockSpec((1, rows, wide), lambda i, sc: (g, 0, 0)),
                pl.BlockSpec(wblock, lambda i, sc: (g, 0, 0, 0)),
                pl.BlockSpec(wblock, lambda i, sc: (g, 0, 0, 0)),
            ],
            full((rows, dim)),
            sds((rows, dim), F32),
            [vmem((dim, wide), BF)],
            (1, 1),
            "normed_grad_z%d" % g,
        )(sc, dg, wzm, wzr)

    dga, dxw = meet(dg, dxw)
    dna = normed_grad_z(1, dga)
    if fast:
        dxw, q2, dna, vor, zk = meet(dxw, q2, dna, vor, zk)
        vo = summed(vo[:, :, 0], vor)
        vor = flip(vo[1], "tensor", 2)
        vz = summed(zk, zsr).reshape((2, count // 2, 2, brow, cols))
        vzr = flip(vz[:, :, 1], "dp", 1)
    else:
        dxw, q2, dna = meet(dxw, q2, dna)
    q3 = lax.ppermute(q2, "tensor", [(1, 0)])
    ka, sa, din1, seg1, end1, dba1, small1, nga = states_backward(1, False, nt, [], [])
    if fast:
        sa, vor, vzr = meet(sa, vor, vzr)
        vo = summed(vo[0], vor)
        vz = summed(vz[:, :, 0], vzr)
        vzr = flip(vz[1], "tensor", 2)
    sar = core(sa)
    dgb, _ = meet(dg, sa)
    dnb = normed_grad_z(0, dgb)
    nt0, sar, dnb = meet(nt, sar, dnb)
    va = summed(ka, sar)
    xa = flip(va, "tensor", 2)
    ks, ss, din0, _, _, _, _, _, din5, skeep, ssend = states_backward(
        0,
        True,
        nt0,
        [fac, sigp, decay, gain, ngz, nga, conv_bc, small1, small5, bc7a, bc7b, corr_a, corr_b, dc5, rowsum, sin, dbc, seg1, end1, dba1],
        [
            full((8, 128)),
            full((L, 128)),
            full((L, 128)),
            full((1, dim)),
            full((dim, 128)),
            full((dim, 128)),
            full((4, 2 * state)),
            full((8, wide)),
            full((2, 8, wide)),
            full((2, rows, state)),
            full((2, rows, state)),
            full((L, 128)),
            full((L, 128)),
            full((rows, state)),
            full((L, 128)),
            full((2, erows, state)),
            full((2, rows, state)),
            full((L, 128)),
            full((8, 128)),
            full((rows, state)),
        ],
    )

    if fast:
        ss, xa, vzr = meet(ss, xa, vzr)
        vw = jnp.stack([vo, summed(vz[0], vzr)]).reshape((2, count // 4, 2, brow, cols))
        vwr = flip(vw[:, :, 1], "dp", 2)
    din0, ssr, got = meet(din0, core(ss), core(ssend))
    own = (skeep + got[:32]).reshape(2, 16, cols)
    flat = ssend[32:] + got[32:]
    vb = summed(ks[..., cols:], ssr[..., cols:])
    px = flip(vb[..., 128:], "tensor", 2)
    vx = (ks[..., :cols].astype(F32) + ssr[..., :cols].astype(F32) + xa.astype(F32)).astype(BF)
    if fast:
        vx = vx.reshape((count // 2, 2) + vx.shape[1:])
        vxr = flip(vx[:, 1], "dp", 1)
    both = jnp.concatenate([own[0], flat], axis=0)
    got = flip(jnp.concatenate([own[1], flat], axis=0), "tensor", 2)

    dn = call(
        k9_body,
        (2,),
        [
            full((erows, wide)),
            full((erows, wide)),
            pl.BlockSpec((erows, 256), lambda g, sc: (0, g)),
            full((rows, dim)),
            full((rows, dim)),
        ]
        + [pl.BlockSpec(p1block, w_g)] * 4,
        full((erows, dim)),
        sds((erows, dim), F32),
        [vmem((dim, wide), BF), vmem((dim, 256), BF)],
        (int(6e9), int(2e7)),
        "normed_grad",
    )(sc, din0, din1, din5, dna, dnb, wam, war, wbm, wbr)

    if fast:
        dn, px, vxr, got, vwr = meet(dn, px, vxr, got, vwr)
        vw = summed(vw[:, :, 0], vwr).reshape((2, count // 8, 2, brow, cols))
        vwr = flip(vw[:, :, 1], "dp", 4)
        vx = summed(vx[:, 0], vxr)
        vp = summed(vb[..., :128], px)
        vp = vp.reshape((count // 2, 2) + vp.shape[1:])
        vpr = flip(vp[:, 1], "dp", 1)
        both = both + got
        got = flip(both, "dp", 1)
    hr = lax.ppermute(dn[rows:].astype(BF), "tensor", [(a + 1, a) for a in range(tcount - 1)])
    if fast:
        hr, vpr, got = meet(hr, vpr, got)
        v1 = jnp.concatenate([vx, summed(vp[:, 0], vpr)], axis=-1)
        v1 = v1.reshape((count // 4, 2) + v1.shape[1:])
        v1r = flip(v1[:, 1], "dp", 2)
        both = both + got
        got = flip(both, "dp", 2)

    ig = call(
        k10_body,
        (slots,),
        [
            pl.BlockSpec((L, dim), lambda s, sc: (s, 0)),
            pl.BlockSpec((16, dim), lambda s, sc: (s, 0)),
            pl.BlockSpec((L, dim), lambda s, sc: (s, 0)),
            pl.BlockSpec((L, dim), lambda s, sc: (s, 0)),
            full((1, dim)),
        ],
        pl.BlockSpec((L, dim), lambda s, sc: (s, 0)),
        sds((rows, dim), BF),
        [],
        (int(1e9), int(1e7)),
        "input_grad",
    )(sc, dn, hr, tok, cot, gain)

    if fast:
        ig, v1r, got, vwr = meet(ig, v1r, got, vwr)
        vw = summed(vw[:, :, 0], vwr)
        grad_w_out, grad_w_z = finish(vw[0], 8), finish(vw[1], 8)
        v1 = summed(v1[:, 0], v1r)
        both = both + got
        bit = 4
        while 2 * bit < dpcount:
            both = both + flip(both, "dp", bit)
            v1 = reduce_dp(v1, bit)
            bit *= 2
        got = flip(both, "dp", bit)
        v1 = v1.reshape((2,) + v1.shape[1:]) if v1.shape[0] == 2 else v1
        v1a, v1r = v1[0], flip(v1[1], "dp", bit)
    else:
        both = lax.psum(both + got, "dp")
        v1 = jnp.concatenate([vx, summed(vb[..., :128], px)], axis=-1)
        grad1 = reduce_slow(v1)
    if fast:
        last = call(
            k11_body,
            (1,),
            [full((shard, 512))] * 2 + [full((24, cols))] * 2,
            [full(shape) for shape in FINAL_SHAPES(dim, cols, heads, state, shard, tcount)],
            [
                sds(shape, F32)
                for shape in FINAL_SHAPES(dim, cols, heads, state, shard, tcount)
            ],
            [vmem((shard, 512), F32), vmem((24, cols), F32)],
            (int(1e6), int(1e6)),
            "last_sums",
        )(sc, v1a, v1r, both, got)
        (
            ngain, grad_w_x, grad_w_bc, grad_w_dt, grad_conv_x, grad_bias_x, grad_conv_bc,
            grad_bias_bc, grad_dt_bias, grad_a_log, grad_skip, grad_out_gain,
        ) = last
        grad_w_dt = grad_w_dt.T
    else:
        own, flat = both[:16], both[16:]
        ngain = flat[5:7].reshape(dim)
        grad_w_x = grad1[:, :cols]
        parts = grad1[:, cols : cols + bq].reshape(tcount, shard // tcount, bq)
        got = lax.all_to_all(parts, "tensor", split_axis=0, concat_axis=0, tiled=True)
        grad_w_bc = jnp.swapaxes(got, 0, 1).reshape(shard // tcount, bq * tcount)
        grad_w_dt = grad1[:, cols + bq : cols + bq + heads]
        grad_conv_x, grad_bias_x, grad_out_gain = own[:4], own[4], own[5]
        grad_conv_bc, grad_bias_bc = flat[:4, : 2 * state], flat[4, : 2 * state]
        grad_dt_bias, grad_a_log = own[7, :heads], own[8, :heads]
        grad_skip = own[6].reshape(heads, cols // heads).sum(axis=1)

    return (
        out.reshape(tokens.shape),
        ig.reshape(tokens.shape),
        ngain,
        grad_w_z,
        grad_w_x,
        grad_w_bc,
        grad_w_dt,
        grad_conv_x,
        grad_bias_x,
        grad_conv_bc,
        grad_bias_bc,
        grad_dt_bias,
        grad_a_log,
        grad_skip,
        grad_out_gain,
        grad_w_out,
    )


def solution(mesh):
    return jax.shard_map(
        per_device,
        mesh=mesh,
        in_specs=(
            P("dp", "tensor", None), P("dp", None), P("dp", "tensor", None), P(),
            P("dp", "tensor"), P("dp", "tensor"), P("dp", None), P("dp", "tensor"),
            P(None, "tensor"), P("tensor"), P(), P(),
            P("tensor"), P("tensor"), P("tensor"), P("tensor"), P("dp", "tensor"),
        ),
        out_specs=(
            P("dp", "tensor", None), P("dp", "tensor", None), P(),
            P("dp", "tensor"), P("dp", "tensor"), P(("dp", "tensor"), None), P("dp", "tensor"),
            P(None, "tensor"), P("tensor"), P(), P(),
            P("tensor"), P("tensor"), P("tensor"), P("tensor"), P("dp", "tensor"),
        ),
        check_vma=False,
    )
```

```python
import functools

import jax
import jax.numpy as jnp
from jax import lax
from jax.experimental import pallas as pl
from jax.experimental.pallas import tpu as pltpu
from jax.sharding import PartitionSpec as P

INNER = 1536
L = 256
HD = 64
SPAN = 32
EPS = 1e-05
LOG2E = 1.4426950408889634
F32 = jnp.float32
BF = jnp.bfloat16
CHUNK = 64
WIDE = 768
VMEM_MIB = 40
K5_MIB = 58


def dot(a, b):
    return jnp.dot(a, b, preferred_element_type=F32)


def dot_nt(a, b):
    return lax.dot_general(a, b, (((1,), (1,)), ((), ())), preferred_element_type=F32)


def dot_high(a, b):
    return jnp.dot(a, b, preferred_element_type=F32, precision=lax.Precision.HIGHEST)


def sigmoid(v):
    return 0.5 * jnp.tanh(0.5 * v) + 0.5


def lane_iota(rows):
    return lax.broadcasted_iota(jnp.int32, (rows, 128), 1)


def row_iota(rows, lanes):
    return lax.broadcasted_iota(jnp.int32, (rows, lanes), 0)


def seg_of(idx, fe, se):
    return (idx >= fe).astype(jnp.int32) + (idx >= se).astype(jnp.int32)


def ends(sc, s):
    return sc[2 * s], sc[2 * s + 1]


def pair_cols(cols, first):
    lane = lane_iota(cols.shape[0])
    left = jnp.broadcast_to(cols[:, first : first + 1], cols.shape)
    right = jnp.broadcast_to(cols[:, first + 1 : first + 2], cols.shape)
    return jnp.where(lane < HD, left, right)


def head_pick():
    r = lax.broadcasted_iota(jnp.int32, (WIDE, 128), 0)
    c = lax.broadcasted_iota(jnp.int32, (WIDE, 128), 1)
    return jnp.where(c == r // HD, 1.0, 0.0)


def head_spread():
    r = lax.broadcasted_iota(jnp.int32, (256, WIDE), 0)
    c = lax.broadcasted_iota(jnp.int32, (256, WIDE), 1)
    return jnp.where(r % 128 == c // HD, 1.0, 0.0).astype(BF)


def expand(dst, cols, spread):
    high = cols.astype(BF)
    low = (cols - high.astype(F32)).astype(BF)
    both = jnp.concatenate([high, low], axis=1)
    for n in range(3):
        dst[:, 256 * n : 256 * n + 256] = dot(both, spread[:, 256 * n : 256 * n + 256])


def three_terms(v):
    high = v.astype(BF).astype(F32)
    mid = (v - high).astype(BF).astype(F32)
    return high, mid, v - high - mid


def tile_spread():
    r = lax.broadcasted_iota(jnp.int32, (256, 2 * WIDE), 0)
    h = lax.broadcasted_iota(jnp.int32, (256, 2 * WIDE), 1) // 128
    return jnp.where((r == h) | (r == h + 128) | (r == h + 144), 1.0, 0.0).astype(BF)


def expand_tiles(dst, cols, spread):
    high, mid, low = three_terms(cols)
    lane = lane_iota(L)
    rest = jnp.where(lane < 16, mid, pltpu.roll(low, 16, 1))
    left = jnp.concatenate([high, rest], axis=1).astype(BF)
    for n in range(6):
        dst[:, 256 * n : 256 * n + 256] = dot(left, spread[:, 256 * n : 256 * n + 256])


def to_lane0(packed, s, g):
    return pltpu.roll(packed, (256 - s * SPAN - g * 12) % 128, 1)


def from_lane0(cols, s, g):
    return pltpu.roll(cols, s * SPAN + g * 12, 1)


def rows_of(s, length=L):
    return pl.ds(pl.multiple_of(s * length, length), length)


def tile(j):
    return slice(128 * j, 128 * j + 128)


def conv_forward(ext, taps, bias, masks, first=0, length=L):
    acc = bias + taps[0] * ext[8 + first : 8 + first + length]
    for k in range(1, 4):
        acc = acc + (taps[k] * ext[8 + first - k : 8 + first - k + length]) * masks[k - 1]
    return acc


def conv_backward(ext, v_ext, taps, masks):
    out, tap_grads = None, []
    for k in range(4):
        part = ext[k : 264 + k]
        if k:
            part = part * masks[k - 1]
        tap_grads.append(jnp.sum(part * v_ext, axis=0, keepdims=True))
        out = taps[k] * part if out is None else out + taps[k] * part
    return out, tap_grads


def slot_masks(packed, s):
    cols = pltpu.roll(packed[...], (128 - 4 * s) % 128, 1)
    return [jnp.broadcast_to(cols[:, k : k + 1], cols.shape) for k in (1, 2, 3)]


def place_rows(dst, blocks, me, at, first=0, width=None, lead=0):
    count, rows = blocks.shape[1:3]
    width = blocks.shape[3] - first if width is None else width
    for n in range(count):
        start = pl.multiple_of((n ^ me) * rows, rows) if count > 1 else 0
        dst[pl.ds(start, rows), at : at + width] = blocks[lead, n, :, first : first + width]


def place_pair(dst, mine, other, me):
    place_rows(dst, mine, me, 0)
    place_rows(dst, other, me, 384)


def place_p1(dst, am, bm, ar, br, me, pieces):
    place_rows(dst, am, me, 0)
    place_rows(dst, bm, me, 256, 0, 128)
    place_rows(dst, ar, me, 384)
    place_rows(dst, br, me, 640, 0, 128)
    place_rows(pieces, bm, me, 0, 128, 128)
    place_rows(pieces, br, me, 128, 128, 128)


def half_at(c, me_t):
    return pl.ds(pl.multiple_of(384 * (c ^ (me_t % 2)), 128), 384)


def k0_body(sc, conv_x, bias_x, out_gain, dt_bias, a_log, skip_d, norm_gain, bias_bc, par, gain, bbc, row):
    par[...] = jnp.zeros_like(par)
    par[0:4] = conv_x[...]
    par[4] = bias_x[...]
    par[5] = out_gain[...]
    par[6, : dt_bias.shape[0]] = dt_bias[...]
    par[7, : a_log.shape[0]] = a_log[...]
    row[...] = jnp.zeros_like(row)
    row[0, : skip_d.shape[0]] = skip_d[...]
    r = lax.broadcasted_iota(jnp.int32, (128, 384), 0)
    c = lax.broadcasted_iota(jnp.int32, (128, 384), 1)
    par[8:9] = dot_high(row[...], jnp.where(r == c // HD, 1.0, 0.0))[0:1]
    gain[0] = norm_gain[...]
    bbc[0] = bias_bc[...]


def prepare_body(sc, tok, halo, cot, gain, nrm, nt, dbr, dt):
    def norm(v):
        v = v.astype(F32)
        r = lax.rsqrt(jnp.mean(v * v, axis=-1, keepdims=True) + EPS)
        return (v * r * gain[...]).astype(BF)

    @pl.loop(0, 16)
    def _(n):
        r = rows_of(n, 64)
        nrm[r] = norm(tok[r])
        keep = row_iota(64, 1) + 64 * (n % 4) < sc[2 * (n // 4) + 1]
        dbr[r] = jnp.where(keep, cot[r].astype(F32), 0.0).astype(BF)

    nrm[4 * L :] = jnp.where(sc[8] > 0, norm(halo[...]).astype(F32), 0.0).astype(BF)

    @pl.loop(0, 4)
    def _(s):
        nt[:, rows_of(s)] = nrm[rows_of(s)].T
        dt[:, rows_of(s)] = dbr[rows_of(s)].T

    nt[:, 4 * L :] = nrm[4 * L :].T


def k1_body(
    sc, nrm, am, ar, bm, br, par, cbc, bbc,
    inx, blow, clow, bto, sin, dbc,
    cumo, stepo, sigo, eto, reacho, decayo, faco, uvo, masko, backo, ct,
    wbuf, wbc, wdt, pcs, ext,
):
    g = pl.program_id(0)
    me_t, me_dp = sc[8], sc[9]

    @pl.when(g == 0)
    def _():
        wbc[...] = jnp.zeros_like(wbc)
        wdt[...] = jnp.zeros_like(wdt)

    place_rows(wbuf, am, me_dp, 0)
    place_rows(wbuf, bm, me_dp, 256, 0, 128)
    place_rows(wbuf, ar, me_dp, 384)
    place_rows(wbuf, br, me_dp, 640, 0, 128)
    count, brow = bm.shape[1:3]
    for c, blocks in ((0, bm), (1, br)):
        i = 2 * g + c
        t = i ^ me_t
        at = pl.ds(pl.multiple_of(128 * (t // 2), 128), 128)
        for n in range(count):
            start = pl.multiple_of((n ^ me_dp) * brow, brow) if count > 1 else 0
            r = pl.ds(start, brow)
            piece = blocks[0, n, :, 128:].astype(F32)
            lane = lane_iota(brow)
            own = pltpu.roll(jnp.where(lane < 64, piece, 0.0), 64 * (t % 2), 1)
            wbc[r, at] += own.astype(BF)
            own = pltpu.roll(jnp.where(lane >= 64, piece, 0.0), (i * 6 + 64) % 128, 1)
            wdt[r] += own.astype(BF)
    for n in range(3):
        cols = slice(256 * n, 256 * n + 256)
        inx[0, :, cols] = dot(nrm[...], wbuf[:, cols]).astype(BF)

    @pl.when(g == 1)
    def _():
        pcs[...] = dot(nrm[...], wbc[...])
        sin[0] = pcs[:, :128]
        sin[1] = pcs[:, 128:]
        pcs[0 : 4 * L, 0:128] = dot(nrm[0 : 4 * L], wdt[...])
        dtacc = pcs[0:L, 0:128]
        for s in range(1, 4):
            dtacc = dtacc + pltpu.roll(pcs[L * s : L * s + L, 0:128], s * SPAN, 1)
        dtb = jnp.zeros((1, 128), F32)
        alog = jnp.zeros((1, 128), F32)
        for i in range(4):
            for s in range(4):
                at = slice(384 * (i % 2), 384 * (i % 2) + 128)
                dtb += pltpu.roll(par[i // 2, 6:7, at], s * SPAN + i * 6, 1)
                alog += pltpu.roll(par[i // 2, 7:8, at], s * SPAN + i * 6, 1)
        raw = dtacc + dtb
        step = jnp.maximum(raw, 0.0) + jnp.log1p(jnp.exp(-jnp.abs(raw)))
        sig = 1.0 / (1.0 + jnp.exp(-raw))
        decay = step * -jnp.exp(alog)
        lower = jnp.where(
            lax.broadcasted_iota(jnp.int32, (L, L), 0) >= lax.broadcasted_iota(jnp.int32, (L, L), 1),
            1.0,
            0.0,
        )
        cum = dot_high(lower, decay)
        row = row_iota(L, 128)
        lane = lane_iota(L)
        slot = lane // SPAN
        tail = jnp.zeros((L, 128), F32)
        enters = jnp.zeros((L, 128), F32)
        follows = jnp.zeros((8, 128), F32)
        masks = jnp.ones((L, 128), F32)
        row_b = row_iota(L + 8, 128) - 8
        lane_b = lane_iota(L + 8)
        back_masks = jnp.ones((L + 8, 128), F32)
        slot8 = lane_iota(8) // SPAN
        inner_block = jnp.where(me_t > 0, 1.0, 0.0)
        back = lane % 4
        for s in range(4):
            fe, se = ends(sc, s)
            seg = seg_of(row, fe, se)
            last = seg_of(L - 1, fe, se)
            before = seg_of(-1, fe, se)
            here = slot == s
            tail = jnp.where(here & (seg == last), 1.0, tail)
            enters = jnp.where(here & (seg == before), inner_block, enters)
            follows = jnp.where(
                (slot8 == s), jnp.where(last == before, inner_block, 0.0), follows
            )
            masks = jnp.where((lane // 4 == s) & (seg != seg_of(row - back, fe, se)), 0.0, masks)
            cut = seg_of(row_b, fe, se) != seg_of(row_b + lane_b % 4, fe, se)
            back_masks = jnp.where((lane_b // 4 == s) & cut, 0.0, back_masks)
        cum_last = cum[L - 1 : L]
        cum2 = cum * LOG2E
        cumo[...] = cum2
        stepo[...] = step
        sigo[...] = sig
        eto[...] = jnp.exp(cum_last - cum) * tail
        reacho[...] = jnp.exp(cum) * enters
        decayo[...] = decay
        faco[...] = jnp.exp(cum_last) * follows
        uvo[...] = jnp.exp2(-jnp.abs(cum2 - cum2[127:128]))
        masko[...] = masks
        backo[...] = back_masks
        ct[...] = cum2.T
        for q, low_out in ((0, blow), (1, clow)):
            taps = [cbc[k : k + 1, tile(q)] for k in range(4)]

            @pl.loop(0, 4)
            def _(s):
                ext[0:8] = sin[q, pl.ds(pl.multiple_of(4 * L + 16 * s + 8, 8), 8)]
                ext[8:] = sin[q, rows_of(s)]
                acc = conv_forward(ext, taps, bbc[:, tile(q)], slot_masks(masko, s))
                sg = sigmoid(acc)
                low = acc * sg
                low_out[rows_of(s)] = low.astype(BF)
                dbc[q, rows_of(s)] = sg + low * (1.0 - sg)
                if q == 0:
                    bto[rows_of(s, 128)] = low.T.astype(BF)


def factor_rows(fac, g):
    rows = []
    for s in range(4):
        f = to_lane0(fac[...], s, g)
        rows.append(jnp.concatenate([pair_cols(f, 2 * j)[0:1] for j in range(6)], axis=1))
    f = jnp.concatenate(rows, axis=0)
    high = f.astype(BF).astype(F32)
    return jnp.concatenate([high, f - high, jnp.zeros((8, WIDE), F32)], axis=0).astype(BF)


def k2_body(g, sc, inx, halo, par, bt, stepp, etp, fac, mask, *rest):
    xo, xso, dslo, sto, xe, ext, spread, stepx, stepe = rest[-9:]
    s = pl.program_id(0)
    me_t = sc[8]

    @pl.when(s == 0)
    def _():
        spread[...] = head_spread()

    masks = slot_masks(mask, s)
    step = to_lane0(stepp[...], s, g)
    expand(stepx, step, spread)
    expand(stepe, step * to_lane0(etp[...], s, g), spread)
    for j in range(6):
        ext[j, 0:8] = halo[0, :, tile(j)].astype(F32)[8:]
        ext[j, 8:] = inx[0, :, tile(j)].astype(F32)
    for n in range(L // CHUNK):
        r = slice(CHUNK * n, CHUNK * n + CHUNK)
        mr = [m[r] for m in masks]
        for j in range(6):
            taps = [0.5 * par[0, k : k + 1, tile(j)] for k in range(4)]
            half = conv_forward(ext.at[j], taps, 0.5 * par[0, 4:5, tile(j)], mr, CHUNK * n, CHUNK)
            th = jnp.tanh(half)
            up = 1.0 + th
            act = half * up
            xo[0, r, tile(j)] = act.astype(BF)
            dslo[0, r, tile(j)] = ((0.5 * up) * (1.0 + half * (1.0 - th))).astype(BF)
            xso[0, r, tile(j)] = (act * stepx[r, tile(j)]).astype(BF)
            xe[r, tile(j)] = (act * stepe[r, tile(j)]).astype(BF)
    for c in range(2):
        sto[rows_of(s, 128), half_at(c, me_t)] = dot(
            bt[...], xe[:, 384 * c : 384 * c + 384]
        ).astype(BF)

    @pl.when(s == 3)
    def _():
        f = factor_rows(fac, g)
        for c in range(2):
            sto[512:528, half_at(c, me_t)] = f[:, 384 * c : 384 * c + 384]


def by_head(pair):
    lane = lane_iota(128)
    zero = jnp.zeros_like(pair)
    return jnp.concatenate(
        [jnp.where(lane < HD, pair, zero), jnp.where(lane < HD, zero, pair)], axis=0
    )


def diag_mask(d, fe, se, key_rows):
    r = lax.broadcasted_iota(jnp.int32, (128, 128), 0) + 128 * d
    c = lax.broadcasted_iota(jnp.int32, (128, 128), 1) + 128 * d
    order = (c >= r) if key_rows else (r >= c)
    return order & (seg_of(r, fe, se) == seg_of(c, fe, se))


def cross_half(fe, se, key_rows):
    r = lax.broadcasted_iota(jnp.int32, (128, 128), 0) + (0 if key_rows else 128)
    c = lax.broadcasted_iota(jnp.int32, (128, 128), 1) + (128 if key_rows else 0)
    return seg_of(r, fe, se) == seg_of(c, fe, se)


def k3_body(g, sc, xs, blow, clow, cump, uvp, ct, *rest):
    within, scores, cross, spread, uvx, tiles, cumx = rest[-7:]
    s = pl.program_id(0)
    fe, se = sc[2 * s], sc[2 * s + 1]

    @pl.when(s == 0)
    def _():
        spread[...] = head_spread()
        tiles[...] = tile_spread()


    for d in range(2):
        r = slice(128 * d, 128 * d + 128)
        scores[d] = jnp.where(diag_mask(d, fe, se, False), dot_nt(clow[r], blow[r]), 0.0)
    cross[...] = jnp.where(cross_half(fe, se, False), dot_nt(clow[128:], blow[:128]), 0.0).astype(BF)

    expand_tiles(cumx, to_lane0(cump[...], s, g), tiles)
    expand(uvx, to_lane0(uvp[...], s, g), spread)
    for j in range(6):
        for d in range(2):
            r = slice(128 * d, 128 * d + 128)
            pair = xs[0, r, tile(j)]
            parts = []
            for b in range(2):
                h = 2 * j + b
                gap = cumx[r, tile(h)] - ct[pl.ds(s * SPAN + g * 12 + h, 1), :][:, r]
                parts.append((jnp.exp2(jnp.minimum(gap, 0.0)) * scores[d]).astype(BF))
            total = dot(jnp.concatenate(parts, axis=1), by_head(pair))
            if d == 1:
                xv = (xs[0, :128, tile(j)].astype(F32) * uvx[:128, tile(j)]).astype(BF)
                total = total + dot(cross[...], xv) * uvx[128:, tile(j)]
            within[0, r, tile(j)] = total


def k4_body(sc, nrm, dbr, wzm, wzr, wom, wor, gate, dgn, wz, wo):
    g = pl.program_id(0)
    n = pl.program_id(1)
    me_dp = sc[9]

    @pl.when(n == 0)
    def _():
        place_pair(wz, wzm, wzr, me_dp)
        place_pair(wo, wom, wor, me_dp)

    cols = pl.ds(pl.multiple_of(n * 256, 256), 256)
    gate[0] = dot(nrm[0 : 4 * L], wz[:, cols]).astype(BF)
    dgn[0] = dot(dbr[...], wo[:, cols]).astype(BF)


def k5_body(
    sc, within, gate, dgn, x, r1, r2, r3, reachp, fac, clow, par, wom, wor, tok,
    out, gno, dgo, dyo, dpo, prevo, rowsum, dco, small,
    mo, sums, branch, wbuf, gnb, frow, dlow, seg_h, seg_l, pick, pv, spread, reachx,
):
    ph = pl.program_id(0)
    g = pl.program_id(1)
    s = pl.program_id(2)
    me_t, me_dp = sc[8], sc[9]
    r = rows_of(s)
    first = (g == 0) & (s == 0)

    @pl.when((ph == 0) & first)
    def _():
        rowsum[...] = jnp.zeros_like(rowsum)
        dco[...] = jnp.zeros_like(dco)
        small[...] = jnp.zeros_like(small)
        pick[...] = head_pick().astype(BF)
        spread[...] = head_spread()

    expand(reachx, to_lane0(reachp[...], s, g), spread)

    @pl.when(ph == 0)
    def _():
        srow = rows_of(s, 128)
        for c in range(2):
            at = half_at(c, me_t)
            frow[...] = r1[512:528, at].astype(F32)
            f = frow[pl.ds(s, 1)] + frow[pl.ds(s + 4, 1)]
            p = (
                jnp.where(me_t % 2 == 1, r1[srow, at].astype(F32), 0.0)
                + jnp.where(me_t == 2, r2[srow, at].astype(F32), 0.0)
                + jnp.where(me_t == 3, f * r3[srow, at].astype(F32), 0.0)
            )
            pv[:, 384 * c : 384 * c + 384] = p.astype(BF)
        prevo[g, srow] = pv[...]
        sq = jnp.zeros((L, 128), F32)
        dd = jnp.zeros((L, 128), F32)
        for j in range(6):
            from_prev = dot(clow[...], pv[:, tile(j)])
            mixed = (
                within[0, :, tile(j)]
                + reachx[:, tile(j)] * from_prev
                + par[0, 8:9, tile(j)] * x[0, :, tile(j)].astype(F32)
            )
            mo[g, r, tile(j)] = mixed
            gv = gate[0, :, tile(j)].astype(F32)
            gated = mixed * (gv * sigmoid(gv))
            sq = sq + gated * gated
            dd = dd + dgn[0, :, tile(j)].astype(F32) * par[0, 5:6, tile(j)] * gated
        sq = jnp.broadcast_to(jnp.sum(sq, axis=1, keepdims=True), (L, 128))
        dd = jnp.broadcast_to(jnp.sum(dd, axis=1, keepdims=True), (L, 128))

        @pl.when(g == 0)
        def _():
            sums[0, r] = sq
            sums[1, r] = dd

        @pl.when(g == 1)
        def _():
            sq2 = sums[0, r] + sq
            dd2 = sums[1, r] + dd
            gscale = lax.rsqrt(sq2 * (1.0 / INNER) + EPS)
            sums[0, r] = gscale
            sums[1, r] = gscale * gscale * gscale * (dd2 * (1.0 / INNER))

    @pl.when(ph == 1)
    def _():
        gscale = sums[0, r]
        coef = sums[1, r]
        srow = rows_of(s, 128)
        for j in range(6):
            gv = gate[0, :, tile(j)].astype(F32)
            mixed = mo[g, r, tile(j)]
            sg = sigmoid(gv)
            silu = gv * sg
            gated = mixed * silu
            gs = gated * gscale
            gain = par[0, 5:6, tile(j)]
            gn = (gs * gain).astype(BF)
            gno[0, :, tile(j)] = gn
            gnb[r, tile(j)] = gn
            d = dgn[0, :, tile(j)].astype(F32)
            small[g, 0:1, tile(j)] += jnp.sum(d * gs, axis=0, keepdims=True)
            dgated = gscale * (d * gain) - gated * coef
            dgo[0, :, tile(j)] = (dgated * mixed * (sg + silu * (1.0 - sg))).astype(BF)
            dy = (dgated * silu).astype(BF)
            dyo[0, :, tile(j)] = dy
            dyf = dy.astype(F32)
            dlow[:, tile(j)] = (dyf * reachx[:, tile(j)]).astype(BF)
            dx_skip = dyf * x[0, :, tile(j)].astype(F32)
            small[g, 1:2, tile(j)] += jnp.sum(dx_skip, axis=0, keepdims=True)
            v = dyf * mixed - par[0, 8:9, tile(j)] * dx_skip
            high = v.astype(BF)
            seg_h[:, tile(j)] = high
            seg_l[:, tile(j)] = (v - high.astype(F32)).astype(BF)
        seg = dot(seg_h[...], pick[...]) + dot(seg_l[...], pick[...])
        rowsum[...] += from_lane0(seg, s, g)
        dco[r] += dot_nt(dlow[...], prevo[g, srow])
        for c in range(2):
            dpo[srow, half_at(c, me_t)] = lax.dot_general(
                clow[...],
                dlow[:, 384 * c : 384 * c + 384],
                (((0,), (0,)), ((), ())),
                preferred_element_type=F32,
            ).astype(BF)

        @pl.when(s == 3)
        def _():
            f = factor_rows(fac, g)
            for c in range(2):
                dpo[512:528, half_at(c, me_t)] = f[:, 384 * c : 384 * c + 384]
            place_pair(wbuf, wom, wor, me_dp)

        @pl.when((s == 3) & (g == 0))
        def _():
            branch[...] = dot_nt(gnb[...], wbuf[...])

        @pl.when((s == 3) & (g == 1))
        def _():
            branch[...] += dot_nt(gnb[...], wbuf[...])

            @pl.loop(0, 16)
            def _(n):
                q = rows_of(n, 64)
                out[q] = (tok[q].astype(F32) + branch[q]).astype(BF)


def store_grad(ref, lead, me_dp, value_ref, first, width, at=0):
    count, rows = ref.shape[-3], ref.shape[-2]
    for n in range(count):
        place = n ^ me_dp if count > 1 else 0
        part = value_ref[n * rows : (n + 1) * rows, first : first + width].astype(BF)
        ref[lead + (place, slice(None), slice(at, at + width))] = part


def add_weighted(total, val, w, lead=()):
    @pl.loop(0, total.shape[0] // 64)
    def _(n):
        r = rows_of(n, 64)
        part = total[r]
        for j in range(w.shape[1] // 128):
            v = val[j, r] if lead else val[r, tile(j)]
            part = part + v * w[r, tile(j)].astype(F32)
        total[r] = part


def k6_body(sc, nt, dt, gn, dg, wzm, wzr, ok, os, zk, zs, ngz, val, wz):
    g = pl.program_id(0)
    me_dp = sc[9]
    place_pair(wz, wzm, wzr, me_dp)

    @pl.when(g == 0)
    def _():
        ngz[...] = jnp.zeros_like(ngz)

    for lhs, rhs, keep, send in ((dt, gn, ok, os), (nt, dg, zk, zs)):
        for n in range(3):
            cols = slice(256 * n, 256 * n + 256)
            val[:, cols] = dot(lhs[:, : 4 * L], rhs[0, :, cols])
        store_grad(keep, (0,), me_dp, val, 0, 384)
        store_grad(send, (0,), me_dp, val, 384, 384)
    add_weighted(ngz, val, wz)


def k7_body(g, sc, xs, dy, blow, clow, cump, uvp, ct, *rest):
    dxo, bco, pko, scores, cross, xvb, udb, spread, uvx, tiles, cumx, pick, corr = rest[-13:]
    s = pl.program_id(0)

    @pl.when(s == 0)
    def _():
        spread[...] = head_spread()
        tiles[...] = tile_spread()
        pick[...] = head_pick().astype(BF)
        pko[...] = jnp.zeros_like(pko)

    fe, se = sc[2 * s], sc[2 * s + 1]

    for d in range(2):
        r = slice(128 * d, 128 * d + 128)
        scores[d] = jnp.where(diag_mask(d, fe, se, True), dot_nt(blow[r], clow[r]), 0.0)
    cross[...] = jnp.where(cross_half(fe, se, True), dot_nt(blow[:128], clow[128:]), 0.0).astype(BF)

    expand_tiles(cumx, to_lane0(cump[...], s, g), tiles)
    expand(uvx, to_lane0(uvp[...], s, g), spread)
    totals = [jnp.zeros((128, 128), F32), jnp.zeros((128, 128), F32)]
    crossq = cross[...].astype(F32).T.astype(BF)
    for j in range(6):
        for d in range(2):
            r = slice(128 * d, 128 * d + 128)
            xp = xs[0, r, tile(j)]
            dyp = dy[0, r, tile(j)]
            grads = dot_nt(by_head(xp), dyp)
            parts = []
            for b in range(2):
                h = 2 * j + b
                gap = ct[pl.ds(s * SPAN + g * 12 + h, 1), :][:, r] - cumx[r, tile(h)]
                kern = jnp.exp2(jnp.minimum(gap, 0.0))
                totals[d] = totals[d] + grads[128 * b : 128 * b + 128] * kern
                parts.append((kern * scores[d]).astype(BF))
            dx = dot(jnp.concatenate(parts, axis=1), by_head(dyp))
            scaled = (xp if d == 0 else dyp).astype(F32) * uvx[r, tile(j)]
            low = scaled.astype(BF)
            diff = low.astype(F32) - scaled
            if d == 0:
                xvb[:, tile(j)] = low
                top, xdiff = dx, diff
            else:
                udb[:, tile(j)] = low
                off = dot(cross[...], low)
                dxo[0, r, tile(j)] = dx
                dxo[0, :128, tile(j)] = top + off * uvx[:128, tile(j)]
                corr[:128, tile(j)] = (xdiff * off).astype(BF)
                corr[128:, tile(j)] = (diff * dot(crossq, xvb[:, tile(j)])).astype(BF)
    dcr = dot_nt(xvb[...], udb[...])
    pko[...] += from_lane0(dot(corr[...], pick[...]), s, g)
    d0 = jnp.where(diag_mask(0, fe, se, True), totals[0], 0.0)
    d1 = jnp.where(diag_mask(1, fe, se, True), totals[1], 0.0)
    dl = jnp.where(cross_half(fe, se, True), dcr, 0.0)
    c0, c1, b0, b1 = clow[:128], clow[128:], blow[:128], blow[128:]
    bco[0, 0:128] = dot(d0.astype(BF), c0) + dot(dl.astype(BF), c1)
    bco[0, 128:] = dot(d1.astype(BF), c1)
    bco[1, 0:128] = dot(d0.T.astype(BF), b0)
    bco[1, 128:] = dot(d1.T.astype(BF), b1) + dot(dl.T.astype(BF), b0)


def k8_body(
    g, last, sc, nt, xs, dy, dsl, inx, halo, dxw, q1, q2, q3, prev, blow, stepp, etp, back, par,
    am, ar, bm, br, *rest,
):
    if last:
        (
            fac, sigp, decay, gain, ngz, nga, cbc, small1, small5, bc7a, bc7b, corr_a, corr_b, dc3, rowsum, sin, dbc, sega, enda, dba,
            keep, send, din, seg, end, dba_o, small, ngx, din5, skeep, ssend,
            val, hsum, gsc, gf, glow, xe, seg_h, seg_l, pick, wbuf, wpc, gbuf, pcs, pblk, sbc, spack, ub, ext, spread, stepx, etx,
        ) = rest
    else:
        (
            keep, send, din, seg, end, dba_o, small, ngx,
            val, hsum, gsc, gf, glow, xe, seg_h, seg_l, pick, wbuf, ub, ext, spread, stepx, etx,
        ) = rest
    s = pl.program_id(0)
    me_t, me_dp = sc[8], sc[9]
    r = rows_of(s)
    hrow = pl.ds(pl.multiple_of(4 * L + 16 * s, 16), 16)

    @pl.when(s == 0)
    def _():
        seg[...] = jnp.zeros_like(seg)
        end[...] = jnp.zeros_like(end)
        small[...] = jnp.zeros_like(small)
        pick[...] = head_pick().astype(BF)
        ext[:, 0:8] = jnp.zeros((6, 8, 128), F32)
        ext[:, 264:] = jnp.zeros((6, 8, 128), F32)
        spread[...] = head_spread()

    srow = rows_of(s, 128)
    for c in range(2):
        at = half_at(c, me_t)
        gf[...] = q1[512:528, at].astype(F32)
        f = gf[pl.ds(s, 1)] + gf[pl.ds(s + 4, 1)]
        v = (
            jnp.where(me_t % 2 == 0, q1[srow, at].astype(F32), 0.0)
            + jnp.where(me_t == 1, q2[srow, at].astype(F32), 0.0)
            + jnp.where(me_t == 0, f * q3[srow, at].astype(F32), 0.0)
        )
        gsc[:, 384 * c : 384 * c + 384] = v
        glow[:, 384 * c : 384 * c + 384] = v.astype(BF)
    for n in range(3):
        cols = slice(256 * n, 256 * n + 256)
        ub[:, cols] = dot(blow[...], glow[:, cols])
    masks = slot_masks(back, s)
    expand(stepx, to_lane0(stepp[...], s, g), spread)
    expand(etx, to_lane0(etp[...], s, g), spread)
    ends_row, gp_row = [], []
    for j in range(6):
        taps = [par[0, k : k + 1, tile(j)] for k in range(4)]
        xf = xs[0, :, tile(j)].astype(F32)
        ec = etx[:, tile(j)]
        eu = ub[:, tile(j)] * ec
        xe[:, tile(j)] = (xf * ec).astype(BF)
        ends_row.append(jnp.sum(xf * eu, axis=0, keepdims=True))
        gp_row.append(
            jnp.sum(gsc[:, tile(j)] * prev[0, srow, tile(j)].astype(F32), axis=0, keepdims=True)
        )
        dxi = dxw[0, :, tile(j)] + eu
        v = xf * dxi
        high = v.astype(BF)
        seg_h[:, tile(j)] = high
        seg_l[:, tile(j)] = (v - high.astype(F32)).astype(BF)
        dx = dxi * stepx[:, tile(j)] + par[0, 8:9, tile(j)] * dy[0, :, tile(j)].astype(F32)
        dconv = dx * dsl[0, :, tile(j)].astype(F32)
        small[4:5, tile(j)] += jnp.sum(dconv, axis=0, keepdims=True)
        v_ext = jnp.concatenate(
            [halo[0, :, tile(j)].astype(F32)[8:], inx[0, :, tile(j)].astype(F32)], axis=0
        )
        ext[j, 8:264] = dconv
        dv, tap_grads = conv_backward(ext.at[j], v_ext, taps, masks)
        for k in range(4):
            small[k : k + 1, tile(j)] += tap_grads[k]
        din[r, tile(j)] = dv[8:].astype(BF)
        din[hrow, tile(j)] = jnp.concatenate([jnp.zeros((8, 128), F32), dv[:8]], axis=0).astype(BF)
    seg[...] += from_lane0(dot(seg_h[...], pick[...]) + dot(seg_l[...], pick[...]), s, g)
    dba_o[r] = dot_nt(xe[...], glow[...])
    rows = jnp.concatenate(
        [
            jnp.concatenate(ends_row, axis=1),
            jnp.concatenate(gp_row, axis=1),
            jnp.zeros((6, WIDE), F32),
        ],
        axis=0,
    )
    end[...] += from_lane0(dot_high(rows, pick[...].astype(F32)), s, g)

    @pl.when(s == 3)
    def _():
        for n in range(3):
            cols = slice(256 * n, 256 * n + 256)
            hsum[...] = dot(nt[:, 4 * L :], din[4 * L :, cols])
            val[:, cols] = dot(nt[:, : 4 * L], din[: 4 * L, cols]) + hsum[...]
        store_grad(keep, (), me_dp, val, 0, 384)
        store_grad(send, (), me_dp, val, 384, 384)
        place_rows(wbuf, am, me_dp, 0)
        place_rows(wbuf, ar, me_dp, 384)
        place_rows(wbuf, bm, me_dp, 256, 0, 128, g if last else 0)
        place_rows(wbuf, br, me_dp, 640, 0, 128, g if last else 0)
        ngx[...] = ngz[...] + nga[...] if last else jnp.zeros_like(ngx)
        add_weighted(ngx, val, wbuf)

    if not last:
        return

    @pl.when(s == 3)
    def _():
        for q in range(2):
            taps = [cbc[k : k + 1, tile(q)] for k in range(4)]
            sbc[q] = jnp.zeros((8, 128), F32)

            @pl.loop(0, 4)
            def _(n):
                rn = rows_of(n)
                if q == 0:
                    grad = bc7a[0, rn] + bc7b[0, rn] + dba_o[rn] + dba[rn]
                else:
                    grad = bc7a[1, rn] + bc7b[1, rn] + dc3[rn]
                dconv = grad * dbc[q, rn]
                hn = pl.ds(pl.multiple_of(4 * L + 16 * n, 16), 16)
                v_ext = jnp.concatenate([sin[q, hn][8:], sin[q, rn]], axis=0)
                ext[q, 8:264] = dconv
                dv, tap_grads = conv_backward(ext.at[q], v_ext, taps, slot_masks(back, n))
                sbc[q, 4:5] += jnp.sum(dconv, axis=0, keepdims=True)
                for k in range(4):
                    sbc[q, k : k + 1] += tap_grads[k]
                gbuf[q, rn] = dv[8:]
                gbuf[q, hn] = jnp.concatenate([jnp.zeros((8, 128), F32), dv[:8]], axis=0)

        row = row_iota(L, 128)
        corr = corr_a[...] + corr_b[...]
        col = seg[...] + sega[...] + jnp.where(row < 128, corr, 0.0)
        ends_all = end[...] + enda[...]
        at_last = ends_all[0:1] + ends_all[1:2] * fac[0:1]
        dcum = rowsum[...] + jnp.where(row < 128, 0.0, corr) - col + jnp.where(row == L - 1, at_last, 0.0)
        upper = jnp.where(
            lax.broadcasted_iota(jnp.int32, (L, L), 0) <= lax.broadcasted_iota(jnp.int32, (L, L), 1),
            1.0,
            0.0,
        )
        dlog = dot_high(upper, dcum)
        alog = jnp.zeros((1, 128), F32)
        for i in range(4):
            at = slice(384 * (i % 2), 384 * (i % 2) + 128)
            for n in range(4):
                alog += pltpu.roll(par[i // 2, 7:8, at], n * SPAN + i * 6, 1)
        step_all, sig = stepp[...], sigp[...]
        ratio = jnp.where(step_all > 1e-30, sig / jnp.maximum(step_all, 1e-30), 1.0)
        ddt = ratio * col - sig * jnp.exp(alog) * dlog
        dts = jnp.concatenate(
            [
                jnp.sum(ddt, axis=0, keepdims=True),
                jnp.sum(dlog * decay[...], axis=0, keepdims=True),
                jnp.zeros((6, 128), F32),
            ],
            axis=0,
        )
        dts = dts + pltpu.roll(dts, 64, 1)
        dts = dts + pltpu.roll(dts, 32, 1)
        spack[...] = jnp.zeros_like(spack)
        for x in range(2):
            spack[x, 0:5] = (small if x == 0 else small1)[0:5]
            spack[x, 5:7] = small5[x, 0:2]
            for c in range(2):
                own = pltpu.roll(dts, (128 - 6 * (2 * x + c)) % 128, 1)
                own = jnp.where(lane_iota(8) < 6, own, 0.0)
                spack[x, 7:9, 384 * c : 384 * c + 128] = own[0:2]
            skeep[16 * x : 16 * x + 16] = spack[x, :, :384]
            ssend[16 * x : 16 * x + 16] = spack[x, :, 384:]
        ssend[32:40] = jnp.zeros((8, 384), F32)
        for q in range(2):
            ssend[32:37, tile(q)] = sbc[q, 0:5]
        for n in range(4):
            t = n ^ me_t
            turn = (64 * (t % 2)) % 128

            @pl.loop(0, 4)
            def _(m):
                rm = rows_of(m)
                lane = lane_iota(L)
                a = pltpu.roll(gbuf[t // 2, rm], turn, 1)
                d = pltpu.roll(ddt, (320 - m * SPAN - n * 6) % 128, 1)
                piece = jnp.where(lane < 64, a, jnp.where(lane < 70, d, 0.0))
                din5[rm, tile(n)] = piece.astype(BF)

            a = pltpu.roll(gbuf[t // 2, 4 * L :], turn, 1)
            din5[4 * L :, tile(n)] = jnp.where(lane_iota(64) < 64, a, 0.0).astype(BF)
        for n in range(2):
            cols = slice(256 * n, 256 * n + 256)
            hsum[...] = dot(nt[:, 4 * L :], din5[4 * L :, cols])
            v = dot(nt[:, : 4 * L], din5[: 4 * L, cols]) + hsum[...]
            pcs[2 * n] = v[:, :128]
            pcs[2 * n + 1] = v[:, 128:]
            place_rows(wpc, bm, me_dp, 256 * n, 128, 128, n)
            place_rows(wpc, br, me_dp, 256 * n + 128, 128, 128, n)
        add_weighted(ngx, pcs, wpc, (0,))
        gain_grad = (
            lax.dot_general(
                jnp.ones((8, 128), F32),
                ngx[...],
                (((1,), (1,)), ((), ())),
                preferred_element_type=F32,
                precision=lax.Precision.HIGHEST,
            )
            / gain[...]
        )
        ssend[37:38] = gain_grad[0:1, :384]
        ssend[38:39] = gain_grad[0:1, 384:]
        count, brow = keep.shape[0], keep.shape[1]
        for n in range(4):
            ref = keep if n % 2 == 0 else send
            at = slice(384 + 128 * (n // 2), 512 + 128 * (n // 2))
            if count == 1:
                ref[0, :, at] = pcs[n].astype(BF)
                continue
            t = n ^ me_t
            quarter = brow // 4
            for m in range(count):
                for c in range(4):
                    pblk[quarter * c : quarter * c + quarter] = pcs[
                        c ^ me_t, pl.ds(pl.multiple_of(brow * m + quarter * t, 8), quarter)
                    ]
                both = jnp.where(
                    lane_iota(brow) < 64, pblk[...], pcs[n, brow * m : brow * m + brow]
                )
                ref[m ^ me_dp, :, at] = both.astype(BF)


def k9z_body(sc, dg, wzm, wzr, dn, wz):
    place_pair(wz, wzm, wzr, sc[9])
    dn[...] = dot_nt(dg[0], wz[...])


def k9_body(sc, din0, din1, din5, dna, dnb, am, ar, bm, br, dn, wx, wpc):
    g = pl.program_id(0)
    place_p1(wx, am, bm, ar, br, sc[9], wpc)

    @pl.when(g == 0)
    def _():
        dn[...] = dot_nt(din0[...], wx[...])

    @pl.when(g == 1)
    def _():
        dn[...] += dot_nt(din1[...], wx[...])
        dn[: 4 * L] += dna[...] + dnb[...]

    dn[...] += dot_nt(din5[...], wpc[...])


def k10_body(sc, dn, hr, tok, cot, gain, ig):
    s = pl.program_id(0)
    d = dn[...]
    extra = jnp.where(sc[8] < 3, hr[...].astype(F32), 0.0)
    width = d.shape[1]
    d = jnp.concatenate([d[: L - 16], d[L - 16 :] + extra], axis=0)
    tv = tok[...].astype(F32)
    r = lax.rsqrt(jnp.mean(tv * tv, axis=-1, keepdims=True) + EPS)
    tr = tv * r
    gd = gain[...] * d
    inner = jnp.sum(gd * tr, axis=-1, keepdims=True) * (1.0 / width)
    keep = row_iota(L, 1) < sc[2 * s + 1]
    res = jnp.where(keep, cot[...].astype(F32), 0.0)
    ig[...] = (res + r * (gd - tr * inner)).astype(BF)


def FINAL_SHAPES(dim, cols, heads, state, shard, tcount):
    return [
        (dim,), (shard, cols), (shard // tcount, 2 * state), (heads, shard), (4, cols), (cols,),
        (4, 2 * state), (2 * state,), (heads,), (heads,), (heads,), (cols,),
    ]


def k11_body(
    sc, va, vr, both, got,
    ngain, wx, wbc, wdt, cx, bx, cb, bb, dtb, alog, skip, og,
    g, sm,
):
    g[...] = va[...].astype(F32) + vr[...].astype(F32)
    sm[...] = both[...] + got[...]
    wx[...] = g[:, :384]
    quarter = g.shape[0] // 4
    lane = lane_iota(quarter)
    parts = [g[quarter * c : quarter * c + quarter, 384:512] for c in range(4)]
    for t in range(2):
        wbc[:, tile(t)] = jnp.where(lane < 64, parts[2 * t], pltpu.roll(parts[2 * t + 1], 64, 1))
    wdt[...] = pltpu.roll(g[:, 384:512], 64, 1).T[: wdt.shape[0]]
    cx[...] = sm[0:4]
    bx[...] = sm[4]
    og[...] = sm[5]
    r = lax.broadcasted_iota(jnp.int32, (384, 128), 0)
    c = lax.broadcasted_iota(jnp.int32, (384, 128), 1)
    sums = dot_high(sm[0:8], jnp.where(c == r // HD, 1.0, 0.0))
    skip[...] = sums[6, : skip.shape[0]]
    dtb[...] = sm[7, : dtb.shape[0]]
    alog[...] = sm[8, : alog.shape[0]]
    cb[...] = sm[16:20, : cb.shape[1]]
    bb[...] = sm[20, : bb.shape[0]]
    half = sm.shape[1]
    ngain[0:half] = sm[21]
    ngain[half : 2 * half] = sm[22]


def full(shape):
    return pl.BlockSpec(shape, lambda *a: (0,) * len(shape))


def call(body, grid, in_specs, out_specs, out_shapes, scratch, cost, name, aliases=None, vmem_mib=VMEM_MIB):
    flops, moved = cost
    return pl.pallas_call(
        body,
        grid_spec=pltpu.PrefetchScalarGridSpec(
            num_scalar_prefetch=1,
            grid=grid,
            in_specs=in_specs,
            out_specs=out_specs,
            scratch_shapes=scratch,
        ),
        out_shape=out_shapes,
        compiler_params=pltpu.CompilerParams(vmem_limit_bytes=vmem_mib * 2**20),
        cost_estimate=pl.CostEstimate(flops=flops, bytes_accessed=moved, transcendentals=0),
        input_output_aliases=aliases or {},
        name=name,
    )


def sds(shape, dtype):
    return pltpu.HBM(shape, dtype)


def anywhere(count):
    return [pl.BlockSpec(memory_space=pl.ANY)] * count


def flip(value, axis, bit):
    count = lax.axis_size(axis)
    return lax.ppermute(value, axis, [(a, a ^ bit) for a in range(count)])


def meet(*values):
    return lax.optimization_barrier(values)


def per_device(
    tokens, lengths, cotangent, norm_gain, w_z, w_x, w_bc, w_dt, conv_x, bias_x, conv_bc, bias_bc,
    dt_bias, a_log, skip_d, out_gain, w_out,
):
    tcount = lax.axis_size("tensor")
    dpcount = lax.axis_size("dp")
    me_t = lax.axis_index("tensor")
    me_dp = lax.axis_index("dp")
    slots, own_len, dim = tokens.shape
    rows = slots * own_len
    shard = w_z.shape[0]
    cols = w_z.shape[1]
    heads = w_dt.shape[1]
    fast = shard % 32 == 0 and dpcount & (dpcount - 1) == 0 and dpcount >= 8
    count = dpcount if fast else 1
    brow = shard if fast else dim

    first = lengths[:, 0] - me_t * own_len
    second = first + lengths[:, 1]
    sc = jnp.concatenate(
        [
            jnp.stack([first, second], axis=1).reshape(-1),
            jnp.stack([me_t, me_dp]),
            jnp.zeros((6,), jnp.int32),
        ]
    ).astype(jnp.int32)
    tok = tokens.reshape(rows, dim)
    cot = cotangent.reshape(rows, dim)

    bq = w_bc.shape[1] // tcount
    state = w_bc.shape[1] // 2
    own_bc = lax.dynamic_slice_in_dim(w_bc, me_t * bq, bq, 1)
    p1 = jnp.concatenate(
        [w_x, own_bc, w_dt, jnp.zeros((shard, 128 - bq - heads), BF)], axis=1
    )
    tail = tokens[:, own_len - 16 :, :].reshape(slots * 16, dim)
    def add_y(v, at):
        return jnp.stack([v, flip(v, "dp", 1)], axis=at)

    def add_x(v):
        return jnp.stack([v, flip(v, "tensor", 2)], axis=0)

    def blocks(v):
        return v.reshape(2, count, brow, v.shape[-1])

    def core(v):
        return flip(v, "tensor", 1)

    def middle(v):
        return lax.ppermute(v, "tensor", [(0, 0), (1, 2), (2, 1), (3, 3)])

    par, gain, bbc = call(
        k0_body,
        (1,),
        [
            full(v.shape)
            for v in (conv_x, bias_x, out_gain, dt_bias, a_log, skip_d, norm_gain, bias_bc)
        ],
        [full((16, cols)), full((1, dim)), full((1, 2 * state))],
        [sds((16, cols), F32), sds((1, dim), F32), sds((1, 2 * state), F32)],
        [pltpu.VMEM((8, 128), F32)],
        (1, 1),
        "parameters",
        vmem_mib=K5_MIB,
    )(sc, conv_x, bias_x, out_gain, dt_bias, a_log, skip_d, norm_gain, bias_bc)

    def prepare(halo):
        return call(
            prepare_body,
            (1,),
            [full((rows, dim)), full((64, dim)), full((rows, dim)), full((1, dim))],
            [full((rows + 64, dim)), full((dim, rows + 64)), full((rows, dim)), full((dim, rows))],
            [
                sds((rows + 64, dim), BF),
                sds((dim, rows + 64), BF),
                sds((rows, dim), BF),
                sds((dim, rows), BF),
            ],
            [],
            (1, 1),
            "prepare",
        )(sc, tok, halo, cot, gain)

    def grown(v, got, at):
        v = jnp.stack([v, got], axis=at)
        return v.reshape(v.shape[: at - 1] + (-1,) + v.shape[at + 1 :])

    if fast:
        v = p1[None]
        w2 = jnp.stack([w_z, w_out])[None]
        bit = dpcount // 2
        got = flip(v, "dp", bit)
        got, w2, sc, par, tail, gain = meet(got, w2, sc, par, tail, gain)
        v = grown(v, got, 1)
        while bit > 4:
            bit //= 2
            v = grown(v, flip(v, "dp", bit), 1)
            w2 = grown(w2, flip(w2, "dp", 2 * bit), 1)
        halo = lax.ppermute(tail, "tensor", [(a, (a + 1) % tcount) for a in range(tcount)])
        got, w2, parx, halo = meet(flip(v, "dp", 2), w2, flip(par, "tensor", 2), halo)
        par = jnp.stack([par, parx], axis=0)
        v = grown(v, got, 1)
        az, bz = v[..., :256], v[..., 256:]
        ax, by, parc, w2z = meet(
            flip(az, "tensor", 2), flip(bz, "dp", 1), core(par), flip(w2, "dp", 4)
        )
        w2 = grown(w2, w2z, 1)
        par = jnp.concatenate([par, parc], axis=-1)
        ax = jnp.stack([az, ax], axis=0)
        by = jnp.stack([bz, by], axis=1)
        nrm, nt, dbr, dt = prepare(halo)
        ay, bx, w2z, par, nrm = meet(
            flip(ax, "dp", 1), flip(by, "tensor", 2), flip(w2, "dp", 2), par, nrm
        )
        w2 = grown(w2, w2z, 1)
        wam = blocks(jnp.stack([ax, ay], axis=2))
        wbm = blocks(jnp.stack([by, bx], axis=0))
        zz, oz = w2[:, 0], w2[:, 1]
        zx, oy = flip(zz, "tensor", 2), flip(oz, "dp", 1)
        war, wbr = core(wam), core(wbm)
    else:
        halo = lax.ppermute(tail, "tensor", [(a, (a + 1) % tcount) for a in range(tcount)])
        par = add_x(par)
        par = jnp.concatenate([par, core(par)], axis=-1)
        z1 = lax.all_gather(p1, "dp", axis=0, tiled=True)[None]
        wam = add_x(z1[..., :256])
        wbm = add_x(z1[..., 256:])
        war, wbr = core(wam), core(wbm)
        nrm, nt, dbr, dt = prepare(halo)

    srows = slots * state
    wide = 2 * cols
    erows = rows + 64
    p1block = (1, count, brow, 256)
    wblock = (1, count, brow, cols)
    vmem = pltpu.VMEM

    def w_g(g, *a):
        return (g, 0, 0, 0)

    inx, blow, clow, bt, sin, dbc, cump, stepp, sigp, etp, reachp, decay, fac, uvp, mask, back, ct = call(
        k1_body,
        (2,),
        [full((erows, dim))]
        + [pl.BlockSpec(p1block, w_g)] * 4
        + [full((2, 16, wide)), full((4, 2 * state)), full((1, 2 * state))],
        [
            pl.BlockSpec((1, erows, wide), lambda g, sc: (g, 0, 0)),
            full((rows, state)),
            full((rows, state)),
            full((srows, L)),
            full((2, erows, state)),
            full((2, rows, state)),
        ]
        + [full((L, 128))] * 6
        + [full((8, 128)), full((L, 128)), full((L, 128)), full((L + 8, 128)), full((128, L))],
        [
            sds((2, erows, wide), BF),
            sds((rows, state), BF),
            sds((rows, state), BF),
            sds((srows, L), BF),
            sds((2, erows, state), F32),
            sds((2, rows, state), F32),
        ]
        + [sds((L, 128), F32)] * 6
        + [sds((8, 128), F32), sds((L, 128), F32), sds((L, 128), F32), sds((L + 8, 128), F32)]
        + [sds((128, L), F32)],
        [
            vmem((dim, wide), BF),
            vmem((dim, 256), BF),
            vmem((dim, 128), BF),
            vmem((erows, 256), F32),
            vmem((L + 8, 128), F32),
        ],
        (int(7e9), int(2e7)),
        "projections",
    )(sc, nrm, wam, war, wbm, wbr, par, conv_bc, bbc)

    def gs(g, s, sc):
        return (g, s, 0)

    def halo_gs(g, s, sc):
        return (g, rows // 16 + s, 0)

    def by_s(g, s, sc):
        return (s, 0)

    def mirror(g, sc):
        return (0, g ^ (sc[8] // 2))

    group = (1, L, wide)

    def gsel(g):
        return lambda s, sc: (g, s, 0)

    def conv_and_states(g, inx, kept):
        return call(
            functools.partial(k2_body, g),
            (slots,),
            [
                pl.BlockSpec(group, gsel(g)),
                pl.BlockSpec((1, 16, wide), lambda s, sc: (g, rows // 16 + s, 0)),
                pl.BlockSpec((1, 16, wide), lambda s, sc: (g, 0, 0)),
                pl.BlockSpec((state, L), lambda s, sc: (s, 0)),
                full((L, 128)),
                full((L, 128)),
                full((8, 128)),
                full((L, 128)),
            ]
            + anywhere(len(kept)),
            [pl.BlockSpec(group, gsel(g))] * 3
            + [pl.BlockSpec((srows + 16, wide), lambda s, sc: mirror(g, sc))],
            [sds((2, rows, wide), BF)] * 3 + [sds((srows + 16, 2 * wide), BF)],
            [
                vmem((L, wide), BF),
                vmem((6, L + 8, 128), F32),
                vmem((256, wide), BF),
                vmem((L, wide), F32),
                vmem((L, wide), F32),
            ],
            (int(5e9) if g else 1, int(2e7) if g else 1),
            "conv_and_states_%d" % g,
            {9 + n: n for n in range(len(kept))},
        )(sc, inx, inx, par, bt, stepp, etp, fac, mask, *kept)

    if fast:
        inx0, zx, oy = meet(inx, zx, oy)
        zx = jnp.stack([zz, zx], axis=0)
        oy = jnp.stack([oz, oy], axis=1)
        zy, ox = flip(zx, "dp", 1), flip(oy, "tensor", 2)
        xl, xs, dsl, st = conv_and_states(1, inx, conv_and_states(0, inx0, []))
        st, zy, ox = meet(st, zy, ox)
        wzm = blocks(jnp.stack([zx, zy], axis=2))
        wom = blocks(jnp.stack([oy, ox], axis=0))
        wzr, wor = core(wzm), core(wom)
    else:
        xl, xs, dsl, st = conv_and_states(1, inx, conv_and_states(0, inx, []))
        wzm = add_x(lax.all_gather(w_z, "dp", axis=0, tiled=True)[None])
        wom = add_x(lax.all_gather(w_out, "dp", axis=0, tiled=True)[None])
        wzr, wor = core(wzm), core(wom)

    def end_state(mine, one):
        f = mine[srows : srows + 4].astype(F32) + mine[srows + 4 : srows + 8].astype(F32)
        width = mine.shape[1]
        end = mine[:srows].astype(F32).reshape(slots, state, width) + f[:, None] * one[
            :srows
        ].astype(F32).reshape(slots, state, width)
        return end.astype(BF).reshape(srows, width)

    r1 = core(st)
    end = end_state(st, r1)
    r2 = middle(end)
    xs3, _ = meet(xs, end)

    def within_of(g, kept):
        return call(
            functools.partial(k3_body, g),
            (slots,),
            [
                pl.BlockSpec(group, gsel(g)),
                pl.BlockSpec((L, state), lambda s, sc: (s, 0)),
                pl.BlockSpec((L, state), lambda s, sc: (s, 0)),
                full((L, 128)),
                full((L, 128)),
                full((128, L)),
            ]
            + anywhere(len(kept)),
            pl.BlockSpec(group, gsel(g)),
            sds((2, rows, wide), F32),
            [
                vmem((2, 128, 128), F32),
                vmem((128, 128), BF),
                vmem((256, wide), BF),
                vmem((L, wide), F32),
                vmem((256, 2 * wide), BF),
                vmem((L, 2 * wide), F32),
            ],
            (int(5e9), int(1e7)),
            "within_%d" % g,
            {7 + n: n for n in range(len(kept))},
        )(sc, xs3, blow, clow, cump, uvp, ct, *kept)

    within = within_of(1, [within_of(0, [])])
    nrm4, within = meet(nrm, within)

    gate, dgn = call(
        k4_body,
        (2, 3),
        [full((erows, dim)), full((rows, dim))] + [pl.BlockSpec(wblock, w_g)] * 4,
        [pl.BlockSpec((1, rows, 256), lambda g, n, sc: (g, 0, n))] * 2,
        [sds((2, rows, wide), BF)] * 2,
        [vmem((dim, wide), BF), vmem((dim, wide), BF)],
        (int(5e9), int(2e7)),
        "gate_and_out_backward",
    )(sc, nrm4, dbr, wzm, wzr, wom, wor)

    gate, r2 = meet(gate, r2)
    r3 = core(r2)

    def p_gs(phase):
        def index(p, g, s, sc):
            return (
                jnp.where(p == phase, g, 0 if phase else 1),
                jnp.where(p == phase, s, 0 if phase else slots - 1),
                0,
            )

        return index

    def p_mirror(phase):
        def index(p, g, s, sc):
            return mirror(jnp.where(p == phase, g, 0 if phase else 1), sc)

        return index

    def pgs(p, g, s, sc):
        return (g, s, 0)

    def p_w(p, g, s, sc):
        return (jnp.where(p == 1, g, 0), 0, 0, 0)

    out, gn, dg, dy, dp, prev, rowsum, dc5, small5 = call(
        k5_body,
        (2, 2, slots),
        [
            pl.BlockSpec(group, p_gs(0)),
            pl.BlockSpec(group, pgs),
            pl.BlockSpec(group, pgs),
            pl.BlockSpec(group, pgs),
            pl.BlockSpec((srows + 16, wide), p_mirror(0)),
            pl.BlockSpec((srows, wide), p_mirror(0)),
            pl.BlockSpec((srows, wide), p_mirror(0)),
            full((L, 128)),
            full((8, 128)),
            pl.BlockSpec((L, state), lambda p, g, s, sc: (s, 0)),
            pl.BlockSpec((1, 16, wide), lambda p, g, s, sc: (g, 0, 0)),
            pl.BlockSpec(wblock, p_w),
            pl.BlockSpec(wblock, p_w),
            full((rows, dim)),
        ],
        [
            full((rows, dim)),
            pl.BlockSpec(group, p_gs(1)),
            pl.BlockSpec(group, p_gs(1)),
            pl.BlockSpec(group, p_gs(1)),
            pl.BlockSpec((srows + 16, wide), p_mirror(1)),
            full((2, srows, wide)),
            full((L, 128)),
            full((rows, state)),
            full((2, 8, wide)),
        ],
        [
            sds((rows, dim), BF),
            sds((2, rows, wide), BF),
            sds((2, rows, wide), BF),
            sds((2, rows, wide), BF),
            sds((srows + 16, 2 * wide), BF),
            sds((2, srows, wide), BF),
            sds((L, 128), F32),
            sds((rows, state), F32),
            sds((2, 8, wide), F32),
        ],
        [
            vmem((2, rows, wide), F32),
            vmem((2, rows, 128), F32),
            vmem((rows, dim), F32),
            vmem((dim, wide), BF),
            vmem((rows, wide), BF),
            vmem((16, cols), F32),
            vmem((L, wide), BF),
            vmem((L, wide), BF),
            vmem((L, wide), BF),
            vmem((wide, 128), BF),
            vmem((state, wide), BF),
            vmem((256, wide), BF),
            vmem((L, wide), F32),
        ],
        (int(1.5e10), int(4e7)),
        "gated_norm",
        vmem_mib=50,
    )(sc, within, gate, dgn, xl, r1, r2, r3, reachp, fac, clow, par, wom, wor, tok)

    q1 = core(dp)

    gshape = (2, count, brow, cols)
    ok, osend, zk, zsend, ngz = call(
        k6_body,
        (2,),
        [full((dim, erows)), full((dim, rows))]
        + [pl.BlockSpec((1, rows, wide), lambda g, sc: (g, 0, 0))] * 2
        + [pl.BlockSpec(wblock, w_g)] * 2,
        [pl.BlockSpec((1,) + gshape[1:], w_g)] * 4 + [full((dim, 128))],
        [sds(gshape, BF)] * 4 + [sds((dim, 128), F32)],
        [vmem((dim, wide), F32), vmem((dim, wide), BF)],
        (int(5e9), int(2e7)),
        "outer_weight_grads",
        vmem_mib=K5_MIB,
    )(sc, nt, dt, gn, dg, wzm, wzr)

    osend, q1 = meet(osend, q1)
    dy1, end = meet(dy, end_state(dp, q1))
    q2 = middle(end)

    def summed(a, b):
        return (a.astype(F32) + b.astype(F32)).astype(BF)

    def reduce_step(v, axis, mesh_axis, bit):
        keep = lax.index_in_dim(v, 0, axis, False)
        send = lax.index_in_dim(v, 1, axis, False)
        return summed(keep, flip(send, mesh_axis, bit))

    def reduce_x(v, axis):
        return reduce_step(v, axis, "tensor", 2)

    def reduce_dp(v, bit):
        v = v.reshape((v.shape[0] // 2, 2) + v.shape[1:])
        return reduce_step(v, 1, "dp", bit)

    def finish(v, bit):
        while bit < dpcount:
            v = reduce_dp(v, bit)
            bit *= 2
        return v[0].astype(F32)

    def reduce_slow(v):
        v = v.reshape(dpcount, shard, v.shape[-1])
        got = lax.all_to_all(v, "dp", split_axis=0, concat_axis=0, tiled=True)
        return got.astype(F32).sum(axis=0)

    def reduce_core(keep, send):
        return summed(keep, core(send))

    if fast:
        vw = summed(jnp.stack([ok, zk]), jnp.stack([core(osend), core(zsend)]))
        vw = vw.reshape((2, 2, count // 2, 2, brow, cols))
        vwr = flip(vw[:, :, :, 1], "dp", 1)
    else:
        grad_w_out = reduce_slow(reduce_x(reduce_core(ok, osend), 0)[0])
        grad_w_z = reduce_slow(reduce_x(reduce_core(zk, zsend), 0)[0])

    def within_backward(g, dy, kept):
        return call(
            functools.partial(k7_body, g),
            (slots,),
            [
                pl.BlockSpec(group, gsel(g)),
                pl.BlockSpec(group, gsel(g)),
                pl.BlockSpec((L, state), lambda s, sc: (s, 0)),
                pl.BlockSpec((L, state), lambda s, sc: (s, 0)),
                full((L, 128)),
                full((L, 128)),
                full((128, L)),
            ]
            + anywhere(len(kept)),
            [
                pl.BlockSpec(group, gsel(g)),
                pl.BlockSpec((2, L, state), lambda s, sc: (0, s, 0)),
                full((L, 128)),
            ],
            [sds((2, rows, wide), F32), sds((2, rows, state), F32), sds((L, 128), F32)],
            [
                vmem((2, 128, 128), F32),
                vmem((128, 128), BF),
                vmem((128, wide), BF),
                vmem((128, wide), BF),
                vmem((256, wide), BF),
                vmem((L, wide), F32),
                vmem((256, 2 * wide), BF),
                vmem((L, 2 * wide), F32),
                vmem((wide, 128), BF),
                vmem((L, wide), BF),
            ],
            (int(1e10) if g else 1, int(2e7) if g else 1),
            "within_backward_%d" % g,
            {8 + n: n for n in range(len(kept))},
        )(sc, xs, dy, blow, clow, cump, uvp, ct, *kept)

    dxw, bc7a, corr_a = within_backward(1, dy1, [])
    dxw, bc7b, corr_b = within_backward(0, dy, [dxw])

    def states_backward(g, last, nt, extra_in, extra_specs):
        width = cols + 256 if last else cols
        gshape = (count, brow, width)

        def at(s, sc):
            return (g, s, 0)

        in_specs = [
            full((dim, erows)),
            pl.BlockSpec(group, at),
            pl.BlockSpec(group, at),
            pl.BlockSpec(group, at),
            pl.BlockSpec(group, at),
            pl.BlockSpec((1, 16, wide), lambda s, sc: (g, rows // 16 + s, 0)),
            pl.BlockSpec(group, at),
            pl.BlockSpec((srows + 16, wide), lambda s, sc: mirror(g, sc)),
            pl.BlockSpec((srows, wide), lambda s, sc: mirror(g, sc)),
            pl.BlockSpec((srows, wide), lambda s, sc: mirror(g, sc)),
            pl.BlockSpec((1, srows, wide), lambda s, sc: (g, 0, 0)),
            pl.BlockSpec((L, state), lambda s, sc: (s, 0)),
            full((L, 128)),
            full((L, 128)),
            full((L + 8, 128)),
            full((2, 16, wide)) if last else pl.BlockSpec((1, 16, wide), lambda s, sc: (g, 0, 0)),
            pl.BlockSpec(p1block, lambda s, sc: (g, 0, 0, 0)),
            pl.BlockSpec(p1block, lambda s, sc: (g, 0, 0, 0)),
        ]
        if last:
            in_specs += [full((2,) + p1block[1:])] * 2
        else:
            in_specs += [pl.BlockSpec(p1block, lambda s, sc: (g, 0, 0, 0))] * 2
        in_specs += extra_specs
        outs = [
            (gshape, BF),
            (gshape, BF),
            ((erows, wide), BF),
            ((L, 128), F32),
            ((8, 128), F32),
            ((rows, state), F32),
            ((8, wide), F32),
            ((dim, 128), F32),
        ]
        scratch = [
            vmem((dim, wide), F32),
            vmem((dim, 256), F32),
            vmem((state, wide), F32),
            vmem((16, cols), F32),
            vmem((state, wide), BF),
            vmem((L, wide), BF),
            vmem((L, wide), BF),
            vmem((L, wide), BF),
            vmem((wide, 128), BF),
            vmem((dim, wide), BF),
        ]
        if last:
            outs += [((erows, 512), BF), ((32, cols), F32), ((40, cols), F32)]
            scratch += [
                vmem((dim, 512), BF),
                vmem((2, erows, state), F32),
                vmem((4, dim, 128), F32),
                vmem((brow, 128), F32),
                vmem((2, 8, state), F32),
                vmem((2, 16, wide), F32),
            ]
        scratch += [vmem((L, wide), F32), vmem((6, L + 16, 128), F32), vmem((256, wide), BF)]
        scratch += [vmem((L, wide), F32), vmem((L, wide), F32)]
        return call(
            functools.partial(k8_body, g, last),
            (slots,),
            in_specs,
            [full(shape) for shape, _ in outs],
            [sds(shape, dtype) for shape, dtype in outs],
            scratch,
            (int(1e10), int(2e7)),
            "states_backward_%d" % g,
        )(sc, nt, xs, dy, dsl, inx, inx, dxw, q1, q2, q3, prev, blow, stepp, etp, back, par, wam, war, wbm, wbr, *extra_in)

    def normed_grad_z(g, dg):
        return call(
            k9z_body,
            (1,),
            [
                pl.BlockSpec((1, rows, wide), lambda i, sc: (g, 0, 0)),
                pl.BlockSpec(wblock, lambda i, sc: (g, 0, 0, 0)),
                pl.BlockSpec(wblock, lambda i, sc: (g, 0, 0, 0)),
            ],
            full((rows, dim)),
            sds((rows, dim), F32),
            [vmem((dim, wide), BF)],
            (1, 1),
            "normed_grad_z%d" % g,
        )(sc, dg, wzm, wzr)

    dga, dxw = meet(dg, dxw)
    dna = normed_grad_z(1, dga)
    if fast:
        dxw, q2, dna, vwr = meet(dxw, q2, dna, vwr)
        vw = summed(vw[:, :, :, 0], vwr)
        vwr = flip(vw[:, 1], "tensor", 2)
    else:
        dxw, q2, dna = meet(dxw, q2, dna)
    q3 = core(q2)
    ka, sa, din1, seg1, end1, dba1, small1, nga = states_backward(1, False, nt, [], [])
    if fast:
        sa, vwr = meet(sa, vwr)
        vw = summed(vw[:, 0], vwr).reshape((2, count // 4, 2, brow, cols))
        vwr = flip(vw[:, :, 1], "dp", 2)
    sar = core(sa)
    dgb, _ = meet(dg, sa)
    dnb = normed_grad_z(0, dgb)
    nt0, sar, dnb = meet(nt, sar, dnb)
    va = summed(ka, sar)
    xa = flip(va, "tensor", 2)
    ks, ss, din0, _, _, _, _, _, din5, skeep, ssend = states_backward(
        0,
        True,
        nt0,
        [fac, sigp, decay, gain, ngz, nga, conv_bc, small1, small5, bc7a, bc7b, corr_a, corr_b, dc5, rowsum, sin, dbc, seg1, end1, dba1],
        [
            full((8, 128)),
            full((L, 128)),
            full((L, 128)),
            full((1, dim)),
            full((dim, 128)),
            full((dim, 128)),
            full((4, 2 * state)),
            full((8, wide)),
            full((2, 8, wide)),
            full((2, rows, state)),
            full((2, rows, state)),
            full((L, 128)),
            full((L, 128)),
            full((rows, state)),
            full((L, 128)),
            full((2, erows, state)),
            full((2, rows, state)),
            full((L, 128)),
            full((8, 128)),
            full((rows, state)),
        ],
    )

    if fast:
        ss, xa, vwr = meet(ss, xa, vwr)
        vw = summed(vw[:, :, 0], vwr).reshape((2, count // 8, 2, brow, cols))
        vwr = flip(vw[:, :, 1], "dp", 4)
    din0, ssr, got = meet(din0, core(ss), core(ssend))
    own = (skeep + got[:32]).reshape(2, 16, cols)
    flat = ssend[32:] + got[32:]
    vb = summed(ks[..., cols:], ssr[..., cols:])
    px = flip(vb[..., 128:], "tensor", 2)
    vx = (ks[..., :cols].astype(F32) + ssr[..., :cols].astype(F32) + xa.astype(F32)).astype(BF)
    if fast:
        vx = vx.reshape((count // 2, 2) + vx.shape[1:])
        vxr = flip(vx[:, 1], "dp", 1)
    both = jnp.concatenate([own[0], flat], axis=0)
    got = flip(jnp.concatenate([own[1], flat], axis=0), "tensor", 2)

    dn = call(
        k9_body,
        (2,),
        [
            full((erows, wide)),
            full((erows, wide)),
            pl.BlockSpec((erows, 256), lambda g, sc: (0, g)),
            full((rows, dim)),
            full((rows, dim)),
        ]
        + [pl.BlockSpec(p1block, w_g)] * 4,
        full((erows, dim)),
        sds((erows, dim), F32),
        [vmem((dim, wide), BF), vmem((dim, 256), BF)],
        (int(6e9), int(2e7)),
        "normed_grad",
    )(sc, din0, din1, din5, dna, dnb, wam, war, wbm, wbr)

    if fast:
        dn, px, vxr, got, vwr = meet(dn, px, vxr, got, vwr)
        vw = summed(vw[:, :, 0], vwr)
        grad_w_out, grad_w_z = finish(vw[0], 8), finish(vw[1], 8)
        vx = summed(vx[:, 0], vxr)
        vp = summed(vb[..., :128], px)
        vp = vp.reshape((count // 2, 2) + vp.shape[1:])
        vpr = flip(vp[:, 1], "dp", 1)
        both = both + got
        got = flip(both, "dp", 1)
    hr = lax.ppermute(dn[rows:].astype(BF), "tensor", [((a + 1) % tcount, a) for a in range(tcount)])
    if fast:
        hr, vpr, got = meet(hr, vpr, got)
        v1 = jnp.concatenate([vx, summed(vp[:, 0], vpr)], axis=-1)
        v1 = v1.reshape((count // 4, 2) + v1.shape[1:])
        v1r = flip(v1[:, 1], "dp", 2)
        both = both + got
        got = flip(both, "dp", 2)

    ig = call(
        k10_body,
        (slots,),
        [
            pl.BlockSpec((L, dim), lambda s, sc: (s, 0)),
            pl.BlockSpec((16, dim), lambda s, sc: (s, 0)),
            pl.BlockSpec((L, dim), lambda s, sc: (s, 0)),
            pl.BlockSpec((L, dim), lambda s, sc: (s, 0)),
            full((1, dim)),
        ],
        pl.BlockSpec((L, dim), lambda s, sc: (s, 0)),
        sds((rows, dim), BF),
        [],
        (int(1e9), int(1e7)),
        "input_grad",
    )(sc, dn, hr, tok, cot, gain)

    if fast:
        ig, v1r, got = meet(ig, v1r, got)
        v1 = summed(v1[:, 0], v1r)
        both = both + got
        bit = 4
        while 2 * bit < dpcount:
            both = both + flip(both, "dp", bit)
            v1 = reduce_dp(v1, bit)
            bit *= 2
        got = flip(both, "dp", bit)
        v1 = v1.reshape((2,) + v1.shape[1:]) if v1.shape[0] == 2 else v1
        v1a, v1r = v1[0], flip(v1[1], "dp", bit)
    else:
        both = lax.psum(both + got, "dp")
        v1 = jnp.concatenate([vx, summed(vb[..., :128], px)], axis=-1)
        grad1 = reduce_slow(v1)
    if fast:
        last = call(
            k11_body,
            (1,),
            [full((shard, 512))] * 2 + [full((24, cols))] * 2,
            [full(shape) for shape in FINAL_SHAPES(dim, cols, heads, state, shard, tcount)],
            [
                sds(shape, F32)
                for shape in FINAL_SHAPES(dim, cols, heads, state, shard, tcount)
            ],
            [vmem((shard, 512), F32), vmem((24, cols), F32)],
            (int(1e6), int(1e6)),
            "last_sums",
        )(sc, v1a, v1r, both, got)
        (
            ngain, grad_w_x, grad_w_bc, grad_w_dt, grad_conv_x, grad_bias_x, grad_conv_bc,
            grad_bias_bc, grad_dt_bias, grad_a_log, grad_skip, grad_out_gain,
        ) = last
        grad_w_dt = grad_w_dt.T
    else:
        own, flat = both[:16], both[16:]
        ngain = flat[5:7].reshape(dim)
        grad_w_x = grad1[:, :cols]
        parts = grad1[:, cols : cols + bq].reshape(tcount, shard // tcount, bq)
        got = lax.all_to_all(parts, "tensor", split_axis=0, concat_axis=0, tiled=True)
        grad_w_bc = jnp.swapaxes(got, 0, 1).reshape(shard // tcount, bq * tcount)
        grad_w_dt = grad1[:, cols + bq : cols + bq + heads]
        grad_conv_x, grad_bias_x, grad_out_gain = own[:4], own[4], own[5]
        grad_conv_bc, grad_bias_bc = flat[:4, : 2 * state], flat[4, : 2 * state]
        grad_dt_bias, grad_a_log = own[7, :heads], own[8, :heads]
        grad_skip = own[6].reshape(heads, cols // heads).sum(axis=1)

    return (
        out.reshape(tokens.shape),
        ig.reshape(tokens.shape),
        ngain,
        grad_w_z,
        grad_w_x,
        grad_w_bc,
        grad_w_dt,
        grad_conv_x,
        grad_bias_x,
        grad_conv_bc,
        grad_bias_bc,
        grad_dt_bias,
        grad_a_log,
        grad_skip,
        grad_out_gain,
        grad_w_out,
    )


def solution(mesh):
    return jax.shard_map(
        per_device,
        mesh=mesh,
        in_specs=(
            P("dp", "tensor", None), P("dp", None), P("dp", "tensor", None), P(),
            P("dp", "tensor"), P("dp", "tensor"), P("dp", None), P("dp", "tensor"),
            P(None, "tensor"), P("tensor"), P(), P(),
            P("tensor"), P("tensor"), P("tensor"), P("tensor"), P("dp", "tensor"),
        ),
        out_specs=(
            P("dp", "tensor", None), P("dp", "tensor", None), P(),
            P("dp", "tensor"), P("dp", "tensor"), P(("dp", "tensor"), None), P("dp", "tensor"),
            P(None, "tensor"), P("tensor"), P(), P(),
            P("tensor"), P("tensor"), P("tensor"), P("tensor"), P("dp", "tensor"),
        ),
        check_vma=False,
    )
```

```python
import functools

import jax
import jax.numpy as jnp
from jax import lax
from jax.experimental import pallas as pl
from jax.experimental.pallas import tpu as pltpu
from jax.sharding import PartitionSpec as P

INNER = 1536
L = 256
HD = 64
SPAN = 32
EPS = 1e-05
LOG2E = 1.4426950408889634
F32 = jnp.float32
BF = jnp.bfloat16
CHUNK = 64
WIDE = 768
VMEM_MIB = 40
K5_MIB = 58


def dot(a, b):
    return jnp.dot(a, b, preferred_element_type=F32)


def dot_nt(a, b):
    return lax.dot_general(a, b, (((1,), (1,)), ((), ())), preferred_element_type=F32)


def dot_high(a, b):
    return jnp.dot(a, b, preferred_element_type=F32, precision=lax.Precision.HIGHEST)


def sigmoid(v):
    return 0.5 * jnp.tanh(0.5 * v) + 0.5


def lane_iota(rows):
    return lax.broadcasted_iota(jnp.int32, (rows, 128), 1)


def row_iota(rows, lanes):
    return lax.broadcasted_iota(jnp.int32, (rows, lanes), 0)


def seg_of(idx, fe, se):
    return (idx >= fe).astype(jnp.int32) + (idx >= se).astype(jnp.int32)


def ends(sc, s):
    return sc[2 * s], sc[2 * s + 1]


def pair_cols(cols, first):
    lane = lane_iota(cols.shape[0])
    left = jnp.broadcast_to(cols[:, first : first + 1], cols.shape)
    right = jnp.broadcast_to(cols[:, first + 1 : first + 2], cols.shape)
    return jnp.where(lane < HD, left, right)


def head_pick():
    r = lax.broadcasted_iota(jnp.int32, (WIDE, 128), 0)
    c = lax.broadcasted_iota(jnp.int32, (WIDE, 128), 1)
    return jnp.where(c == r // HD, 1.0, 0.0)


def head_spread():
    r = lax.broadcasted_iota(jnp.int32, (256, WIDE), 0)
    c = lax.broadcasted_iota(jnp.int32, (256, WIDE), 1)
    return jnp.where(r % 128 == c // HD, 1.0, 0.0).astype(BF)


def expand(dst, cols, spread):
    high = cols.astype(BF)
    low = (cols - high.astype(F32)).astype(BF)
    both = jnp.concatenate([high, low], axis=1)
    for n in range(3):
        dst[:, 256 * n : 256 * n + 256] = dot(both, spread[:, 256 * n : 256 * n + 256])


def three_terms(v):
    high = v.astype(BF).astype(F32)
    mid = (v - high).astype(BF).astype(F32)
    return high, mid, v - high - mid


def tile_spread():
    r = lax.broadcasted_iota(jnp.int32, (256, 2 * WIDE), 0)
    h = lax.broadcasted_iota(jnp.int32, (256, 2 * WIDE), 1) // 128
    return jnp.where((r == h) | (r == h + 128) | (r == h + 144), 1.0, 0.0).astype(BF)


def expand_tiles(dst, cols, spread):
    high, mid, low = three_terms(cols)
    lane = lane_iota(L)
    rest = jnp.where(lane < 16, mid, pltpu.roll(low, 16, 1))
    left = jnp.concatenate([high, rest], axis=1).astype(BF)
    for n in range(6):
        dst[:, 256 * n : 256 * n + 256] = dot(left, spread[:, 256 * n : 256 * n + 256])


def to_lane0(packed, s, g):
    return pltpu.roll(packed, (256 - s * SPAN - g * 12) % 128, 1)


def from_lane0(cols, s, g):
    return pltpu.roll(cols, s * SPAN + g * 12, 1)


def rows_of(s, length=L):
    return pl.ds(pl.multiple_of(s * length, length), length)


def tile(j):
    return slice(128 * j, 128 * j + 128)


def conv_forward(ext, taps, bias, masks, first=0, length=L):
    acc = bias + taps[0] * ext[8 + first : 8 + first + length]
    for k in range(1, 4):
        acc = acc + (taps[k] * ext[8 + first - k : 8 + first - k + length]) * masks[k - 1]
    return acc


def conv_backward(ext, v_ext, taps, masks):
    out, tap_grads = None, []
    for k in range(4):
        part = ext[k : 264 + k]
        if k:
            part = part * masks[k - 1]
        tap_grads.append(jnp.sum(part * v_ext, axis=0, keepdims=True))
        out = taps[k] * part if out is None else out + taps[k] * part
    return out, tap_grads


def slot_masks(packed, s):
    cols = pltpu.roll(packed[...], (128 - 4 * s) % 128, 1)
    return [jnp.broadcast_to(cols[:, k : k + 1], cols.shape) for k in (1, 2, 3)]


def place_rows(dst, blocks, me, at, first=0, width=None, lead=0):
    count, rows = blocks.shape[1:3]
    width = blocks.shape[3] - first if width is None else width
    for n in range(count):
        start = pl.multiple_of((n ^ me) * rows, rows) if count > 1 else 0
        dst[pl.ds(start, rows), at : at + width] = blocks[lead, n, :, first : first + width]


def place_pair(dst, mine, other, me):
    place_rows(dst, mine, me, 0)
    place_rows(dst, other, me, 384)


def place_p1(dst, am, bm, ar, br, me, pieces):
    place_rows(dst, am, me, 0)
    place_rows(dst, bm, me, 256, 0, 128)
    place_rows(dst, ar, me, 384)
    place_rows(dst, br, me, 640, 0, 128)
    place_rows(pieces, bm, me, 0, 128, 128)
    place_rows(pieces, br, me, 128, 128, 128)


def half_at(c, me_t):
    return pl.ds(pl.multiple_of(384 * (c ^ (me_t % 2)), 128), 384)


def k0_body(sc, conv_x, bias_x, out_gain, dt_bias, a_log, skip_d, norm_gain, bias_bc, par, gain, bbc, row):
    par[...] = jnp.zeros_like(par)
    par[0:4] = conv_x[...]
    par[4] = bias_x[...]
    par[5] = out_gain[...]
    par[6, : dt_bias.shape[0]] = dt_bias[...]
    par[7, : a_log.shape[0]] = a_log[...]
    row[...] = jnp.zeros_like(row)
    row[0, : skip_d.shape[0]] = skip_d[...]
    r = lax.broadcasted_iota(jnp.int32, (128, 384), 0)
    c = lax.broadcasted_iota(jnp.int32, (128, 384), 1)
    par[8:9] = dot_high(row[...], jnp.where(r == c // HD, 1.0, 0.0))[0:1]
    gain[0] = norm_gain[...]
    bbc[0] = bias_bc[...]


def prepare_body(sc, tok, halo, cot, gain, nrm, nt, dbr, dt):
    def norm(v):
        v = v.astype(F32)
        r = lax.rsqrt(jnp.mean(v * v, axis=-1, keepdims=True) + EPS)
        return (v * r * gain[...]).astype(BF)

    @pl.loop(0, 16)
    def _(n):
        r = rows_of(n, 64)
        nrm[r] = norm(tok[r])
        keep = row_iota(64, 1) + 64 * (n % 4) < sc[2 * (n // 4) + 1]
        dbr[r] = jnp.where(keep, cot[r].astype(F32), 0.0).astype(BF)

    nrm[4 * L :] = jnp.where(sc[8] > 0, norm(halo[...]).astype(F32), 0.0).astype(BF)

    @pl.loop(0, 4)
    def _(s):
        nt[:, rows_of(s)] = nrm[rows_of(s)].T
        dt[:, rows_of(s)] = dbr[rows_of(s)].T

    nt[:, 4 * L :] = nrm[4 * L :].T


def k1_body(
    sc, nrm, am, ar, bm, br, par, cbc, bbc,
    inx, blow, clow, bto, sin, dbc,
    cumo, stepo, sigo, eto, reacho, decayo, faco, uvo, masko, backo, ct,
    wbuf, wbc, wdt, pcs, ext,
):
    g = pl.program_id(0)
    me_t, me_dp = sc[8], sc[9]

    @pl.when(g == 0)
    def _():
        wbc[...] = jnp.zeros_like(wbc)
        wdt[...] = jnp.zeros_like(wdt)

    place_rows(wbuf, am, me_dp, 0)
    place_rows(wbuf, bm, me_dp, 256, 0, 128)
    place_rows(wbuf, ar, me_dp, 384)
    place_rows(wbuf, br, me_dp, 640, 0, 128)
    count, brow = bm.shape[1:3]
    for c, blocks in ((0, bm), (1, br)):
        i = 2 * g + c
        t = i ^ me_t
        at = pl.ds(pl.multiple_of(128 * (t // 2), 128), 128)
        for n in range(count):
            start = pl.multiple_of((n ^ me_dp) * brow, brow) if count > 1 else 0
            r = pl.ds(start, brow)
            piece = blocks[0, n, :, 128:].astype(F32)
            lane = lane_iota(brow)
            own = pltpu.roll(jnp.where(lane < 64, piece, 0.0), 64 * (t % 2), 1)
            wbc[r, at] += own.astype(BF)
            own = pltpu.roll(jnp.where(lane >= 64, piece, 0.0), (i * 6 + 64) % 128, 1)
            wdt[r] += own.astype(BF)
    for n in range(3):
        cols = slice(256 * n, 256 * n + 256)
        inx[0, :, cols] = dot(nrm[...], wbuf[:, cols]).astype(BF)

    @pl.when(g == 1)
    def _():
        pcs[...] = dot(nrm[...], wbc[...])
        sin[0] = pcs[:, :128]
        sin[1] = pcs[:, 128:]
        pcs[0 : 4 * L, 0:128] = dot(nrm[0 : 4 * L], wdt[...])
        dtacc = pcs[0:L, 0:128]
        for s in range(1, 4):
            dtacc = dtacc + pltpu.roll(pcs[L * s : L * s + L, 0:128], s * SPAN, 1)
        dtb = jnp.zeros((1, 128), F32)
        alog = jnp.zeros((1, 128), F32)
        for i in range(4):
            for s in range(4):
                at = slice(384 * (i % 2), 384 * (i % 2) + 128)
                dtb += pltpu.roll(par[i // 2, 6:7, at], s * SPAN + i * 6, 1)
                alog += pltpu.roll(par[i // 2, 7:8, at], s * SPAN + i * 6, 1)
        raw = dtacc + dtb
        step = jnp.maximum(raw, 0.0) + jnp.log1p(jnp.exp(-jnp.abs(raw)))
        sig = 1.0 / (1.0 + jnp.exp(-raw))
        decay = step * -jnp.exp(alog)
        lower = jnp.where(
            lax.broadcasted_iota(jnp.int32, (L, L), 0) >= lax.broadcasted_iota(jnp.int32, (L, L), 1),
            1.0,
            0.0,
        )
        cum = dot_high(lower, decay)
        row = row_iota(L, 128)
        lane = lane_iota(L)
        slot = lane // SPAN
        tail = jnp.zeros((L, 128), F32)
        enters = jnp.zeros((L, 128), F32)
        follows = jnp.zeros((8, 128), F32)
        masks = jnp.ones((L, 128), F32)
        row_b = row_iota(L + 8, 128) - 8
        lane_b = lane_iota(L + 8)
        back_masks = jnp.ones((L + 8, 128), F32)
        slot8 = lane_iota(8) // SPAN
        inner_block = jnp.where(me_t > 0, 1.0, 0.0)
        back = lane % 4
        for s in range(4):
            fe, se = ends(sc, s)
            seg = seg_of(row, fe, se)
            last = seg_of(L - 1, fe, se)
            before = seg_of(-1, fe, se)
            here = slot == s
            tail = jnp.where(here & (seg == last), 1.0, tail)
            enters = jnp.where(here & (seg == before), inner_block, enters)
            follows = jnp.where(
                (slot8 == s), jnp.where(last == before, inner_block, 0.0), follows
            )
            masks = jnp.where((lane // 4 == s) & (seg != seg_of(row - back, fe, se)), 0.0, masks)
            cut = seg_of(row_b, fe, se) != seg_of(row_b + lane_b % 4, fe, se)
            back_masks = jnp.where((lane_b // 4 == s) & cut, 0.0, back_masks)
        cum_last = cum[L - 1 : L]
        cum2 = cum * LOG2E
        cumo[...] = cum2
        stepo[...] = step
        sigo[...] = sig
        eto[...] = jnp.exp(cum_last - cum) * tail
        reacho[...] = jnp.exp(cum) * enters
        decayo[...] = decay
        faco[...] = jnp.exp(cum_last) * follows
        uvo[...] = jnp.exp2(-jnp.abs(cum2 - cum2[127:128]))
        masko[...] = masks
        backo[...] = back_masks
        ct[...] = cum2.T
        for q, low_out in ((0, blow), (1, clow)):
            taps = [cbc[k : k + 1, tile(q)] for k in range(4)]

            @pl.loop(0, 4)
            def _(s):
                ext[0:8] = sin[q, pl.ds(pl.multiple_of(4 * L + 16 * s + 8, 8), 8)]
                ext[8:] = sin[q, rows_of(s)]
                acc = conv_forward(ext, taps, bbc[:, tile(q)], slot_masks(masko, s))
                sg = sigmoid(acc)
                low = acc * sg
                low_out[rows_of(s)] = low.astype(BF)
                dbc[q, rows_of(s)] = sg + low * (1.0 - sg)
                if q == 0:
                    bto[rows_of(s, 128)] = low.T.astype(BF)


def factor_rows(fac, g):
    rows = []
    for s in range(4):
        f = to_lane0(fac[...], s, g)
        rows.append(jnp.concatenate([pair_cols(f, 2 * j)[0:1] for j in range(6)], axis=1))
    f = jnp.concatenate(rows, axis=0)
    high = f.astype(BF).astype(F32)
    return jnp.concatenate([high, f - high, jnp.zeros((8, WIDE), F32)], axis=0).astype(BF)


def k2_body(g, sc, inx, halo, par, bt, stepp, etp, fac, mask, *rest):
    xo, xso, dslo, sto, xe, ext, spread, stepx, stepe = rest[-9:]
    s = pl.program_id(0)
    me_t = sc[8]

    @pl.when(s == 0)
    def _():
        spread[...] = head_spread()

    masks = slot_masks(mask, s)
    step = to_lane0(stepp[...], s, g)
    expand(stepx, step, spread)
    expand(stepe, step * to_lane0(etp[...], s, g), spread)
    for j in range(6):
        ext[j, 0:8] = halo[0, :, tile(j)].astype(F32)[8:]
        ext[j, 8:] = inx[0, :, tile(j)].astype(F32)
    for n in range(L // CHUNK):
        r = slice(CHUNK * n, CHUNK * n + CHUNK)
        mr = [m[r] for m in masks]
        for j in range(6):
            taps = [0.5 * par[0, k : k + 1, tile(j)] for k in range(4)]
            half = conv_forward(ext.at[j], taps, 0.5 * par[0, 4:5, tile(j)], mr, CHUNK * n, CHUNK)
            th = jnp.tanh(half)
            up = 1.0 + th
            act = half * up
            xo[0, r, tile(j)] = act.astype(BF)
            dslo[0, r, tile(j)] = ((0.5 * up) * (1.0 + half * (1.0 - th))).astype(BF)
            xso[0, r, tile(j)] = (act * stepx[r, tile(j)]).astype(BF)
            xe[r, tile(j)] = (act * stepe[r, tile(j)]).astype(BF)
    for c in range(2):
        sto[rows_of(s, 128), half_at(c, me_t)] = dot(
            bt[...], xe[:, 384 * c : 384 * c + 384]
        ).astype(BF)

    @pl.when(s == 3)
    def _():
        f = factor_rows(fac, g)
        for c in range(2):
            sto[512:528, half_at(c, me_t)] = f[:, 384 * c : 384 * c + 384]


def by_head(pair):
    lane = lane_iota(128)
    zero = jnp.zeros_like(pair)
    return jnp.concatenate(
        [jnp.where(lane < HD, pair, zero), jnp.where(lane < HD, zero, pair)], axis=0
    )


def diag_mask(d, fe, se, key_rows):
    r = lax.broadcasted_iota(jnp.int32, (128, 128), 0) + 128 * d
    c = lax.broadcasted_iota(jnp.int32, (128, 128), 1) + 128 * d
    order = (c >= r) if key_rows else (r >= c)
    return order & (seg_of(r, fe, se) == seg_of(c, fe, se))


def cross_half(fe, se, key_rows):
    r = lax.broadcasted_iota(jnp.int32, (128, 128), 0) + (0 if key_rows else 128)
    c = lax.broadcasted_iota(jnp.int32, (128, 128), 1) + (128 if key_rows else 0)
    return seg_of(r, fe, se) == seg_of(c, fe, se)


def k3_body(g, sc, xs, blow, clow, cump, uvp, ct, *rest):
    within, scores, cross, spread, uvx, tiles, cumx = rest[-7:]
    s = pl.program_id(0)
    fe, se = sc[2 * s], sc[2 * s + 1]

    @pl.when(s == 0)
    def _():
        spread[...] = head_spread()
        tiles[...] = tile_spread()


    for d in range(2):
        r = slice(128 * d, 128 * d + 128)
        scores[d] = jnp.where(diag_mask(d, fe, se, False), dot_nt(clow[r], blow[r]), 0.0)
    cross[...] = jnp.where(cross_half(fe, se, False), dot_nt(clow[128:], blow[:128]), 0.0).astype(BF)

    expand_tiles(cumx, to_lane0(cump[...], s, g), tiles)
    expand(uvx, to_lane0(uvp[...], s, g), spread)
    for j in range(6):
        for d in range(2):
            r = slice(128 * d, 128 * d + 128)
            pair = xs[0, r, tile(j)]
            parts = []
            for b in range(2):
                h = 2 * j + b
                gap = cumx[r, tile(h)] - ct[pl.ds(s * SPAN + g * 12 + h, 1), :][:, r]
                parts.append((jnp.exp2(jnp.minimum(gap, 0.0)) * scores[d]).astype(BF))
            total = dot(jnp.concatenate(parts, axis=1), by_head(pair))
            if d == 1:
                xv = (xs[0, :128, tile(j)].astype(F32) * uvx[:128, tile(j)]).astype(BF)
                total = total + dot(cross[...], xv) * uvx[128:, tile(j)]
            within[0, r, tile(j)] = total


def k4_body(sc, nrm, dbr, wzm, wzr, wom, wor, gate, dgn, wz, wo):
    g = pl.program_id(0)
    n = pl.program_id(1)
    me_dp = sc[9]

    @pl.when(n == 0)
    def _():
        place_pair(wz, wzm, wzr, me_dp)
        place_pair(wo, wom, wor, me_dp)

    cols = pl.ds(pl.multiple_of(n * 256, 256), 256)
    gate[0] = dot(nrm[0 : 4 * L], wz[:, cols]).astype(BF)
    dgn[0] = dot(dbr[...], wo[:, cols]).astype(BF)


def k5_body(
    sc, within, gate, dgn, x, r1, r2, r3, reachp, fac, clow, par, wom, wor, tok,
    out, gno, dgo, dyo, dpo, prevo, rowsum, dco, small,
    mo, sums, branch, wbuf, gnb, frow, dlow, seg_h, seg_l, pick, pv, spread, reachx,
):
    ph = pl.program_id(0)
    g = pl.program_id(1)
    s = pl.program_id(2)
    me_t, me_dp = sc[8], sc[9]
    r = rows_of(s)
    first = (g == 0) & (s == 0)

    @pl.when((ph == 0) & first)
    def _():
        rowsum[...] = jnp.zeros_like(rowsum)
        dco[...] = jnp.zeros_like(dco)
        small[...] = jnp.zeros_like(small)
        pick[...] = head_pick().astype(BF)
        spread[...] = head_spread()

    expand(reachx, to_lane0(reachp[...], s, g), spread)

    @pl.when(ph == 0)
    def _():
        srow = rows_of(s, 128)
        for c in range(2):
            at = half_at(c, me_t)
            frow[...] = r1[512:528, at].astype(F32)
            f = frow[pl.ds(s, 1)] + frow[pl.ds(s + 4, 1)]
            p = (
                jnp.where(me_t % 2 == 1, r1[srow, at].astype(F32), 0.0)
                + jnp.where(me_t == 2, r2[srow, at].astype(F32), 0.0)
                + jnp.where(me_t == 3, f * r3[srow, at].astype(F32), 0.0)
            )
            pv[:, 384 * c : 384 * c + 384] = p.astype(BF)
        prevo[g, srow] = pv[...]
        sq = jnp.zeros((L, 128), F32)
        dd = jnp.zeros((L, 128), F32)
        for j in range(6):
            from_prev = dot(clow[...], pv[:, tile(j)])
            mixed = (
                within[0, :, tile(j)]
                + reachx[:, tile(j)] * from_prev
                + par[0, 8:9, tile(j)] * x[0, :, tile(j)].astype(F32)
            )
            mo[g, r, tile(j)] = mixed
            gv = gate[0, :, tile(j)].astype(F32)
            gated = mixed * (gv * sigmoid(gv))
            sq = sq + gated * gated
            dd = dd + dgn[0, :, tile(j)].astype(F32) * par[0, 5:6, tile(j)] * gated
        sq = jnp.broadcast_to(jnp.sum(sq, axis=1, keepdims=True), (L, 128))
        dd = jnp.broadcast_to(jnp.sum(dd, axis=1, keepdims=True), (L, 128))

        @pl.when(g == 0)
        def _():
            sums[0, r] = sq
            sums[1, r] = dd

        @pl.when(g == 1)
        def _():
            sq2 = sums[0, r] + sq
            dd2 = sums[1, r] + dd
            gscale = lax.rsqrt(sq2 * (1.0 / INNER) + EPS)
            sums[0, r] = gscale
            sums[1, r] = gscale * gscale * gscale * (dd2 * (1.0 / INNER))

    @pl.when(ph == 1)
    def _():
        gscale = sums[0, r]
        coef = sums[1, r]
        srow = rows_of(s, 128)
        for j in range(6):
            gv = gate[0, :, tile(j)].astype(F32)
            mixed = mo[g, r, tile(j)]
            sg = sigmoid(gv)
            silu = gv * sg
            gated = mixed * silu
            gs = gated * gscale
            gain = par[0, 5:6, tile(j)]
            gn = (gs * gain).astype(BF)
            gno[0, :, tile(j)] = gn
            gnb[r, tile(j)] = gn
            d = dgn[0, :, tile(j)].astype(F32)
            small[g, 0:1, tile(j)] += jnp.sum(d * gs, axis=0, keepdims=True)
            dgated = gscale * (d * gain) - gated * coef
            dgo[0, :, tile(j)] = (dgated * mixed * (sg + silu * (1.0 - sg))).astype(BF)
            dy = (dgated * silu).astype(BF)
            dyo[0, :, tile(j)] = dy
            dyf = dy.astype(F32)
            dlow[:, tile(j)] = (dyf * reachx[:, tile(j)]).astype(BF)
            dx_skip = dyf * x[0, :, tile(j)].astype(F32)
            small[g, 1:2, tile(j)] += jnp.sum(dx_skip, axis=0, keepdims=True)
            v = dyf * mixed - par[0, 8:9, tile(j)] * dx_skip
            high = v.astype(BF)
            seg_h[:, tile(j)] = high
            seg_l[:, tile(j)] = (v - high.astype(F32)).astype(BF)
        seg = dot(seg_h[...], pick[...]) + dot(seg_l[...], pick[...])
        rowsum[...] += from_lane0(seg, s, g)
        dco[r] += dot_nt(dlow[...], prevo[g, srow])
        for c in range(2):
            dpo[srow, half_at(c, me_t)] = lax.dot_general(
                clow[...],
                dlow[:, 384 * c : 384 * c + 384],
                (((0,), (0,)), ((), ())),
                preferred_element_type=F32,
            ).astype(BF)

        @pl.when(s == 3)
        def _():
            f = factor_rows(fac, g)
            for c in range(2):
                dpo[512:528, half_at(c, me_t)] = f[:, 384 * c : 384 * c + 384]
            place_pair(wbuf, wom, wor, me_dp)

        @pl.when((s == 3) & (g == 0))
        def _():
            branch[...] = dot_nt(gnb[...], wbuf[...])

        @pl.when((s == 3) & (g == 1))
        def _():
            branch[...] += dot_nt(gnb[...], wbuf[...])

            @pl.loop(0, 16)
            def _(n):
                q = rows_of(n, 64)
                out[q] = (tok[q].astype(F32) + branch[q]).astype(BF)


def store_grad(ref, lead, me_dp, value_ref, first, width, at=0):
    count, rows = ref.shape[-3], ref.shape[-2]
    for n in range(count):
        place = n ^ me_dp if count > 1 else 0
        part = value_ref[n * rows : (n + 1) * rows, first : first + width].astype(BF)
        ref[lead + (place, slice(None), slice(at, at + width))] = part


def add_weighted(total, val, w, lead=()):
    @pl.loop(0, total.shape[0] // 64)
    def _(n):
        r = rows_of(n, 64)
        part = total[r]
        for j in range(w.shape[1] // 128):
            v = val[j, r] if lead else val[r, tile(j)]
            part = part + v * w[r, tile(j)].astype(F32)
        total[r] = part


def k6_body(sc, nt, dt, gn, dg, wzm, wzr, ok, os, zk, zs, ngz, val, wz):
    g = pl.program_id(0)
    me_dp = sc[9]
    place_pair(wz, wzm, wzr, me_dp)

    @pl.when(g == 0)
    def _():
        ngz[...] = jnp.zeros_like(ngz)

    for lhs, rhs, keep, send in ((dt, gn, ok, os), (nt, dg, zk, zs)):
        for n in range(3):
            cols = slice(256 * n, 256 * n + 256)
            val[:, cols] = dot(lhs[:, : 4 * L], rhs[0, :, cols])
        store_grad(keep, (0,), me_dp, val, 0, 384)
        store_grad(send, (0,), me_dp, val, 384, 384)
    add_weighted(ngz, val, wz)


def k7_body(g, sc, xs, dy, blow, clow, cump, uvp, ct, *rest):
    dxo, bco, pko, scores, cross, xvb, udb, spread, uvx, tiles, cumx, pick, corr = rest[-13:]
    s = pl.program_id(0)

    @pl.when(s == 0)
    def _():
        spread[...] = head_spread()
        tiles[...] = tile_spread()
        pick[...] = head_pick().astype(BF)
        pko[...] = jnp.zeros_like(pko)

    fe, se = sc[2 * s], sc[2 * s + 1]

    for d in range(2):
        r = slice(128 * d, 128 * d + 128)
        scores[d] = jnp.where(diag_mask(d, fe, se, True), dot_nt(blow[r], clow[r]), 0.0)
    cross[...] = jnp.where(cross_half(fe, se, True), dot_nt(blow[:128], clow[128:]), 0.0).astype(BF)

    expand_tiles(cumx, to_lane0(cump[...], s, g), tiles)
    expand(uvx, to_lane0(uvp[...], s, g), spread)
    totals = [jnp.zeros((128, 128), F32), jnp.zeros((128, 128), F32)]
    crossq = cross[...].astype(F32).T.astype(BF)
    for j in range(6):
        for d in range(2):
            r = slice(128 * d, 128 * d + 128)
            xp = xs[0, r, tile(j)]
            dyp = dy[0, r, tile(j)]
            grads = dot_nt(by_head(xp), dyp)
            parts = []
            for b in range(2):
                h = 2 * j + b
                gap = ct[pl.ds(s * SPAN + g * 12 + h, 1), :][:, r] - cumx[r, tile(h)]
                kern = jnp.exp2(jnp.minimum(gap, 0.0))
                totals[d] = totals[d] + grads[128 * b : 128 * b + 128] * kern
                parts.append((kern * scores[d]).astype(BF))
            dx = dot(jnp.concatenate(parts, axis=1), by_head(dyp))
            scaled = (xp if d == 0 else dyp).astype(F32) * uvx[r, tile(j)]
            low = scaled.astype(BF)
            diff = low.astype(F32) - scaled
            if d == 0:
                xvb[:, tile(j)] = low
                top, xdiff = dx, diff
            else:
                udb[:, tile(j)] = low
                off = dot(cross[...], low)
                dxo[0, r, tile(j)] = dx
                dxo[0, :128, tile(j)] = top + off * uvx[:128, tile(j)]
                corr[:128, tile(j)] = (xdiff * off).astype(BF)
                corr[128:, tile(j)] = (diff * dot(crossq, xvb[:, tile(j)])).astype(BF)
    dcr = dot_nt(xvb[...], udb[...])
    pko[...] += from_lane0(dot(corr[...], pick[...]), s, g)
    d0 = jnp.where(diag_mask(0, fe, se, True), totals[0], 0.0)
    d1 = jnp.where(diag_mask(1, fe, se, True), totals[1], 0.0)
    dl = jnp.where(cross_half(fe, se, True), dcr, 0.0)
    c0, c1, b0, b1 = clow[:128], clow[128:], blow[:128], blow[128:]
    bco[0, 0:128] = dot(d0.astype(BF), c0) + dot(dl.astype(BF), c1)
    bco[0, 128:] = dot(d1.astype(BF), c1)
    bco[1, 0:128] = dot(d0.T.astype(BF), b0)
    bco[1, 128:] = dot(d1.T.astype(BF), b1) + dot(dl.T.astype(BF), b0)


def k8_body(
    g, last, sc, nt, xs, dy, dsl, inx, halo, dxw, q1, q2, q3, prev, blow, stepp, etp, back, par,
    am, ar, bm, br, *rest,
):
    if last:
        (
            fac, sigp, decay, gain, ngz, nga, cbc, small1, small5, bc7a, bc7b, corr_a, corr_b, dc3, rowsum, sin, dbc, sega, enda, dba,
            keep, send, din, seg, end, dba_o, small, ngx, din5, skeep, ssend,
            val, hsum, gsc, gf, glow, xe, seg_h, seg_l, pick, wbuf, wpc, gbuf, pcs, pblk, sbc, spack, ub, ext, spread, stepx, etx,
        ) = rest
    else:
        (
            keep, send, din, seg, end, dba_o, small, ngx,
            val, hsum, gsc, gf, glow, xe, seg_h, seg_l, pick, wbuf, ub, ext, spread, stepx, etx,
        ) = rest
    s = pl.program_id(0)
    me_t, me_dp = sc[8], sc[9]
    r = rows_of(s)
    hrow = pl.ds(pl.multiple_of(4 * L + 16 * s, 16), 16)

    @pl.when(s == 0)
    def _():
        seg[...] = jnp.zeros_like(seg)
        end[...] = jnp.zeros_like(end)
        small[...] = jnp.zeros_like(small)
        pick[...] = head_pick().astype(BF)
        ext[:, 0:8] = jnp.zeros((6, 8, 128), F32)
        ext[:, 264:] = jnp.zeros((6, 8, 128), F32)
        spread[...] = head_spread()

    srow = rows_of(s, 128)
    for c in range(2):
        at = half_at(c, me_t)
        gf[...] = q1[512:528, at].astype(F32)
        f = gf[pl.ds(s, 1)] + gf[pl.ds(s + 4, 1)]
        v = (
            jnp.where(me_t % 2 == 0, q1[srow, at].astype(F32), 0.0)
            + jnp.where(me_t == 1, q2[srow, at].astype(F32), 0.0)
            + jnp.where(me_t == 0, f * q3[srow, at].astype(F32), 0.0)
        )
        gsc[:, 384 * c : 384 * c + 384] = v
        glow[:, 384 * c : 384 * c + 384] = v.astype(BF)
    for n in range(3):
        cols = slice(256 * n, 256 * n + 256)
        ub[:, cols] = dot(blow[...], glow[:, cols])
    masks = slot_masks(back, s)
    expand(stepx, to_lane0(stepp[...], s, g), spread)
    expand(etx, to_lane0(etp[...], s, g), spread)
    ends_row, gp_row = [], []
    for j in range(6):
        taps = [par[0, k : k + 1, tile(j)] for k in range(4)]
        xf = xs[0, :, tile(j)].astype(F32)
        ec = etx[:, tile(j)]
        eu = ub[:, tile(j)] * ec
        xe[:, tile(j)] = (xf * ec).astype(BF)
        ends_row.append(jnp.sum(xf * eu, axis=0, keepdims=True))
        gp_row.append(
            jnp.sum(gsc[:, tile(j)] * prev[0, srow, tile(j)].astype(F32), axis=0, keepdims=True)
        )
        dxi = dxw[0, :, tile(j)] + eu
        v = xf * dxi
        high = v.astype(BF)
        seg_h[:, tile(j)] = high
        seg_l[:, tile(j)] = (v - high.astype(F32)).astype(BF)
        dx = dxi * stepx[:, tile(j)] + par[0, 8:9, tile(j)] * dy[0, :, tile(j)].astype(F32)
        dconv = dx * dsl[0, :, tile(j)].astype(F32)
        small[4:5, tile(j)] += jnp.sum(dconv, axis=0, keepdims=True)
        v_ext = jnp.concatenate(
            [halo[0, :, tile(j)].astype(F32)[8:], inx[0, :, tile(j)].astype(F32)], axis=0
        )
        ext[j, 8:264] = dconv
        dv, tap_grads = conv_backward(ext.at[j], v_ext, taps, masks)
        for k in range(4):
            small[k : k + 1, tile(j)] += tap_grads[k]
        din[r, tile(j)] = dv[8:].astype(BF)
        din[hrow, tile(j)] = jnp.concatenate([jnp.zeros((8, 128), F32), dv[:8]], axis=0).astype(BF)
    seg[...] += from_lane0(dot(seg_h[...], pick[...]) + dot(seg_l[...], pick[...]), s, g)
    dba_o[r] = dot_nt(xe[...], glow[...])
    rows = jnp.concatenate(
        [
            jnp.concatenate(ends_row, axis=1),
            jnp.concatenate(gp_row, axis=1),
            jnp.zeros((6, WIDE), F32),
        ],
        axis=0,
    )
    end[...] += from_lane0(dot_high(rows, pick[...].astype(F32)), s, g)

    @pl.when(s == 3)
    def _():
        for n in range(3):
            cols = slice(256 * n, 256 * n + 256)
            hsum[...] = dot(nt[:, 4 * L :], din[4 * L :, cols])
            val[:, cols] = dot(nt[:, : 4 * L], din[: 4 * L, cols]) + hsum[...]
        store_grad(keep, (), me_dp, val, 0, 384)
        store_grad(send, (), me_dp, val, 384, 384)
        place_rows(wbuf, am, me_dp, 0)
        place_rows(wbuf, ar, me_dp, 384)
        place_rows(wbuf, bm, me_dp, 256, 0, 128, g if last else 0)
        place_rows(wbuf, br, me_dp, 640, 0, 128, g if last else 0)
        ngx[...] = ngz[...] + nga[...] if last else jnp.zeros_like(ngx)
        add_weighted(ngx, val, wbuf)

    if not last:
        return

    @pl.when(s == 3)
    def _():
        for q in range(2):
            taps = [cbc[k : k + 1, tile(q)] for k in range(4)]
            sbc[q] = jnp.zeros((8, 128), F32)

            @pl.loop(0, 4)
            def _(n):
                rn = rows_of(n)
                if q == 0:
                    grad = bc7a[0, rn] + bc7b[0, rn] + dba_o[rn] + dba[rn]
                else:
                    grad = bc7a[1, rn] + bc7b[1, rn] + dc3[rn]
                dconv = grad * dbc[q, rn]
                hn = pl.ds(pl.multiple_of(4 * L + 16 * n, 16), 16)
                v_ext = jnp.concatenate([sin[q, hn][8:], sin[q, rn]], axis=0)
                ext[q, 8:264] = dconv
                dv, tap_grads = conv_backward(ext.at[q], v_ext, taps, slot_masks(back, n))
                sbc[q, 4:5] += jnp.sum(dconv, axis=0, keepdims=True)
                for k in range(4):
                    sbc[q, k : k + 1] += tap_grads[k]
                gbuf[q, rn] = dv[8:]
                gbuf[q, hn] = jnp.concatenate([jnp.zeros((8, 128), F32), dv[:8]], axis=0)

        row = row_iota(L, 128)
        corr = corr_a[...] + corr_b[...]
        col = seg[...] + sega[...] + jnp.where(row < 128, corr, 0.0)
        ends_all = end[...] + enda[...]
        at_last = ends_all[0:1] + ends_all[1:2] * fac[0:1]
        dcum = rowsum[...] + jnp.where(row < 128, 0.0, corr) - col + jnp.where(row == L - 1, at_last, 0.0)
        upper = jnp.where(
            lax.broadcasted_iota(jnp.int32, (L, L), 0) <= lax.broadcasted_iota(jnp.int32, (L, L), 1),
            1.0,
            0.0,
        )
        dlog = dot_high(upper, dcum)
        alog = jnp.zeros((1, 128), F32)
        for i in range(4):
            at = slice(384 * (i % 2), 384 * (i % 2) + 128)
            for n in range(4):
                alog += pltpu.roll(par[i // 2, 7:8, at], n * SPAN + i * 6, 1)
        step_all, sig = stepp[...], sigp[...]
        ratio = jnp.where(step_all > 1e-30, sig / jnp.maximum(step_all, 1e-30), 1.0)
        ddt = ratio * col - sig * jnp.exp(alog) * dlog
        dts = jnp.concatenate(
            [
                jnp.sum(ddt, axis=0, keepdims=True),
                jnp.sum(dlog * decay[...], axis=0, keepdims=True),
                jnp.zeros((6, 128), F32),
            ],
            axis=0,
        )
        dts = dts + pltpu.roll(dts, 64, 1)
        dts = dts + pltpu.roll(dts, 32, 1)
        spack[...] = jnp.zeros_like(spack)
        for x in range(2):
            spack[x, 0:5] = (small if x == 0 else small1)[0:5]
            spack[x, 5:7] = small5[x, 0:2]
            for c in range(2):
                own = pltpu.roll(dts, (128 - 6 * (2 * x + c)) % 128, 1)
                own = jnp.where(lane_iota(8) < 6, own, 0.0)
                spack[x, 7:9, 384 * c : 384 * c + 128] = own[0:2]
            skeep[16 * x : 16 * x + 16] = spack[x, :, :384]
            ssend[16 * x : 16 * x + 16] = spack[x, :, 384:]
        ssend[32:40] = jnp.zeros((8, 384), F32)
        for q in range(2):
            ssend[32:37, tile(q)] = sbc[q, 0:5]
        for n in range(4):
            t = n ^ me_t
            turn = (64 * (t % 2)) % 128

            @pl.loop(0, 4)
            def _(m):
                rm = rows_of(m)
                lane = lane_iota(L)
                a = pltpu.roll(gbuf[t // 2, rm], turn, 1)
                d = pltpu.roll(ddt, (320 - m * SPAN - n * 6) % 128, 1)
                piece = jnp.where(lane < 64, a, jnp.where(lane < 70, d, 0.0))
                din5[rm, tile(n)] = piece.astype(BF)

            a = pltpu.roll(gbuf[t // 2, 4 * L :], turn, 1)
            din5[4 * L :, tile(n)] = jnp.where(lane_iota(64) < 64, a, 0.0).astype(BF)
        for n in range(2):
            cols = slice(256 * n, 256 * n + 256)
            hsum[...] = dot(nt[:, 4 * L :], din5[4 * L :, cols])
            v = dot(nt[:, : 4 * L], din5[: 4 * L, cols]) + hsum[...]
            pcs[2 * n] = v[:, :128]
            pcs[2 * n + 1] = v[:, 128:]
            place_rows(wpc, bm, me_dp, 256 * n, 128, 128, n)
            place_rows(wpc, br, me_dp, 256 * n + 128, 128, 128, n)
        add_weighted(ngx, pcs, wpc, (0,))
        gain_grad = (
            lax.dot_general(
                jnp.ones((8, 128), F32),
                ngx[...],
                (((1,), (1,)), ((), ())),
                preferred_element_type=F32,
                precision=lax.Precision.HIGHEST,
            )
            / gain[...]
        )
        ssend[37:38] = gain_grad[0:1, :384]
        ssend[38:39] = gain_grad[0:1, 384:]
        count, brow = keep.shape[0], keep.shape[1]
        for n in range(4):
            ref = keep if n % 2 == 0 else send
            at = slice(384 + 128 * (n // 2), 512 + 128 * (n // 2))
            if count == 1:
                ref[0, :, at] = pcs[n].astype(BF)
                continue
            t = n ^ me_t
            quarter = brow // 4
            for m in range(count):
                for c in range(4):
                    pblk[quarter * c : quarter * c + quarter] = pcs[
                        c ^ me_t, pl.ds(pl.multiple_of(brow * m + quarter * t, 8), quarter)
                    ]
                both = jnp.where(
                    lane_iota(brow) < 64, pblk[...], pcs[n, brow * m : brow * m + brow]
                )
                ref[m ^ me_dp, :, at] = both.astype(BF)


def k9z_body(sc, dg, wzm, wzr, dn, wz):
    place_pair(wz, wzm, wzr, sc[9])
    dn[...] = dot_nt(dg[0], wz[...]).astype(BF)


def k9_body(sc, din0, din1, din5, dna, dnb, am, ar, bm, br, out, dn, wx, wpc):
    g = pl.program_id(0)
    place_p1(wx, am, bm, ar, br, sc[9], wpc)

    @pl.when(g == 0)
    def _():
        dn[...] = dot_nt(din0[...], wx[...]) + dot_nt(din5[...], wpc[...])

    @pl.when(g == 1)
    def _():
        dn[...] += dot_nt(din1[...], wx[...])
        dn[...] += dot_nt(din5[...], wpc[...])

        @pl.loop(0, 16)
        def _(n):
            r = rows_of(n, 64)
            out[r] = (dn[r] + dna[r].astype(F32) + dnb[r].astype(F32)).astype(BF)

        out[4 * L :] = dn[4 * L :].astype(BF)


def k10_body(sc, dn, hr, tok, cot, gain, ig):
    s = pl.program_id(0)
    d = dn[...].astype(F32)
    extra = jnp.where(sc[8] < 3, hr[...].astype(F32), 0.0)
    width = d.shape[1]
    d = jnp.concatenate([d[: L - 16], d[L - 16 :] + extra], axis=0)
    tv = tok[...].astype(F32)
    r = lax.rsqrt(jnp.mean(tv * tv, axis=-1, keepdims=True) + EPS)
    tr = tv * r
    gd = gain[...] * d
    inner = jnp.sum(gd * tr, axis=-1, keepdims=True) * (1.0 / width)
    keep = row_iota(L, 1) < sc[2 * s + 1]
    res = jnp.where(keep, cot[...].astype(F32), 0.0)
    ig[...] = (res + r * (gd - tr * inner)).astype(BF)


def FINAL_SHAPES(dim, cols, heads, state, shard, tcount):
    return [
        (dim,), (shard, cols), (shard // tcount, 2 * state), (heads, shard), (4, cols), (cols,),
        (4, 2 * state), (2 * state,), (heads,), (heads,), (heads,), (cols,),
    ]


def k11_body(
    sc, va, vr, both, got,
    ngain, wx, wbc, wdt, cx, bx, cb, bb, dtb, alog, skip, og,
    g, sm,
):
    g[...] = va[...].astype(F32) + vr[...].astype(F32)
    sm[...] = both[...] + got[...]
    wx[...] = g[:, :384]
    quarter = g.shape[0] // 4
    lane = lane_iota(quarter)
    parts = [g[quarter * c : quarter * c + quarter, 384:512] for c in range(4)]
    for t in range(2):
        wbc[:, tile(t)] = jnp.where(lane < 64, parts[2 * t], pltpu.roll(parts[2 * t + 1], 64, 1))
    wdt[...] = pltpu.roll(g[:, 384:512], 64, 1).T[: wdt.shape[0]]
    cx[...] = sm[0:4]
    bx[...] = sm[4]
    og[...] = sm[5]
    r = lax.broadcasted_iota(jnp.int32, (384, 128), 0)
    c = lax.broadcasted_iota(jnp.int32, (384, 128), 1)
    sums = dot_high(sm[0:8], jnp.where(c == r // HD, 1.0, 0.0))
    skip[...] = sums[6, : skip.shape[0]]
    dtb[...] = sm[7, : dtb.shape[0]]
    alog[...] = sm[8, : alog.shape[0]]
    cb[...] = sm[16:20, : cb.shape[1]]
    bb[...] = sm[20, : bb.shape[0]]
    half = sm.shape[1]
    ngain[0:half] = sm[21]
    ngain[half : 2 * half] = sm[22]


def full(shape):
    return pl.BlockSpec(shape, lambda *a: (0,) * len(shape))


def call(body, grid, in_specs, out_specs, out_shapes, scratch, cost, name, aliases=None, vmem_mib=VMEM_MIB):
    flops, moved = cost
    return pl.pallas_call(
        body,
        grid_spec=pltpu.PrefetchScalarGridSpec(
            num_scalar_prefetch=1,
            grid=grid,
            in_specs=in_specs,
            out_specs=out_specs,
            scratch_shapes=scratch,
        ),
        out_shape=out_shapes,
        compiler_params=pltpu.CompilerParams(vmem_limit_bytes=vmem_mib * 2**20),
        cost_estimate=pl.CostEstimate(flops=flops, bytes_accessed=moved, transcendentals=0),
        input_output_aliases=aliases or {},
        name=name,
    )


def sds(shape, dtype):
    return pltpu.HBM(shape, dtype)


def anywhere(count):
    return [pl.BlockSpec(memory_space=pl.ANY)] * count


def flip(value, axis, bit):
    count = lax.axis_size(axis)
    return lax.ppermute(value, axis, [(a, a ^ bit) for a in range(count)])


def meet(*values):
    return lax.optimization_barrier(values)


def per_device(
    tokens, lengths, cotangent, norm_gain, w_z, w_x, w_bc, w_dt, conv_x, bias_x, conv_bc, bias_bc,
    dt_bias, a_log, skip_d, out_gain, w_out,
):
    tcount = lax.axis_size("tensor")
    dpcount = lax.axis_size("dp")
    me_t = lax.axis_index("tensor")
    me_dp = lax.axis_index("dp")
    slots, own_len, dim = tokens.shape
    rows = slots * own_len
    shard = w_z.shape[0]
    cols = w_z.shape[1]
    heads = w_dt.shape[1]
    fast = shard % 32 == 0 and dpcount & (dpcount - 1) == 0 and dpcount >= 8
    count = dpcount if fast else 1
    brow = shard if fast else dim

    first = lengths[:, 0] - me_t * own_len
    second = first + lengths[:, 1]
    sc = jnp.concatenate(
        [
            jnp.stack([first, second], axis=1).reshape(-1),
            jnp.stack([me_t, me_dp]),
            jnp.zeros((6,), jnp.int32),
        ]
    ).astype(jnp.int32)
    tok = tokens.reshape(rows, dim)
    cot = cotangent.reshape(rows, dim)

    bq = w_bc.shape[1] // tcount
    state = w_bc.shape[1] // 2
    own_bc = lax.dynamic_slice_in_dim(w_bc, me_t * bq, bq, 1)
    p1 = jnp.concatenate(
        [w_x, own_bc, w_dt, jnp.zeros((shard, 128 - bq - heads), BF)], axis=1
    )
    tail = tokens[:, own_len - 16 :, :].reshape(slots * 16, dim)
    def add_y(v, at):
        return jnp.stack([v, flip(v, "dp", 1)], axis=at)

    def add_x(v):
        return jnp.stack([v, flip(v, "tensor", 2)], axis=0)

    def blocks(v):
        return v.reshape(2, count, brow, v.shape[-1])

    def core(v):
        return flip(v, "tensor", 1)

    def middle(v):
        return lax.ppermute(v, "tensor", [(0, 0), (1, 2), (2, 1), (3, 3)])

    par, gain, bbc = call(
        k0_body,
        (1,),
        [
            full(v.shape)
            for v in (conv_x, bias_x, out_gain, dt_bias, a_log, skip_d, norm_gain, bias_bc)
        ],
        [full((16, cols)), full((1, dim)), full((1, 2 * state))],
        [sds((16, cols), F32), sds((1, dim), F32), sds((1, 2 * state), F32)],
        [pltpu.VMEM((8, 128), F32)],
        (1, 1),
        "parameters",
        vmem_mib=K5_MIB,
    )(sc, conv_x, bias_x, out_gain, dt_bias, a_log, skip_d, norm_gain, bias_bc)

    def prepare(halo):
        return call(
            prepare_body,
            (1,),
            [full((rows, dim)), full((64, dim)), full((rows, dim)), full((1, dim))],
            [full((rows + 64, dim)), full((dim, rows + 64)), full((rows, dim)), full((dim, rows))],
            [
                sds((rows + 64, dim), BF),
                sds((dim, rows + 64), BF),
                sds((rows, dim), BF),
                sds((dim, rows), BF),
            ],
            [],
            (1, 1),
            "prepare",
        )(sc, tok, halo, cot, gain)

    def grown(v, got, at):
        v = jnp.stack([v, got], axis=at)
        return v.reshape(v.shape[: at - 1] + (-1,) + v.shape[at + 1 :])

    if fast:
        v = p1[None]
        w2 = jnp.stack([w_z, w_out])[None]
        bit = dpcount // 2
        got = flip(v, "dp", bit)
        got, w2, sc, par, tail, gain = meet(got, w2, sc, par, tail, gain)
        v = grown(v, got, 1)
        while bit > 4:
            bit //= 2
            v = grown(v, flip(v, "dp", bit), 1)
            w2 = grown(w2, flip(w2, "dp", 2 * bit), 1)
        halo = lax.ppermute(tail, "tensor", [(a, (a + 1) % tcount) for a in range(tcount)])
        got, w2, parx, halo = meet(flip(v, "dp", 2), w2, flip(par, "tensor", 2), halo)
        par = jnp.stack([par, parx], axis=0)
        v = grown(v, got, 1)
        az, bz = v[..., :256], v[..., 256:]
        ax, by, parc, w2z = meet(
            flip(az, "tensor", 2), flip(bz, "dp", 1), core(par), flip(w2, "dp", 4)
        )
        w2 = grown(w2, w2z, 1)
        par = jnp.concatenate([par, parc], axis=-1)
        ax = jnp.stack([az, ax], axis=0)
        by = jnp.stack([bz, by], axis=1)
        nrm, nt, dbr, dt = prepare(halo)
        ay, bx, w2z, par, nrm = meet(
            flip(ax, "dp", 1), flip(by, "tensor", 2), flip(w2, "dp", 2), par, nrm
        )
        w2 = grown(w2, w2z, 1)
        wam = blocks(jnp.stack([ax, ay], axis=2))
        wbm = blocks(jnp.stack([by, bx], axis=0))
        zz, oz = w2[:, 0], w2[:, 1]
        zx, oy = flip(zz, "tensor", 2), flip(oz, "dp", 1)
        war, wbr = core(wam), core(wbm)
    else:
        halo = lax.ppermute(tail, "tensor", [(a, (a + 1) % tcount) for a in range(tcount)])
        par = add_x(par)
        par = jnp.concatenate([par, core(par)], axis=-1)
        z1 = lax.all_gather(p1, "dp", axis=0, tiled=True)[None]
        wam = add_x(z1[..., :256])
        wbm = add_x(z1[..., 256:])
        war, wbr = core(wam), core(wbm)
        nrm, nt, dbr, dt = prepare(halo)

    srows = slots * state
    wide = 2 * cols
    erows = rows + 64
    p1block = (1, count, brow, 256)
    wblock = (1, count, brow, cols)
    vmem = pltpu.VMEM

    def w_g(g, *a):
        return (g, 0, 0, 0)

    inx, blow, clow, bt, sin, dbc, cump, stepp, sigp, etp, reachp, decay, fac, uvp, mask, back, ct = call(
        k1_body,
        (2,),
        [full((erows, dim))]
        + [pl.BlockSpec(p1block, w_g)] * 4
        + [full((2, 16, wide)), full((4, 2 * state)), full((1, 2 * state))],
        [
            pl.BlockSpec((1, erows, wide), lambda g, sc: (g, 0, 0)),
            full((rows, state)),
            full((rows, state)),
            full((srows, L)),
            full((2, erows, state)),
            full((2, rows, state)),
        ]
        + [full((L, 128))] * 6
        + [full((8, 128)), full((L, 128)), full((L, 128)), full((L + 8, 128)), full((128, L))],
        [
            sds((2, erows, wide), BF),
            sds((rows, state), BF),
            sds((rows, state), BF),
            sds((srows, L), BF),
            sds((2, erows, state), F32),
            sds((2, rows, state), F32),
        ]
        + [sds((L, 128), F32)] * 6
        + [sds((8, 128), F32), sds((L, 128), F32), sds((L, 128), F32), sds((L + 8, 128), F32)]
        + [sds((128, L), F32)],
        [
            vmem((dim, wide), BF),
            vmem((dim, 256), BF),
            vmem((dim, 128), BF),
            vmem((erows, 256), F32),
            vmem((L + 8, 128), F32),
        ],
        (int(7e9), int(2e7)),
        "projections",
    )(sc, nrm, wam, war, wbm, wbr, par, conv_bc, bbc)

    def gs(g, s, sc):
        return (g, s, 0)

    def halo_gs(g, s, sc):
        return (g, rows // 16 + s, 0)

    def by_s(g, s, sc):
        return (s, 0)

    def mirror(g, sc):
        return (0, g ^ (sc[8] // 2))

    group = (1, L, wide)

    def gsel(g):
        return lambda s, sc: (g, s, 0)

    def conv_and_states(g, inx, kept):
        return call(
            functools.partial(k2_body, g),
            (slots,),
            [
                pl.BlockSpec(group, gsel(g)),
                pl.BlockSpec((1, 16, wide), lambda s, sc: (g, rows // 16 + s, 0)),
                pl.BlockSpec((1, 16, wide), lambda s, sc: (g, 0, 0)),
                pl.BlockSpec((state, L), lambda s, sc: (s, 0)),
                full((L, 128)),
                full((L, 128)),
                full((8, 128)),
                full((L, 128)),
            ]
            + anywhere(len(kept)),
            [pl.BlockSpec(group, gsel(g))] * 3
            + [pl.BlockSpec((srows + 16, wide), lambda s, sc: mirror(g, sc))],
            [sds((2, rows, wide), BF)] * 3 + [sds((srows + 16, 2 * wide), BF)],
            [
                vmem((L, wide), BF),
                vmem((6, L + 8, 128), F32),
                vmem((256, wide), BF),
                vmem((L, wide), F32),
                vmem((L, wide), F32),
            ],
            (int(5e9) if g else 1, int(2e7) if g else 1),
            "conv_and_states_%d" % g,
            {9 + n: n for n in range(len(kept))},
        )(sc, inx, inx, par, bt, stepp, etp, fac, mask, *kept)

    if fast:
        inx0, zx, oy = meet(inx, zx, oy)
        zx = jnp.stack([zz, zx], axis=0)
        oy = jnp.stack([oz, oy], axis=1)
        zy, ox = flip(zx, "dp", 1), flip(oy, "tensor", 2)
        xl, xs, dsl, st = conv_and_states(1, inx, conv_and_states(0, inx0, []))
        st, zy, ox = meet(st, zy, ox)
        wzm = blocks(jnp.stack([zx, zy], axis=2))
        wom = blocks(jnp.stack([oy, ox], axis=0))
        wzr, wor = core(wzm), core(wom)
    else:
        xl, xs, dsl, st = conv_and_states(1, inx, conv_and_states(0, inx, []))
        wzm = add_x(lax.all_gather(w_z, "dp", axis=0, tiled=True)[None])
        wom = add_x(lax.all_gather(w_out, "dp", axis=0, tiled=True)[None])
        wzr, wor = core(wzm), core(wom)

    def end_state(mine, one):
        f = mine[srows : srows + 4].astype(F32) + mine[srows + 4 : srows + 8].astype(F32)
        width = mine.shape[1]
        end = mine[:srows].astype(F32).reshape(slots, state, width) + f[:, None] * one[
            :srows
        ].astype(F32).reshape(slots, state, width)
        return end.astype(BF).reshape(srows, width)

    r1 = core(st)
    end = end_state(st, r1)
    r2 = middle(end)
    xs3, _ = meet(xs, end)

    def within_of(g, kept):
        return call(
            functools.partial(k3_body, g),
            (slots,),
            [
                pl.BlockSpec(group, gsel(g)),
                pl.BlockSpec((L, state), lambda s, sc: (s, 0)),
                pl.BlockSpec((L, state), lambda s, sc: (s, 0)),
                full((L, 128)),
                full((L, 128)),
                full((128, L)),
            ]
            + anywhere(len(kept)),
            pl.BlockSpec(group, gsel(g)),
            sds((2, rows, wide), F32),
            [
                vmem((2, 128, 128), F32),
                vmem((128, 128), BF),
                vmem((256, wide), BF),
                vmem((L, wide), F32),
                vmem((256, 2 * wide), BF),
                vmem((L, 2 * wide), F32),
            ],
            (int(5e9), int(1e7)),
            "within_%d" % g,
            {7 + n: n for n in range(len(kept))},
        )(sc, xs3, blow, clow, cump, uvp, ct, *kept)

    within = within_of(1, [within_of(0, [])])
    nrm4, within = meet(nrm, within)

    gate, dgn = call(
        k4_body,
        (2, 3),
        [full((erows, dim)), full((rows, dim))] + [pl.BlockSpec(wblock, w_g)] * 4,
        [pl.BlockSpec((1, rows, 256), lambda g, n, sc: (g, 0, n))] * 2,
        [sds((2, rows, wide), BF)] * 2,
        [vmem((dim, wide), BF), vmem((dim, wide), BF)],
        (int(5e9), int(2e7)),
        "gate_and_out_backward",
    )(sc, nrm4, dbr, wzm, wzr, wom, wor)

    gate, r2 = meet(gate, r2)
    r3 = core(r2)

    def p_gs(phase):
        def index(p, g, s, sc):
            return (
                jnp.where(p == phase, g, 0 if phase else 1),
                jnp.where(p == phase, s, 0 if phase else slots - 1),
                0,
            )

        return index

    def p_mirror(phase):
        def index(p, g, s, sc):
            return mirror(jnp.where(p == phase, g, 0 if phase else 1), sc)

        return index

    def pgs(p, g, s, sc):
        return (g, s, 0)

    def p_w(p, g, s, sc):
        return (jnp.where(p == 1, g, 0), 0, 0, 0)

    out, gn, dg, dy, dp, prev, rowsum, dc5, small5 = call(
        k5_body,
        (2, 2, slots),
        [
            pl.BlockSpec(group, p_gs(0)),
            pl.BlockSpec(group, pgs),
            pl.BlockSpec(group, pgs),
            pl.BlockSpec(group, pgs),
            pl.BlockSpec((srows + 16, wide), p_mirror(0)),
            pl.BlockSpec((srows, wide), p_mirror(0)),
            pl.BlockSpec((srows, wide), p_mirror(0)),
            full((L, 128)),
            full((8, 128)),
            pl.BlockSpec((L, state), lambda p, g, s, sc: (s, 0)),
            pl.BlockSpec((1, 16, wide), lambda p, g, s, sc: (g, 0, 0)),
            pl.BlockSpec(wblock, p_w),
            pl.BlockSpec(wblock, p_w),
            full((rows, dim)),
        ],
        [
            full((rows, dim)),
            pl.BlockSpec(group, p_gs(1)),
            pl.BlockSpec(group, p_gs(1)),
            pl.BlockSpec(group, p_gs(1)),
            pl.BlockSpec((srows + 16, wide), p_mirror(1)),
            full((2, srows, wide)),
            full((L, 128)),
            full((rows, state)),
            full((2, 8, wide)),
        ],
        [
            sds((rows, dim), BF),
            sds((2, rows, wide), BF),
            sds((2, rows, wide), BF),
            sds((2, rows, wide), BF),
            sds((srows + 16, 2 * wide), BF),
            sds((2, srows, wide), BF),
            sds((L, 128), F32),
            sds((rows, state), F32),
            sds((2, 8, wide), F32),
        ],
        [
            vmem((2, rows, wide), F32),
            vmem((2, rows, 128), F32),
            vmem((rows, dim), F32),
            vmem((dim, wide), BF),
            vmem((rows, wide), BF),
            vmem((16, cols), F32),
            vmem((L, wide), BF),
            vmem((L, wide), BF),
            vmem((L, wide), BF),
            vmem((wide, 128), BF),
            vmem((state, wide), BF),
            vmem((256, wide), BF),
            vmem((L, wide), F32),
        ],
        (int(1.5e10), int(4e7)),
        "gated_norm",
        vmem_mib=50,
    )(sc, within, gate, dgn, xl, r1, r2, r3, reachp, fac, clow, par, wom, wor, tok)

    q1 = core(dp)

    gshape = (2, count, brow, cols)
    ok, osend, zk, zsend, ngz = call(
        k6_body,
        (2,),
        [full((dim, erows)), full((dim, rows))]
        + [pl.BlockSpec((1, rows, wide), lambda g, sc: (g, 0, 0))] * 2
        + [pl.BlockSpec(wblock, w_g)] * 2,
        [pl.BlockSpec((1,) + gshape[1:], w_g)] * 4 + [full((dim, 128))],
        [sds(gshape, BF)] * 4 + [sds((dim, 128), F32)],
        [vmem((dim, wide), F32), vmem((dim, wide), BF)],
        (int(5e9), int(2e7)),
        "outer_weight_grads",
        vmem_mib=K5_MIB,
    )(sc, nt, dt, gn, dg, wzm, wzr)

    osend, q1 = meet(osend, q1)
    dy1, end = meet(dy, end_state(dp, q1))
    q2 = middle(end)

    def summed(a, b):
        return (a.astype(F32) + b.astype(F32)).astype(BF)

    def reduce_step(v, axis, mesh_axis, bit):
        keep = lax.index_in_dim(v, 0, axis, False)
        send = lax.index_in_dim(v, 1, axis, False)
        return summed(keep, flip(send, mesh_axis, bit))

    def reduce_x(v, axis):
        return reduce_step(v, axis, "tensor", 2)

    def reduce_dp(v, bit):
        v = v.reshape((v.shape[0] // 2, 2) + v.shape[1:])
        return reduce_step(v, 1, "dp", bit)

    def finish(v, bit):
        while bit < dpcount:
            v = reduce_dp(v, bit)
            bit *= 2
        return v[0].astype(F32)

    def reduce_slow(v):
        v = v.reshape(dpcount, shard, v.shape[-1])
        got = lax.all_to_all(v, "dp", split_axis=0, concat_axis=0, tiled=True)
        return got.astype(F32).sum(axis=0)

    def reduce_core(keep, send):
        return summed(keep, core(send))

    if fast:
        vw = summed(jnp.stack([ok, zk]), jnp.stack([core(osend), core(zsend)]))
        vw = vw.reshape((2, 2, count // 2, 2, brow, cols))
        vwr = flip(vw[:, :, :, 1], "dp", 1)
    else:
        grad_w_out = reduce_slow(reduce_x(reduce_core(ok, osend), 0)[0])
        grad_w_z = reduce_slow(reduce_x(reduce_core(zk, zsend), 0)[0])

    def within_backward(g, dy, kept):
        return call(
            functools.partial(k7_body, g),
            (slots,),
            [
                pl.BlockSpec(group, gsel(g)),
                pl.BlockSpec(group, gsel(g)),
                pl.BlockSpec((L, state), lambda s, sc: (s, 0)),
                pl.BlockSpec((L, state), lambda s, sc: (s, 0)),
                full((L, 128)),
                full((L, 128)),
                full((128, L)),
            ]
            + anywhere(len(kept)),
            [
                pl.BlockSpec(group, gsel(g)),
                pl.BlockSpec((2, L, state), lambda s, sc: (0, s, 0)),
                full((L, 128)),
            ],
            [sds((2, rows, wide), F32), sds((2, rows, state), F32), sds((L, 128), F32)],
            [
                vmem((2, 128, 128), F32),
                vmem((128, 128), BF),
                vmem((128, wide), BF),
                vmem((128, wide), BF),
                vmem((256, wide), BF),
                vmem((L, wide), F32),
                vmem((256, 2 * wide), BF),
                vmem((L, 2 * wide), F32),
                vmem((wide, 128), BF),
                vmem((L, wide), BF),
            ],
            (int(1e10) if g else 1, int(2e7) if g else 1),
            "within_backward_%d" % g,
            {8 + n: n for n in range(len(kept))},
        )(sc, xs, dy, blow, clow, cump, uvp, ct, *kept)

    dxw, bc7a, corr_a = within_backward(1, dy1, [])
    dxw, bc7b, corr_b = within_backward(0, dy, [dxw])

    def states_backward(g, last, nt, extra_in, extra_specs):
        width = cols + 256 if last else cols
        gshape = (count, brow, width)

        def at(s, sc):
            return (g, s, 0)

        in_specs = [
            full((dim, erows)),
            pl.BlockSpec(group, at),
            pl.BlockSpec(group, at),
            pl.BlockSpec(group, at),
            pl.BlockSpec(group, at),
            pl.BlockSpec((1, 16, wide), lambda s, sc: (g, rows // 16 + s, 0)),
            pl.BlockSpec(group, at),
            pl.BlockSpec((srows + 16, wide), lambda s, sc: mirror(g, sc)),
            pl.BlockSpec((srows, wide), lambda s, sc: mirror(g, sc)),
            pl.BlockSpec((srows, wide), lambda s, sc: mirror(g, sc)),
            pl.BlockSpec((1, srows, wide), lambda s, sc: (g, 0, 0)),
            pl.BlockSpec((L, state), lambda s, sc: (s, 0)),
            full((L, 128)),
            full((L, 128)),
            full((L + 8, 128)),
            full((2, 16, wide)) if last else pl.BlockSpec((1, 16, wide), lambda s, sc: (g, 0, 0)),
            pl.BlockSpec(p1block, lambda s, sc: (g, 0, 0, 0)),
            pl.BlockSpec(p1block, lambda s, sc: (g, 0, 0, 0)),
        ]
        if last:
            in_specs += [full((2,) + p1block[1:])] * 2
        else:
            in_specs += [pl.BlockSpec(p1block, lambda s, sc: (g, 0, 0, 0))] * 2
        in_specs += extra_specs
        outs = [
            (gshape, BF),
            (gshape, BF),
            ((erows, wide), BF),
            ((L, 128), F32),
            ((8, 128), F32),
            ((rows, state), F32),
            ((8, wide), F32),
            ((dim, 128), F32),
        ]
        scratch = [
            vmem((dim, wide), F32),
            vmem((dim, 256), F32),
            vmem((state, wide), F32),
            vmem((16, cols), F32),
            vmem((state, wide), BF),
            vmem((L, wide), BF),
            vmem((L, wide), BF),
            vmem((L, wide), BF),
            vmem((wide, 128), BF),
            vmem((dim, wide), BF),
        ]
        if last:
            outs += [((erows, 512), BF), ((32, cols), F32), ((40, cols), F32)]
            scratch += [
                vmem((dim, 512), BF),
                vmem((2, erows, state), F32),
                vmem((4, dim, 128), F32),
                vmem((brow, 128), F32),
                vmem((2, 8, state), F32),
                vmem((2, 16, wide), F32),
            ]
        scratch += [vmem((L, wide), F32), vmem((6, L + 16, 128), F32), vmem((256, wide), BF)]
        scratch += [vmem((L, wide), F32), vmem((L, wide), F32)]
        return call(
            functools.partial(k8_body, g, last),
            (slots,),
            in_specs,
            [full(shape) for shape, _ in outs],
            [sds(shape, dtype) for shape, dtype in outs],
            scratch,
            (int(1e10), int(2e7)),
            "states_backward_%d" % g,
        )(sc, nt, xs, dy, dsl, inx, inx, dxw, q1, q2, q3, prev, blow, stepp, etp, back, par, wam, war, wbm, wbr, *extra_in)

    def normed_grad_z(g, dg):
        return call(
            k9z_body,
            (1,),
            [
                pl.BlockSpec((1, rows, wide), lambda i, sc: (g, 0, 0)),
                pl.BlockSpec(wblock, lambda i, sc: (g, 0, 0, 0)),
                pl.BlockSpec(wblock, lambda i, sc: (g, 0, 0, 0)),
            ],
            full((rows, dim)),
            sds((rows, dim), BF),
            [vmem((dim, wide), BF)],
            (1, 1),
            "normed_grad_z%d" % g,
        )(sc, dg, wzm, wzr)

    dga, dxw = meet(dg, dxw)
    dna = normed_grad_z(1, dga)
    dnb = normed_grad_z(0, dga)
    if fast:
        dxw, q2, dna, dnb, vwr = meet(dxw, q2, dna, dnb, vwr)
        vw = summed(vw[:, :, :, 0], vwr)
        vwr = flip(vw[:, 1], "tensor", 2)
    else:
        dxw, q2, dna, dnb = meet(dxw, q2, dna, dnb)
    q3 = core(q2)
    ka, sa, din1, seg1, end1, dba1, small1, nga = states_backward(1, False, nt, [], [])
    if fast:
        sa, vwr = meet(sa, vwr)
        vw = summed(vw[:, 0], vwr).reshape((2, count // 4, 2, brow, cols))
        vwr = flip(vw[:, :, 1], "dp", 2)
    sar = core(sa)
    nt0, sar = meet(nt, sar)
    va = summed(ka, sar)
    xa = flip(va, "tensor", 2)
    ks, ss, din0, _, _, _, _, _, din5, skeep, ssend = states_backward(
        0,
        True,
        nt0,
        [fac, sigp, decay, gain, ngz, nga, conv_bc, small1, small5, bc7a, bc7b, corr_a, corr_b, dc5, rowsum, sin, dbc, seg1, end1, dba1],
        [
            full((8, 128)),
            full((L, 128)),
            full((L, 128)),
            full((1, dim)),
            full((dim, 128)),
            full((dim, 128)),
            full((4, 2 * state)),
            full((8, wide)),
            full((2, 8, wide)),
            full((2, rows, state)),
            full((2, rows, state)),
            full((L, 128)),
            full((L, 128)),
            full((rows, state)),
            full((L, 128)),
            full((2, erows, state)),
            full((2, rows, state)),
            full((L, 128)),
            full((8, 128)),
            full((rows, state)),
        ],
    )

    if fast:
        ss, xa, vwr = meet(ss, xa, vwr)
        vw = summed(vw[:, :, 0], vwr).reshape((2, count // 8, 2, brow, cols))
        vwr = flip(vw[:, :, 1], "dp", 4)
    din0, ssr, got = meet(din0, core(ss), core(ssend))
    own = (skeep + got[:32]).reshape(2, 16, cols)
    flat = ssend[32:] + got[32:]
    vb = summed(ks[..., cols:], ssr[..., cols:])
    px = flip(vb[..., 128:], "tensor", 2)
    vx = (ks[..., :cols].astype(F32) + ssr[..., :cols].astype(F32) + xa.astype(F32)).astype(BF)
    if fast:
        vx = vx.reshape((count // 2, 2) + vx.shape[1:])
        vxr = flip(vx[:, 1], "dp", 1)
    both = jnp.concatenate([own[0], flat], axis=0)
    got = flip(jnp.concatenate([own[1], flat], axis=0), "tensor", 2)

    dn = call(
        k9_body,
        (2,),
        [
            full((erows, wide)),
            full((erows, wide)),
            pl.BlockSpec((erows, 256), lambda g, sc: (0, g)),
            full((rows, dim)),
            full((rows, dim)),
        ]
        + [pl.BlockSpec(p1block, w_g)] * 4,
        full((erows, dim)),
        sds((erows, dim), BF),
        [vmem((erows, dim), F32), vmem((dim, wide), BF), vmem((dim, 256), BF)],
        (int(6e9), int(2e7)),
        "normed_grad",
    )(sc, din0, din1, din5, dna, dnb, wam, war, wbm, wbr)

    if fast:
        dn, px, vxr, got, vwr = meet(dn, px, vxr, got, vwr)
        vw = summed(vw[:, :, 0], vwr)
        grad_w_out, grad_w_z = finish(vw[0], 8), finish(vw[1], 8)
        vx = summed(vx[:, 0], vxr)
        vp = summed(vb[..., :128], px)
        vp = vp.reshape((count // 2, 2) + vp.shape[1:])
        vpr = flip(vp[:, 1], "dp", 1)
        both = both + got
        got = flip(both, "dp", 1)
    hr = lax.ppermute(dn[rows:], "tensor", [((a + 1) % tcount, a) for a in range(tcount)])
    if fast:
        hr, vpr, got = meet(hr, vpr, got)
        v1 = jnp.concatenate([vx, summed(vp[:, 0], vpr)], axis=-1)
        v1 = v1.reshape((count // 4, 2) + v1.shape[1:])
        v1r = flip(v1[:, 1], "dp", 2)
        both = both + got
        got = flip(both, "dp", 2)

    ig = call(
        k10_body,
        (slots,),
        [
            pl.BlockSpec((L, dim), lambda s, sc: (s, 0)),
            pl.BlockSpec((16, dim), lambda s, sc: (s, 0)),
            pl.BlockSpec((L, dim), lambda s, sc: (s, 0)),
            pl.BlockSpec((L, dim), lambda s, sc: (s, 0)),
            full((1, dim)),
        ],
        pl.BlockSpec((L, dim), lambda s, sc: (s, 0)),
        sds((rows, dim), BF),
        [],
        (int(1e9), int(1e7)),
        "input_grad",
    )(sc, dn, hr, tok, cot, gain)

    if fast:
        ig, v1r, got = meet(ig, v1r, got)
        v1 = summed(v1[:, 0], v1r)
        both = both + got
        bit = 4
        while 2 * bit < dpcount:
            both = both + flip(both, "dp", bit)
            v1 = reduce_dp(v1, bit)
            bit *= 2
        got = flip(both, "dp", bit)
        v1 = v1.reshape((2,) + v1.shape[1:]) if v1.shape[0] == 2 else v1
        v1a, v1r = v1[0], flip(v1[1], "dp", bit)
    else:
        both = lax.psum(both + got, "dp")
        v1 = jnp.concatenate([vx, summed(vb[..., :128], px)], axis=-1)
        grad1 = reduce_slow(v1)
    if fast:
        last = call(
            k11_body,
            (1,),
            [full((shard, 512))] * 2 + [full((24, cols))] * 2,
            [full(shape) for shape in FINAL_SHAPES(dim, cols, heads, state, shard, tcount)],
            [
                sds(shape, F32)
                for shape in FINAL_SHAPES(dim, cols, heads, state, shard, tcount)
            ],
            [vmem((shard, 512), F32), vmem((24, cols), F32)],
            (int(1e6), int(1e6)),
            "last_sums",
        )(sc, v1a, v1r, both, got)
        (
            ngain, grad_w_x, grad_w_bc, grad_w_dt, grad_conv_x, grad_bias_x, grad_conv_bc,
            grad_bias_bc, grad_dt_bias, grad_a_log, grad_skip, grad_out_gain,
        ) = last
        grad_w_dt = grad_w_dt.T
    else:
        own, flat = both[:16], both[16:]
        ngain = flat[5:7].reshape(dim)
        grad_w_x = grad1[:, :cols]
        parts = grad1[:, cols : cols + bq].reshape(tcount, shard // tcount, bq)
        got = lax.all_to_all(parts, "tensor", split_axis=0, concat_axis=0, tiled=True)
        grad_w_bc = jnp.swapaxes(got, 0, 1).reshape(shard // tcount, bq * tcount)
        grad_w_dt = grad1[:, cols + bq : cols + bq + heads]
        grad_conv_x, grad_bias_x, grad_out_gain = own[:4], own[4], own[5]
        grad_conv_bc, grad_bias_bc = flat[:4, : 2 * state], flat[4, : 2 * state]
        grad_dt_bias, grad_a_log = own[7, :heads], own[8, :heads]
        grad_skip = own[6].reshape(heads, cols // heads).sum(axis=1)

    return (
        out.reshape(tokens.shape),
        ig.reshape(tokens.shape),
        ngain,
        grad_w_z,
        grad_w_x,
        grad_w_bc,
        grad_w_dt,
        grad_conv_x,
        grad_bias_x,
        grad_conv_bc,
        grad_bias_bc,
        grad_dt_bias,
        grad_a_log,
        grad_skip,
        grad_out_gain,
        grad_w_out,
    )


def solution(mesh):
    return jax.shard_map(
        per_device,
        mesh=mesh,
        in_specs=(
            P("dp", "tensor", None), P("dp", None), P("dp", "tensor", None), P(),
            P("dp", "tensor"), P("dp", "tensor"), P("dp", None), P("dp", "tensor"),
            P(None, "tensor"), P("tensor"), P(), P(),
            P("tensor"), P("tensor"), P("tensor"), P("tensor"), P("dp", "tensor"),
        ),
        out_specs=(
            P("dp", "tensor", None), P("dp", "tensor", None), P(),
            P("dp", "tensor"), P("dp", "tensor"), P(("dp", "tensor"), None), P("dp", "tensor"),
            P(None, "tensor"), P("tensor"), P(), P(),
            P("tensor"), P("tensor"), P("tensor"), P("tensor"), P("dp", "tensor"),
        ),
        check_vma=False,
    )
```

```python
import functools

import jax
import jax.numpy as jnp
from jax import lax
from jax.experimental import pallas as pl
from jax.experimental.pallas import tpu as pltpu
from jax.sharding import PartitionSpec as P

INNER = 1536
L = 256
HD = 64
SPAN = 32
EPS = 1e-05
LOG2E = 1.4426950408889634
F32 = jnp.float32
BF = jnp.bfloat16
CHUNK = 64
WIDE = 768
VMEM_MIB = 36
K5_MIB = 58


def dot(a, b):
    return jnp.dot(a, b, preferred_element_type=F32)


def dot_nt(a, b):
    return lax.dot_general(a, b, (((1,), (1,)), ((), ())), preferred_element_type=F32)


def dot_high(a, b):
    return jnp.dot(a, b, preferred_element_type=F32, precision=lax.Precision.HIGHEST)


def sigmoid(v):
    return 0.5 * jnp.tanh(0.5 * v) + 0.5


def lane_iota(rows):
    return lax.broadcasted_iota(jnp.int32, (rows, 128), 1)


def row_iota(rows, lanes):
    return lax.broadcasted_iota(jnp.int32, (rows, lanes), 0)


def seg_of(idx, fe, se):
    return (idx >= fe).astype(jnp.int32) + (idx >= se).astype(jnp.int32)


def ends(sc, s):
    return sc[2 * s], sc[2 * s + 1]


def pair_cols(cols, first):
    lane = lane_iota(cols.shape[0])
    left = jnp.broadcast_to(cols[:, first : first + 1], cols.shape)
    right = jnp.broadcast_to(cols[:, first + 1 : first + 2], cols.shape)
    return jnp.where(lane < HD, left, right)


def head_pick():
    r = lax.broadcasted_iota(jnp.int32, (WIDE, 128), 0)
    c = lax.broadcasted_iota(jnp.int32, (WIDE, 128), 1)
    return jnp.where(c == r // HD, 1.0, 0.0)


def head_spread():
    r = lax.broadcasted_iota(jnp.int32, (256, WIDE), 0)
    c = lax.broadcasted_iota(jnp.int32, (256, WIDE), 1)
    return jnp.where(r % 128 == c // HD, 1.0, 0.0).astype(BF)


def expand(dst, cols, spread):
    high = cols.astype(BF)
    low = (cols - high.astype(F32)).astype(BF)
    both = jnp.concatenate([high, low], axis=1)
    for n in range(3):
        dst[:, 256 * n : 256 * n + 256] = dot(both, spread[:, 256 * n : 256 * n + 256])


def three_terms(v):
    high = v.astype(BF).astype(F32)
    mid = (v - high).astype(BF).astype(F32)
    return high, mid, v - high - mid


def tile_spread():
    r = lax.broadcasted_iota(jnp.int32, (256, 2 * WIDE), 0)
    h = lax.broadcasted_iota(jnp.int32, (256, 2 * WIDE), 1) // 128
    return jnp.where((r == h) | (r == h + 128) | (r == h + 144), 1.0, 0.0).astype(BF)


def expand_tiles(dst, cols, spread):
    high, mid, low = three_terms(cols)
    lane = lane_iota(L)
    rest = jnp.where(lane < 16, mid, pltpu.roll(low, 16, 1))
    left = jnp.concatenate([high, rest], axis=1).astype(BF)
    for n in range(6):
        dst[:, 256 * n : 256 * n + 256] = dot(left, spread[:, 256 * n : 256 * n + 256])


def to_lane0(packed, s, g):
    return pltpu.roll(packed, (256 - s * SPAN - g * 12) % 128, 1)


def from_lane0(cols, s, g):
    return pltpu.roll(cols, s * SPAN + g * 12, 1)


def rows_of(s, length=L):
    return pl.ds(pl.multiple_of(s * length, length), length)


def tile(j):
    return slice(128 * j, 128 * j + 128)


def conv_forward(ext, taps, bias, masks, first=0, length=L):
    acc = bias + taps[0] * ext[8 + first : 8 + first + length]
    for k in range(1, 4):
        acc = acc + (taps[k] * ext[8 + first - k : 8 + first - k + length]) * masks[k - 1]
    return acc


def conv_backward(ext, v_ext, taps, masks):
    out, tap_grads = None, []
    for k in range(4):
        part = ext[k : 264 + k]
        if k:
            part = part * masks[k - 1]
        tap_grads.append(jnp.sum(part * v_ext, axis=0, keepdims=True))
        out = taps[k] * part if out is None else out + taps[k] * part
    return out, tap_grads


def slot_masks(packed, s):
    cols = pltpu.roll(packed[...], (128 - 4 * s) % 128, 1)
    return [jnp.broadcast_to(cols[:, k : k + 1], cols.shape) for k in (1, 2, 3)]


def place_rows(dst, blocks, me, at, first=0, width=None, lead=0):
    count, rows = blocks.shape[1:3]
    width = blocks.shape[3] - first if width is None else width
    for n in range(count):
        start = pl.multiple_of((n ^ me) * rows, rows) if count > 1 else 0
        dst[pl.ds(start, rows), at : at + width] = blocks[lead, n, :, first : first + width]


def place_pair(dst, mine, other, me):
    place_rows(dst, mine, me, 0)
    place_rows(dst, other, me, 384)


def place_p1(dst, am, bm, ar, br, me, pieces):
    place_rows(dst, am, me, 0)
    place_rows(dst, bm, me, 256, 0, 128)
    place_rows(dst, ar, me, 384)
    place_rows(dst, br, me, 640, 0, 128)
    place_rows(pieces, bm, me, 0, 128, 128)
    place_rows(pieces, br, me, 128, 128, 128)


def half_at(c, me_t):
    return pl.ds(pl.multiple_of(384 * (c ^ (me_t % 2)), 128), 384)


def k0_body(sc, conv_x, bias_x, out_gain, dt_bias, a_log, skip_d, norm_gain, bias_bc, par, gain, bbc, row):
    par[...] = jnp.zeros_like(par)
    par[0:4] = conv_x[...]
    par[4] = bias_x[...]
    par[5] = out_gain[...]
    par[6, : dt_bias.shape[0]] = dt_bias[...]
    par[7, : a_log.shape[0]] = a_log[...]
    row[...] = jnp.zeros_like(row)
    row[0, : skip_d.shape[0]] = skip_d[...]
    r = lax.broadcasted_iota(jnp.int32, (128, 384), 0)
    c = lax.broadcasted_iota(jnp.int32, (128, 384), 1)
    par[8:9] = dot_high(row[...], jnp.where(r == c // HD, 1.0, 0.0))[0:1]
    gain[0] = norm_gain[...]
    bbc[0] = bias_bc[...]


def prepare_body(sc, tok, halo, cot, gain, nrm, nt, dbr, dt):
    def norm(v):
        v = v.astype(F32)
        r = lax.rsqrt(jnp.mean(v * v, axis=-1, keepdims=True) + EPS)
        return (v * r * gain[...]).astype(BF)

    @pl.loop(0, 16)
    def _(n):
        r = rows_of(n, 64)
        nrm[r] = norm(tok[r])
        keep = row_iota(64, 1) + 64 * (n % 4) < sc[2 * (n // 4) + 1]
        dbr[r] = jnp.where(keep, cot[r].astype(F32), 0.0).astype(BF)

    nrm[4 * L :] = jnp.where(sc[8] > 0, norm(halo[...]).astype(F32), 0.0).astype(BF)

    @pl.loop(0, 4)
    def _(s):
        nt[:, rows_of(s)] = nrm[rows_of(s)].T
        dt[:, rows_of(s)] = dbr[rows_of(s)].T

    nt[:, 4 * L :] = nrm[4 * L :].T


def k1_body(
    sc, nrm, am, ar, bm, br, par, cbc, bbc,
    inx, blow, clow, bto, sin, dbc,
    cumo, stepo, sigo, eto, reacho, decayo, faco, uvo, masko, backo, ct,
    wbuf, wbc, wdt, pcs, ext,
):
    g = pl.program_id(0)
    me_t, me_dp = sc[8], sc[9]

    @pl.when(g == 0)
    def _():
        wbc[...] = jnp.zeros_like(wbc)
        wdt[...] = jnp.zeros_like(wdt)

    place_rows(wbuf, am, me_dp, 0)
    place_rows(wbuf, bm, me_dp, 256, 0, 128)
    place_rows(wbuf, ar, me_dp, 384)
    place_rows(wbuf, br, me_dp, 640, 0, 128)
    count, brow = bm.shape[1:3]
    for c, blocks in ((0, bm), (1, br)):
        i = 2 * g + c
        t = i ^ me_t
        at = pl.ds(pl.multiple_of(128 * (t // 2), 128), 128)
        for n in range(count):
            start = pl.multiple_of((n ^ me_dp) * brow, brow) if count > 1 else 0
            r = pl.ds(start, brow)
            piece = blocks[0, n, :, 128:].astype(F32)
            lane = lane_iota(brow)
            own = pltpu.roll(jnp.where(lane < 64, piece, 0.0), 64 * (t % 2), 1)
            wbc[r, at] += own.astype(BF)
            own = pltpu.roll(jnp.where(lane >= 64, piece, 0.0), (i * 6 + 64) % 128, 1)
            wdt[r] += own.astype(BF)
    for n in range(3):
        cols = slice(256 * n, 256 * n + 256)
        inx[0, :, cols] = dot(nrm[...], wbuf[:, cols]).astype(BF)

    @pl.when(g == 1)
    def _():
        pcs[...] = dot(nrm[...], wbc[...])
        sin[0] = pcs[:, :128]
        sin[1] = pcs[:, 128:]
        pcs[0 : 4 * L, 0:128] = dot(nrm[0 : 4 * L], wdt[...])
        dtacc = pcs[0:L, 0:128]
        for s in range(1, 4):
            dtacc = dtacc + pltpu.roll(pcs[L * s : L * s + L, 0:128], s * SPAN, 1)
        dtb = jnp.zeros((1, 128), F32)
        alog = jnp.zeros((1, 128), F32)
        for i in range(4):
            for s in range(4):
                at = slice(384 * (i % 2), 384 * (i % 2) + 128)
                dtb += pltpu.roll(par[i // 2, 6:7, at], s * SPAN + i * 6, 1)
                alog += pltpu.roll(par[i // 2, 7:8, at], s * SPAN + i * 6, 1)
        raw = dtacc + dtb
        step = jnp.maximum(raw, 0.0) + jnp.log1p(jnp.exp(-jnp.abs(raw)))
        sig = 1.0 / (1.0 + jnp.exp(-raw))
        decay = step * -jnp.exp(alog)
        lower = jnp.where(
            lax.broadcasted_iota(jnp.int32, (L, L), 0) >= lax.broadcasted_iota(jnp.int32, (L, L), 1),
            1.0,
            0.0,
        )
        cum = dot_high(lower, decay)
        row = row_iota(L, 128)
        lane = lane_iota(L)
        slot = lane // SPAN
        tail = jnp.zeros((L, 128), F32)
        enters = jnp.zeros((L, 128), F32)
        follows = jnp.zeros((8, 128), F32)
        masks = jnp.ones((L, 128), F32)
        row_b = row_iota(L + 8, 128) - 8
        lane_b = lane_iota(L + 8)
        back_masks = jnp.ones((L + 8, 128), F32)
        slot8 = lane_iota(8) // SPAN
        inner_block = jnp.where(me_t > 0, 1.0, 0.0)
        back = lane % 4
        for s in range(4):
            fe, se = ends(sc, s)
            seg = seg_of(row, fe, se)
            last = seg_of(L - 1, fe, se)
            before = seg_of(-1, fe, se)
            here = slot == s
            tail = jnp.where(here & (seg == last), 1.0, tail)
            enters = jnp.where(here & (seg == before), inner_block, enters)
            follows = jnp.where(
                (slot8 == s), jnp.where(last == before, inner_block, 0.0), follows
            )
            masks = jnp.where((lane // 4 == s) & (seg != seg_of(row - back, fe, se)), 0.0, masks)
            cut = seg_of(row_b, fe, se) != seg_of(row_b + lane_b % 4, fe, se)
            back_masks = jnp.where((lane_b // 4 == s) & cut, 0.0, back_masks)
        cum_last = cum[L - 1 : L]
        cum2 = cum * LOG2E
        cumo[...] = cum2
        stepo[...] = step
        sigo[...] = sig
        eto[...] = jnp.exp(cum_last - cum) * tail
        reacho[...] = jnp.exp(cum) * enters
        decayo[...] = decay
        faco[...] = jnp.exp(cum_last) * follows
        uvo[...] = jnp.exp2(-jnp.abs(cum2 - cum2[127:128]))
        masko[...] = masks
        backo[...] = back_masks
        ct[...] = cum2.T
        for q, low_out in ((0, blow), (1, clow)):
            taps = [cbc[k : k + 1, tile(q)] for k in range(4)]

            @pl.loop(0, 4)
            def _(s):
                ext[0:8] = sin[q, pl.ds(pl.multiple_of(4 * L + 16 * s + 8, 8), 8)]
                ext[8:] = sin[q, rows_of(s)]
                acc = conv_forward(ext, taps, bbc[:, tile(q)], slot_masks(masko, s))
                sg = sigmoid(acc)
                low = acc * sg
                low_out[rows_of(s)] = low.astype(BF)
                dbc[q, rows_of(s)] = sg + low * (1.0 - sg)
                if q == 0:
                    bto[rows_of(s, 128)] = low.T.astype(BF)


def factor_rows(fac, g):
    rows = []
    for s in range(4):
        f = to_lane0(fac[...], s, g)
        rows.append(jnp.concatenate([pair_cols(f, 2 * j)[0:1] for j in range(6)], axis=1))
    f = jnp.concatenate(rows, axis=0)
    high = f.astype(BF).astype(F32)
    return jnp.concatenate([high, f - high, jnp.zeros((8, WIDE), F32)], axis=0).astype(BF)


def k2_body(g, sc, inx, halo, par, bt, stepp, etp, fac, mask, *rest):
    xo, xso, dslo, sto, xe, ext, spread, stepx, stepe = rest[-9:]
    s = pl.program_id(0)
    me_t = sc[8]

    @pl.when(s == 0)
    def _():
        spread[...] = head_spread()

    masks = slot_masks(mask, s)
    step = to_lane0(stepp[...], s, g)
    expand(stepx, step, spread)
    expand(stepe, step * to_lane0(etp[...], s, g), spread)
    for j in range(6):
        ext[j, 0:8] = halo[0, :, tile(j)].astype(F32)[8:]
        ext[j, 8:] = inx[0, :, tile(j)].astype(F32)
    for n in range(L // CHUNK):
        r = slice(CHUNK * n, CHUNK * n + CHUNK)
        mr = [m[r] for m in masks]
        for j in range(6):
            taps = [0.5 * par[0, k : k + 1, tile(j)] for k in range(4)]
            half = conv_forward(ext.at[j], taps, 0.5 * par[0, 4:5, tile(j)], mr, CHUNK * n, CHUNK)
            th = jnp.tanh(half)
            up = 1.0 + th
            act = half * up
            xo[0, r, tile(j)] = act.astype(BF)
            dslo[0, r, tile(j)] = ((0.5 * up) * (1.0 + half * (1.0 - th))).astype(BF)
            xso[0, r, tile(j)] = (act * stepx[r, tile(j)]).astype(BF)
            xe[r, tile(j)] = (act * stepe[r, tile(j)]).astype(BF)
    for c in range(2):
        sto[rows_of(s, 128), half_at(c, me_t)] = dot(
            bt[...], xe[:, 384 * c : 384 * c + 384]
        ).astype(BF)

    @pl.when(s == 3)
    def _():
        f = factor_rows(fac, g)
        for c in range(2):
            sto[512:528, half_at(c, me_t)] = f[:, 384 * c : 384 * c + 384]


def by_head(pair):
    lane = lane_iota(128)
    zero = jnp.zeros_like(pair)
    return jnp.concatenate(
        [jnp.where(lane < HD, pair, zero), jnp.where(lane < HD, zero, pair)], axis=0
    )


def diag_mask(d, fe, se, key_rows):
    r = lax.broadcasted_iota(jnp.int32, (128, 128), 0) + 128 * d
    c = lax.broadcasted_iota(jnp.int32, (128, 128), 1) + 128 * d
    order = (c >= r) if key_rows else (r >= c)
    return order & (seg_of(r, fe, se) == seg_of(c, fe, se))


def cross_half(fe, se, key_rows):
    r = lax.broadcasted_iota(jnp.int32, (128, 128), 0) + (0 if key_rows else 128)
    c = lax.broadcasted_iota(jnp.int32, (128, 128), 1) + (128 if key_rows else 0)
    return seg_of(r, fe, se) == seg_of(c, fe, se)


def k3_body(g, sc, xs, blow, clow, cump, uvp, ct, *rest):
    within, scores, cross, spread, uvx, tiles, cumx = rest[-7:]
    s = pl.program_id(0)
    fe, se = sc[2 * s], sc[2 * s + 1]

    @pl.when(s == 0)
    def _():
        spread[...] = head_spread()
        tiles[...] = tile_spread()


    for d in range(2):
        r = slice(128 * d, 128 * d + 128)
        scores[d] = jnp.where(diag_mask(d, fe, se, False), dot_nt(clow[r], blow[r]), 0.0)
    cross[...] = jnp.where(cross_half(fe, se, False), dot_nt(clow[128:], blow[:128]), 0.0).astype(BF)

    expand_tiles(cumx, to_lane0(cump[...], s, g), tiles)
    expand(uvx, to_lane0(uvp[...], s, g), spread)
    for j in range(6):
        for d in range(2):
            r = slice(128 * d, 128 * d + 128)
            pair = xs[0, r, tile(j)]
            parts = []
            for b in range(2):
                h = 2 * j + b
                gap = cumx[r, tile(h)] - ct[pl.ds(s * SPAN + g * 12 + h, 1), :][:, r]
                parts.append((jnp.exp2(jnp.minimum(gap, 0.0)) * scores[d]).astype(BF))
            total = dot(jnp.concatenate(parts, axis=1), by_head(pair))
            if d == 1:
                xv = (xs[0, :128, tile(j)].astype(F32) * uvx[:128, tile(j)]).astype(BF)
                total = total + dot(cross[...], xv) * uvx[128:, tile(j)]
            within[0, r, tile(j)] = total


def k4_body(sc, nrm, dbr, wzm, wzr, wom, wor, gate, dgn, wz, wo):
    g = pl.program_id(0)
    n = pl.program_id(1)
    me_dp = sc[9]

    @pl.when(n == 0)
    def _():
        place_pair(wz, wzm, wzr, me_dp)
        place_pair(wo, wom, wor, me_dp)

    cols = pl.ds(pl.multiple_of(n * 256, 256), 256)
    gate[0] = dot(nrm[0 : 4 * L], wz[:, cols]).astype(BF)
    dgn[0] = dot(dbr[...], wo[:, cols]).astype(BF)


def k5_body(
    sc, within, gate, dgn, x, r1, r2, r3, reachp, fac, clow, par, wom, wor, tok,
    out, gno, dgo, dyo, dpo, prevo, rowsum, dco, small,
    mo, sums, branch, wbuf, gnb, frow, dlow, seg_h, seg_l, pick, pv, spread, reachx,
):
    ph = pl.program_id(0)
    g = pl.program_id(1)
    s = pl.program_id(2)
    me_t, me_dp = sc[8], sc[9]
    r = rows_of(s)
    first = (g == 0) & (s == 0)

    @pl.when((ph == 0) & first)
    def _():
        rowsum[...] = jnp.zeros_like(rowsum)
        dco[...] = jnp.zeros_like(dco)
        small[...] = jnp.zeros_like(small)
        pick[...] = head_pick().astype(BF)
        spread[...] = head_spread()

    expand(reachx, to_lane0(reachp[...], s, g), spread)

    @pl.when(ph == 0)
    def _():
        srow = rows_of(s, 128)
        for c in range(2):
            at = half_at(c, me_t)
            frow[...] = r1[512:528, at].astype(F32)
            f = frow[pl.ds(s, 1)] + frow[pl.ds(s + 4, 1)]
            p = (
                jnp.where(me_t % 2 == 1, r1[srow, at].astype(F32), 0.0)
                + jnp.where(me_t == 2, r2[srow, at].astype(F32), 0.0)
                + jnp.where(me_t == 3, f * r3[srow, at].astype(F32), 0.0)
            )
            pv[:, 384 * c : 384 * c + 384] = p.astype(BF)
        prevo[g, srow] = pv[...]
        sq = jnp.zeros((L, 128), F32)
        dd = jnp.zeros((L, 128), F32)
        for j in range(6):
            from_prev = dot(clow[...], pv[:, tile(j)])
            mixed = (
                within[0, :, tile(j)]
                + reachx[:, tile(j)] * from_prev
                + par[0, 8:9, tile(j)] * x[0, :, tile(j)].astype(F32)
            )
            mo[g, r, tile(j)] = mixed
            gv = gate[0, :, tile(j)].astype(F32)
            gated = mixed * (gv * sigmoid(gv))
            sq = sq + gated * gated
            dd = dd + dgn[0, :, tile(j)].astype(F32) * par[0, 5:6, tile(j)] * gated
        sq = jnp.broadcast_to(jnp.sum(sq, axis=1, keepdims=True), (L, 128))
        dd = jnp.broadcast_to(jnp.sum(dd, axis=1, keepdims=True), (L, 128))

        @pl.when(g == 0)
        def _():
            sums[0, r] = sq
            sums[1, r] = dd

        @pl.when(g == 1)
        def _():
            sq2 = sums[0, r] + sq
            dd2 = sums[1, r] + dd
            gscale = lax.rsqrt(sq2 * (1.0 / INNER) + EPS)
            sums[0, r] = gscale
            sums[1, r] = gscale * gscale * gscale * (dd2 * (1.0 / INNER))

    @pl.when(ph == 1)
    def _():
        gscale = sums[0, r]
        coef = sums[1, r]
        srow = rows_of(s, 128)
        for j in range(6):
            gv = gate[0, :, tile(j)].astype(F32)
            mixed = mo[g, r, tile(j)]
            sg = sigmoid(gv)
            silu = gv * sg
            gated = mixed * silu
            gs = gated * gscale
            gain = par[0, 5:6, tile(j)]
            gn = (gs * gain).astype(BF)
            gno[0, :, tile(j)] = gn
            gnb[r, tile(j)] = gn
            d = dgn[0, :, tile(j)].astype(F32)
            small[g, 0:1, tile(j)] += jnp.sum(d * gs, axis=0, keepdims=True)
            dgated = gscale * (d * gain) - gated * coef
            dgo[0, :, tile(j)] = (dgated * mixed * (sg + silu * (1.0 - sg))).astype(BF)
            dy = (dgated * silu).astype(BF)
            dyo[0, :, tile(j)] = dy
            dyf = dy.astype(F32)
            dlow[:, tile(j)] = (dyf * reachx[:, tile(j)]).astype(BF)
            dx_skip = dyf * x[0, :, tile(j)].astype(F32)
            small[g, 1:2, tile(j)] += jnp.sum(dx_skip, axis=0, keepdims=True)
            v = dyf * mixed - par[0, 8:9, tile(j)] * dx_skip
            high = v.astype(BF)
            seg_h[:, tile(j)] = high
            seg_l[:, tile(j)] = (v - high.astype(F32)).astype(BF)
        seg = dot(seg_h[...], pick[...]) + dot(seg_l[...], pick[...])
        rowsum[...] += from_lane0(seg, s, g)
        dco[r] += dot_nt(dlow[...], prevo[g, srow])
        for c in range(2):
            dpo[srow, half_at(c, me_t)] = lax.dot_general(
                clow[...],
                dlow[:, 384 * c : 384 * c + 384],
                (((0,), (0,)), ((), ())),
                preferred_element_type=F32,
            ).astype(BF)

        @pl.when(s == 3)
        def _():
            f = factor_rows(fac, g)
            for c in range(2):
                dpo[512:528, half_at(c, me_t)] = f[:, 384 * c : 384 * c + 384]
            place_pair(wbuf, wom, wor, me_dp)

        @pl.when((s == 3) & (g == 0))
        def _():
            branch[...] = dot_nt(gnb[...], wbuf[...])

        @pl.when((s == 3) & (g == 1))
        def _():
            branch[...] += dot_nt(gnb[...], wbuf[...])

            @pl.loop(0, 16)
            def _(n):
                q = rows_of(n, 64)
                out[q] = (tok[q].astype(F32) + branch[q]).astype(BF)


def store_grad(ref, lead, me_dp, value_ref, first, width, at=0):
    count, rows = ref.shape[-3], ref.shape[-2]
    for n in range(count):
        place = n ^ me_dp if count > 1 else 0
        part = value_ref[n * rows : (n + 1) * rows, first : first + width].astype(BF)
        ref[lead + (place, slice(None), slice(at, at + width))] = part


def add_weighted(total, val, w, lead=()):
    @pl.loop(0, total.shape[0] // 64)
    def _(n):
        r = rows_of(n, 64)
        part = total[r]
        for j in range(w.shape[1] // 128):
            v = val[j, r] if lead else val[r, tile(j)]
            part = part + v * w[r, tile(j)].astype(F32)
        total[r] = part


def k6_body(sc, nt, dt, gn, dg, wzm, wzr, ok, os, zk, zs, ngz, val, wz):
    g = pl.program_id(0)
    me_dp = sc[9]
    place_pair(wz, wzm, wzr, me_dp)

    @pl.when(g == 0)
    def _():
        ngz[...] = jnp.zeros_like(ngz)

    for lhs, rhs, keep, send in ((dt, gn, ok, os), (nt, dg, zk, zs)):
        for n in range(3):
            cols = slice(256 * n, 256 * n + 256)
            val[:, cols] = dot(lhs[:, : 4 * L], rhs[0, :, cols])
        store_grad(keep, (0,), me_dp, val, 0, 384)
        store_grad(send, (0,), me_dp, val, 384, 384)
    add_weighted(ngz, val, wz)


def k7_body(g, sc, xs, dy, blow, clow, cump, uvp, ct, *rest):
    dxo, bco, pko, scores, cross, xvb, udb, spread, uvx, tiles, cumx, pick, corr = rest[-13:]
    s = pl.program_id(0)

    @pl.when(s == 0)
    def _():
        spread[...] = head_spread()
        tiles[...] = tile_spread()
        pick[...] = head_pick().astype(BF)
        pko[...] = jnp.zeros_like(pko)

    fe, se = sc[2 * s], sc[2 * s + 1]

    for d in range(2):
        r = slice(128 * d, 128 * d + 128)
        scores[d] = jnp.where(diag_mask(d, fe, se, True), dot_nt(blow[r], clow[r]), 0.0)
    cross[...] = jnp.where(cross_half(fe, se, True), dot_nt(blow[:128], clow[128:]), 0.0).astype(BF)

    expand_tiles(cumx, to_lane0(cump[...], s, g), tiles)
    expand(uvx, to_lane0(uvp[...], s, g), spread)
    totals = [jnp.zeros((128, 128), F32), jnp.zeros((128, 128), F32)]
    crossq = cross[...].astype(F32).T.astype(BF)
    for j in range(6):
        for d in range(2):
            r = slice(128 * d, 128 * d + 128)
            xp = xs[0, r, tile(j)]
            dyp = dy[0, r, tile(j)]
            grads = dot_nt(by_head(xp), dyp)
            parts = []
            for b in range(2):
                h = 2 * j + b
                gap = ct[pl.ds(s * SPAN + g * 12 + h, 1), :][:, r] - cumx[r, tile(h)]
                kern = jnp.exp2(jnp.minimum(gap, 0.0))
                totals[d] = totals[d] + grads[128 * b : 128 * b + 128] * kern
                parts.append((kern * scores[d]).astype(BF))
            dx = dot(jnp.concatenate(parts, axis=1), by_head(dyp))
            scaled = (xp if d == 0 else dyp).astype(F32) * uvx[r, tile(j)]
            low = scaled.astype(BF)
            diff = low.astype(F32) - scaled
            if d == 0:
                xvb[:, tile(j)] = low
                top, xdiff = dx, diff
            else:
                udb[:, tile(j)] = low
                off = dot(cross[...], low)
                dxo[0, r, tile(j)] = dx
                dxo[0, :128, tile(j)] = top + off * uvx[:128, tile(j)]
                corr[:128, tile(j)] = (xdiff * off).astype(BF)
                corr[128:, tile(j)] = (diff * dot(crossq, xvb[:, tile(j)])).astype(BF)
    dcr = dot_nt(xvb[...], udb[...])
    pko[...] += from_lane0(dot(corr[...], pick[...]), s, g)
    d0 = jnp.where(diag_mask(0, fe, se, True), totals[0], 0.0)
    d1 = jnp.where(diag_mask(1, fe, se, True), totals[1], 0.0)
    dl = jnp.where(cross_half(fe, se, True), dcr, 0.0)
    c0, c1, b0, b1 = clow[:128], clow[128:], blow[:128], blow[128:]
    bco[0, 0:128] = dot(d0.astype(BF), c0) + dot(dl.astype(BF), c1)
    bco[0, 128:] = dot(d1.astype(BF), c1)
    bco[1, 0:128] = dot(d0.T.astype(BF), b0)
    bco[1, 128:] = dot(d1.T.astype(BF), b1) + dot(dl.T.astype(BF), b0)


def k8_body(
    g, last, sc, nt, xs, dy, dsl, inx, halo, dxw, q1, q2, q3, prev, blow, stepp, etp, back, par,
    am, ar, bm, br, *rest,
):
    if last:
        (
            fac, sigp, decay, gain, ngz, nga, cbc, small1, small5, bc7a, bc7b, corr_a, corr_b, dc3, rowsum, sin, dbc, sega, enda, dba,
            keep, send, din, seg, end, dba_o, small, ngx, din5, skeep, ssend,
            val, hsum, gsc, gf, glow, xe, seg_h, seg_l, pick, wbuf, wpc, gbuf, pcs, pblk, sbc, spack, ub, ext, spread, stepx, etx,
        ) = rest
    else:
        (
            keep, send, din, seg, end, dba_o, small, ngx,
            val, hsum, gsc, gf, glow, xe, seg_h, seg_l, pick, wbuf, ub, ext, spread, stepx, etx,
        ) = rest
    s = pl.program_id(0)
    me_t, me_dp = sc[8], sc[9]
    r = rows_of(s)
    hrow = pl.ds(pl.multiple_of(4 * L + 16 * s, 16), 16)

    @pl.when(s == 0)
    def _():
        seg[...] = jnp.zeros_like(seg)
        end[...] = jnp.zeros_like(end)
        small[...] = jnp.zeros_like(small)
        pick[...] = head_pick().astype(BF)
        ext[:, 0:8] = jnp.zeros((6, 8, 128), F32)
        ext[:, 264:] = jnp.zeros((6, 8, 128), F32)
        spread[...] = head_spread()

    srow = rows_of(s, 128)
    for c in range(2):
        at = half_at(c, me_t)
        gf[...] = q1[512:528, at].astype(F32)
        f = gf[pl.ds(s, 1)] + gf[pl.ds(s + 4, 1)]
        v = (
            jnp.where(me_t % 2 == 0, q1[srow, at].astype(F32), 0.0)
            + jnp.where(me_t == 1, q2[srow, at].astype(F32), 0.0)
            + jnp.where(me_t == 0, f * q3[srow, at].astype(F32), 0.0)
        )
        gsc[:, 384 * c : 384 * c + 384] = v
        glow[:, 384 * c : 384 * c + 384] = v.astype(BF)
    for n in range(3):
        cols = slice(256 * n, 256 * n + 256)
        ub[:, cols] = dot(blow[...], glow[:, cols])
    masks = slot_masks(back, s)
    expand(stepx, to_lane0(stepp[...], s, g), spread)
    expand(etx, to_lane0(etp[...], s, g), spread)
    ends_row, gp_row = [], []
    for j in range(6):
        taps = [par[0, k : k + 1, tile(j)] for k in range(4)]
        xf = xs[0, :, tile(j)].astype(F32)
        ec = etx[:, tile(j)]
        eu = ub[:, tile(j)] * ec
        xe[:, tile(j)] = (xf * ec).astype(BF)
        ends_row.append(jnp.sum(xf * eu, axis=0, keepdims=True))
        gp_row.append(
            jnp.sum(gsc[:, tile(j)] * prev[0, srow, tile(j)].astype(F32), axis=0, keepdims=True)
        )
        dxi = dxw[0, :, tile(j)] + eu
        v = xf * dxi
        high = v.astype(BF)
        seg_h[:, tile(j)] = high
        seg_l[:, tile(j)] = (v - high.astype(F32)).astype(BF)
        dx = dxi * stepx[:, tile(j)] + par[0, 8:9, tile(j)] * dy[0, :, tile(j)].astype(F32)
        dconv = dx * dsl[0, :, tile(j)].astype(F32)
        small[4:5, tile(j)] += jnp.sum(dconv, axis=0, keepdims=True)
        v_ext = jnp.concatenate(
            [halo[0, :, tile(j)].astype(F32)[8:], inx[0, :, tile(j)].astype(F32)], axis=0
        )
        ext[j, 8:264] = dconv
        dv, tap_grads = conv_backward(ext.at[j], v_ext, taps, masks)
        for k in range(4):
            small[k : k + 1, tile(j)] += tap_grads[k]
        din[r, tile(j)] = dv[8:].astype(BF)
        din[hrow, tile(j)] = jnp.concatenate([jnp.zeros((8, 128), F32), dv[:8]], axis=0).astype(BF)
    seg[...] += from_lane0(dot(seg_h[...], pick[...]) + dot(seg_l[...], pick[...]), s, g)
    dba_o[r] = dot_nt(xe[...], glow[...])
    rows = jnp.concatenate(
        [
            jnp.concatenate(ends_row, axis=1),
            jnp.concatenate(gp_row, axis=1),
            jnp.zeros((6, WIDE), F32),
        ],
        axis=0,
    )
    end[...] += from_lane0(dot_high(rows, pick[...].astype(F32)), s, g)

    @pl.when(s == 3)
    def _():
        for n in range(3):
            cols = slice(256 * n, 256 * n + 256)
            hsum[...] = dot(nt[:, 4 * L :], din[4 * L :, cols])
            val[:, cols] = dot(nt[:, : 4 * L], din[: 4 * L, cols]) + hsum[...]
        store_grad(keep, (), me_dp, val, 0, 384)
        store_grad(send, (), me_dp, val, 384, 384)
        place_rows(wbuf, am, me_dp, 0)
        place_rows(wbuf, ar, me_dp, 384)
        place_rows(wbuf, bm, me_dp, 256, 0, 128, g if last else 0)
        place_rows(wbuf, br, me_dp, 640, 0, 128, g if last else 0)
        ngx[...] = ngz[...] + nga[...] if last else jnp.zeros_like(ngx)
        add_weighted(ngx, val, wbuf)

    if not last:
        return

    @pl.when(s == 3)
    def _():
        for q in range(2):
            taps = [cbc[k : k + 1, tile(q)] for k in range(4)]
            sbc[q] = jnp.zeros((8, 128), F32)

            @pl.loop(0, 4)
            def _(n):
                rn = rows_of(n)
                if q == 0:
                    grad = bc7a[0, rn] + bc7b[0, rn] + dba_o[rn] + dba[rn]
                else:
                    grad = bc7a[1, rn] + bc7b[1, rn] + dc3[rn]
                dconv = grad * dbc[q, rn]
                hn = pl.ds(pl.multiple_of(4 * L + 16 * n, 16), 16)
                v_ext = jnp.concatenate([sin[q, hn][8:], sin[q, rn]], axis=0)
                ext[q, 8:264] = dconv
                dv, tap_grads = conv_backward(ext.at[q], v_ext, taps, slot_masks(back, n))
                sbc[q, 4:5] += jnp.sum(dconv, axis=0, keepdims=True)
                for k in range(4):
                    sbc[q, k : k + 1] += tap_grads[k]
                gbuf[q, rn] = dv[8:]
                gbuf[q, hn] = jnp.concatenate([jnp.zeros((8, 128), F32), dv[:8]], axis=0)

        row = row_iota(L, 128)
        corr = corr_a[...] + corr_b[...]
        col = seg[...] + sega[...] + jnp.where(row < 128, corr, 0.0)
        ends_all = end[...] + enda[...]
        at_last = ends_all[0:1] + ends_all[1:2] * fac[0:1]
        dcum = rowsum[...] + jnp.where(row < 128, 0.0, corr) - col + jnp.where(row == L - 1, at_last, 0.0)
        upper = jnp.where(
            lax.broadcasted_iota(jnp.int32, (L, L), 0) <= lax.broadcasted_iota(jnp.int32, (L, L), 1),
            1.0,
            0.0,
        )
        dlog = dot_high(upper, dcum)
        alog = jnp.zeros((1, 128), F32)
        for i in range(4):
            at = slice(384 * (i % 2), 384 * (i % 2) + 128)
            for n in range(4):
                alog += pltpu.roll(par[i // 2, 7:8, at], n * SPAN + i * 6, 1)
        step_all, sig = stepp[...], sigp[...]
        ratio = jnp.where(step_all > 1e-30, sig / jnp.maximum(step_all, 1e-30), 1.0)
        ddt = ratio * col - sig * jnp.exp(alog) * dlog
        dts = jnp.concatenate(
            [
                jnp.sum(ddt, axis=0, keepdims=True),
                jnp.sum(dlog * decay[...], axis=0, keepdims=True),
                jnp.zeros((6, 128), F32),
            ],
            axis=0,
        )
        dts = dts + pltpu.roll(dts, 64, 1)
        dts = dts + pltpu.roll(dts, 32, 1)
        spack[...] = jnp.zeros_like(spack)
        for x in range(2):
            spack[x, 0:5] = (small if x == 0 else small1)[0:5]
            spack[x, 5:7] = small5[x, 0:2]
            for c in range(2):
                own = pltpu.roll(dts, (128 - 6 * (2 * x + c)) % 128, 1)
                own = jnp.where(lane_iota(8) < 6, own, 0.0)
                spack[x, 7:9, 384 * c : 384 * c + 128] = own[0:2]
            skeep[16 * x : 16 * x + 16] = spack[x, :, :384]
            ssend[16 * x : 16 * x + 16] = spack[x, :, 384:]
        ssend[32:40] = jnp.zeros((8, 384), F32)
        for q in range(2):
            ssend[32:37, tile(q)] = sbc[q, 0:5]
        for n in range(4):
            t = n ^ me_t
            turn = (64 * (t % 2)) % 128

            @pl.loop(0, 4)
            def _(m):
                rm = rows_of(m)
                lane = lane_iota(L)
                a = pltpu.roll(gbuf[t // 2, rm], turn, 1)
                d = pltpu.roll(ddt, (320 - m * SPAN - n * 6) % 128, 1)
                piece = jnp.where(lane < 64, a, jnp.where(lane < 70, d, 0.0))
                din5[rm, tile(n)] = piece.astype(BF)

            a = pltpu.roll(gbuf[t // 2, 4 * L :], turn, 1)
            din5[4 * L :, tile(n)] = jnp.where(lane_iota(64) < 64, a, 0.0).astype(BF)
        for n in range(2):
            cols = slice(256 * n, 256 * n + 256)
            hsum[...] = dot(nt[:, 4 * L :], din5[4 * L :, cols])
            v = dot(nt[:, : 4 * L], din5[: 4 * L, cols]) + hsum[...]
            pcs[2 * n] = v[:, :128]
            pcs[2 * n + 1] = v[:, 128:]
            place_rows(wpc, bm, me_dp, 256 * n, 128, 128, n)
            place_rows(wpc, br, me_dp, 256 * n + 128, 128, 128, n)
        add_weighted(ngx, pcs, wpc, (0,))
        gain_grad = (
            lax.dot_general(
                jnp.ones((8, 128), F32),
                ngx[...],
                (((1,), (1,)), ((), ())),
                preferred_element_type=F32,
                precision=lax.Precision.HIGHEST,
            )
            / gain[...]
        )
        ssend[37:38] = gain_grad[0:1, :384]
        ssend[38:39] = gain_grad[0:1, 384:]
        count, brow = keep.shape[0], keep.shape[1]
        for n in range(4):
            ref = keep if n % 2 == 0 else send
            at = slice(384 + 128 * (n // 2), 512 + 128 * (n // 2))
            if count == 1:
                ref[0, :, at] = pcs[n].astype(BF)
                continue
            t = n ^ me_t
            quarter = brow // 4
            for m in range(count):
                for c in range(4):
                    pblk[quarter * c : quarter * c + quarter] = pcs[
                        c ^ me_t, pl.ds(pl.multiple_of(brow * m + quarter * t, 8), quarter)
                    ]
                both = jnp.where(
                    lane_iota(brow) < 64, pblk[...], pcs[n, brow * m : brow * m + brow]
                )
                ref[m ^ me_dp, :, at] = both.astype(BF)


def k9z_body(sc, dg, wzm, wzr, dn, wz):
    place_pair(wz, wzm, wzr, sc[9])
    dn[...] = dot_nt(dg[0], wz[...]).astype(BF)


def k9_body(sc, din0, din1, din5, dna, dnb, am, ar, bm, br, out, dn, wx, wpc):
    g = pl.program_id(0)
    place_p1(wx, am, bm, ar, br, sc[9], wpc)

    @pl.when(g == 0)
    def _():
        dn[...] = dot_nt(din0[...], wx[...]) + dot_nt(din5[...], wpc[...])

    @pl.when(g == 1)
    def _():
        dn[...] += dot_nt(din1[...], wx[...])
        dn[...] += dot_nt(din5[...], wpc[...])

        @pl.loop(0, 16)
        def _(n):
            r = rows_of(n, 64)
            out[r] = (dn[r] + dna[r].astype(F32) + dnb[r].astype(F32)).astype(BF)

        out[4 * L :] = dn[4 * L :].astype(BF)


def k10_body(sc, dn, hr, tok, cot, gain, ig):
    s = pl.program_id(0)
    d = dn[...].astype(F32)
    extra = jnp.where(sc[8] < 3, hr[...].astype(F32), 0.0)
    width = d.shape[1]
    d = jnp.concatenate([d[: L - 16], d[L - 16 :] + extra], axis=0)
    tv = tok[...].astype(F32)
    r = lax.rsqrt(jnp.mean(tv * tv, axis=-1, keepdims=True) + EPS)
    tr = tv * r
    gd = gain[...] * d
    inner = jnp.sum(gd * tr, axis=-1, keepdims=True) * (1.0 / width)
    keep = row_iota(L, 1) < sc[2 * s + 1]
    res = jnp.where(keep, cot[...].astype(F32), 0.0)
    ig[...] = (res + r * (gd - tr * inner)).astype(BF)


def FINAL_SHAPES(dim, cols, heads, state, shard, tcount):
    return [
        (dim,), (shard, cols), (shard // tcount, 2 * state), (heads, shard), (4, cols), (cols,),
        (4, 2 * state), (2 * state,), (heads,), (heads,), (heads,), (cols,),
    ]


def k11_body(
    sc, va, vr, both, got,
    ngain, wx, wbc, wdt, cx, bx, cb, bb, dtb, alog, skip, og,
    g, sm,
):
    g[...] = va[...].astype(F32) + vr[...].astype(F32)
    sm[...] = both[...] + got[...]
    wx[...] = g[:, :384]
    quarter = g.shape[0] // 4
    lane = lane_iota(quarter)
    parts = [g[quarter * c : quarter * c + quarter, 384:512] for c in range(4)]
    for t in range(2):
        wbc[:, tile(t)] = jnp.where(lane < 64, parts[2 * t], pltpu.roll(parts[2 * t + 1], 64, 1))
    wdt[...] = pltpu.roll(g[:, 384:512], 64, 1).T[: wdt.shape[0]]
    cx[...] = sm[0:4]
    bx[...] = sm[4]
    og[...] = sm[5]
    r = lax.broadcasted_iota(jnp.int32, (384, 128), 0)
    c = lax.broadcasted_iota(jnp.int32, (384, 128), 1)
    sums = dot_high(sm[0:8], jnp.where(c == r // HD, 1.0, 0.0))
    skip[...] = sums[6, : skip.shape[0]]
    dtb[...] = sm[7, : dtb.shape[0]]
    alog[...] = sm[8, : alog.shape[0]]
    cb[...] = sm[16:20, : cb.shape[1]]
    bb[...] = sm[20, : bb.shape[0]]
    half = sm.shape[1]
    ngain[0:half] = sm[21]
    ngain[half : 2 * half] = sm[22]


def full(shape):
    return pl.BlockSpec(shape, lambda *a: (0,) * len(shape))


def call(body, grid, in_specs, out_specs, out_shapes, scratch, cost, name, aliases=None, vmem_mib=VMEM_MIB):
    flops, moved = cost
    return pl.pallas_call(
        body,
        grid_spec=pltpu.PrefetchScalarGridSpec(
            num_scalar_prefetch=1,
            grid=grid,
            in_specs=in_specs,
            out_specs=out_specs,
            scratch_shapes=scratch,
        ),
        out_shape=out_shapes,
        compiler_params=pltpu.CompilerParams(vmem_limit_bytes=vmem_mib * 2**20),
        cost_estimate=pl.CostEstimate(flops=flops, bytes_accessed=moved, transcendentals=0),
        input_output_aliases=aliases or {},
        name=name,
    )


def sds(shape, dtype):
    return pltpu.HBM(shape, dtype)


def anywhere(count):
    return [pl.BlockSpec(memory_space=pl.ANY)] * count


def flip(value, axis, bit):
    count = lax.axis_size(axis)
    return lax.ppermute(value, axis, [(a, a ^ bit) for a in range(count)])


def meet(*values):
    return lax.optimization_barrier(values)


def per_device(
    tokens, lengths, cotangent, norm_gain, w_z, w_x, w_bc, w_dt, conv_x, bias_x, conv_bc, bias_bc,
    dt_bias, a_log, skip_d, out_gain, w_out,
):
    tcount = lax.axis_size("tensor")
    dpcount = lax.axis_size("dp")
    me_t = lax.axis_index("tensor")
    me_dp = lax.axis_index("dp")
    slots, own_len, dim = tokens.shape
    rows = slots * own_len
    shard = w_z.shape[0]
    cols = w_z.shape[1]
    heads = w_dt.shape[1]
    fast = shard % 32 == 0 and dpcount & (dpcount - 1) == 0 and dpcount >= 8
    count = dpcount if fast else 1
    brow = shard if fast else dim

    first = lengths[:, 0] - me_t * own_len
    second = first + lengths[:, 1]
    sc = jnp.concatenate(
        [
            jnp.stack([first, second], axis=1).reshape(-1),
            jnp.stack([me_t, me_dp]),
            jnp.zeros((6,), jnp.int32),
        ]
    ).astype(jnp.int32)
    tok = tokens.reshape(rows, dim)
    cot = cotangent.reshape(rows, dim)

    bq = w_bc.shape[1] // tcount
    state = w_bc.shape[1] // 2
    own_bc = lax.dynamic_slice_in_dim(w_bc, me_t * bq, bq, 1)
    p1 = jnp.concatenate(
        [w_x, own_bc, w_dt, jnp.zeros((shard, 128 - bq - heads), BF)], axis=1
    )
    tail = tokens[:, own_len - 16 :, :].reshape(slots * 16, dim)
    def add_y(v, at):
        return jnp.stack([v, flip(v, "dp", 1)], axis=at)

    def add_x(v):
        return jnp.stack([v, flip(v, "tensor", 2)], axis=0)

    def blocks(v):
        return v.reshape(2, count, brow, v.shape[-1])

    def core(v):
        return flip(v, "tensor", 1)

    def middle(v):
        return lax.ppermute(v, "tensor", [(0, 0), (1, 2), (2, 1), (3, 3)])

    par, gain, bbc = call(
        k0_body,
        (1,),
        [
            full(v.shape)
            for v in (conv_x, bias_x, out_gain, dt_bias, a_log, skip_d, norm_gain, bias_bc)
        ],
        [full((16, cols)), full((1, dim)), full((1, 2 * state))],
        [sds((16, cols), F32), sds((1, dim), F32), sds((1, 2 * state), F32)],
        [pltpu.VMEM((8, 128), F32)],
        (1, 1),
        "parameters",
        vmem_mib=K5_MIB,
    )(sc, conv_x, bias_x, out_gain, dt_bias, a_log, skip_d, norm_gain, bias_bc)

    def prepare(halo):
        return call(
            prepare_body,
            (1,),
            [full((rows, dim)), full((64, dim)), full((rows, dim)), full((1, dim))],
            [full((rows + 64, dim)), full((dim, rows + 64)), full((rows, dim)), full((dim, rows))],
            [
                sds((rows + 64, dim), BF),
                sds((dim, rows + 64), BF),
                sds((rows, dim), BF),
                sds((dim, rows), BF),
            ],
            [],
            (1, 1),
            "prepare",
        )(sc, tok, halo, cot, gain)

    def grown(v, got, at):
        v = jnp.stack([v, got], axis=at)
        return v.reshape(v.shape[: at - 1] + (-1,) + v.shape[at + 1 :])

    if fast:
        v = p1[None]
        w2 = jnp.stack([w_z, w_out])[None]
        bit = dpcount // 2
        got = flip(v, "dp", bit)
        got, w2, sc, par, tail, gain = meet(got, w2, sc, par, tail, gain)
        v = grown(v, got, 1)
        while bit > 4:
            bit //= 2
            v = grown(v, flip(v, "dp", bit), 1)
            w2 = grown(w2, flip(w2, "dp", 2 * bit), 1)
        halo = lax.ppermute(tail, "tensor", [(a, (a + 1) % tcount) for a in range(tcount)])
        got, w2, parx, halo = meet(flip(v, "dp", 2), w2, flip(par, "tensor", 2), halo)
        par = jnp.stack([par, parx], axis=0)
        v = grown(v, got, 1)
        az, bz = v[..., :256], v[..., 256:]
        ax, by, parc, w2z = meet(
            flip(az, "tensor", 2), flip(bz, "dp", 1), core(par), flip(w2, "dp", 4)
        )
        w2 = grown(w2, w2z, 1)
        par = jnp.concatenate([par, parc], axis=-1)
        ax = jnp.stack([az, ax], axis=0)
        by = jnp.stack([bz, by], axis=1)
        nrm, nt, dbr, dt = prepare(halo)
        ay, bx, w2z, par, nrm = meet(
            flip(ax, "dp", 1), flip(by, "tensor", 2), flip(w2, "dp", 2), par, nrm
        )
        w2 = grown(w2, w2z, 1)
        wam = blocks(jnp.stack([ax, ay], axis=2))
        wbm = blocks(jnp.stack([by, bx], axis=0))
        zz, oz = w2[:, 0], w2[:, 1]
        zx, oy = flip(zz, "tensor", 2), flip(oz, "dp", 1)
        war, wbr = core(wam), core(wbm)
    else:
        halo = lax.ppermute(tail, "tensor", [(a, (a + 1) % tcount) for a in range(tcount)])
        par = add_x(par)
        par = jnp.concatenate([par, core(par)], axis=-1)
        z1 = lax.all_gather(p1, "dp", axis=0, tiled=True)[None]
        wam = add_x(z1[..., :256])
        wbm = add_x(z1[..., 256:])
        war, wbr = core(wam), core(wbm)
        nrm, nt, dbr, dt = prepare(halo)

    srows = slots * state
    wide = 2 * cols
    erows = rows + 64
    p1block = (1, count, brow, 256)
    wblock = (1, count, brow, cols)
    vmem = pltpu.VMEM

    def w_g(g, *a):
        return (g, 0, 0, 0)

    inx, blow, clow, bt, sin, dbc, cump, stepp, sigp, etp, reachp, decay, fac, uvp, mask, back, ct = call(
        k1_body,
        (2,),
        [full((erows, dim))]
        + [pl.BlockSpec(p1block, w_g)] * 4
        + [full((2, 16, wide)), full((4, 2 * state)), full((1, 2 * state))],
        [
            pl.BlockSpec((1, erows, wide), lambda g, sc: (g, 0, 0)),
            full((rows, state)),
            full((rows, state)),
            full((srows, L)),
            full((2, erows, state)),
            full((2, rows, state)),
        ]
        + [full((L, 128))] * 6
        + [full((8, 128)), full((L, 128)), full((L, 128)), full((L + 8, 128)), full((128, L))],
        [
            sds((2, erows, wide), BF),
            sds((rows, state), BF),
            sds((rows, state), BF),
            sds((srows, L), BF),
            sds((2, erows, state), F32),
            sds((2, rows, state), F32),
        ]
        + [sds((L, 128), F32)] * 6
        + [sds((8, 128), F32), sds((L, 128), F32), sds((L, 128), F32), sds((L + 8, 128), F32)]
        + [sds((128, L), F32)],
        [
            vmem((dim, wide), BF),
            vmem((dim, 256), BF),
            vmem((dim, 128), BF),
            vmem((erows, 256), F32),
            vmem((L + 8, 128), F32),
        ],
        (int(7e9), int(2e7)),
        "projections",
    )(sc, nrm, wam, war, wbm, wbr, par, conv_bc, bbc)

    def gs(g, s, sc):
        return (g, s, 0)

    def halo_gs(g, s, sc):
        return (g, rows // 16 + s, 0)

    def by_s(g, s, sc):
        return (s, 0)

    def mirror(g, sc):
        return (0, g ^ (sc[8] // 2))

    group = (1, L, wide)

    def gsel(g):
        return lambda s, sc: (g, s, 0)

    def conv_and_states(g, inx, kept):
        return call(
            functools.partial(k2_body, g),
            (slots,),
            [
                pl.BlockSpec(group, gsel(g)),
                pl.BlockSpec((1, 16, wide), lambda s, sc: (g, rows // 16 + s, 0)),
                pl.BlockSpec((1, 16, wide), lambda s, sc: (g, 0, 0)),
                pl.BlockSpec((state, L), lambda s, sc: (s, 0)),
                full((L, 128)),
                full((L, 128)),
                full((8, 128)),
                full((L, 128)),
            ]
            + anywhere(len(kept)),
            [pl.BlockSpec(group, gsel(g))] * 3
            + [pl.BlockSpec((srows + 16, wide), lambda s, sc: mirror(g, sc))],
            [sds((2, rows, wide), BF)] * 3 + [sds((srows + 16, 2 * wide), BF)],
            [
                vmem((L, wide), BF),
                vmem((6, L + 8, 128), F32),
                vmem((256, wide), BF),
                vmem((L, wide), F32),
                vmem((L, wide), F32),
            ],
            (int(5e9) if g else 1, int(2e7) if g else 1),
            "conv_and_states_%d" % g,
            {9 + n: n for n in range(len(kept))},
        )(sc, inx, inx, par, bt, stepp, etp, fac, mask, *kept)

    if fast:
        inx0, zx, oy = meet(inx, zx, oy)
        zx = jnp.stack([zz, zx], axis=0)
        oy = jnp.stack([oz, oy], axis=1)
        zy, ox = flip(zx, "dp", 1), flip(oy, "tensor", 2)
        xl, xs, dsl, st = conv_and_states(1, inx, conv_and_states(0, inx0, []))
        st, zy, ox = meet(st, zy, ox)
        wzm = blocks(jnp.stack([zx, zy], axis=2))
        wom = blocks(jnp.stack([oy, ox], axis=0))
        wzr, wor = core(wzm), core(wom)
    else:
        xl, xs, dsl, st = conv_and_states(1, inx, conv_and_states(0, inx, []))
        wzm = add_x(lax.all_gather(w_z, "dp", axis=0, tiled=True)[None])
        wom = add_x(lax.all_gather(w_out, "dp", axis=0, tiled=True)[None])
        wzr, wor = core(wzm), core(wom)

    def end_state(mine, one):
        f = mine[srows : srows + 4].astype(F32) + mine[srows + 4 : srows + 8].astype(F32)
        width = mine.shape[1]
        end = mine[:srows].astype(F32).reshape(slots, state, width) + f[:, None] * one[
            :srows
        ].astype(F32).reshape(slots, state, width)
        return end.astype(BF).reshape(srows, width)

    r1 = core(st)
    end = end_state(st, r1)
    r2 = middle(end)
    xs3, _ = meet(xs, end)

    def within_of(g, kept):
        return call(
            functools.partial(k3_body, g),
            (slots,),
            [
                pl.BlockSpec(group, gsel(g)),
                pl.BlockSpec((L, state), lambda s, sc: (s, 0)),
                pl.BlockSpec((L, state), lambda s, sc: (s, 0)),
                full((L, 128)),
                full((L, 128)),
                full((128, L)),
            ]
            + anywhere(len(kept)),
            pl.BlockSpec(group, gsel(g)),
            sds((2, rows, wide), F32),
            [
                vmem((2, 128, 128), F32),
                vmem((128, 128), BF),
                vmem((256, wide), BF),
                vmem((L, wide), F32),
                vmem((256, 2 * wide), BF),
                vmem((L, 2 * wide), F32),
            ],
            (int(5e9), int(1e7)),
            "within_%d" % g,
            {7 + n: n for n in range(len(kept))},
        )(sc, xs3, blow, clow, cump, uvp, ct, *kept)

    within = within_of(1, [within_of(0, [])])
    nrm4, within = meet(nrm, within)

    gate, dgn = call(
        k4_body,
        (2, 3),
        [full((erows, dim)), full((rows, dim))] + [pl.BlockSpec(wblock, w_g)] * 4,
        [pl.BlockSpec((1, rows, 256), lambda g, n, sc: (g, 0, n))] * 2,
        [sds((2, rows, wide), BF)] * 2,
        [vmem((dim, wide), BF), vmem((dim, wide), BF)],
        (int(5e9), int(2e7)),
        "gate_and_out_backward",
    )(sc, nrm4, dbr, wzm, wzr, wom, wor)

    gate, r2 = meet(gate, r2)
    r3 = core(r2)

    def p_gs(phase):
        def index(p, g, s, sc):
            return (
                jnp.where(p == phase, g, 0 if phase else 1),
                jnp.where(p == phase, s, 0 if phase else slots - 1),
                0,
            )

        return index

    def p_mirror(phase):
        def index(p, g, s, sc):
            return mirror(jnp.where(p == phase, g, 0 if phase else 1), sc)

        return index

    def pgs(p, g, s, sc):
        return (g, s, 0)

    def p_w(p, g, s, sc):
        return (jnp.where(p == 1, g, 0), 0, 0, 0)

    out, gn, dg, dy, dp, prev, rowsum, dc5, small5 = call(
        k5_body,
        (2, 2, slots),
        [
            pl.BlockSpec(group, p_gs(0)),
            pl.BlockSpec(group, pgs),
            pl.BlockSpec(group, pgs),
            pl.BlockSpec(group, pgs),
            pl.BlockSpec((srows + 16, wide), p_mirror(0)),
            pl.BlockSpec((srows, wide), p_mirror(0)),
            pl.BlockSpec((srows, wide), p_mirror(0)),
            full((L, 128)),
            full((8, 128)),
            pl.BlockSpec((L, state), lambda p, g, s, sc: (s, 0)),
            pl.BlockSpec((1, 16, wide), lambda p, g, s, sc: (g, 0, 0)),
            pl.BlockSpec(wblock, p_w),
            pl.BlockSpec(wblock, p_w),
            full((rows, dim)),
        ],
        [
            full((rows, dim)),
            pl.BlockSpec(group, p_gs(1)),
            pl.BlockSpec(group, p_gs(1)),
            pl.BlockSpec(group, p_gs(1)),
            pl.BlockSpec((srows + 16, wide), p_mirror(1)),
            full((2, srows, wide)),
            full((L, 128)),
            full((rows, state)),
            full((2, 8, wide)),
        ],
        [
            sds((rows, dim), BF),
            sds((2, rows, wide), BF),
            sds((2, rows, wide), BF),
            sds((2, rows, wide), BF),
            sds((srows + 16, 2 * wide), BF),
            sds((2, srows, wide), BF),
            sds((L, 128), F32),
            sds((rows, state), F32),
            sds((2, 8, wide), F32),
        ],
        [
            vmem((2, rows, wide), F32),
            vmem((2, rows, 128), F32),
            vmem((rows, dim), F32),
            vmem((dim, wide), BF),
            vmem((rows, wide), BF),
            vmem((16, cols), F32),
            vmem((L, wide), BF),
            vmem((L, wide), BF),
            vmem((L, wide), BF),
            vmem((wide, 128), BF),
            vmem((state, wide), BF),
            vmem((256, wide), BF),
            vmem((L, wide), F32),
        ],
        (int(1.5e10), int(4e7)),
        "gated_norm",
        vmem_mib=50,
    )(sc, within, gate, dgn, xl, r1, r2, r3, reachp, fac, clow, par, wom, wor, tok)

    q1 = core(dp)

    gshape = (2, count, brow, cols)
    ok, osend, zk, zsend, ngz = call(
        k6_body,
        (2,),
        [full((dim, erows)), full((dim, rows))]
        + [pl.BlockSpec((1, rows, wide), lambda g, sc: (g, 0, 0))] * 2
        + [pl.BlockSpec(wblock, w_g)] * 2,
        [pl.BlockSpec((1,) + gshape[1:], w_g)] * 4 + [full((dim, 128))],
        [sds(gshape, BF)] * 4 + [sds((dim, 128), F32)],
        [vmem((dim, wide), F32), vmem((dim, wide), BF)],
        (int(5e9), int(2e7)),
        "outer_weight_grads",
        vmem_mib=K5_MIB,
    )(sc, nt, dt, gn, dg, wzm, wzr)

    osend, q1 = meet(osend, q1)
    dy1, end = meet(dy, end_state(dp, q1))
    q2 = middle(end)

    def summed(a, b):
        return (a.astype(F32) + b.astype(F32)).astype(BF)

    def reduce_step(v, axis, mesh_axis, bit):
        keep = lax.index_in_dim(v, 0, axis, False)
        send = lax.index_in_dim(v, 1, axis, False)
        return summed(keep, flip(send, mesh_axis, bit))

    def reduce_x(v, axis):
        return reduce_step(v, axis, "tensor", 2)

    def reduce_dp(v, bit):
        v = v.reshape((v.shape[0] // 2, 2) + v.shape[1:])
        return reduce_step(v, 1, "dp", bit)

    def finish(v, bit):
        while bit < dpcount:
            v = reduce_dp(v, bit)
            bit *= 2
        return v[0].astype(F32)

    def reduce_slow(v):
        v = v.reshape(dpcount, shard, v.shape[-1])
        got = lax.all_to_all(v, "dp", split_axis=0, concat_axis=0, tiled=True)
        return got.astype(F32).sum(axis=0)

    def reduce_core(keep, send):
        return summed(keep, core(send))

    if fast:
        vw = summed(jnp.stack([ok, zk]), jnp.stack([core(osend), core(zsend)]))
        vw = vw.reshape((2, 2, count // 2, 2, brow, cols))
        vwr = flip(vw[:, :, :, 1], "dp", 1)
    else:
        grad_w_out = reduce_slow(reduce_x(reduce_core(ok, osend), 0)[0])
        grad_w_z = reduce_slow(reduce_x(reduce_core(zk, zsend), 0)[0])

    def within_backward(g, dy, kept):
        return call(
            functools.partial(k7_body, g),
            (slots,),
            [
                pl.BlockSpec(group, gsel(g)),
                pl.BlockSpec(group, gsel(g)),
                pl.BlockSpec((L, state), lambda s, sc: (s, 0)),
                pl.BlockSpec((L, state), lambda s, sc: (s, 0)),
                full((L, 128)),
                full((L, 128)),
                full((128, L)),
            ]
            + anywhere(len(kept)),
            [
                pl.BlockSpec(group, gsel(g)),
                pl.BlockSpec((2, L, state), lambda s, sc: (0, s, 0)),
                full((L, 128)),
            ],
            [sds((2, rows, wide), F32), sds((2, rows, state), F32), sds((L, 128), F32)],
            [
                vmem((2, 128, 128), F32),
                vmem((128, 128), BF),
                vmem((128, wide), BF),
                vmem((128, wide), BF),
                vmem((256, wide), BF),
                vmem((L, wide), F32),
                vmem((256, 2 * wide), BF),
                vmem((L, 2 * wide), F32),
                vmem((wide, 128), BF),
                vmem((L, wide), BF),
            ],
            (int(1e10) if g else 1, int(2e7) if g else 1),
            "within_backward_%d" % g,
            {8 + n: n for n in range(len(kept))},
        )(sc, xs, dy, blow, clow, cump, uvp, ct, *kept)

    dxw, bc7a, corr_a = within_backward(1, dy1, [])
    dxw, bc7b, corr_b = within_backward(0, dy, [dxw])

    def states_backward(g, last, nt, extra_in, extra_specs):
        width = cols + 256 if last else cols
        gshape = (count, brow, width)

        def at(s, sc):
            return (g, s, 0)

        in_specs = [
            full((dim, erows)),
            pl.BlockSpec(group, at),
            pl.BlockSpec(group, at),
            pl.BlockSpec(group, at),
            pl.BlockSpec(group, at),
            pl.BlockSpec((1, 16, wide), lambda s, sc: (g, rows // 16 + s, 0)),
            pl.BlockSpec(group, at),
            pl.BlockSpec((srows + 16, wide), lambda s, sc: mirror(g, sc)),
            pl.BlockSpec((srows, wide), lambda s, sc: mirror(g, sc)),
            pl.BlockSpec((srows, wide), lambda s, sc: mirror(g, sc)),
            pl.BlockSpec((1, srows, wide), lambda s, sc: (g, 0, 0)),
            pl.BlockSpec((L, state), lambda s, sc: (s, 0)),
            full((L, 128)),
            full((L, 128)),
            full((L + 8, 128)),
            full((2, 16, wide)) if last else pl.BlockSpec((1, 16, wide), lambda s, sc: (g, 0, 0)),
            pl.BlockSpec(p1block, lambda s, sc: (g, 0, 0, 0)),
            pl.BlockSpec(p1block, lambda s, sc: (g, 0, 0, 0)),
        ]
        if last:
            in_specs += [full((2,) + p1block[1:])] * 2
        else:
            in_specs += [pl.BlockSpec(p1block, lambda s, sc: (g, 0, 0, 0))] * 2
        in_specs += extra_specs
        outs = [
            (gshape, BF),
            (gshape, BF),
            ((erows, wide), BF),
            ((L, 128), F32),
            ((8, 128), F32),
            ((rows, state), F32),
            ((8, wide), F32),
            ((dim, 128), F32),
        ]
        scratch = [
            vmem((dim, wide), F32),
            vmem((dim, 256), F32),
            vmem((state, wide), F32),
            vmem((16, cols), F32),
            vmem((state, wide), BF),
            vmem((L, wide), BF),
            vmem((L, wide), BF),
            vmem((L, wide), BF),
            vmem((wide, 128), BF),
            vmem((dim, wide), BF),
        ]
        if last:
            outs += [((erows, 512), BF), ((32, cols), F32), ((40, cols), F32)]
            scratch += [
                vmem((dim, 512), BF),
                vmem((2, erows, state), F32),
                vmem((4, dim, 128), F32),
                vmem((brow, 128), F32),
                vmem((2, 8, state), F32),
                vmem((2, 16, wide), F32),
            ]
        scratch += [vmem((L, wide), F32), vmem((6, L + 16, 128), F32), vmem((256, wide), BF)]
        scratch += [vmem((L, wide), F32), vmem((L, wide), F32)]
        return call(
            functools.partial(k8_body, g, last),
            (slots,),
            in_specs,
            [full(shape) for shape, _ in outs],
            [sds(shape, dtype) for shape, dtype in outs],
            scratch,
            (int(1e10), int(2e7)),
            "states_backward_%d" % g,
        )(sc, nt, xs, dy, dsl, inx, inx, dxw, q1, q2, q3, prev, blow, stepp, etp, back, par, wam, war, wbm, wbr, *extra_in)

    def normed_grad_z(g, dg):
        return call(
            k9z_body,
            (1,),
            [
                pl.BlockSpec((1, rows, wide), lambda i, sc: (g, 0, 0)),
                pl.BlockSpec(wblock, lambda i, sc: (g, 0, 0, 0)),
                pl.BlockSpec(wblock, lambda i, sc: (g, 0, 0, 0)),
            ],
            full((rows, dim)),
            sds((rows, dim), BF),
            [vmem((dim, wide), BF)],
            (1, 1),
            "normed_grad_z%d" % g,
        )(sc, dg, wzm, wzr)

    dga, dxw = meet(dg, dxw)
    dna = normed_grad_z(1, dga)
    dnb = normed_grad_z(0, dga)
    if fast:
        dxw, q2, dna, dnb, vwr = meet(dxw, q2, dna, dnb, vwr)
        vw = summed(vw[:, :, :, 0], vwr)
        vwr = flip(vw[:, 1], "tensor", 2)
    else:
        dxw, q2, dna, dnb = meet(dxw, q2, dna, dnb)
    q3 = core(q2)
    ka, sa, din1, seg1, end1, dba1, small1, nga = states_backward(1, False, nt, [], [])
    if fast:
        sa, vwr = meet(sa, vwr)
        vw = summed(vw[:, 0], vwr).reshape((2, count // 4, 2, brow, cols))
        vwr = flip(vw[:, :, 1], "dp", 2)
    sar = core(sa)
    nt0, sar = meet(nt, sar)
    va = summed(ka, sar)
    xa = flip(va, "tensor", 2)
    ks, ss, din0, _, _, _, _, _, din5, skeep, ssend = states_backward(
        0,
        True,
        nt0,
        [fac, sigp, decay, gain, ngz, nga, conv_bc, small1, small5, bc7a, bc7b, corr_a, corr_b, dc5, rowsum, sin, dbc, seg1, end1, dba1],
        [
            full((8, 128)),
            full((L, 128)),
            full((L, 128)),
            full((1, dim)),
            full((dim, 128)),
            full((dim, 128)),
            full((4, 2 * state)),
            full((8, wide)),
            full((2, 8, wide)),
            full((2, rows, state)),
            full((2, rows, state)),
            full((L, 128)),
            full((L, 128)),
            full((rows, state)),
            full((L, 128)),
            full((2, erows, state)),
            full((2, rows, state)),
            full((L, 128)),
            full((8, 128)),
            full((rows, state)),
        ],
    )

    if fast:
        ss, xa, vwr = meet(ss, xa, vwr)
        vw = summed(vw[:, :, 0], vwr).reshape((2, count // 8, 2, brow, cols))
        vwr = flip(vw[:, :, 1], "dp", 4)
    din0, ssr, got = meet(din0, core(ss), core(ssend))
    own = (skeep + got[:32]).reshape(2, 16, cols)
    flat = ssend[32:] + got[32:]
    vb = summed(ks[..., cols:], ssr[..., cols:])
    px = flip(vb[..., 128:], "tensor", 2)
    vx = (ks[..., :cols].astype(F32) + ssr[..., :cols].astype(F32) + xa.astype(F32)).astype(BF)
    if fast:
        vx = vx.reshape((count // 2, 2) + vx.shape[1:])
        vxr = flip(vx[:, 1], "dp", 1)
    both = jnp.concatenate([own[0], flat], axis=0)
    got = flip(jnp.concatenate([own[1], flat], axis=0), "tensor", 2)

    dn = call(
        k9_body,
        (2,),
        [
            full((erows, wide)),
            full((erows, wide)),
            pl.BlockSpec((erows, 256), lambda g, sc: (0, g)),
            full((rows, dim)),
            full((rows, dim)),
        ]
        + [pl.BlockSpec(p1block, w_g)] * 4,
        full((erows, dim)),
        sds((erows, dim), BF),
        [vmem((erows, dim), F32), vmem((dim, wide), BF), vmem((dim, 256), BF)],
        (int(6e9), int(2e7)),
        "normed_grad",
    )(sc, din0, din1, din5, dna, dnb, wam, war, wbm, wbr)

    if fast:
        dn, px, vxr, got, vwr = meet(dn, px, vxr, got, vwr)
        vw = summed(vw[:, :, 0], vwr)
        grad_w_out, grad_w_z = finish(vw[0], 8), finish(vw[1], 8)
        vx = summed(vx[:, 0], vxr)
        vp = summed(vb[..., :128], px)
        vp = vp.reshape((count // 2, 2) + vp.shape[1:])
        vpr = flip(vp[:, 1], "dp", 1)
        both = both + got
        got = flip(both, "dp", 1)
    hr = lax.ppermute(dn[rows:], "tensor", [((a + 1) % tcount, a) for a in range(tcount)])
    if fast:
        hr, vpr, got = meet(hr, vpr, got)
        v1 = jnp.concatenate([vx, summed(vp[:, 0], vpr)], axis=-1)
        v1 = v1.reshape((count // 4, 2) + v1.shape[1:])
        v1r = flip(v1[:, 1], "dp", 2)
        both = both + got
        got = flip(both, "dp", 2)

    ig = call(
        k10_body,
        (slots,),
        [
            pl.BlockSpec((L, dim), lambda s, sc: (s, 0)),
            pl.BlockSpec((16, dim), lambda s, sc: (s, 0)),
            pl.BlockSpec((L, dim), lambda s, sc: (s, 0)),
            pl.BlockSpec((L, dim), lambda s, sc: (s, 0)),
            full((1, dim)),
        ],
        pl.BlockSpec((L, dim), lambda s, sc: (s, 0)),
        sds((rows, dim), BF),
        [],
        (int(1e9), int(1e7)),
        "input_grad",
    )(sc, dn, hr, tok, cot, gain)

    if fast:
        ig, v1r, got = meet(ig, v1r, got)
        v1 = summed(v1[:, 0], v1r)
        both = both + got
        bit = 4
        while 2 * bit < dpcount:
            both = both + flip(both, "dp", bit)
            v1 = reduce_dp(v1, bit)
            bit *= 2
        got = flip(both, "dp", bit)
        v1 = v1.reshape((2,) + v1.shape[1:]) if v1.shape[0] == 2 else v1
        v1a, v1r = v1[0], flip(v1[1], "dp", bit)
    else:
        both = lax.psum(both + got, "dp")
        v1 = jnp.concatenate([vx, summed(vb[..., :128], px)], axis=-1)
        grad1 = reduce_slow(v1)
    if fast:
        last = call(
            k11_body,
            (1,),
            [full((shard, 512))] * 2 + [full((24, cols))] * 2,
            [full(shape) for shape in FINAL_SHAPES(dim, cols, heads, state, shard, tcount)],
            [
                sds(shape, F32)
                for shape in FINAL_SHAPES(dim, cols, heads, state, shard, tcount)
            ],
            [vmem((shard, 512), F32), vmem((24, cols), F32)],
            (int(1e6), int(1e6)),
            "last_sums",
        )(sc, v1a, v1r, both, got)
        (
            ngain, grad_w_x, grad_w_bc, grad_w_dt, grad_conv_x, grad_bias_x, grad_conv_bc,
            grad_bias_bc, grad_dt_bias, grad_a_log, grad_skip, grad_out_gain,
        ) = last
        grad_w_dt = grad_w_dt.T
    else:
        own, flat = both[:16], both[16:]
        ngain = flat[5:7].reshape(dim)
        grad_w_x = grad1[:, :cols]
        parts = grad1[:, cols : cols + bq].reshape(tcount, shard // tcount, bq)
        got = lax.all_to_all(parts, "tensor", split_axis=0, concat_axis=0, tiled=True)
        grad_w_bc = jnp.swapaxes(got, 0, 1).reshape(shard // tcount, bq * tcount)
        grad_w_dt = grad1[:, cols + bq : cols + bq + heads]
        grad_conv_x, grad_bias_x, grad_out_gain = own[:4], own[4], own[5]
        grad_conv_bc, grad_bias_bc = flat[:4, : 2 * state], flat[4, : 2 * state]
        grad_dt_bias, grad_a_log = own[7, :heads], own[8, :heads]
        grad_skip = own[6].reshape(heads, cols // heads).sum(axis=1)

    return (
        out.reshape(tokens.shape),
        ig.reshape(tokens.shape),
        ngain,
        grad_w_z,
        grad_w_x,
        grad_w_bc,
        grad_w_dt,
        grad_conv_x,
        grad_bias_x,
        grad_conv_bc,
        grad_bias_bc,
        grad_dt_bias,
        grad_a_log,
        grad_skip,
        grad_out_gain,
        grad_w_out,
    )


def solution(mesh):
    return jax.shard_map(
        per_device,
        mesh=mesh,
        in_specs=(
            P("dp", "tensor", None), P("dp", None), P("dp", "tensor", None), P(),
            P("dp", "tensor"), P("dp", "tensor"), P("dp", None), P("dp", "tensor"),
            P(None, "tensor"), P("tensor"), P(), P(),
            P("tensor"), P("tensor"), P("tensor"), P("tensor"), P("dp", "tensor"),
        ),
        out_specs=(
            P("dp", "tensor", None), P("dp", "tensor", None), P(),
            P("dp", "tensor"), P("dp", "tensor"), P(("dp", "tensor"), None), P("dp", "tensor"),
            P(None, "tensor"), P("tensor"), P(), P(),
            P("tensor"), P("tensor"), P("tensor"), P("tensor"), P("dp", "tensor"),
        ),
        check_vma=False,
    )
```
